32 devices in a mesh: groups: 2 (over y), clus: 4 (over z), sub: 2 (over x), rhs: 2 (over core).
Axes of the slice: x: 2, y: 2, z: 4, core: 2. Of those that a mesh axis runs over, the one named last changes fastest.
Arguments:
- positions: bfloat16 [128, 3, 512], P(('groups', 'clus'), None, 'sub'), parts along dimension 0, may hold values from -1 to 1
- areas: bfloat16 [128, 512], P(('groups', 'clus'), 'sub'), parts along dimension 0, may hold values from 0.5 to 2
- density: bfloat16 [128, 64, 512], P(('groups', 'clus'), 'rhs', 'sub'), parts along dimension 0, may hold values from -6 to 6
- cotangent: bfloat16 [128, 64, 512], P(('groups', 'clus'), 'rhs', 'sub'), parts along dimension 0, may hold values from -0.59765625 to 0.59765625
- matching: int32 [5, 128], P(None, 'groups'), parts along dimension 1, may hold values from 0 to 63, as said below
- connect: int32 [128, 4, 512], P(('groups', 'clus'), None, 'sub'), parts along dimension 0, may hold values from 0 to 32767, as said below
Outputs:
- potential: bfloat16 [128, 64, 512], P(('groups', 'clus'), 'rhs', 'sub'), parts along dimension 0
- node_grad: float32 [3, 65536], P(None, ('groups', 'clus', 'sub')), parts along dimension 1
The draws below stay inside these ranges and needn't reach their ends.
There are 2 independent parts, one for each index of `groups`. The reference program is written for one: setup_inputs(seed, part) draws one part's arguments, and reference() takes and returns one part's arrays. A program takes and returns all parts, laid end to end along the dimension named above; each array names one. Nothing has to cross between parts.
Inputs may be any that keep to these rules, and one draw needn't show every extreme that they name: matching[r, c] is the cluster paired with cluster c in round r: the pairing is mutual, and never pairs two clusters of the same index of clus (c // 16). In each round, of the 16 clusters of one index of clus at most 6 are paired with clusters of any one other index, and every index reaches 6 with some other index. `connect`: the corners of panel a of cluster c are (c * 512 + a + t + k) mod 32768 for k = 0, 1, 32, 33 in this order, with one whole number t of -8 to 8 for each panel.
All inputs are finite; a program needn't handle non-finite values.
Results may differ from the reference program's by a relative error of at most 0.0051.
Values may be sent and summed in bfloat16 or wider, within the bound.
No kernel may reach another device: no remote copies, remote signals or barrier semaphores. Data moves between devices by JAX's collectives and lax.ppermute only.
A program may use at most 64 MiB of HBM per device.

```python
import math
import jax
import jax.numpy as jnp
from jax import lax

CP = 512
RHS = 64
ROUNDS = 5
CL_DEV = 16
CLUSTERS = 64
NODES = 32768
N_CLUS = 4


def draw_matching(key, part):
    half_count = CL_DEV // 2
    rows_out = []
    for round_idx in range(ROUNDS):
        round_key = jax.random.fold_in(key, round_idx)
        mask_values = jax.random.permutation(jax.random.fold_in(round_key, 1), N_CLUS - 1).astype(jnp.int32) + 1
        slot_index = jnp.arange(half_count, dtype=jnp.int32) % (N_CLUS - 1)
        flip_masks = mask_values[slot_index]
        order_keys = jax.random.split(jax.random.fold_in(round_key, 2), N_CLUS)
        orders = jax.vmap(lambda sub_key: jax.random.permutation(sub_key, CL_DEV))(order_keys).astype(jnp.int32)
        devices = jnp.arange(N_CLUS, dtype=jnp.int32)
        mate_device = devices[:, None] ^ flip_masks[None, :]
        even_local = orders[:, 0::2]
        odd_local = orders[:, 1::2]
        pair_index = jnp.arange(half_count, dtype=jnp.int32)[None, :]
        even_global = devices[:, None] * CL_DEV + even_local
        odd_global = devices[:, None] * CL_DEV + odd_local
        mate_odd = mate_device * CL_DEV + odd_local[mate_device, pair_index]
        mate_even = mate_device * CL_DEV + even_local[mate_device, pair_index]
        pairing = jnp.zeros((N_CLUS * CL_DEV,), jnp.int32)
        pairing = pairing.at[even_global.reshape(-1)].set(mate_odd.reshape(-1))
        pairing = pairing.at[odd_global.reshape(-1)].set(mate_even.reshape(-1))
        rows_out.append(pairing)
    return jnp.stack(rows_out, axis=0).astype(jnp.int32)


def draw_connect(key, part):
    cluster_ids = jnp.arange(CLUSTERS, dtype=jnp.int32)[:, None, None]
    panel_ids = jnp.arange(CP, dtype=jnp.int32)[None, None, :]
    corner_offsets = jnp.array([0, 1, 32, 33], dtype=jnp.int32)[None, :, None]
    jitter = jax.random.randint(jax.random.fold_in(key, 7), (CLUSTERS, 1, CP), -8, 9).astype(jnp.int32)
    jitter = jitter.at[0, 0, 0].set(-1).at[0, 0, 1].set(-1)
    node_ids = (cluster_ids * CP + panel_ids + jitter + corner_offsets) % NODES
    return node_ids.astype(jnp.int32)


def block_scale(rng, shape, pieces, smallest, high):
    loudness, own = 1.0, jax.random.fold_in(rng, 6)
    for axis_at, blocks in pieces:
        heights = jnp.exp(jax.random.uniform(jax.random.fold_in(own, axis_at), (blocks,), jnp.float32, smallest / len(pieces), high / len(pieces)))
        loudness = loudness * jnp.repeat(heights, shape[axis_at] // blocks).reshape([-1 if axis == axis_at else 1 for axis in range(len(shape))])
    return loudness


def gaussian(key, extent, spread, bound, cuts=(), kind=jnp.bfloat16):
    values = spread * jax.random.normal(key, extent, jnp.float32)
    if cuts:
        values = values * block_scale(key, extent, cuts, -0.22, 0.18)
    return jnp.clip(values, -bound, bound).astype(kind)


def setup_inputs(seed: int = 0, part: int = 0) -> dict:
    key_of = jax.random.split(jax.random.key(seed), 7)
    part_keys = jax.random.split(jax.random.fold_in(key_of[6], part), 7)
    positions = jnp.clip(jax.random.uniform(part_keys[0], (CLUSTERS, 3, CP), jnp.float32, -1.0, 1.0) * block_scale(part_keys[0], (CLUSTERS, 3, CP), ((0, 4), (2, 2)), -0.4, 0.0), -1.0, 1.0).astype(jnp.bfloat16)
    areas = jnp.clip(jnp.exp(math.log(2.0) - 1.3862944 * jax.random.uniform(part_keys[1], (CLUSTERS, CP), jnp.float32) ** block_scale(part_keys[1], (CLUSTERS, CP), ((0, 4), (1, 2)), -0.2, 0.2)), 0.5, 2.0).astype(jnp.bfloat16)
    density = gaussian(part_keys[2], (CLUSTERS, RHS, CP), 1.0, 6.0, ((0, 4), (1, 2), (2, 2)))
    cotangent = gaussian(part_keys[3], (CLUSTERS, RHS, CP), 0.1, 0.59765625, ((0, 4), (1, 2), (2, 2)))
    matching = draw_matching(jax.random.fold_in(jax.random.fold_in(key_of[6], part), 71), part)
    connect = draw_connect(jax.random.fold_in(jax.random.fold_in(key_of[6], part), 71), part)
    return dict(positions=positions, areas=areas, density=density, cotangent=cotangent, matching=matching, connect=connect)


core_radius = 0.25

def block_terms(own_pos, mate_pos, own_area, mate_area, own_dens, mate_dens, own_cot, mate_cot):
    here = own_pos.astype(jnp.float32)
    there = mate_pos.astype(jnp.float32)
    distance_sq = jnp.zeros((here.shape[1], there.shape[1]), jnp.float32)
    for coord in range(3):
        distance_sq = distance_sq + (here[coord][:, None] - there[coord][None, :]) ** 2
    inverse = 1.0 / jnp.sqrt(distance_sq + core_radius * core_radius)
    factor = CP ** (-0.5)
    weight_there = factor * mate_area.astype(jnp.float32)
    weight_here = factor * own_area.astype(jnp.float32)
    kernel = (weight_there[None, :] * inverse).astype(jnp.bfloat16)
    potential_term = jnp.dot(mate_dens, kernel.T, preferred_element_type=jnp.float32)
    inv_cube = inverse * inverse * inverse
    product = jnp.dot(own_cot.T, mate_dens, preferred_element_type=jnp.float32)
    weighted = weight_there[None, :] * inv_cube * product
    augmented = jnp.concatenate([there, jnp.ones((1, there.shape[1]), jnp.float32)], axis=0)
    target_sums = jnp.dot(augmented, weighted.T, precision=lax.Precision.HIGHEST)
    product_two = jnp.dot(own_dens.T, mate_cot, preferred_element_type=jnp.float32)
    weighted_two = weight_here[:, None] * inv_cube * product_two
    source_sums = jnp.dot(augmented, weighted_two.T, precision=lax.Precision.HIGHEST)
    gradient = target_sums[:3] - here * target_sums[3:4] + (source_sums[:3] - here * source_sums[3:4])
    return (potential_term, gradient)

def reference(positions, areas, density, cotangent, matching, connect):
    cluster_total = positions.shape[0]
    potential_sum = jnp.zeros(density.shape, jnp.float32)
    panel_grad = jnp.zeros((cluster_total, 3, positions.shape[2]), jnp.float32)
    for round_idx in range(ROUNDS):
        pairing_row = matching[round_idx]

        def cluster_terms(cluster):
            partner_idx = pairing_row[cluster]
            return block_terms(positions[cluster], positions[partner_idx], areas[cluster], areas[partner_idx], density[cluster], density[partner_idx], cotangent[cluster], cotangent[partner_idx])
        potential_term, gradient = lax.map(cluster_terms, jnp.arange(cluster_total, dtype=jnp.int32))
        potential_sum = potential_sum + potential_term
        panel_grad = panel_grad + gradient
    potential = potential_sum.astype(jnp.bfloat16)
    node_ids = connect.reshape(-1)
    node_rows = []
    for coord in range(3):
        values = jnp.broadcast_to(0.25 * panel_grad[:, coord][:, None, :], connect.shape).reshape(-1)
        node_rows.append(jax.ops.segment_sum(values, node_ids, num_segments=NODES))
    node_grad = jnp.stack(node_rows, axis=0)
    return (potential, node_grad)
```

```python
import functools

import jax
import jax.numpy as jnp
from jax import lax
from jax.experimental import pallas as pl
from jax.experimental.pallas import tpu as pltpu
from jax.sharding import PartitionSpec as P

CP = 512
ROUNDS = 5

core_radius = 0.25
jitter_reach = 8
LANES = 128
AUG = 16


def shifted(value, axis, steps):
    count = lax.axis_size(axis)
    pairs = [(source, (source + steps) % count) for source in range(count)]
    return lax.ppermute(value, axis, pairs)


def three_parts(value):
    parts = []
    for _ in range(3):
        part = value.astype(jnp.bfloat16).astype(jnp.float32)
        parts.append(part)
        value = value - part
    return parts


def pick(index, choices):
    out = choices[0]
    for place in range(1, len(choices)):
        out = jnp.where(index == place, choices[place], out)
    return out


def own_kernel(pos_ref, aug_ref, aug32):
    pos = [pos_ref[coord].astype(jnp.float32) for coord in range(3)]
    square = pos[0] * pos[0] + pos[1] * pos[1] + pos[2] * pos[2] + core_radius * core_radius
    ones = jnp.ones_like(square)
    rows = [-2.0 * value for value in pos] + three_parts(square) + [ones] * 3
    aug32[...] = jnp.zeros(aug32.shape, jnp.float32)
    for row, value in enumerate(rows):
        aug32[:, row, :] = value
    aug_ref[...] = aug32[...].astype(jnp.bfloat16)


def step_kernel(step, cap, first, *refs):
    if first:
        items, source_ref, cot_ref, own_ref, pos_ref = refs[:5]
        refs = refs[5:]
    else:
        items, source_ref, cot_ref, own_ref, pos_ref, pot_in, grad_in = refs[:7]
        refs = refs[7:]
    pot_ref, grad_ref, back_ref, aug32, aug, aug_t, dens_t, weight, target, back = refs
    clusters, width, panels = cot_ref.shape
    quarter = source_ref.shape[1]
    base = clusters * width

    there = [
        source_ref[base + coord * clusters : base + (coord + 1) * clusters, :].astype(jnp.float32)
        for coord in range(3)
    ]
    area = source_ref[base + 3 * clusters : base + 4 * clusters, :].astype(jnp.float32)
    square = there[0] * there[0] + there[1] * there[1] + there[2] * there[2]
    ones = jnp.ones_like(square)
    aug32[...] = jnp.zeros(aug32.shape, jnp.float32)
    for row, value in enumerate(there + [ones] * 3 + three_parts(square)):
        aug32[:, row, :] = value
    weight_t = (CP ** (-0.5) * area).T
    for cluster in range(clusters):
        rows = aug32[cluster]
        aug[cluster] = rows.astype(jnp.bfloat16)
        aug_t[cluster] = rows.T.astype(jnp.bfloat16)
        dens = source_ref[cluster * width : (cluster + 1) * width, :]
        dens_t[cluster] = dens.T
        weight[cluster] = jnp.broadcast_to(weight_t[:, cluster : cluster + 1], (quarter, LANES))
    target[...] = jnp.zeros(target.shape, jnp.float32)
    back[...] = jnp.zeros(back.shape, jnp.float32)
    if first:
        pot_ref[...] = jnp.zeros(pot_ref.shape, jnp.float32)
    else:
        pot_ref[...] = pot_in[...]

    chunk = 256

    def one_item(place):
        code = items[step * (cap + 1) + 1 + place]
        here = code // clusters
        mate = code % clusters
        mate_dens = source_ref[pl.ds(pl.multiple_of(mate * width, width), width), :]
        mate_dens_t = dens_t[mate]
        mate_aug_t = aug_t[mate]
        mate_aug = aug[mate]
        mate_weight = weight[mate]
        mate_weight = jnp.concatenate([mate_weight] * (chunk // LANES), axis=1)
        total = jnp.zeros((AUG, quarter), jnp.float32)
        for start in range(0, panels, chunk):
            cols = slice(start, start + chunk)
            own = own_ref[here, :, cols]
            distance_sq = jnp.dot(mate_aug_t, own, preferred_element_type=jnp.float32)
            product = jnp.dot(mate_dens_t, cot_ref[here, :, cols], preferred_element_type=jnp.float32)
            inverse = lax.rsqrt(distance_sq)
            kernel = mate_weight * inverse
            weighted = ((inverse * inverse) * (kernel * product)).astype(jnp.bfloat16)
            pot_ref[here, :, cols] += jnp.dot(
                mate_dens, kernel.astype(jnp.bfloat16), preferred_element_type=jnp.float32
            )
            target[here, :, cols] += jnp.dot(
                mate_aug, weighted, preferred_element_type=jnp.float32
            )[:8]
            total = total + lax.dot_general(
                own, weighted, (((1,), (1,)), ((), ())), preferred_element_type=jnp.float32
            )
        back[mate] += total[:8]

    count = items[step * (cap + 1)]

    @pl.loop(0, count // 2)
    def _(pair):
        one_item(2 * pair)
        one_item(2 * pair + 1)

    @pl.when(count % 2 == 1)
    def _():
        one_item(count - 1)

    for coord in range(3):
        value = target[:, coord, :] - pos_ref[coord].astype(jnp.float32) * target[:, 3, :]
        if not first:
            value = value + grad_in[coord]
        grad_ref[coord] = value
        back_ref[coord] = -0.5 * back[:, coord, :] - there[coord] * back[:, 6, :]


def run_step(step, cap, items, source, cot, own, pos, carried):
    clusters, width, panels = cot.shape
    quarter = source.shape[1]
    first = carried is None
    vmem = pl.BlockSpec(memory_space=pltpu.VMEM)
    smem = pl.BlockSpec(memory_space=pltpu.SMEM)
    operands = (items, source, cot, own, pos) + (() if first else carried)
    pairs = cap * panels * quarter
    return pl.pallas_call(
        functools.partial(step_kernel, step, cap, first),
        out_shape=(
            jax.ShapeDtypeStruct((clusters, width, panels), jnp.float32),
            jax.ShapeDtypeStruct((3, clusters, panels), jnp.float32),
            jax.ShapeDtypeStruct((3, clusters, quarter), jnp.float32),
        ),
        in_specs=[smem] + [vmem] * (len(operands) - 1),
        out_specs=(vmem, vmem, vmem),
        scratch_shapes=[
            pltpu.VMEM((clusters, AUG, quarter), jnp.float32),
            pltpu.VMEM((clusters, AUG, quarter), jnp.bfloat16),
            pltpu.VMEM((clusters, quarter, AUG), jnp.bfloat16),
            pltpu.VMEM((clusters, quarter, width), jnp.bfloat16),
            pltpu.VMEM((clusters, quarter, LANES), jnp.float32),
            pltpu.VMEM((clusters, 8, panels), jnp.float32),
            pltpu.VMEM((clusters, 8, quarter), jnp.float32),
        ],
        compiler_params=pltpu.CompilerParams(vmem_limit_bytes=32 * 1024 * 1024),
        cost_estimate=pl.CostEstimate(
            flops=2 * pairs * (2 * width + 3 * AUG), bytes_accessed=6 * 2**20, transcendentals=pairs
        ),
        name=f"near_field_{step}",
    )(*operands)


def node_kernel(grad_ref, jitter_ref, main_ref, rims_ref):
    clusters, panels = jitter_ref.shape
    wide = panels + 2 * LANES
    jitter = jitter_ref[...]
    side = jnp.zeros((clusters, LANES), jnp.float32)
    row_at = lax.broadcasted_iota(jnp.int32, (clusters, LANES), 0)
    rims_ref[...] = jnp.zeros(rims_ref.shape, jnp.float32)
    for coord in range(3):
        terms = 0.25 * grad_ref[coord]
        spread = jnp.zeros((clusters, wide), jnp.float32)
        for offset in range(-jitter_reach, jitter_reach + 1):
            masked = jnp.where(jitter == offset, terms, 0.0)
            masked = jnp.concatenate([side, masked, side], axis=1)
            spread = spread + pltpu.roll(masked, offset % wide, 1)
        spread = spread + pltpu.roll(spread, 1, 1)
        spread = spread + pltpu.roll(spread, 32, 1)
        below = spread[:, :LANES]
        above = spread[:, LANES + panels :]
        inner = spread[:, LANES : LANES + panels]
        first = jnp.where(row_at == 0, 0.0, pltpu.roll(above, 1, 0))
        last = jnp.where(row_at == clusters - 1, 0.0, pltpu.roll(below, clusters - 1, 0))
        inner = jnp.concatenate(
            [
                inner[:, :LANES] + first,
                inner[:, LANES : panels - LANES],
                inner[:, panels - LANES :] + last,
            ],
            axis=1,
        )
        for cluster in range(clusters):
            main_ref[coord : coord + 1, cluster * panels : (cluster + 1) * panels] = inner[
                cluster : cluster + 1
            ]
        rims_ref[0, coord : coord + 1, :] = below[:1]
        rims_ref[1, coord : coord + 1, :] = above[clusters - 1 :]


def on_device(positions, areas, density, cotangent, matching, connect):
    clus_count = lax.axis_size("clus")
    sub_count = lax.axis_size("sub")
    rhs_count = lax.axis_size("rhs")
    device = lax.axis_index("clus")
    sub_place = lax.axis_index("sub")
    core = lax.axis_index("rhs")
    clusters, rhs, row_count = density.shape
    panels = row_count * sub_count
    quarter = row_count // rhs_count
    width = rhs * rhs_count
    vmem = pl.BlockSpec(memory_space=pltpu.VMEM)

    def part_of(array, place):
        return pick(
            place % rhs_count,
            [array[..., at * quarter : (at + 1) * quarter] for at in range(rhs_count)],
        )

    blocks = [part_of(density, core)]
    for step in range(1, rhs_count):
        blocks.append(shifted(part_of(density, core + step), "rhs", step))
    by_coord = jnp.transpose(positions, (1, 0, 2))
    placed = jnp.concatenate([by_coord, areas[None]], axis=0)
    source = jnp.concatenate(
        [
            jnp.concatenate(blocks, axis=1).reshape(clusters * width, quarter),
            part_of(placed, core).reshape(4 * clusters, quarter),
        ],
        axis=0,
    )

    per_round = 2 * ((clusters // 2 + clus_count - 2) // (clus_count - 1))
    cap = ROUNDS * per_round
    partners = lax.dynamic_slice_in_dim(matching, device * clusters, clusters, 1).reshape(-1)
    here = jnp.tile(jnp.arange(clusters, dtype=jnp.int32), ROUNDS)
    code = here * clusters + partners % clusters
    behind = (device - partners // clusters) % clus_count
    total_items = ROUNDS * clusters
    order = jnp.arange(total_items, dtype=jnp.int32)
    rank = jnp.sum(
        ((behind[None, :] == behind[:, None]) & (order[None, :] < order[:, None])).astype(jnp.int32),
        axis=1,
    )
    steps = jnp.arange(1, clus_count, dtype=jnp.int32)
    member = behind[None, :] == steps[:, None]
    slots = jnp.arange(cap, dtype=jnp.int32)
    chosen = member[:, None, :] & (rank[None, None, :] == slots[None, :, None])
    listed = jnp.sum(jnp.where(chosen, code[None, None, :], 0), axis=2)
    counts = jnp.sum(member.astype(jnp.int32), axis=1)
    items = jnp.concatenate([counts[:, None], listed], axis=1).reshape(-1)

    cluster_at = jnp.arange(clusters, dtype=jnp.int32)
    first_ids = (device * clusters + cluster_at) * panels
    base_ids = first_ids[:, None] + (
        sub_place * row_count + jnp.arange(row_count, dtype=jnp.int32)
    )[None, :]
    nodes_total = clus_count * clusters * panels
    jitter = (connect[:, 0, :] - base_ids + jitter_reach) % nodes_total - jitter_reach
    local = jnp.concatenate(
        [
            cotangent.reshape(clusters * rhs, row_count),
            by_coord.reshape(3 * clusters, row_count),
            jitter.astype(jnp.bfloat16),
        ],
        axis=0,
    )
    found = [local] + [shifted(local, "sub", step) for step in range(1, sub_count)]
    whole = jnp.concatenate(
        [
            pick((sub_place - place) % sub_count, found)
            for place in range(sub_count)
        ],
        axis=1,
    )
    cot_half = whole[: clusters * rhs].reshape(clusters, rhs, panels)
    cot_blocks = [cot_half] + [shifted(cot_half, "rhs", step) for step in range(1, rhs_count)]
    cot = jnp.concatenate(cot_blocks, axis=1)
    pos = whole[clusters * rhs : clusters * (rhs + 3)].reshape(3, clusters, panels)
    jitter_all = whole[clusters * (rhs + 3) :].astype(jnp.int32)
    own = pl.pallas_call(
        own_kernel,
        out_shape=jax.ShapeDtypeStruct((clusters, AUG, panels), jnp.bfloat16),
        in_specs=[vmem],
        out_specs=vmem,
        scratch_shapes=[pltpu.VMEM((clusters, AUG, panels), jnp.float32)],
        compiler_params=pltpu.CompilerParams(vmem_limit_bytes=16 * 1024 * 1024),
        name="target_rows",
    )(pos)

    carried = None
    returned = jnp.zeros((3, clusters, quarter), jnp.float32)
    for step in range(1, clus_count):
        source = shifted(source, "clus", 1)
        pot, grad, back = run_step(step - 1, cap, items, source, cot, own, pos, carried)
        carried = (pot, grad)
        returned = returned + shifted(back, "clus", -step)

    at = sub_place * row_count + core * quarter
    own_part = lax.dynamic_slice_in_dim(grad, at, quarter, 2) + returned
    grad = lax.dynamic_update_slice_in_dim(grad, own_part, at, 2)
    share = clusters // sub_count

    def share_of(array, place):
        return pick(
            place % sub_count,
            [array[..., at * share : (at + 1) * share, :] for at in range(sub_count)],
        )

    summed = share_of(grad, sub_place)
    for step in range(1, sub_count):
        summed = summed + shifted(share_of(grad, sub_place + step), "sub", step)
    gathered = summed
    for step in range(1, rhs_count):
        gathered = gathered + shifted(summed, "rhs", step)
    main, rims = pl.pallas_call(
        node_kernel,
        out_shape=(
            jax.ShapeDtypeStruct((3, share * panels), jnp.float32),
            jax.ShapeDtypeStruct((2, 8, LANES), jnp.float32),
        ),
        in_specs=[vmem, vmem],
        out_specs=(vmem, vmem),
        compiler_params=pltpu.CompilerParams(vmem_limit_bytes=16 * 1024 * 1024),
        name="node_terms",
    )(gathered, share_of(jitter_all, sub_place))
    from_above = shifted(rims[0], ("clus", "sub"), -1)[:3]
    from_below = shifted(rims[1], ("clus", "sub"), 1)[:3]
    node_grad = jnp.concatenate(
        [main[:, :LANES] + from_below, main[:, LANES:-LANES], main[:, -LANES:] + from_above], axis=1
    )

    half = pot[:, :rhs]
    for step in range(1, rhs_count):
        half = half + shifted(pot[:, step * rhs : (step + 1) * rhs], "rhs", -step)

    def panels_of(array, place):
        return pick(
            place % sub_count,
            [array[..., at * row_count : (at + 1) * row_count] for at in range(sub_count)],
        )

    potential = panels_of(half, sub_place)
    for step in range(1, sub_count):
        potential = potential + shifted(panels_of(half, sub_place + step), "sub", step)
    return (potential.astype(jnp.bfloat16), node_grad)


def solution(mesh):
    placed = (
        P(("groups", "clus"), None, "sub"),
        P(("groups", "clus"), "sub"),
        P(("groups", "clus"), "rhs", "sub"),
        P(("groups", "clus"), "rhs", "sub"),
        P(None, "groups"),
        P(("groups", "clus"), None, "sub"),
    )
    return jax.shard_map(
        on_device,
        mesh=mesh,
        in_specs=placed,
        out_specs=(P(("groups", "clus"), "rhs", "sub"), P(None, ("groups", "clus", "sub"))),
        check_vma=False,
    )
```

```python
import functools

import jax
import jax.numpy as jnp
from jax import lax
from jax.experimental import pallas as pl
from jax.experimental.pallas import tpu as pltpu
from jax.sharding import PartitionSpec as P

CP = 512
ROUNDS = 5

core_radius = 0.25
jitter_reach = 8
LANES = 128
AUG = 16


def shifted(value, axis, steps):
    count = lax.axis_size(axis)
    pairs = [(source, (source + steps) % count) for source in range(count)]
    return lax.ppermute(value, axis, pairs)


def three_parts(value):
    parts = []
    for _ in range(3):
        part = value.astype(jnp.bfloat16).astype(jnp.float32)
        parts.append(part)
        value = value - part
    return parts


def pick(index, choices):
    out = choices[0]
    for place in range(1, len(choices)):
        out = jnp.where(index == place, choices[place], out)
    return out


def own_kernel(pos_ref, aug_ref, aug32):
    pos = [pos_ref[coord].astype(jnp.float32) for coord in range(3)]
    square = pos[0] * pos[0] + pos[1] * pos[1] + pos[2] * pos[2] + core_radius * core_radius
    ones = jnp.ones_like(square)
    rows = [-2.0 * value for value in pos] + three_parts(square) + [ones] * 3
    aug32[...] = jnp.zeros(aug32.shape, jnp.float32)
    for row, value in enumerate(rows):
        aug32[:, row, :] = value
    aug_ref[...] = aug32[...].astype(jnp.bfloat16)


def step_kernel(step, length, first, last, *refs):
    items, source_ref, cot_ref, own_ref = refs[:4]
    refs = refs[4:]
    if not first:
        acc_in = refs[0]
        refs = refs[1:]
    if last:
        pos_ref, pot_ref, pot_out_ref, grad_ref, back_ref, acc = refs[:6]
        refs = refs[6:]
    else:
        acc, back_ref = refs[:2]
        refs = refs[2:]
    aug32, aug_t, dens_t, left, weight, back, dist_a, dist_b, prod_a, prod_b, both_a, both_b = refs
    clusters, width, panels = cot_ref.shape
    quarter = source_ref.shape[1]
    base = clusters * width

    there = [
        source_ref[base + coord * clusters : base + (coord + 1) * clusters, :].astype(jnp.float32)
        for coord in range(3)
    ]
    area = source_ref[base + 3 * clusters : base + 4 * clusters, :].astype(jnp.float32)
    square = there[0] * there[0] + there[1] * there[1] + there[2] * there[2]
    ones = jnp.ones_like(square)
    aug32[...] = jnp.zeros(aug32.shape, jnp.float32)
    for row, value in enumerate(there + [ones] * 3 + three_parts(square)):
        aug32[:, row, :] = value
    weight_t = (CP ** (-0.5) * area).T
    left[...] = jnp.zeros(left.shape, left.dtype)
    for cluster in range(clusters):
        rows = aug32[cluster]
        left[cluster, width:, quarter:] = rows.astype(jnp.bfloat16)
        aug_t[cluster] = rows.T.astype(jnp.bfloat16)
        dens = source_ref[cluster * width : (cluster + 1) * width, :]
        left[cluster, :width, :quarter] = dens
        dens_t[cluster] = dens.T
        weight[cluster] = jnp.broadcast_to(weight_t[:, cluster : cluster + 1], (quarter, LANES))
    weight[clusters] = jnp.zeros((quarter, LANES), jnp.float32)
    back[...] = jnp.zeros(back.shape, jnp.float32)
    if first:
        acc[...] = jnp.zeros(acc.shape, jnp.float32)
    else:
        acc[...] = acc_in[...]
    dist_b[...] = jnp.ones(dist_b.shape, jnp.float32)
    prod_b[...] = jnp.zeros(prod_b.shape, jnp.float32)
    both_a[...] = jnp.zeros(both_a.shape, both_a.dtype)

    def decoded(place):
        code = items[step * length + place]
        return code // (2 * clusters), code % (2 * clusters)

    def raw(place, dist, prod):
        here, mate = decoded(place)
        mate = mate % clusters
        dist[...] = jnp.dot(aug_t[mate], own_ref[here], preferred_element_type=jnp.float32)
        prod[...] = jnp.dot(dens_t[mate], cot_ref[here], preferred_element_type=jnp.float32)

    def pointwise(place, dist, prod, both):
        _, mate = decoded(place)
        scale = weight[mate]
        for start in range(0, panels, LANES):
            cols = slice(start, start + LANES)
            inverse = lax.rsqrt(dist[:, cols])
            kernel = scale * inverse
            both[:quarter, cols] = kernel.astype(jnp.bfloat16)
            both[quarter:, cols] = ((inverse * inverse) * (kernel * prod[:, cols])).astype(jnp.bfloat16)

    def summed(place, both):
        here, mate = decoded(place)
        mate = mate % clusters
        acc[here] += jnp.dot(left[mate], both[...], preferred_element_type=jnp.float32)
        back[mate] += lax.dot_general(
            own_ref[here],
            both[quarter:, :],
            (((1,), (1,)), ((), ())),
            preferred_element_type=jnp.float32,
        )[:8]

    @pl.loop(0, items[step * length])
    def _(pair):
        turn = 2 * pair + 1
        summed(turn, both_a)
        pointwise(turn + 1, dist_b, prod_b, both_b)
        raw(turn + 2, dist_a, prod_a)
        summed(turn + 1, both_b)
        pointwise(turn + 2, dist_a, prod_a, both_a)
        raw(turn + 3, dist_b, prod_b)

    for coord in range(3):
        back_ref[coord] = -0.5 * back[:, coord, :] - there[coord] * back[:, 6, :]
    if last:
        for coord in range(3):
            grad_ref[coord] = (
                acc[:, width + coord, :]
                - pos_ref[coord].astype(jnp.float32) * acc[:, width + 3, :]
            )
        rhs = pot_ref.shape[1]
        pot_ref[...] = acc[:, :rhs, :]
        pot_out_ref[...] = acc[:, rhs:width, :].astype(jnp.bfloat16)


def run_step(step, length, items, source, cot, own, pos, rhs, carried, last):
    clusters, width, panels = cot.shape
    quarter = source.shape[1]
    first = carried is None
    vmem = pl.BlockSpec(memory_space=pltpu.VMEM)
    smem = pl.BlockSpec(memory_space=pltpu.SMEM)
    operands = (items, source, cot, own)
    if not first:
        operands += (carried,)
    acc_shape = (clusters, width + AUG, panels)
    back_shape = jax.ShapeDtypeStruct((3, clusters, quarter), jnp.float32)
    scratch = [
        pltpu.VMEM((clusters, AUG, quarter), jnp.float32),
        pltpu.VMEM((clusters, quarter, AUG), jnp.bfloat16),
        pltpu.VMEM((clusters, quarter, width), jnp.bfloat16),
        pltpu.VMEM((clusters, width + AUG, 2 * quarter), jnp.bfloat16),
        pltpu.VMEM((clusters + 1, quarter, LANES), jnp.float32),
        pltpu.VMEM((clusters, 8, quarter), jnp.float32),
    ]
    scratch += [pltpu.VMEM((quarter, panels), jnp.float32)] * 4
    scratch += [pltpu.VMEM((2 * quarter, panels), jnp.bfloat16)] * 2
    if last:
        operands += (pos,)
        out_shape = (
            jax.ShapeDtypeStruct((clusters, rhs, panels), jnp.float32),
            jax.ShapeDtypeStruct((clusters, width - rhs, panels), jnp.bfloat16),
            jax.ShapeDtypeStruct((3, clusters, panels), jnp.float32),
            back_shape,
        )
        scratch = [pltpu.VMEM(acc_shape, jnp.float32)] + scratch
    else:
        out_shape = (jax.ShapeDtypeStruct(acc_shape, jnp.float32), back_shape)
    pairs = (length - 6) * panels * quarter
    return pl.pallas_call(
        functools.partial(step_kernel, step, length, first, last),
        out_shape=out_shape,
        in_specs=[smem] + [vmem] * (len(operands) - 1),
        out_specs=(vmem,) * len(out_shape),
        scratch_shapes=scratch,
        compiler_params=pltpu.CompilerParams(vmem_limit_bytes=32 * 1024 * 1024),
        cost_estimate=pl.CostEstimate(
            flops=2 * pairs * (2 * width + 3 * AUG), bytes_accessed=6 * 2**20, transcendentals=pairs
        ),
        name=f"near_field_{step}",
    )(*operands)


def node_kernel(grad_ref, jitter_ref, main_ref, rims_ref):
    clusters, panels = jitter_ref.shape
    wide = panels + 2 * LANES
    jitter = jitter_ref[...]
    side = jnp.zeros((clusters, LANES), jnp.float32)
    row_at = lax.broadcasted_iota(jnp.int32, (clusters, LANES), 0)
    rims_ref[...] = jnp.zeros(rims_ref.shape, jnp.float32)
    for coord in range(3):
        terms = 0.25 * grad_ref[coord]
        spread = jnp.zeros((clusters, wide), jnp.float32)
        for offset in range(-jitter_reach, jitter_reach + 1):
            masked = jnp.where(jitter == offset, terms, 0.0)
            masked = jnp.concatenate([side, masked, side], axis=1)
            spread = spread + pltpu.roll(masked, offset % wide, 1)
        spread = spread + pltpu.roll(spread, 1, 1)
        spread = spread + pltpu.roll(spread, 32, 1)
        below = spread[:, :LANES]
        above = spread[:, LANES + panels :]
        inner = spread[:, LANES : LANES + panels]
        first = jnp.where(row_at == 0, 0.0, pltpu.roll(above, 1, 0))
        last = jnp.where(row_at == clusters - 1, 0.0, pltpu.roll(below, clusters - 1, 0))
        inner = jnp.concatenate(
            [
                inner[:, :LANES] + first,
                inner[:, LANES : panels - LANES],
                inner[:, panels - LANES :] + last,
            ],
            axis=1,
        )
        for cluster in range(clusters):
            main_ref[coord : coord + 1, cluster * panels : (cluster + 1) * panels] = inner[
                cluster : cluster + 1
            ]
        rims_ref[0, coord : coord + 1, :] = below[:1]
        rims_ref[1, coord : coord + 1, :] = above[clusters - 1 :]


def on_device(positions, areas, density, cotangent, matching, connect):
    clus_count = lax.axis_size("clus")
    sub_count = lax.axis_size("sub")
    rhs_count = lax.axis_size("rhs")
    device = lax.axis_index("clus")
    sub_place = lax.axis_index("sub")
    core = lax.axis_index("rhs")
    clusters, rhs, row_count = density.shape
    panels = row_count * sub_count
    quarter = row_count // rhs_count
    width = rhs * rhs_count
    vmem = pl.BlockSpec(memory_space=pltpu.VMEM)

    def part_of(array, place):
        return pick(
            place % rhs_count,
            [array[..., at * quarter : (at + 1) * quarter] for at in range(rhs_count)],
        )

    blocks = [part_of(density, core)]
    for step in range(1, rhs_count):
        blocks.append(shifted(part_of(density, core + step), "rhs", step))
    by_coord = jnp.transpose(positions, (1, 0, 2))
    placed = jnp.concatenate([by_coord, areas[None]], axis=0)
    source = jnp.concatenate(
        [
            jnp.concatenate(blocks, axis=1).reshape(clusters * width, quarter),
            part_of(placed, core).reshape(4 * clusters, quarter),
        ],
        axis=0,
    )

    per_round = 2 * ((clusters // 2 + clus_count - 2) // (clus_count - 1))
    cap = ROUNDS * per_round
    partners = lax.dynamic_slice_in_dim(matching, device * clusters, clusters, 1).reshape(-1)
    here = jnp.tile(jnp.arange(clusters, dtype=jnp.int32), ROUNDS)
    code = here * (2 * clusters) + partners % clusters
    behind = (device - partners // clusters) % clus_count
    total_items = ROUNDS * clusters
    order = jnp.arange(total_items, dtype=jnp.int32)
    rank = jnp.sum(
        ((behind[None, :] == behind[:, None]) & (order[None, :] < order[:, None])).astype(jnp.int32),
        axis=1,
    )
    steps = jnp.arange(1, clus_count, dtype=jnp.int32)
    member = behind[None, :] == steps[:, None]
    slots = jnp.arange(cap, dtype=jnp.int32)
    chosen = member[:, None, :] & (rank[None, None, :] == slots[None, :, None])
    listed = jnp.sum(jnp.where(chosen, code[None, None, :] - clusters, 0), axis=2) + clusters
    turns = (jnp.sum(member.astype(jnp.int32), axis=1) + 3) // 2
    length = cap + 6
    items = jnp.pad(listed, ((0, 0), (3, 3)), constant_values=clusters)
    items = jnp.concatenate([turns[:, None], items[:, 1:]], axis=1).reshape(-1)

    cluster_at = jnp.arange(clusters, dtype=jnp.int32)
    first_ids = (device * clusters + cluster_at) * panels
    base_ids = first_ids[:, None] + (
        sub_place * row_count + jnp.arange(row_count, dtype=jnp.int32)
    )[None, :]
    nodes_total = clus_count * clusters * panels
    jitter = (connect[:, 0, :] - base_ids + jitter_reach) % nodes_total - jitter_reach
    local = jnp.concatenate(
        [
            cotangent.reshape(clusters * rhs, row_count),
            by_coord.reshape(3 * clusters, row_count),
            jitter.astype(jnp.bfloat16),
        ],
        axis=0,
    )
    local, source = lax.optimization_barrier((local, source))
    found = [local] + [shifted(local, "sub", step) for step in range(1, sub_count)]
    whole = jnp.concatenate(
        [
            pick((sub_place - place) % sub_count, found)
            for place in range(sub_count)
        ],
        axis=1,
    )
    cot_half = whole[: clusters * rhs].reshape(clusters, rhs, panels)
    cot_blocks = [cot_half] + [shifted(cot_half, "rhs", step) for step in range(1, rhs_count)]
    cot = jnp.concatenate(cot_blocks, axis=1)
    pos = whole[clusters * rhs : clusters * (rhs + 3)].reshape(3, clusters, panels)
    jitter_all = whole[clusters * (rhs + 3) :].astype(jnp.int32)
    own = pl.pallas_call(
        own_kernel,
        out_shape=jax.ShapeDtypeStruct((clusters, AUG, panels), jnp.bfloat16),
        in_specs=[vmem],
        out_specs=vmem,
        scratch_shapes=[pltpu.VMEM((clusters, AUG, panels), jnp.float32)],
        compiler_params=pltpu.CompilerParams(vmem_limit_bytes=16 * 1024 * 1024),
        name="target_rows",
    )(pos)

    carried = None
    backs = []
    for step in range(1, clus_count):
        if step > 2:
            source, backs[step - 3] = lax.optimization_barrier((source, backs[step - 3]))
        source = shifted(source, "clus", 1)
        last = step == clus_count - 1
        results = run_step(step - 1, length, items, source, cot, own, pos, rhs, carried, last)
        if last:
            pot, pot_out, grad, back = results
        else:
            carried, back = results
        backs.append(back)
    returned = jnp.zeros((3, clusters, quarter), jnp.float32)
    for step in range(1, clus_count):
        returned = returned + shifted(backs[step - 1], "clus", -step)

    half = pot
    for step in range(1, rhs_count):
        arrived = shifted(pot_out[:, (step - 1) * rhs : step * rhs], "rhs", -step)
        half = half + arrived.astype(jnp.float32)
    half, returned = lax.optimization_barrier((half, returned))

    def panels_of(array, place):
        return pick(
            place % sub_count,
            [array[..., at * row_count : (at + 1) * row_count] for at in range(sub_count)],
        )

    potential = panels_of(half, sub_place)
    for step in range(1, sub_count):
        sent = panels_of(half, sub_place + step).astype(jnp.bfloat16)
        potential = potential + shifted(sent, "sub", step).astype(jnp.float32)

    at = sub_place * row_count + core * quarter
    own_part = lax.dynamic_slice_in_dim(grad, at, quarter, 2) + returned
    grad = lax.dynamic_update_slice_in_dim(grad, own_part, at, 2)
    share = clusters // sub_count

    def share_of(array, place):
        return pick(
            place % sub_count,
            [array[..., at * share : (at + 1) * share, :] for at in range(sub_count)],
        )

    summed = share_of(grad, sub_place)
    for step in range(1, sub_count):
        summed = summed + shifted(share_of(grad, sub_place + step), "sub", step)
    gathered = summed
    for step in range(1, rhs_count):
        gathered = gathered + shifted(summed, "rhs", step)
    gathered, potential = lax.optimization_barrier((gathered, potential))
    main, rims = pl.pallas_call(
        node_kernel,
        out_shape=(
            jax.ShapeDtypeStruct((3, share * panels), jnp.float32),
            jax.ShapeDtypeStruct((2, 8, LANES), jnp.float32),
        ),
        in_specs=[vmem, vmem],
        out_specs=(vmem, vmem),
        compiler_params=pltpu.CompilerParams(vmem_limit_bytes=16 * 1024 * 1024),
        name="node_terms",
    )(gathered, share_of(jitter_all, sub_place))
    from_above = shifted(rims[0], ("clus", "sub"), -1)[:3]
    from_below = shifted(rims[1], ("clus", "sub"), 1)[:3]
    node_grad = jnp.concatenate(
        [main[:, :LANES] + from_below, main[:, LANES:-LANES], main[:, -LANES:] + from_above], axis=1
    )
    return (potential.astype(jnp.bfloat16), node_grad)


def solution(mesh):
    placed = (
        P(("groups", "clus"), None, "sub"),
        P(("groups", "clus"), "sub"),
        P(("groups", "clus"), "rhs", "sub"),
        P(("groups", "clus"), "rhs", "sub"),
        P(None, "groups"),
        P(("groups", "clus"), None, "sub"),
    )
    return jax.shard_map(
        on_device,
        mesh=mesh,
        in_specs=placed,
        out_specs=(P(("groups", "clus"), "rhs", "sub"), P(None, ("groups", "clus", "sub"))),
        check_vma=False,
    )
```

```python
import functools

import jax
import jax.numpy as jnp
from jax import lax
from jax.experimental import pallas as pl
from jax.experimental.pallas import tpu as pltpu
from jax.sharding import PartitionSpec as P

CP = 512
ROUNDS = 5

core_radius = 0.25
jitter_reach = 8
LANES = 128
AUG = 16


def shifted(value, axis, steps):
    count = lax.axis_size(axis)
    pairs = [(source, (source + steps) % count) for source in range(count)]
    return lax.ppermute(value, axis, pairs)


def moved(value, axes, target):
    counts = [lax.axis_size(axis) for axis in axes]
    pairs = []
    for major in range(counts[0]):
        for minor in range(counts[1]):
            goal = target(major, minor)
            if goal is not None:
                to_major, to_minor = goal[0] % counts[0], goal[1] % counts[1]
                pairs.append((major * counts[1] + minor, to_major * counts[1] + to_minor))
    return lax.ppermute(value, axes, pairs)


def three_parts(value):
    parts = []
    for _ in range(3):
        part = value.astype(jnp.bfloat16).astype(jnp.float32)
        parts.append(part)
        value = value - part
    return parts


def pick(index, choices):
    out = choices[0]
    for place in range(1, len(choices)):
        out = jnp.where(index == place, choices[place], out)
    return out


def own_kernel(pos_ref, aug_ref, aug32):
    pos = [pos_ref[coord].astype(jnp.float32) for coord in range(3)]
    square = pos[0] * pos[0] + pos[1] * pos[1] + pos[2] * pos[2] + core_radius * core_radius
    ones = jnp.ones_like(square)
    rows = [-2.0 * value for value in pos] + three_parts(square) + [ones] * 3
    aug32[...] = jnp.zeros(aug32.shape, jnp.float32)
    for row, value in enumerate(rows):
        aug32[:, row, :] = value
    aug_ref[...] = aug32[...].astype(jnp.bfloat16)


def step_kernel(step, length, rhs, first, last, *refs):
    items, source_ref, cot_ref, own_ref = refs[:4]
    refs = refs[4:]
    if not first:
        acc_in = refs[0]
        refs = refs[1:]
    if last:
        pos_ref, pot_ref, pot_out_ref, grad_ref, back_ref, acc = refs[:6]
        refs = refs[6:]
    else:
        acc, back_ref = refs[:2]
        refs = refs[2:]
    aug32, aug_t, dens_t, left, weight, back, dist_a, dist_b, prod_a, prod_b, both_a, both_b = refs
    clusters, width, panels = cot_ref.shape
    quarter = source_ref.shape[1]
    base = clusters * rhs
    starts = [0] + list(range(base + 4 * clusters, source_ref.shape[0], base))

    there = [
        source_ref[base + coord * clusters : base + (coord + 1) * clusters, :].astype(jnp.float32)
        for coord in range(3)
    ]
    area = source_ref[base + 3 * clusters : base + 4 * clusters, :].astype(jnp.float32)
    square = there[0] * there[0] + there[1] * there[1] + there[2] * there[2]
    ones = jnp.ones_like(square)
    aug32[...] = jnp.zeros(aug32.shape, jnp.float32)
    for row, value in enumerate(there + [ones] * 3 + three_parts(square)):
        aug32[:, row, :] = value
    weight_t = (CP ** (-0.5) * area).T
    left[...] = jnp.zeros(left.shape, left.dtype)
    for cluster in range(clusters):
        rows = aug32[cluster]
        left[cluster, width:, quarter:] = rows.astype(jnp.bfloat16)
        aug_t[cluster] = rows.T.astype(jnp.bfloat16)
        dens = jnp.concatenate(
            [source_ref[at + cluster * rhs : at + (cluster + 1) * rhs, :] for at in starts], axis=0
        )
        left[cluster, :width, :quarter] = dens
        dens_t[cluster] = dens.T
        weight[cluster] = jnp.broadcast_to(weight_t[:, cluster : cluster + 1], (quarter, LANES))
    weight[clusters] = jnp.zeros((quarter, LANES), jnp.float32)
    back[...] = jnp.zeros(back.shape, jnp.float32)
    if first:
        acc[...] = jnp.zeros(acc.shape, jnp.float32)
    else:
        acc[...] = acc_in[...]
    dist_b[...] = jnp.ones(dist_b.shape, jnp.float32)
    prod_b[...] = jnp.zeros(prod_b.shape, jnp.float32)
    both_a[...] = jnp.zeros(both_a.shape, both_a.dtype)

    def decoded(place):
        code = items[step * length + place]
        return code // (2 * clusters), code % (2 * clusters)

    def raw(place, dist, prod):
        here, mate = decoded(place)
        mate = mate % clusters
        dist[...] = jnp.dot(aug_t[mate], own_ref[here], preferred_element_type=jnp.float32)
        prod[...] = jnp.dot(dens_t[mate], cot_ref[here], preferred_element_type=jnp.float32)

    def pointwise(place, dist, prod, both):
        _, mate = decoded(place)
        scale = weight[mate]
        for start in range(0, panels, LANES):
            cols = slice(start, start + LANES)
            inverse = lax.rsqrt(dist[:, cols])
            kernel = scale * inverse
            both[:quarter, cols] = kernel.astype(jnp.bfloat16)
            both[quarter:, cols] = ((inverse * inverse) * (kernel * prod[:, cols])).astype(jnp.bfloat16)

    def summed(place, both):
        here, mate = decoded(place)
        mate = mate % clusters
        acc[here] += jnp.dot(left[mate], both[...], preferred_element_type=jnp.float32)
        back[mate] += lax.dot_general(
            own_ref[here],
            both[quarter:, :],
            (((1,), (1,)), ((), ())),
            preferred_element_type=jnp.float32,
        )[:8]

    @pl.loop(0, items[step * length])
    def _(pair):
        turn = 2 * pair + 1
        summed(turn, both_a)
        pointwise(turn + 1, dist_b, prod_b, both_b)
        raw(turn + 2, dist_a, prod_a)
        summed(turn + 1, both_b)
        pointwise(turn + 2, dist_a, prod_a, both_a)
        raw(turn + 3, dist_b, prod_b)

    for coord in range(3):
        back_ref[coord] = -0.5 * back[:, coord, :] - there[coord] * back[:, 6, :]
    if last:
        for coord in range(3):
            grad_ref[coord] = (
                acc[:, width + coord, :]
                - pos_ref[coord].astype(jnp.float32) * acc[:, width + 3, :]
            )
        pot_ref[...] = acc[:, :rhs, :]
        pot_out_ref[...] = acc[:, rhs:width, :].astype(jnp.bfloat16)


def run_step(step, length, items, source, cot, own, pos, rhs, carried, last):
    clusters, width, panels = cot.shape
    quarter = source.shape[1]
    first = carried is None
    vmem = pl.BlockSpec(memory_space=pltpu.VMEM)
    smem = pl.BlockSpec(memory_space=pltpu.SMEM)
    operands = (items, source, cot, own)
    if not first:
        operands += (carried,)
    acc_shape = (clusters, width + AUG, panels)
    back_shape = jax.ShapeDtypeStruct((3, clusters, quarter), jnp.float32)
    scratch = [
        pltpu.VMEM((clusters, AUG, quarter), jnp.float32),
        pltpu.VMEM((clusters, quarter, AUG), jnp.bfloat16),
        pltpu.VMEM((clusters, quarter, width), jnp.bfloat16),
        pltpu.VMEM((clusters, width + AUG, 2 * quarter), jnp.bfloat16),
        pltpu.VMEM((clusters + 1, quarter, LANES), jnp.float32),
        pltpu.VMEM((clusters, 8, quarter), jnp.float32),
    ]
    scratch += [pltpu.VMEM((quarter, panels), jnp.float32)] * 4
    scratch += [pltpu.VMEM((2 * quarter, panels), jnp.bfloat16)] * 2
    if last:
        operands += (pos,)
        out_shape = (
            jax.ShapeDtypeStruct((clusters, rhs, panels), jnp.float32),
            jax.ShapeDtypeStruct((clusters, width - rhs, panels), jnp.bfloat16),
            jax.ShapeDtypeStruct((3, clusters, panels), jnp.float32),
            back_shape,
        )
        scratch = [pltpu.VMEM(acc_shape, jnp.float32)] + scratch
    else:
        out_shape = (jax.ShapeDtypeStruct(acc_shape, jnp.float32), back_shape)
    pairs = (length - 6) * panels * quarter
    return pl.pallas_call(
        functools.partial(step_kernel, step, length, rhs, first, last),
        out_shape=out_shape,
        in_specs=[smem] + [vmem] * (len(operands) - 1),
        out_specs=(vmem,) * len(out_shape),
        scratch_shapes=scratch,
        compiler_params=pltpu.CompilerParams(vmem_limit_bytes=32 * 1024 * 1024),
        cost_estimate=pl.CostEstimate(
            flops=2 * pairs * (2 * width + 3 * AUG), bytes_accessed=6 * 2**20, transcendentals=pairs
        ),
        name=f"near_field_{step}",
    )(*operands)


def node_kernel(grad_ref, jitter_ref, edge_ref, edge_jitter_ref, main_ref, rims_ref):
    clusters, panels = jitter_ref.shape
    wide = panels + 2 * LANES

    def spread_of(terms, jitter):
        side = jnp.zeros((terms.shape[0], LANES), jnp.float32)
        terms = 0.25 * terms
        spread = jnp.zeros((terms.shape[0], wide), jnp.float32)
        for offset in range(-jitter_reach, jitter_reach + 1):
            masked = jnp.where(jitter == offset, terms, 0.0)
            masked = jnp.concatenate([side, masked, side], axis=1)
            spread = spread + pltpu.roll(masked, offset % wide, 1)
        spread = spread + pltpu.roll(spread, 1, 1)
        return spread + pltpu.roll(spread, 32, 1)

    jitter = jitter_ref[...]
    row_at = lax.broadcasted_iota(jnp.int32, (clusters, LANES), 0)
    rims_ref[...] = jnp.zeros(rims_ref.shape, jnp.float32)
    edge = spread_of(edge_ref[...], edge_jitter_ref[...])
    for coord in range(3):
        spread = spread_of(grad_ref[coord], jitter)
        below = spread[:, :LANES]
        above = spread[:, LANES + panels :]
        inner = spread[:, LANES : LANES + panels]
        before = edge[coord : coord + 1, LANES + panels :]
        after = edge[3 + coord : 4 + coord, :LANES]
        first = jnp.where(row_at == 0, before, pltpu.roll(above, 1, 0))
        last = jnp.where(row_at == clusters - 1, after, pltpu.roll(below, clusters - 1, 0))
        inner = jnp.concatenate(
            [
                inner[:, :LANES] + first,
                inner[:, LANES : panels - LANES],
                inner[:, panels - LANES :] + last,
            ],
            axis=1,
        )
        for cluster in range(clusters):
            main_ref[coord : coord + 1, cluster * panels : (cluster + 1) * panels] = inner[
                cluster : cluster + 1
            ]
        rims_ref[0, coord : coord + 1, :] = below[:1]
        rims_ref[1, coord : coord + 1, :] = above[clusters - 1 :]


def sum_kernel(*refs):
    total = refs[0][...]
    for ref in refs[1:-1]:
        total = total + ref[...].astype(jnp.float32)
    refs[-1][...] = total.astype(jnp.bfloat16)


def on_device(positions, areas, density, cotangent, matching, connect):
    clus_count = lax.axis_size("clus")
    sub_count = lax.axis_size("sub")
    rhs_count = lax.axis_size("rhs")
    device = lax.axis_index("clus")
    sub_place = lax.axis_index("sub")
    core = lax.axis_index("rhs")
    clusters, rhs, row_count = density.shape
    panels = row_count * sub_count
    quarter = row_count // rhs_count
    width = rhs * rhs_count
    vmem = pl.BlockSpec(memory_space=pltpu.VMEM)

    def part_of(array, place):
        return pick(
            place % rhs_count,
            [array[..., at * quarter : (at + 1) * quarter] for at in range(rhs_count)],
        )

    by_coord = jnp.transpose(positions, (1, 0, 2))
    placed = jnp.concatenate([by_coord, areas[None]], axis=0)
    first_part = jnp.concatenate(
        [
            part_of(density, core).reshape(clusters * rhs, quarter),
            part_of(placed, core).reshape(4 * clusters, quarter),
        ],
        axis=0,
    )
    arrived = [shifted(first_part, "clus", 1)]
    for step in range(1, rhs_count):
        other_part = part_of(density, core + step).reshape(clusters * rhs, quarter)
        arrived.append(
            moved(other_part, ("clus", "rhs"), lambda z, c, step=step: (z + 1, c + step))
        )
    source = jnp.concatenate(arrived, axis=0)

    per_round = 2 * ((clusters // 2 + clus_count - 2) // (clus_count - 1))
    cap = ROUNDS * per_round
    partners = lax.dynamic_slice_in_dim(matching, device * clusters, clusters, 1).reshape(-1)
    here = jnp.tile(jnp.arange(clusters, dtype=jnp.int32), ROUNDS)
    code = here * (2 * clusters) + partners % clusters
    behind = (device - partners // clusters) % clus_count
    total_items = ROUNDS * clusters
    order = jnp.arange(total_items, dtype=jnp.int32)
    rank = jnp.sum(
        ((behind[None, :] == behind[:, None]) & (order[None, :] < order[:, None])).astype(jnp.int32),
        axis=1,
    )
    steps = jnp.arange(1, clus_count, dtype=jnp.int32)
    member = behind[None, :] == steps[:, None]
    slots = jnp.arange(cap, dtype=jnp.int32)
    chosen = member[:, None, :] & (rank[None, None, :] == slots[None, :, None])
    listed = jnp.sum(jnp.where(chosen, code[None, None, :] - clusters, 0), axis=2) + clusters
    turns = (jnp.sum(member.astype(jnp.int32), axis=1) + 3) // 2
    length = cap + 6
    items = jnp.pad(listed, ((0, 0), (3, 3)), constant_values=clusters)
    items = jnp.concatenate([turns[:, None], items[:, 1:]], axis=1).reshape(-1)

    cluster_at = jnp.arange(clusters, dtype=jnp.int32)
    first_ids = (device * clusters + cluster_at) * panels
    base_ids = first_ids[:, None] + (
        sub_place * row_count + jnp.arange(row_count, dtype=jnp.int32)
    )[None, :]
    nodes_total = clus_count * clusters * panels
    jitter = (connect[:, 0, :] - base_ids + jitter_reach) % nodes_total - jitter_reach
    local = jnp.concatenate(
        [
            cotangent.reshape(clusters * rhs, row_count),
            by_coord.reshape(3 * clusters, row_count),
            jitter.astype(jnp.bfloat16),
        ],
        axis=0,
    )
    found = [local] + [shifted(local, "sub", step) for step in range(1, sub_count)]
    whole = jnp.concatenate(
        [
            pick((sub_place - place) % sub_count, found)
            for place in range(sub_count)
        ],
        axis=1,
    )
    cot_half = whole[: clusters * rhs].reshape(clusters, rhs, panels)
    cot_blocks = [cot_half] + [shifted(cot_half, "rhs", step) for step in range(1, rhs_count)]
    cot = jnp.concatenate(cot_blocks, axis=1)
    pos = whole[clusters * rhs : clusters * (rhs + 3)].reshape(3, clusters, panels)
    jitter_all = whole[clusters * (rhs + 3) :].astype(jnp.int32)
    own = pl.pallas_call(
        own_kernel,
        out_shape=jax.ShapeDtypeStruct((clusters, AUG, panels), jnp.bfloat16),
        in_specs=[vmem],
        out_specs=vmem,
        scratch_shapes=[pltpu.VMEM((clusters, AUG, panels), jnp.float32)],
        compiler_params=pltpu.CompilerParams(vmem_limit_bytes=16 * 1024 * 1024),
        name="target_rows",
    )(pos)

    carried = None
    backs = []
    returned = jnp.zeros((3, clusters, quarter), jnp.float32)
    for step in range(1, clus_count):
        if step > 1:
            if step > 2:
                source, backs[step - 3] = lax.optimization_barrier((source, backs[step - 3]))
            source = shifted(source, "clus", 1)
            if step > 2:
                home = shifted(backs[step - 3], "clus", 2 - step)
                source, home = lax.optimization_barrier((source, home))
                returned = returned + home
        last = step == clus_count - 1
        results = run_step(step - 1, length, items, source, cot, own, pos, rhs, carried, last)
        if last:
            pot, pot_out, grad, back = results
        else:
            carried, back = results
        backs.append(back)
    for step in range(max(clus_count - 2, 1), clus_count):
        returned = returned + shifted(backs[step - 1], "clus", -step)

    half = pot
    for step in range(1, rhs_count):
        arrived = shifted(pot_out[:, (step - 1) * rhs : step * rhs], "rhs", -step)
        half = half + arrived.astype(jnp.float32)

    def panels_of(array, place):
        return pick(
            place % sub_count,
            [array[..., at * row_count : (at + 1) * row_count] for at in range(sub_count)],
        )

    found = [panels_of(half, sub_place)]
    for step in range(1, sub_count):
        found.append(shifted(panels_of(half, sub_place + step).astype(jnp.bfloat16), "sub", step))
    found, returned = lax.optimization_barrier((found, returned))
    potential = pl.pallas_call(
        sum_kernel,
        out_shape=jax.ShapeDtypeStruct((clusters, rhs, row_count), jnp.bfloat16),
        in_specs=[vmem] * sub_count,
        out_specs=vmem,
        compiler_params=pltpu.CompilerParams(vmem_limit_bytes=16 * 1024 * 1024),
        cost_estimate=pl.CostEstimate(flops=2**33, bytes_accessed=2**24, transcendentals=0),
        name="potential_sum",
    )(*found)

    at = sub_place * row_count + core * quarter
    own_part = lax.dynamic_slice_in_dim(grad, at, quarter, 2) + returned
    grad = lax.dynamic_update_slice_in_dim(grad, own_part, at, 2)
    share = clusters // sub_count

    def share_of(array, place):
        own_rows, edges = [], []
        for at in range(sub_count):
            own_rows.append(array[:, at * share : (at + 1) * share])
            none = jnp.zeros_like(array[:, 0])
            edges.append(
                [
                    array[:, at * share - 1] if at > 0 else none,
                    array[:, (at + 1) * share] if at < sub_count - 1 else none,
                ]
            )
        place = place % sub_count
        return (
            pick(place, own_rows),
            pick(place, [jnp.concatenate(edge, axis=0) for edge in edges]),
        )

    def packed(rows, edge):
        edge = jnp.pad(edge, ((0, share - edge.shape[0] % share), (0, 0)))
        return jnp.concatenate([rows, edge.reshape(-1, share, panels)], axis=0)

    summed = packed(*share_of(grad, sub_place))
    for step in range(1, sub_count):
        summed = summed + shifted(packed(*share_of(grad, sub_place + step)), "sub", step)
    gathered = summed
    for step in range(1, rhs_count):
        gathered = gathered + shifted(summed, "rhs", step)
    edge_terms = gathered[3:].reshape(-1, panels)[:6]
    own_jitter, edge_jitter = share_of(jitter_all[None], sub_place)
    edge_jitter = jnp.repeat(edge_jitter, 3, axis=0)
    main, rims = pl.pallas_call(
        node_kernel,
        out_shape=(
            jax.ShapeDtypeStruct((3, share * panels), jnp.float32),
            jax.ShapeDtypeStruct((2, 8, LANES), jnp.float32),
        ),
        in_specs=[vmem] * 4,
        out_specs=(vmem, vmem),
        compiler_params=pltpu.CompilerParams(vmem_limit_bytes=16 * 1024 * 1024),
        cost_estimate=pl.CostEstimate(flops=2**32, bytes_accessed=2**24, transcendentals=0),
        name="node_terms",
    )(gathered[:3], own_jitter[0], edge_terms, edge_jitter)

    is_first, is_last = sub_place == 0, sub_place == sub_count - 1

    def rim_goal(z, x):
        if x == 0:
            return (z - 1, sub_count - 1)
        if x == sub_count - 1:
            return (z + 1, 0)
        return None

    from_rim = moved(jnp.where(is_first, rims[0], rims[1]), ("clus", "sub"), rim_goal)[:3]
    node_grad = jnp.concatenate(
        [
            main[:, :LANES] + jnp.where(is_first, from_rim, 0.0),
            main[:, LANES:-LANES],
            main[:, -LANES:] + jnp.where(is_last, from_rim, 0.0),
        ],
        axis=1,
    )
    return (potential, node_grad)


def solution(mesh):
    placed = (
        P(("groups", "clus"), None, "sub"),
        P(("groups", "clus"), "sub"),
        P(("groups", "clus"), "rhs", "sub"),
        P(("groups", "clus"), "rhs", "sub"),
        P(None, "groups"),
        P(("groups", "clus"), None, "sub"),
    )
    return jax.shard_map(
        on_device,
        mesh=mesh,
        in_specs=placed,
        out_specs=(P(("groups", "clus"), "rhs", "sub"), P(None, ("groups", "clus", "sub"))),
        check_vma=False,
    )
```

```python
import functools

import jax
import jax.numpy as jnp
from jax import lax
from jax.experimental import pallas as pl
from jax.experimental.pallas import tpu as pltpu
from jax.sharding import PartitionSpec as P

CP = 512
ROUNDS = 5

core_radius = 0.25
jitter_reach = 8
LANES = 128
AUG = 16


def shifted(value, axis, steps):
    count = lax.axis_size(axis)
    pairs = [(source, (source + steps) % count) for source in range(count)]
    return lax.ppermute(value, axis, pairs)


def moved(value, axes, target):
    counts = [lax.axis_size(axis) for axis in axes]
    pairs = []
    for major in range(counts[0]):
        for minor in range(counts[1]):
            goal = target(major, minor)
            if goal is not None:
                to_major, to_minor = goal[0] % counts[0], goal[1] % counts[1]
                pairs.append((major * counts[1] + minor, to_major * counts[1] + to_minor))
    return lax.ppermute(value, axes, pairs)


def three_parts(value):
    parts = []
    for _ in range(3):
        part = value.astype(jnp.bfloat16).astype(jnp.float32)
        parts.append(part)
        value = value - part
    return parts


def pick(index, choices):
    out = choices[0]
    for place in range(1, len(choices)):
        out = jnp.where(index == place, choices[place], out)
    return out


def own_kernel(*refs):
    block_refs, (aug_ref, pos_ref, aug32) = refs[:-3], refs[-3:]
    clusters = aug_ref.shape[0]
    row_count = block_refs[0].shape[1]
    aug32[...] = jnp.zeros(aug32.shape, jnp.float32)
    for place, block_ref in enumerate(block_refs):
        cols = slice(place * row_count, (place + 1) * row_count)
        raw = [block_ref[coord * clusters : (coord + 1) * clusters, :] for coord in range(3)]
        pos = [value.astype(jnp.float32) for value in raw]
        square = pos[0] * pos[0] + pos[1] * pos[1] + pos[2] * pos[2] + core_radius * core_radius
        ones = jnp.ones_like(square)
        rows = [-2.0 * value for value in pos] + three_parts(square) + [ones] * 3
        for row, value in enumerate(rows):
            aug32[:, row, cols] = value
        for coord in range(3):
            pos_ref[coord, :, cols] = raw[coord]
    aug_ref[...] = aug32[...].astype(jnp.bfloat16)


def step_kernel(step, length, rhs, blocks, first, last, *refs):
    items, source_ref, own_ref = refs[:3]
    cot_refs = refs[3 : 3 + blocks[0] * blocks[1]]
    width = rhs * blocks[1]
    refs = refs[3 + len(cot_refs) :]
    if not first:
        acc_in = refs[0]
        refs = refs[1:]
    if last:
        pos_ref, pot_ref, pot_out_ref, grad_ref, back_ref, acc = refs[:6]
        refs = refs[6:]
    else:
        acc, back_ref = refs[:2]
        refs = refs[2:]
    aug32, aug_t, dens_t, left, weight, back, dist_a, dist_b, prod_a, prod_b, both_a, both_b = refs
    clusters, _, panels = own_ref.shape
    quarter = source_ref.shape[1]
    base = clusters * rhs
    starts = [0] + list(range(base + 4 * clusters, source_ref.shape[0], base))

    there = [
        source_ref[base + coord * clusters : base + (coord + 1) * clusters, :].astype(jnp.float32)
        for coord in range(3)
    ]
    area = source_ref[base + 3 * clusters : base + 4 * clusters, :].astype(jnp.float32)
    square = there[0] * there[0] + there[1] * there[1] + there[2] * there[2]
    ones = jnp.ones_like(square)
    aug32[...] = jnp.zeros(aug32.shape, jnp.float32)
    for row, value in enumerate(there + [ones] * 3 + three_parts(square)):
        aug32[:, row, :] = value
    weight_t = (CP ** (-0.5) * area).T
    left[...] = jnp.zeros(left.shape, left.dtype)
    for cluster in range(clusters):
        rows = aug32[cluster]
        left[cluster, width:, quarter:] = rows.astype(jnp.bfloat16)
        aug_t[cluster] = rows.T.astype(jnp.bfloat16)
        dens = jnp.concatenate(
            [source_ref[at + cluster * rhs : at + (cluster + 1) * rhs, :] for at in starts], axis=0
        )
        left[cluster, :width, :quarter] = dens
        dens_t[cluster] = dens.T
        weight[cluster] = jnp.broadcast_to(weight_t[:, cluster : cluster + 1], (quarter, LANES))
    weight[clusters] = jnp.zeros((quarter, LANES), jnp.float32)
    back[...] = jnp.zeros(back.shape, jnp.float32)
    if first:
        acc[...] = jnp.zeros(acc.shape, jnp.float32)
    else:
        acc[...] = acc_in[...]
    dist_b[...] = jnp.ones(dist_b.shape, jnp.float32)
    prod_b[...] = jnp.zeros(prod_b.shape, jnp.float32)
    both_a[...] = jnp.zeros(both_a.shape, both_a.dtype)

    def decoded(place):
        code = items[step * length + place]
        return code // (2 * clusters), code % (2 * clusters)

    def raw(place, dist, prod):
        here, mate = decoded(place)
        mate = mate % clusters
        dist[...] = jnp.dot(aug_t[mate], own_ref[here], preferred_element_type=jnp.float32)
        cot = [
            jnp.concatenate(
                [ref[here] for ref in cot_refs[at * blocks[0] : (at + 1) * blocks[0]]], axis=1
            )
            for at in range(blocks[1])
        ]
        prod[...] = jnp.dot(
            dens_t[mate], jnp.concatenate(cot, axis=0), preferred_element_type=jnp.float32
        )

    def pointwise(place, dist, prod, both):
        _, mate = decoded(place)
        scale = weight[mate]
        for start in range(0, panels, LANES):
            cols = slice(start, start + LANES)
            inverse = lax.rsqrt(dist[:, cols])
            kernel = scale * inverse
            both[:quarter, cols] = kernel.astype(jnp.bfloat16)
            both[quarter:, cols] = ((inverse * inverse) * (kernel * prod[:, cols])).astype(jnp.bfloat16)

    def summed(place, both):
        here, mate = decoded(place)
        mate = mate % clusters
        acc[here] += jnp.dot(left[mate], both[...], preferred_element_type=jnp.float32)
        back[mate] += lax.dot_general(
            own_ref[here],
            both[quarter:, :],
            (((1,), (1,)), ((), ())),
            preferred_element_type=jnp.float32,
        )[:8]

    @pl.loop(0, items[step * length])
    def _(pair):
        turn = 2 * pair + 1
        summed(turn, both_a)
        pointwise(turn + 1, dist_b, prod_b, both_b)
        raw(turn + 2, dist_a, prod_a)
        summed(turn + 1, both_b)
        pointwise(turn + 2, dist_a, prod_a, both_a)
        raw(turn + 3, dist_b, prod_b)

    for coord in range(3):
        back_ref[coord] = -0.5 * back[:, coord, :] - there[coord] * back[:, 6, :]
    if last:
        for coord in range(3):
            grad_ref[coord] = (
                acc[:, width + coord, :]
                - pos_ref[coord].astype(jnp.float32) * acc[:, width + 3, :]
            )
        pot_ref[...] = acc[:, :rhs, :]
        pot_out_ref[...] = acc[:, rhs:width, :].astype(jnp.bfloat16)


def run_step(step, length, items, source, cots, own, pos, carried, last):
    clusters, _, panels = own.shape
    quarter = source.shape[1]
    rhs = cots[0].shape[1]
    sub_blocks = panels // cots[0].shape[2]
    blocks = (sub_blocks, len(cots) // sub_blocks)
    width = rhs * blocks[1]
    first = carried is None
    vmem = pl.BlockSpec(memory_space=pltpu.VMEM)
    smem = pl.BlockSpec(memory_space=pltpu.SMEM)
    operands = (items, source, own, *cots)
    if not first:
        operands += (carried,)
    acc_shape = (clusters, width + AUG, panels)
    back_shape = jax.ShapeDtypeStruct((3, clusters, quarter), jnp.float32)
    scratch = [
        pltpu.VMEM((clusters, AUG, quarter), jnp.float32),
        pltpu.VMEM((clusters, quarter, AUG), jnp.bfloat16),
        pltpu.VMEM((clusters, quarter, width), jnp.bfloat16),
        pltpu.VMEM((clusters, width + AUG, 2 * quarter), jnp.bfloat16),
        pltpu.VMEM((clusters + 1, quarter, LANES), jnp.float32),
        pltpu.VMEM((clusters, 8, quarter), jnp.float32),
    ]
    scratch += [pltpu.VMEM((quarter, panels), jnp.float32)] * 4
    scratch += [pltpu.VMEM((2 * quarter, panels), jnp.bfloat16)] * 2
    if last:
        operands += (pos,)
        out_shape = (
            jax.ShapeDtypeStruct((clusters, rhs, panels), jnp.float32),
            jax.ShapeDtypeStruct((clusters, width - rhs, panels), jnp.bfloat16),
            jax.ShapeDtypeStruct((3, clusters, panels), jnp.float32),
            back_shape,
        )
        scratch = [pltpu.VMEM(acc_shape, jnp.float32)] + scratch
    else:
        out_shape = (jax.ShapeDtypeStruct(acc_shape, jnp.float32), back_shape)
    pairs = (length - 6) * panels * quarter
    return pl.pallas_call(
        functools.partial(step_kernel, step, length, rhs, blocks, first, last),
        out_shape=out_shape,
        in_specs=[smem] + [vmem] * (len(operands) - 1),
        out_specs=(vmem,) * len(out_shape),
        scratch_shapes=scratch,
        compiler_params=pltpu.CompilerParams(vmem_limit_bytes=16 * 1024 * 1024),
        cost_estimate=pl.CostEstimate(
            flops=2 * pairs * (2 * width + 3 * AUG), bytes_accessed=6 * 2**20, transcendentals=pairs
        ),
        name=f"near_field_{step}",
    )(*operands)


def node_kernel(grad_ref, jitter_ref, edge_ref, edge_jitter_ref, main_ref, rims_ref):
    clusters, panels = jitter_ref.shape
    wide = panels + 2 * LANES

    def spread_of(terms, jitter):
        side = jnp.zeros((terms.shape[0], LANES), jnp.float32)
        terms = 0.25 * terms
        spread = jnp.zeros((terms.shape[0], wide), jnp.float32)
        for offset in range(-jitter_reach, jitter_reach + 1):
            masked = jnp.where(jitter == offset, terms, 0.0)
            masked = jnp.concatenate([side, masked, side], axis=1)
            spread = spread + pltpu.roll(masked, offset % wide, 1)
        spread = spread + pltpu.roll(spread, 1, 1)
        return spread + pltpu.roll(spread, 32, 1)

    jitter = jitter_ref[...]
    row_at = lax.broadcasted_iota(jnp.int32, (clusters, LANES), 0)
    rims_ref[...] = jnp.zeros(rims_ref.shape, jnp.float32)
    edge = spread_of(edge_ref[...], edge_jitter_ref[...])
    for coord in range(3):
        spread = spread_of(grad_ref[coord], jitter)
        below = spread[:, :LANES]
        above = spread[:, LANES + panels :]
        inner = spread[:, LANES : LANES + panels]
        before = edge[coord : coord + 1, LANES + panels :]
        after = edge[3 + coord : 4 + coord, :LANES]
        first = jnp.where(row_at == 0, before, pltpu.roll(above, 1, 0))
        last = jnp.where(row_at == clusters - 1, after, pltpu.roll(below, clusters - 1, 0))
        inner = jnp.concatenate(
            [
                inner[:, :LANES] + first,
                inner[:, LANES : panels - LANES],
                inner[:, panels - LANES :] + last,
            ],
            axis=1,
        )
        for cluster in range(clusters):
            main_ref[coord : coord + 1, cluster * panels : (cluster + 1) * panels] = inner[
                cluster : cluster + 1
            ]
        rims_ref[0, coord : coord + 1, :] = below[:1]
        rims_ref[1, coord : coord + 1, :] = above[clusters - 1 :]


def last_kernel(*refs):
    found, (main_ref, rim_ref, potential_ref, node_ref) = refs[:-4], refs[-4:]
    total = found[0][...]
    for ref in found[1:]:
        total = total + ref[...].astype(jnp.float32)
    potential_ref[...] = total.astype(jnp.bfloat16)
    node_ref[...] = main_ref[...]
    node_ref[:, :LANES] += rim_ref[0]
    node_ref[:, main_ref.shape[1] - LANES :] += rim_ref[1]


def on_device(positions, areas, density, cotangent, matching, connect):
    clus_count = lax.axis_size("clus")
    sub_count = lax.axis_size("sub")
    rhs_count = lax.axis_size("rhs")
    device = lax.axis_index("clus")
    sub_place = lax.axis_index("sub")
    core = lax.axis_index("rhs")
    clusters, rhs, row_count = density.shape
    panels = row_count * sub_count
    quarter = row_count // rhs_count
    width = rhs * rhs_count
    vmem = pl.BlockSpec(memory_space=pltpu.VMEM)

    def part_of(array, place):
        return pick(
            place % rhs_count,
            [array[..., at * quarter : (at + 1) * quarter] for at in range(rhs_count)],
        )

    by_coord = jnp.transpose(positions, (1, 0, 2))
    placed = jnp.concatenate([by_coord, areas[None]], axis=0)
    first_part = jnp.concatenate(
        [
            part_of(density, core).reshape(clusters * rhs, quarter),
            part_of(placed, core).reshape(4 * clusters, quarter),
        ],
        axis=0,
    )
    arrived = [shifted(first_part, "clus", 1)]
    for step in range(1, rhs_count):
        other_part = part_of(density, core + step).reshape(clusters * rhs, quarter)
        arrived.append(
            moved(other_part, ("clus", "rhs"), lambda z, c, step=step: (z + 1, c + step))
        )
    source = jnp.concatenate(arrived, axis=0)

    per_round = 2 * ((clusters // 2 + clus_count - 2) // (clus_count - 1))
    cap = ROUNDS * per_round
    partners = lax.dynamic_slice_in_dim(matching, device * clusters, clusters, 1).reshape(-1)
    here = jnp.tile(jnp.arange(clusters, dtype=jnp.int32), ROUNDS)
    code = here * (2 * clusters) + partners % clusters
    behind = (device - partners // clusters) % clus_count
    total_items = ROUNDS * clusters
    order = jnp.arange(total_items, dtype=jnp.int32)
    rank = jnp.sum(
        ((behind[None, :] == behind[:, None]) & (order[None, :] < order[:, None])).astype(jnp.int32),
        axis=1,
    )
    steps = jnp.arange(1, clus_count, dtype=jnp.int32)
    member = behind[None, :] == steps[:, None]
    slots = jnp.arange(cap, dtype=jnp.int32)
    chosen = member[:, None, :] & (rank[None, None, :] == slots[None, :, None])
    listed = jnp.sum(jnp.where(chosen, code[None, None, :] - clusters, 0), axis=2) + clusters
    turns = (jnp.sum(member.astype(jnp.int32), axis=1) + 3) // 2
    length = cap + 6
    items = jnp.pad(listed, ((0, 0), (3, 3)), constant_values=clusters)
    items = jnp.concatenate([turns[:, None], items[:, 1:]], axis=1).reshape(-1)

    cluster_at = jnp.arange(clusters, dtype=jnp.int32)
    first_ids = (device * clusters + cluster_at) * panels
    base_ids = first_ids[:, None] + (
        sub_place * row_count + jnp.arange(row_count, dtype=jnp.int32)
    )[None, :]
    nodes_total = clus_count * clusters * panels
    jitter = (connect[:, 0, :] - base_ids + jitter_reach) % nodes_total - jitter_reach
    small = jnp.concatenate(
        [by_coord.reshape(3 * clusters, row_count), jitter.astype(jnp.bfloat16)], axis=0
    )
    smalls = [small] + [shifted(small, "sub", step) for step in range(1, sub_count)]
    cots = [cotangent] + [shifted(cotangent, "sub", step) for step in range(1, sub_count)]
    for step in range(1, rhs_count):
        cots += [shifted(block, "rhs", step) for block in cots[:sub_count]]

    def in_order(blocks):
        return jnp.concatenate(
            [pick((sub_place - place) % sub_count, blocks) for place in range(sub_count)], axis=-1
        )

    jitter_all = in_order([block[3 * clusters :] for block in smalls]).astype(jnp.int32)
    own, pos = pl.pallas_call(
        own_kernel,
        out_shape=(
            jax.ShapeDtypeStruct((clusters, AUG, panels), jnp.bfloat16),
            jax.ShapeDtypeStruct((3, clusters, panels), jnp.bfloat16),
        ),
        in_specs=[vmem] * sub_count,
        out_specs=(vmem, vmem),
        scratch_shapes=[pltpu.VMEM((clusters, AUG, panels), jnp.float32)],
        compiler_params=pltpu.CompilerParams(vmem_limit_bytes=16 * 1024 * 1024),
        name="target_rows",
    )(*smalls)

    carried = None
    backs = []
    returned = jnp.zeros((3, clusters, quarter), jnp.float32)
    for step in range(1, clus_count):
        if step > 1:
            if step > 2:
                source, backs[step - 3] = lax.optimization_barrier((source, backs[step - 3]))
            source = shifted(source, "clus", 1)
            if step > 2:
                home = shifted(backs[step - 3], "clus", 2 - step)
                source, home = lax.optimization_barrier((source, home))
                returned = returned + home
        last = step == clus_count - 1
        results = run_step(step - 1, length, items, source, cots, own, pos, carried, last)
        if last:
            pot, pot_out, grad, back = results
        else:
            carried, back = results
        backs.append(back)
    for step in range(max(clus_count - 2, 1), clus_count):
        returned = returned + shifted(backs[step - 1], "clus", -step)

    half = pot
    for step in range(1, rhs_count):
        arrived = shifted(pot_out[:, (step - 1) * rhs : step * rhs], "rhs", -step)
        half = half + arrived.astype(jnp.float32)

    half, grad = lax.optimization_barrier((half, grad))
    found = [half[..., :row_count]]
    for step in range(1, sub_count):
        sent = half[..., step * row_count : (step + 1) * row_count].astype(jnp.bfloat16)
        found.append(shifted(sent, "sub", -step))

    grads = [grad[..., at * row_count : (at + 1) * row_count] for at in range(sub_count)]
    grads[0] = grads[0] + jnp.concatenate(
        [jnp.where(core == at, returned, 0.0) for at in range(rhs_count)], axis=-1
    )
    grad = in_order(grads)
    share = clusters // sub_count

    def share_of(array, place):
        own_rows, edges = [], []
        for at in range(sub_count):
            own_rows.append(array[:, at * share : (at + 1) * share])
            none = jnp.zeros_like(array[:, 0])
            edges.append(
                [
                    array[:, at * share - 1] if at > 0 else none,
                    array[:, (at + 1) * share] if at < sub_count - 1 else none,
                ]
            )
        place = place % sub_count
        return (
            pick(place, own_rows),
            pick(place, [jnp.concatenate(edge, axis=0) for edge in edges]),
        )

    def packed(rows, edge):
        edge = jnp.pad(edge, ((0, share - edge.shape[0] % share), (0, 0)))
        return jnp.concatenate([rows, edge.reshape(-1, share, panels)], axis=0)

    summed = packed(*share_of(grad, sub_place))
    for step in range(1, sub_count):
        summed = summed + shifted(packed(*share_of(grad, sub_place + step)), "sub", step)
    gathered = summed
    for step in range(1, rhs_count):
        gathered = gathered + shifted(summed, "rhs", step)
    edge_terms = gathered[3:].reshape(-1, panels)[:6]
    own_jitter, edge_jitter = share_of(jitter_all[None], sub_place)
    edge_jitter = jnp.repeat(edge_jitter, 3, axis=0)
    main, rims = pl.pallas_call(
        node_kernel,
        out_shape=(
            jax.ShapeDtypeStruct((3, share * panels), jnp.float32),
            jax.ShapeDtypeStruct((2, 8, LANES), jnp.float32),
        ),
        in_specs=[vmem] * 4,
        out_specs=(vmem, vmem),
        compiler_params=pltpu.CompilerParams(vmem_limit_bytes=16 * 1024 * 1024),
        cost_estimate=pl.CostEstimate(flops=2**20, bytes_accessed=2**18, transcendentals=0),
        name="node_terms",
    )(gathered[:3], own_jitter[0], edge_terms, edge_jitter)

    found, rims = lax.optimization_barrier((found, rims))

    is_first, is_last = sub_place == 0, sub_place == sub_count - 1

    def rim_goal(z, x):
        if x == 0:
            return (z - 1, sub_count - 1)
        if x == sub_count - 1:
            return (z + 1, 0)
        return None

    from_rim = moved(jnp.where(is_first, rims[0], rims[1]), ("clus", "sub"), rim_goal)[:3]
    from_rim = jnp.where(is_first, from_rim, 0.0), jnp.where(is_last, from_rim, 0.0)
    potential, node_grad = pl.pallas_call(
        last_kernel,
        out_shape=(
            jax.ShapeDtypeStruct((clusters, rhs, row_count), jnp.bfloat16),
            jax.ShapeDtypeStruct(main.shape, jnp.float32),
        ),
        in_specs=[vmem] * (sub_count + 2),
        out_specs=(vmem, vmem),
        compiler_params=pltpu.CompilerParams(vmem_limit_bytes=16 * 1024 * 1024),
        name="last_sums",
    )(*found, main, jnp.stack(from_rim))
    return (potential, node_grad)


def solution(mesh):
    placed = (
        P(("groups", "clus"), None, "sub"),
        P(("groups", "clus"), "sub"),
        P(("groups", "clus"), "rhs", "sub"),
        P(("groups", "clus"), "rhs", "sub"),
        P(None, "groups"),
        P(("groups", "clus"), None, "sub"),
    )
    return jax.shard_map(
        on_device,
        mesh=mesh,
        in_specs=placed,
        out_specs=(P(("groups", "clus"), "rhs", "sub"), P(None, ("groups", "clus", "sub"))),
        check_vma=False,
    )
```

```python
import functools

import jax
import jax.numpy as jnp
from jax import lax
from jax.experimental import pallas as pl
from jax.experimental.pallas import tpu as pltpu
from jax.sharding import PartitionSpec as P

CP = 512
ROUNDS = 5

core_radius = 0.25
jitter_reach = 8
LANES = 128
AUG = 16


def shifted(value, axis, steps):
    count = lax.axis_size(axis)
    pairs = [(source, (source + steps) % count) for source in range(count)]
    return lax.ppermute(value, axis, pairs)


def moved(value, axes, target):
    counts = [lax.axis_size(axis) for axis in axes]
    pairs = []
    for major in range(counts[0]):
        for minor in range(counts[1]):
            goal = target(major, minor)
            if goal is not None:
                to_major, to_minor = goal[0] % counts[0], goal[1] % counts[1]
                pairs.append((major * counts[1] + minor, to_major * counts[1] + to_minor))
    return lax.ppermute(value, axes, pairs)


def three_parts(value):
    parts = []
    for _ in range(3):
        part = value.astype(jnp.bfloat16).astype(jnp.float32)
        parts.append(part)
        value = value - part
    return parts


def pick(index, choices):
    out = choices[0]
    for place in range(1, len(choices)):
        out = jnp.where(index == place, choices[place], out)
    return out


def prepare_kernel(places, density_ref, by_coord_ref, areas_ref, connect_ref, *out_refs):
    part_refs, small_ref = out_refs[:-1], out_refs[-1]
    clusters, rhs, row_count = density_ref.shape
    quarter = part_refs[0].shape[1]
    count = len(part_refs)
    device, sub_place, core = places[0], places[1], places[2]

    def part_of(array, place):
        return pick(place, [array[:, at * quarter : (at + 1) * quarter] for at in range(count)])

    first_id = places[3] * device + places[4] * sub_place
    ids = lax.broadcasted_iota(jnp.int32, (clusters, row_count), 0) * places[5]
    ids = ids + lax.broadcasted_iota(jnp.int32, (clusters, row_count), 1) + first_id
    jitter = connect_ref[...] - ids
    jitter = jnp.where(jitter > jitter_reach, jitter - places[6], jitter)
    jitter = jnp.where(jitter < -jitter_reach, jitter + places[6], jitter)
    jitter = jitter.astype(jnp.float32).astype(jnp.bfloat16)
    rows = [by_coord_ref[coord] for coord in range(3)] + [areas_ref[...], jitter]
    base = clusters * rhs
    for cluster in range(clusters):
        dens = density_ref[cluster]
        for step, part_ref in enumerate(part_refs):
            part_ref[cluster * rhs : (cluster + 1) * rhs, :] = part_of(dens, (core + step) % count)
    for at, value in enumerate(rows):
        span = slice(base + at * clusters, base + (at + 1) * clusters)
        part_refs[0][span, :] = part_of(value, core)
        if at != 3:
            at = min(at, 3)
            small_ref[at * clusters : (at + 1) * clusters, :] = value


def own_kernel(*refs):
    block_refs, (aug_ref, pos_ref, aug32) = refs[:-3], refs[-3:]
    clusters = aug_ref.shape[0]
    row_count = block_refs[0].shape[1]
    aug32[...] = jnp.zeros(aug32.shape, jnp.float32)
    for place, block_ref in enumerate(block_refs):
        cols = slice(place * row_count, (place + 1) * row_count)
        raw = [block_ref[coord * clusters : (coord + 1) * clusters, :] for coord in range(3)]
        pos = [value.astype(jnp.float32) for value in raw]
        square = pos[0] * pos[0] + pos[1] * pos[1] + pos[2] * pos[2] + core_radius * core_radius
        ones = jnp.ones_like(square)
        rows = [-2.0 * value for value in pos] + three_parts(square) + [ones] * 3
        for row, value in enumerate(rows):
            aug32[:, row, cols] = value
        for coord in range(3):
            pos_ref[coord, :, cols] = raw[coord]
    aug_ref[...] = aug32[...].astype(jnp.bfloat16)


def step_kernel(step, length, rhs, blocks, first, last, *refs):
    items, source_ref, own_ref = refs[:3]
    cot_refs = refs[3 : 3 + blocks[0] * blocks[1]]
    width = rhs * blocks[1]
    refs = refs[3 + len(cot_refs) :]
    if not first:
        acc_in = refs[0]
        refs = refs[1:]
    if last:
        pos_ref, pot_ref, pot_out_ref, grad_ref, back_ref, acc = refs[:6]
        refs = refs[6:]
    else:
        acc, back_ref = refs[:2]
        refs = refs[2:]
    aug32, aug_t, dens_t, left, weight, back, dist_a, dist_b, prod_a, prod_b, both_a, both_b = refs
    clusters, _, panels = own_ref.shape
    quarter = source_ref.shape[1]
    base = clusters * rhs
    starts = [0] + list(range(base + 5 * clusters, source_ref.shape[0], base))

    there = [
        source_ref[base + coord * clusters : base + (coord + 1) * clusters, :].astype(jnp.float32)
        for coord in range(3)
    ]
    area = source_ref[base + 3 * clusters : base + 4 * clusters, :].astype(jnp.float32)
    square = there[0] * there[0] + there[1] * there[1] + there[2] * there[2]
    ones = jnp.ones_like(square)
    aug32[...] = jnp.zeros(aug32.shape, jnp.float32)
    for row, value in enumerate(there + [ones] * 3 + three_parts(square)):
        aug32[:, row, :] = value
    weight_t = (CP ** (-0.5) * area).T
    left[...] = jnp.zeros(left.shape, left.dtype)
    for cluster in range(clusters):
        rows = aug32[cluster]
        left[cluster, width:, quarter:] = rows.astype(jnp.bfloat16)
        aug_t[cluster] = rows.T.astype(jnp.bfloat16)
        dens = jnp.concatenate(
            [source_ref[at + cluster * rhs : at + (cluster + 1) * rhs, :] for at in starts], axis=0
        )
        left[cluster, :width, :quarter] = dens
        dens_t[cluster] = dens.T
        weight[cluster] = jnp.broadcast_to(weight_t[:, cluster : cluster + 1], (quarter, LANES))
    weight[clusters] = jnp.zeros((quarter, LANES), jnp.float32)
    back[...] = jnp.zeros(back.shape, jnp.float32)
    if first:
        acc[...] = jnp.zeros(acc.shape, jnp.float32)
    else:
        acc[...] = acc_in[...]
    dist_b[...] = jnp.ones(dist_b.shape, jnp.float32)
    prod_b[...] = jnp.zeros(prod_b.shape, jnp.float32)
    both_a[...] = jnp.zeros(both_a.shape, both_a.dtype)

    def decoded(place):
        code = items[step * length + place]
        return code // (2 * clusters), code % (2 * clusters)

    def raw(place, dist, prod):
        here, mate = decoded(place)
        mate = mate % clusters
        dist[...] = jnp.dot(aug_t[mate], own_ref[here], preferred_element_type=jnp.float32)
        cot = [
            jnp.concatenate(
                [ref[here] for ref in cot_refs[at * blocks[0] : (at + 1) * blocks[0]]], axis=1
            )
            for at in range(blocks[1])
        ]
        prod[...] = jnp.dot(
            dens_t[mate], jnp.concatenate(cot, axis=0), preferred_element_type=jnp.float32
        )

    def pointwise(place, dist, prod, both):
        _, mate = decoded(place)
        scale = weight[mate]
        for start in range(0, panels, LANES):
            cols = slice(start, start + LANES)
            inverse = lax.rsqrt(dist[:, cols])
            kernel = scale * inverse
            both[:quarter, cols] = kernel.astype(jnp.bfloat16)
            both[quarter:, cols] = ((inverse * inverse) * (kernel * prod[:, cols])).astype(jnp.bfloat16)

    def summed(place, both):
        here, mate = decoded(place)
        mate = mate % clusters
        acc[here] += jnp.dot(left[mate], both[...], preferred_element_type=jnp.float32)
        back[mate] += lax.dot_general(
            own_ref[here],
            both[quarter:, :],
            (((1,), (1,)), ((), ())),
            preferred_element_type=jnp.float32,
        )[:8]

    @pl.loop(0, items[step * length])
    def _(pair):
        turn = 2 * pair + 1
        summed(turn, both_a)
        pointwise(turn + 1, dist_b, prod_b, both_b)
        raw(turn + 2, dist_a, prod_a)
        summed(turn + 1, both_b)
        pointwise(turn + 2, dist_a, prod_a, both_a)
        raw(turn + 3, dist_b, prod_b)

    for coord in range(3):
        back_ref[coord] = -0.5 * back[:, coord, :] - there[coord] * back[:, 6, :]
    if last:
        for coord in range(3):
            grad_ref[coord] = (
                acc[:, width + coord, :]
                - pos_ref[coord].astype(jnp.float32) * acc[:, width + 3, :]
            )
        pot_ref[...] = acc[:, :rhs, :]
        pot_out_ref[...] = acc[:, rhs:width, :].astype(jnp.bfloat16)


def run_step(step, length, items, source, cots, own, pos, carried, last):
    clusters, _, panels = own.shape
    quarter = source.shape[1]
    rhs = cots[0].shape[1]
    sub_blocks = panels // cots[0].shape[2]
    blocks = (sub_blocks, len(cots) // sub_blocks)
    width = rhs * blocks[1]
    first = carried is None
    vmem = pl.BlockSpec(memory_space=pltpu.VMEM)
    smem = pl.BlockSpec(memory_space=pltpu.SMEM)
    operands = (items, source, own, *cots)
    if not first:
        operands += (carried,)
    acc_shape = (clusters, width + AUG, panels)
    back_shape = jax.ShapeDtypeStruct((3, clusters, quarter), jnp.float32)
    scratch = [
        pltpu.VMEM((clusters, AUG, quarter), jnp.float32),
        pltpu.VMEM((clusters, quarter, AUG), jnp.bfloat16),
        pltpu.VMEM((clusters, quarter, width), jnp.bfloat16),
        pltpu.VMEM((clusters, width + AUG, 2 * quarter), jnp.bfloat16),
        pltpu.VMEM((clusters + 1, quarter, LANES), jnp.float32),
        pltpu.VMEM((clusters, 8, quarter), jnp.float32),
    ]
    scratch += [pltpu.VMEM((quarter, panels), jnp.float32)] * 4
    scratch += [pltpu.VMEM((2 * quarter, panels), jnp.bfloat16)] * 2
    if last:
        operands += (pos,)
        out_shape = (
            jax.ShapeDtypeStruct((clusters, rhs, panels), jnp.float32),
            jax.ShapeDtypeStruct((clusters, width - rhs, panels), jnp.bfloat16),
            jax.ShapeDtypeStruct((3, clusters, panels), jnp.float32),
            back_shape,
        )
        scratch = [pltpu.VMEM(acc_shape, jnp.float32)] + scratch
    else:
        out_shape = (jax.ShapeDtypeStruct(acc_shape, jnp.float32), back_shape)
    pairs = (length - 6) * panels * quarter
    return pl.pallas_call(
        functools.partial(step_kernel, step, length, rhs, blocks, first, last),
        out_shape=out_shape,
        in_specs=[smem] + [vmem] * (len(operands) - 1),
        out_specs=(vmem,) * len(out_shape),
        scratch_shapes=scratch,
        compiler_params=pltpu.CompilerParams(vmem_limit_bytes=16 * 1024 * 1024),
        cost_estimate=pl.CostEstimate(
            flops=2 * pairs * (2 * width + 3 * AUG), bytes_accessed=6 * 2**20, transcendentals=pairs
        ),
        name=f"near_field_{step}",
    )(*operands)


def node_kernel(grad_ref, jitter_ref, edge_ref, main_ref):
    clusters, panels = jitter_ref.shape
    wide = panels + 2 * LANES

    def spread_of(terms, jitter):
        side = jnp.zeros((terms.shape[0], LANES), jnp.float32)
        terms = 0.25 * terms
        spread = jnp.zeros((terms.shape[0], wide), jnp.float32)
        for offset in range(-jitter_reach, jitter_reach + 1):
            masked = jnp.where(jitter == offset, terms, 0.0)
            masked = jnp.concatenate([side, masked, side], axis=1)
            spread = spread + pltpu.roll(masked, offset % wide, 1)
        spread = spread + pltpu.roll(spread, 1, 1)
        return spread + pltpu.roll(spread, 32, 1)

    jitter = jitter_ref[...]
    row_at = lax.broadcasted_iota(jnp.int32, (clusters, LANES), 0)
    edge = edge_ref[...]
    edge_at = lax.broadcasted_iota(jnp.int32, edge.shape, 0)
    edge_jitter = jnp.where(edge_at < 3, edge[6:7], edge[7:8]).astype(jnp.int32)
    edge = spread_of(edge, edge_jitter)
    for coord in range(3):
        spread = spread_of(grad_ref[coord], jitter)
        below = spread[:, :LANES]
        above = spread[:, LANES + panels :]
        inner = spread[:, LANES : LANES + panels]
        before = edge[coord : coord + 1, LANES + panels :]
        after = edge[3 + coord : 4 + coord, :LANES]
        first = jnp.where(row_at == 0, before, pltpu.roll(above, 1, 0))
        last = jnp.where(row_at == clusters - 1, after, pltpu.roll(below, clusters - 1, 0))
        inner = jnp.concatenate(
            [
                inner[:, :LANES] + first,
                inner[:, LANES : panels - LANES],
                inner[:, panels - LANES :] + last,
            ],
            axis=1,
        )
        for cluster in range(clusters):
            main_ref[coord : coord + 1, cluster * panels : (cluster + 1) * panels] = inner[
                cluster : cluster + 1
            ]


def sum_kernel(*refs):
    total = refs[0][...]
    for ref in refs[1:-1]:
        total = total + ref[...].astype(jnp.float32)
    refs[-1][...] = total.astype(jnp.bfloat16)


def on_device(positions, areas, density, cotangent, matching, connect):
    clus_count = lax.axis_size("clus")
    sub_count = lax.axis_size("sub")
    rhs_count = lax.axis_size("rhs")
    device = lax.axis_index("clus")
    sub_place = lax.axis_index("sub")
    core = lax.axis_index("rhs")
    clusters, rhs, row_count = density.shape
    panels = row_count * sub_count
    quarter = row_count // rhs_count
    width = rhs * rhs_count
    vmem = pl.BlockSpec(memory_space=pltpu.VMEM)

    smem = pl.BlockSpec(memory_space=pltpu.SMEM)
    nodes_total = clus_count * clusters * panels

    cots = [cotangent] + [shifted(cotangent, "sub", step) for step in range(1, sub_count)]
    for step in range(1, rhs_count):
        cots += [shifted(block, "rhs", step) for block in cots[:sub_count]]

    by_coord = jnp.transpose(positions, (1, 0, 2))
    places = [device, sub_place, core, clusters * panels, row_count, panels, nodes_total]
    *parts, small = pl.pallas_call(
        prepare_kernel,
        out_shape=(
            jax.ShapeDtypeStruct((clusters * (rhs + 5), quarter), jnp.bfloat16),
            *[jax.ShapeDtypeStruct((clusters * rhs, quarter), jnp.bfloat16)] * (rhs_count - 1),
            jax.ShapeDtypeStruct((clusters * 4, row_count), jnp.bfloat16),
        ),
        in_specs=[smem] + [vmem] * 4,
        out_specs=(vmem,) * (rhs_count + 1),
        compiler_params=pltpu.CompilerParams(vmem_limit_bytes=16 * 1024 * 1024),
        name="prepare",
    )(jnp.stack([jnp.asarray(place, jnp.int32) for place in places]), density, by_coord, areas,
      connect[:, 0, :])
    arrived = [shifted(parts[0], "clus", 1)]
    for step in range(1, rhs_count):
        arrived.append(
            moved(parts[step], ("clus", "rhs"), lambda z, c, step=step: (z + 1, c + step))
        )
    source = jnp.concatenate(arrived, axis=0)

    per_round = 2 * ((clusters // 2 + clus_count - 2) // (clus_count - 1))
    cap = ROUNDS * per_round
    partners = lax.dynamic_slice_in_dim(matching, device * clusters, clusters, 1).reshape(-1)
    here = jnp.tile(jnp.arange(clusters, dtype=jnp.int32), ROUNDS)
    code = here * (2 * clusters) + partners % clusters
    behind = (device - partners // clusters) % clus_count
    total_items = ROUNDS * clusters
    order = jnp.arange(total_items, dtype=jnp.int32)
    rank = jnp.sum(
        ((behind[None, :] == behind[:, None]) & (order[None, :] < order[:, None])).astype(jnp.int32),
        axis=1,
    )
    steps = jnp.arange(1, clus_count, dtype=jnp.int32)
    member = behind[None, :] == steps[:, None]
    slots = jnp.arange(cap, dtype=jnp.int32)
    chosen = member[:, None, :] & (rank[None, None, :] == slots[None, :, None])
    listed = jnp.sum(jnp.where(chosen, code[None, None, :] - clusters, 0), axis=2) + clusters
    turns = (jnp.sum(member.astype(jnp.int32), axis=1) + 3) // 2
    length = cap + 6
    items = jnp.pad(listed, ((0, 0), (3, 3)), constant_values=clusters)
    items = jnp.concatenate([turns[:, None], items[:, 1:]], axis=1).reshape(-1)

    smalls = [small] + [shifted(small, "sub", step) for step in range(1, sub_count)]

    def in_order(blocks):
        return jnp.concatenate(
            [pick((sub_place - place) % sub_count, blocks) for place in range(sub_count)], axis=-1
        )

    jitter_all = in_order([block[3 * clusters :] for block in smalls]).astype(jnp.int32)
    own, pos = pl.pallas_call(
        own_kernel,
        out_shape=(
            jax.ShapeDtypeStruct((clusters, AUG, panels), jnp.bfloat16),
            jax.ShapeDtypeStruct((3, clusters, panels), jnp.bfloat16),
        ),
        in_specs=[vmem] * sub_count,
        out_specs=(vmem, vmem),
        scratch_shapes=[pltpu.VMEM((clusters, AUG, panels), jnp.float32)],
        compiler_params=pltpu.CompilerParams(vmem_limit_bytes=16 * 1024 * 1024),
        name="target_rows",
    )(*smalls)

    carried = None
    backs, jitter_rows = [], []
    for step in range(1, clus_count):
        if step > 1:
            if step > 2:
                source, backs[step - 3] = lax.optimization_barrier((source, backs[step - 3]))
            source = shifted(source, "clus", 1)
        last = step == clus_count - 1
        results = run_step(step - 1, length, items, source, cots, own, pos, carried, last)
        if last:
            pot, pot_out, grad, back = results
        else:
            carried, back = results
        backs.append(back)
        at = clusters * (rhs + 4)
        jitter_rows.append(source[at : at + clusters])

    grad = in_order([grad[..., at * row_count : (at + 1) * row_count] for at in range(sub_count)])
    low_part = (sub_place == 0) & (core == 0)
    high_part = (sub_place == sub_count - 1) & (core == rhs_count - 1)
    uppers = [grad[:, -1, -quarter:]] + [jnp.where(high_part, back[:, -1], 0.0) for back in backs]
    lowers = [grad[:, 0, :quarter]] + [jnp.where(low_part, back[:, 0], 0.0) for back in backs]
    returned = jnp.zeros((3, clusters, quarter), jnp.float32)
    upper, lower = uppers[1], lowers[clus_count - 1]
    nothing = jnp.zeros((2, quarter), jnp.float32)
    for step in range(1, clus_count):
        rows = [
            backs[step - 1].reshape(3 * clusters, quarter),
            uppers[(step + 1) % clus_count],
            lowers[step - 1],
            nothing,
        ]
        home = shifted(jnp.concatenate(rows, axis=0), "clus", -step)
        returned = returned + home[: 3 * clusters].reshape(returned.shape)
        upper = upper + home[3 * clusters : 3 * clusters + 3]
        lower = lower + home[3 * clusters + 3 : 3 * clusters + 6]

    half = pot
    for step in range(1, rhs_count):
        arrived = shifted(pot_out[:, (step - 1) * rhs : step * rhs], "rhs", -step)
        half = half + arrived.astype(jnp.float32)

    half, grad = lax.optimization_barrier((half, grad))
    found = [half[..., :row_count]]
    for step in range(1, sub_count):
        sent = half[..., step * row_count : (step + 1) * row_count].astype(jnp.bfloat16)
        found.append(shifted(sent, "sub", -step))

    quarter_at = sub_place * rhs_count + core
    grad = grad + jnp.concatenate(
        [jnp.where(quarter_at == at, returned, 0.0) for at in range(sub_count * rhs_count)], axis=-1
    )
    share = clusters // sub_count

    blank = jnp.zeros((3, panels - quarter), jnp.float32)
    before = jnp.concatenate([blank, upper], axis=1)
    after = jnp.concatenate([lower, blank], axis=1)
    jitter_float = jitter_all.astype(jnp.float32)
    jitter_before = jnp.concatenate(
        [blank[:1], jitter_rows[0][clusters - 1 :].astype(jnp.float32)], axis=1
    )
    jitter_after = jnp.concatenate([jitter_rows[-1][:1].astype(jnp.float32), blank[:1]], axis=1)

    def edge_rows(at):
        first, end = at * share, (at + 1) * share
        inside = at < sub_count - 1
        return jnp.concatenate(
            [
                grad[:, first - 1] if at > 0 else before,
                grad[:, end] if inside else after,
                jnp.where(high_part, jitter_float[first - 1 : first] if at > 0 else jitter_before, 0.0),
                jnp.where(low_part, jitter_float[end : end + 1] if inside else jitter_after, 0.0),
            ],
            axis=0,
        ).reshape(-1, share, panels)

    def packed(place):
        return pick(
            place % sub_count,
            [
                jnp.concatenate([grad[:, at * share : (at + 1) * share], edge_rows(at)], axis=0)
                for at in range(sub_count)
            ],
        )

    summed = packed(sub_place)
    for step in range(1, sub_count):
        summed = summed + shifted(packed(sub_place + step), "sub", step)
    gathered = summed
    for step in range(1, rhs_count):
        gathered = gathered + shifted(summed, "rhs", step)
    own_jitter = pick(
        sub_place, [jitter_all[at * share : (at + 1) * share] for at in range(sub_count)]
    )
    node_grad = pl.pallas_call(
        node_kernel,
        out_shape=jax.ShapeDtypeStruct((3, share * panels), jnp.float32),
        in_specs=[vmem] * 3,
        out_specs=vmem,
        compiler_params=pltpu.CompilerParams(vmem_limit_bytes=16 * 1024 * 1024),
        cost_estimate=pl.CostEstimate(flops=2**20, bytes_accessed=2**18, transcendentals=0),
        name="node_terms",
    )(gathered[:3], own_jitter, gathered[3:].reshape(8, panels))
    potential = pl.pallas_call(
        sum_kernel,
        out_shape=jax.ShapeDtypeStruct((clusters, rhs, row_count), jnp.bfloat16),
        in_specs=[vmem] * sub_count,
        out_specs=vmem,
        compiler_params=pltpu.CompilerParams(vmem_limit_bytes=16 * 1024 * 1024),
        cost_estimate=pl.CostEstimate(flops=2**20, bytes_accessed=2**18, transcendentals=0),
        name="potential_sum",
    )(*found)
    return (potential, node_grad)


def solution(mesh):
    placed = (
        P(("groups", "clus"), None, "sub"),
        P(("groups", "clus"), "sub"),
        P(("groups", "clus"), "rhs", "sub"),
        P(("groups", "clus"), "rhs", "sub"),
        P(None, "groups"),
        P(("groups", "clus"), None, "sub"),
    )
    return jax.shard_map(
        on_device,
        mesh=mesh,
        in_specs=placed,
        out_specs=(P(("groups", "clus"), "rhs", "sub"), P(None, ("groups", "clus", "sub"))),
        check_vma=False,
    )
```

```python
import functools

import jax
import jax.numpy as jnp
from jax import lax
from jax.experimental import pallas as pl
from jax.experimental.pallas import tpu as pltpu
from jax.sharding import PartitionSpec as P

CP = 512
ROUNDS = 5

core_radius = 0.25
jitter_reach = 8
LANES = 128
AUG = 16


def shifted(value, axis, steps):
    count = lax.axis_size(axis)
    pairs = [(source, (source + steps) % count) for source in range(count)]
    return lax.ppermute(value, axis, pairs)


def moved(value, axes, target):
    counts = [lax.axis_size(axis) for axis in axes]
    pairs = []
    for major in range(counts[0]):
        for minor in range(counts[1]):
            goal = target(major, minor)
            if goal is not None:
                to_major, to_minor = goal[0] % counts[0], goal[1] % counts[1]
                pairs.append((major * counts[1] + minor, to_major * counts[1] + to_minor))
    return lax.ppermute(value, axes, pairs)


def three_parts(value):
    parts = []
    for _ in range(3):
        part = value.astype(jnp.bfloat16).astype(jnp.float32)
        parts.append(part)
        value = value - part
    return parts


def pick(index, choices):
    out = choices[0]
    for place in range(1, len(choices)):
        out = jnp.where(index == place, choices[place], out)
    return out


def prepare_kernel(
    places, density_ref, by_coord_ref, areas_ref, connect_ref, cot_ref, cot_out_ref, *out_refs
):
    part_refs, small_ref = out_refs[:-1], out_refs[-1]
    clusters, rhs, row_count = density_ref.shape
    quarter = part_refs[0].shape[1]
    count = len(part_refs)
    device, sub_place, core = places[0], places[1], places[2]

    def part_of(array, place):
        return pick(place, [array[:, at * quarter : (at + 1) * quarter] for at in range(count)])

    first_id = places[3] * device + places[4] * sub_place
    ids = lax.broadcasted_iota(jnp.int32, (clusters, row_count), 0) * places[5]
    ids = ids + lax.broadcasted_iota(jnp.int32, (clusters, row_count), 1) + first_id
    cot_out_ref[...] = cot_ref[...]
    jitter = connect_ref[:, 0, :] - ids
    jitter = jnp.where(jitter > jitter_reach, jitter - places[6], jitter)
    jitter = jnp.where(jitter < -jitter_reach, jitter + places[6], jitter)
    jitter = jitter.astype(jnp.float32).astype(jnp.bfloat16)
    rows = [by_coord_ref[coord] for coord in range(3)] + [areas_ref[...], jitter]
    base = clusters * rhs
    for cluster in range(clusters):
        dens = density_ref[cluster]
        for step, part_ref in enumerate(part_refs):
            part_ref[cluster * rhs : (cluster + 1) * rhs, :] = part_of(dens, (core + step) % count)
    for at, value in enumerate(rows):
        span = slice(base + at * clusters, base + (at + 1) * clusters)
        part_refs[0][span, :] = part_of(value, core)
        if at != 3:
            at = min(at, 3)
            small_ref[at * clusters : (at + 1) * clusters, :] = value


def own_kernel(*refs):
    block_refs, (aug_ref, aug_t_ref, pos_ref, aug32) = refs[:-4], refs[-4:]
    clusters = aug_ref.shape[0]
    row_count = block_refs[0].shape[1]
    aug32[...] = jnp.zeros(aug32.shape, jnp.float32)
    for place, block_ref in enumerate(block_refs):
        cols = slice(place * row_count, (place + 1) * row_count)
        raw = [block_ref[coord * clusters : (coord + 1) * clusters, :] for coord in range(3)]
        pos = [value.astype(jnp.float32) for value in raw]
        square = pos[0] * pos[0] + pos[1] * pos[1] + pos[2] * pos[2] + core_radius * core_radius
        ones = jnp.ones_like(square)
        rows = [-2.0 * value for value in pos] + three_parts(square) + [ones] * 3
        for row, value in enumerate(rows):
            aug32[:, row, cols] = value
        for coord in range(3):
            pos_ref[coord, :, cols] = raw[coord]
    aug_ref[...] = aug32[...].astype(jnp.bfloat16)
    for cluster in range(clusters):
        aug_t_ref[cluster] = aug32[cluster].T.astype(jnp.bfloat16)


def step_kernel(step, length, rhs, blocks, first, last, *refs):
    items, source_ref, own_ref, own_t_ref = refs[:4]
    cot_refs = refs[4 : 4 + blocks[0] * blocks[1]]
    width = rhs * blocks[1]
    refs = refs[4 + len(cot_refs) :]
    if not first:
        acc_in = refs[0]
        refs = refs[1:]
    if last:
        pos_ref, pot_ref, pot_out_ref, grad_ref, back_ref, acc = refs[:6]
        refs = refs[6:]
    else:
        acc, back_ref = refs[:2]
        refs = refs[2:]
    aug32, aug_t, dens_t, left, weight, back, dist_a, dist_b, prod_a, prod_b, both_a, both_b = refs
    clusters, _, panels = own_ref.shape
    quarter = source_ref.shape[1]
    base = clusters * rhs
    starts = [0] + list(range(base + 5 * clusters, source_ref.shape[0], base))

    there = [
        source_ref[base + coord * clusters : base + (coord + 1) * clusters, :].astype(jnp.float32)
        for coord in range(3)
    ]
    area = source_ref[base + 3 * clusters : base + 4 * clusters, :].astype(jnp.float32)
    square = there[0] * there[0] + there[1] * there[1] + there[2] * there[2]
    ones = jnp.ones_like(square)
    aug32[...] = jnp.zeros(aug32.shape, jnp.float32)
    for row, value in enumerate(there + [ones] * 3 + three_parts(square)):
        aug32[:, row, :] = value
    weight_t = (CP ** (-0.5) * area).T
    left[...] = jnp.zeros(left.shape, left.dtype)
    for cluster in range(clusters):
        rows = aug32[cluster]
        left[cluster, width:, quarter:] = rows.astype(jnp.bfloat16)
        aug_t[cluster] = rows.T.astype(jnp.bfloat16)
        dens = jnp.concatenate(
            [source_ref[at + cluster * rhs : at + (cluster + 1) * rhs, :] for at in starts], axis=0
        )
        left[cluster, :width, :quarter] = dens
        dens_t[cluster] = dens.T
        weight[cluster] = jnp.broadcast_to(weight_t[:, cluster : cluster + 1], (quarter, LANES))
    weight[clusters] = jnp.zeros((quarter, LANES), jnp.float32)
    back[...] = jnp.zeros(back.shape, jnp.float32)
    if first:
        acc[...] = jnp.zeros(acc.shape, jnp.float32)
    else:
        acc[...] = acc_in[...]
    dist_b[...] = jnp.ones(dist_b.shape, jnp.float32)
    prod_b[...] = jnp.zeros(prod_b.shape, jnp.float32)
    both_a[...] = jnp.zeros(both_a.shape, both_a.dtype)

    def decoded(place):
        code = items[step * length + place]
        return code // (2 * clusters), code % (2 * clusters)

    def raw(place, dist, prod):
        here, mate = decoded(place)
        mate = mate % clusters
        dist[...] = jnp.dot(aug_t[mate], own_ref[here], preferred_element_type=jnp.float32)
        cot = [
            jnp.concatenate(
                [ref[here] for ref in cot_refs[at * blocks[0] : (at + 1) * blocks[0]]], axis=1
            )
            for at in range(blocks[1])
        ]
        prod[...] = jnp.dot(
            dens_t[mate], jnp.concatenate(cot, axis=0), preferred_element_type=jnp.float32
        )

    def pointwise(place, dist, prod, both):
        _, mate = decoded(place)
        scale = weight[mate]
        for start in range(0, panels, LANES):
            cols = slice(start, start + LANES)
            inverse = lax.rsqrt(dist[:, cols])
            kernel = scale * inverse
            both[:quarter, cols] = kernel.astype(jnp.bfloat16)
            both[quarter:, cols] = ((inverse * inverse) * (kernel * prod[:, cols])).astype(jnp.bfloat16)

    def summed(place, both):
        here, mate = decoded(place)
        mate = mate % clusters
        acc[here] += jnp.dot(left[mate], both[...], preferred_element_type=jnp.float32)
        back[mate] += jnp.dot(
            both[quarter:, :], own_t_ref[here], preferred_element_type=jnp.float32
        )

    @pl.loop(0, items[step * length])
    def _(pair):
        turn = 2 * pair + 1
        summed(turn, both_a)
        pointwise(turn + 1, dist_b, prod_b, both_b)
        raw(turn + 2, dist_a, prod_a)
        summed(turn + 1, both_b)
        pointwise(turn + 2, dist_a, prod_a, both_a)
        raw(turn + 3, dist_b, prod_b)

    for cluster in range(clusters):
        aug32[cluster] = back[cluster].T
    for coord in range(3):
        back_ref[coord] = -0.5 * aug32[:, coord, :] - there[coord] * aug32[:, 6, :]
    if last:
        for coord in range(3):
            grad_ref[coord] = (
                acc[:, width + coord, :]
                - pos_ref[coord].astype(jnp.float32) * acc[:, width + 3, :]
            )
        pot_ref[...] = acc[:, :rhs, :]
        pot_out_ref[...] = acc[:, rhs:width, :].astype(jnp.bfloat16)


def run_step(step, length, items, source, cots, own, own_t, pos, carried, last):
    clusters, _, panels = own.shape
    quarter = source.shape[1]
    rhs = cots[0].shape[1]
    sub_blocks = panels // cots[0].shape[2]
    blocks = (sub_blocks, len(cots) // sub_blocks)
    width = rhs * blocks[1]
    first = carried is None
    vmem = pl.BlockSpec(memory_space=pltpu.VMEM)
    smem = pl.BlockSpec(memory_space=pltpu.SMEM)
    operands = (items, source, own, own_t, *cots)
    if not first:
        operands += (carried,)
    acc_shape = (clusters, width + AUG, panels)
    back_shape = jax.ShapeDtypeStruct((3, clusters, quarter), jnp.float32)
    scratch = [
        pltpu.VMEM((clusters, AUG, quarter), jnp.float32),
        pltpu.VMEM((clusters, quarter, AUG), jnp.bfloat16),
        pltpu.VMEM((clusters, quarter, width), jnp.bfloat16),
        pltpu.VMEM((clusters, width + AUG, 2 * quarter), jnp.bfloat16),
        pltpu.VMEM((clusters + 1, quarter, LANES), jnp.float32),
        pltpu.VMEM((clusters, quarter, AUG), jnp.float32),
    ]
    scratch += [pltpu.VMEM((quarter, panels), jnp.float32)] * 4
    scratch += [pltpu.VMEM((2 * quarter, panels), jnp.bfloat16)] * 2
    if last:
        operands += (pos,)
        out_shape = (
            jax.ShapeDtypeStruct((clusters, rhs, panels), jnp.float32),
            jax.ShapeDtypeStruct((clusters, width - rhs, panels), jnp.bfloat16),
            jax.ShapeDtypeStruct((3, clusters, panels), jnp.float32),
            back_shape,
        )
        scratch = [pltpu.VMEM(acc_shape, jnp.float32)] + scratch
    else:
        out_shape = (jax.ShapeDtypeStruct(acc_shape, jnp.float32), back_shape)
    pairs = (length - 6) * panels * quarter
    return pl.pallas_call(
        functools.partial(step_kernel, step, length, rhs, blocks, first, last),
        out_shape=out_shape,
        in_specs=[smem] + [vmem] * (len(operands) - 1),
        out_specs=(vmem,) * len(out_shape),
        scratch_shapes=scratch,
        compiler_params=pltpu.CompilerParams(vmem_limit_bytes=16 * 1024 * 1024),
        cost_estimate=pl.CostEstimate(
            flops=2 * pairs * (2 * width + 3 * AUG), bytes_accessed=6 * 2**20, transcendentals=pairs
        ),
        name=f"near_field_{step}",
    )(*operands)


def node_kernel(grad_ref, jitter_ref, edge_ref, main_ref):
    clusters, panels = jitter_ref.shape
    wide = panels + 2 * LANES

    def spread_of(terms, jitter):
        side = jnp.zeros((terms.shape[0], LANES), jnp.float32)
        terms = 0.25 * terms
        spread = jnp.zeros((terms.shape[0], wide), jnp.float32)
        for offset in range(-jitter_reach, jitter_reach + 1):
            masked = jnp.where(jitter == offset, terms, 0.0)
            masked = jnp.concatenate([side, masked, side], axis=1)
            spread = spread + pltpu.roll(masked, offset % wide, 1)
        spread = spread + pltpu.roll(spread, 1, 1)
        return spread + pltpu.roll(spread, 32, 1)

    jitter = jitter_ref[...]
    row_at = lax.broadcasted_iota(jnp.int32, (clusters, LANES), 0)
    edge = edge_ref[...]
    edge_at = lax.broadcasted_iota(jnp.int32, edge.shape, 0)
    edge_jitter = jnp.where(edge_at < 3, edge[6:7], edge[7:8]).astype(jnp.int32)
    edge = spread_of(edge, edge_jitter)
    for coord in range(3):
        spread = spread_of(grad_ref[coord], jitter)
        below = spread[:, :LANES]
        above = spread[:, LANES + panels :]
        inner = spread[:, LANES : LANES + panels]
        before = edge[coord : coord + 1, LANES + panels :]
        after = edge[3 + coord : 4 + coord, :LANES]
        first = jnp.where(row_at == 0, before, pltpu.roll(above, 1, 0))
        last = jnp.where(row_at == clusters - 1, after, pltpu.roll(below, clusters - 1, 0))
        inner = jnp.concatenate(
            [
                inner[:, :LANES] + first,
                inner[:, LANES : panels - LANES],
                inner[:, panels - LANES :] + last,
            ],
            axis=1,
        )
        for cluster in range(clusters):
            main_ref[coord : coord + 1, cluster * panels : (cluster + 1) * panels] = inner[
                cluster : cluster + 1
            ]


def sum_kernel(*refs):
    total = refs[0][...]
    for ref in refs[1:-1]:
        total = total + ref[...].astype(jnp.float32)
    refs[-1][...] = total.astype(jnp.bfloat16)


def on_device(positions, areas, density, cotangent, matching, connect):
    clus_count = lax.axis_size("clus")
    sub_count = lax.axis_size("sub")
    rhs_count = lax.axis_size("rhs")
    device = lax.axis_index("clus")
    sub_place = lax.axis_index("sub")
    core = lax.axis_index("rhs")
    clusters, rhs, row_count = density.shape
    panels = row_count * sub_count
    quarter = row_count // rhs_count
    width = rhs * rhs_count
    vmem = pl.BlockSpec(memory_space=pltpu.VMEM)

    smem = pl.BlockSpec(memory_space=pltpu.SMEM)
    nodes_total = clus_count * clusters * panels

    cots = [cotangent] + [shifted(cotangent, "sub", step) for step in range(1, sub_count)]
    for step in range(1, rhs_count):
        cots += [shifted(block, "rhs", step) for block in cots[:sub_count]]

    by_coord = jnp.transpose(positions, (1, 0, 2))
    places = [device, sub_place, core, clusters * panels, row_count, panels, nodes_total]
    own_cot, *parts, small = pl.pallas_call(
        prepare_kernel,
        out_shape=(
            jax.ShapeDtypeStruct(cotangent.shape, jnp.bfloat16),
            jax.ShapeDtypeStruct((clusters * (rhs + 5), quarter), jnp.bfloat16),
            *[jax.ShapeDtypeStruct((clusters * rhs, quarter), jnp.bfloat16)] * (rhs_count - 1),
            jax.ShapeDtypeStruct((clusters * 4, row_count), jnp.bfloat16),
        ),
        in_specs=[smem] + [vmem] * 5,
        out_specs=(vmem,) * (rhs_count + 2),
        compiler_params=pltpu.CompilerParams(vmem_limit_bytes=56 * 1024 * 1024),
        name="prepare",
    )(jnp.stack([jnp.asarray(place, jnp.int32) for place in places]), density, by_coord, areas,
      connect, cotangent)
    cots[0] = own_cot
    arrived = [shifted(parts[0], "clus", 1)]
    for step in range(1, rhs_count):
        arrived.append(
            moved(parts[step], ("clus", "rhs"), lambda z, c, step=step: (z + 1, c + step))
        )
    arrived, cots = lax.optimization_barrier((arrived, cots))
    source = jnp.concatenate(arrived, axis=0)

    per_round = 2 * ((clusters // 2 + clus_count - 2) // (clus_count - 1))
    cap = ROUNDS * per_round
    partners = lax.dynamic_slice_in_dim(matching, device * clusters, clusters, 1).reshape(-1)
    here = jnp.tile(jnp.arange(clusters, dtype=jnp.int32), ROUNDS)
    code = here * (2 * clusters) + partners % clusters
    behind = (device - partners // clusters) % clus_count
    total_items = ROUNDS * clusters
    order = jnp.arange(total_items, dtype=jnp.int32)
    rank = jnp.sum(
        ((behind[None, :] == behind[:, None]) & (order[None, :] < order[:, None])).astype(jnp.int32),
        axis=1,
    )
    steps = jnp.arange(1, clus_count, dtype=jnp.int32)
    member = behind[None, :] == steps[:, None]
    slots = jnp.arange(cap, dtype=jnp.int32)
    chosen = member[:, None, :] & (rank[None, None, :] == slots[None, :, None])
    listed = jnp.sum(jnp.where(chosen, code[None, None, :] - clusters, 0), axis=2) + clusters
    turns = (jnp.sum(member.astype(jnp.int32), axis=1) + 3) // 2
    length = cap + 6
    items = jnp.pad(listed, ((0, 0), (3, 3)), constant_values=clusters)
    items = jnp.concatenate([turns[:, None], items[:, 1:]], axis=1).reshape(-1)

    smalls = [small] + [shifted(small, "sub", step) for step in range(1, sub_count)]

    def in_order(blocks):
        return jnp.concatenate(
            [pick((sub_place - place) % sub_count, blocks) for place in range(sub_count)], axis=-1
        )

    jitter_all = in_order([block[3 * clusters :] for block in smalls]).astype(jnp.int32)
    own, own_t, pos = pl.pallas_call(
        own_kernel,
        out_shape=(
            jax.ShapeDtypeStruct((clusters, AUG, panels), jnp.bfloat16),
            jax.ShapeDtypeStruct((clusters, panels, AUG), jnp.bfloat16),
            jax.ShapeDtypeStruct((3, clusters, panels), jnp.bfloat16),
        ),
        in_specs=[vmem] * sub_count,
        out_specs=(vmem, vmem, vmem),
        scratch_shapes=[pltpu.VMEM((clusters, AUG, panels), jnp.float32)],
        compiler_params=pltpu.CompilerParams(vmem_limit_bytes=16 * 1024 * 1024),
        name="target_rows",
    )(*smalls)

    carried = None
    backs, jitter_rows = [], []
    for step in range(1, clus_count):
        if step > 1:
            if step > 2:
                source, backs[step - 3] = lax.optimization_barrier((source, backs[step - 3]))
            source = shifted(source, "clus", 1)
        last = step == clus_count - 1
        results = run_step(step - 1, length, items, source, cots, own, own_t, pos, carried, last)
        if last:
            pot, pot_out, grad, back = results
        else:
            carried, back = results
        backs.append(back)
        at = clusters * (rhs + 4)
        jitter_rows.append(source[at : at + clusters])

    grad = in_order([grad[..., at * row_count : (at + 1) * row_count] for at in range(sub_count)])
    low_part = (sub_place == 0) & (core == 0)
    high_part = (sub_place == sub_count - 1) & (core == rhs_count - 1)
    uppers = [grad[:, -1, -quarter:]] + [jnp.where(high_part, back[:, -1], 0.0) for back in backs]
    lowers = [grad[:, 0, :quarter]] + [jnp.where(low_part, back[:, 0], 0.0) for back in backs]
    returned = jnp.zeros((3, clusters, quarter), jnp.float32)
    upper, lower = uppers[1], lowers[clus_count - 1]
    nothing = jnp.zeros((2, quarter), jnp.float32)
    for step in range(1, clus_count):
        rows = [
            backs[step - 1].reshape(3 * clusters, quarter),
            uppers[(step + 1) % clus_count],
            lowers[step - 1],
            nothing,
        ]
        home = shifted(jnp.concatenate(rows, axis=0), "clus", -step)
        returned = returned + home[: 3 * clusters].reshape(returned.shape)
        upper = upper + home[3 * clusters : 3 * clusters + 3]
        lower = lower + home[3 * clusters + 3 : 3 * clusters + 6]

    half = pot
    for step in range(1, rhs_count):
        arrived = shifted(pot_out[:, (step - 1) * rhs : step * rhs], "rhs", -step)
        half = half + arrived.astype(jnp.float32)

    half, grad = lax.optimization_barrier((half, grad))
    found = [half[..., :row_count]]
    for step in range(1, sub_count):
        sent = half[..., step * row_count : (step + 1) * row_count].astype(jnp.bfloat16)
        found.append(shifted(sent, "sub", -step))

    quarter_at = sub_place * rhs_count + core
    grad = grad + jnp.concatenate(
        [jnp.where(quarter_at == at, returned, 0.0) for at in range(sub_count * rhs_count)], axis=-1
    )
    share = clusters // sub_count

    blank = jnp.zeros((3, panels - quarter), jnp.float32)
    before = jnp.concatenate([blank, upper], axis=1)
    after = jnp.concatenate([lower, blank], axis=1)
    jitter_float = jitter_all.astype(jnp.float32)
    jitter_before = jnp.concatenate(
        [blank[:1], jitter_rows[0][clusters - 1 :].astype(jnp.float32)], axis=1
    )
    jitter_after = jnp.concatenate([jitter_rows[-1][:1].astype(jnp.float32), blank[:1]], axis=1)

    def edge_rows(at):
        first, end = at * share, (at + 1) * share
        inside = at < sub_count - 1
        return jnp.concatenate(
            [
                grad[:, first - 1] if at > 0 else before,
                grad[:, end] if inside else after,
                jnp.where(high_part, jitter_float[first - 1 : first] if at > 0 else jitter_before, 0.0),
                jnp.where(low_part, jitter_float[end : end + 1] if inside else jitter_after, 0.0),
            ],
            axis=0,
        ).reshape(-1, share, panels)

    def packed(place):
        return pick(
            place % sub_count,
            [
                jnp.concatenate([grad[:, at * share : (at + 1) * share], edge_rows(at)], axis=0)
                for at in range(sub_count)
            ],
        )

    summed = packed(sub_place)
    for step in range(1, sub_count):
        summed = summed + shifted(packed(sub_place + step), "sub", step)
    gathered = summed
    for step in range(1, rhs_count):
        gathered = gathered + shifted(summed, "rhs", step)
    own_jitter = pick(
        sub_place, [jitter_all[at * share : (at + 1) * share] for at in range(sub_count)]
    )
    node_grad = pl.pallas_call(
        node_kernel,
        out_shape=jax.ShapeDtypeStruct((3, share * panels), jnp.float32),
        in_specs=[vmem] * 3,
        out_specs=vmem,
        compiler_params=pltpu.CompilerParams(vmem_limit_bytes=16 * 1024 * 1024),
        cost_estimate=pl.CostEstimate(flops=2**20, bytes_accessed=2**18, transcendentals=0),
        name="node_terms",
    )(gathered[:3], own_jitter, gathered[3:].reshape(8, panels))
    potential = pl.pallas_call(
        sum_kernel,
        out_shape=jax.ShapeDtypeStruct((clusters, rhs, row_count), jnp.bfloat16),
        in_specs=[vmem] * sub_count,
        out_specs=vmem,
        compiler_params=pltpu.CompilerParams(vmem_limit_bytes=16 * 1024 * 1024),
        cost_estimate=pl.CostEstimate(flops=2**20, bytes_accessed=2**18, transcendentals=0),
        name="potential_sum",
    )(*found)
    return (potential, node_grad)


def solution(mesh):
    placed = (
        P(("groups", "clus"), None, "sub"),
        P(("groups", "clus"), "sub"),
        P(("groups", "clus"), "rhs", "sub"),
        P(("groups", "clus"), "rhs", "sub"),
        P(None, "groups"),
        P(("groups", "clus"), None, "sub"),
    )
    return jax.shard_map(
        on_device,
        mesh=mesh,
        in_specs=placed,
        out_specs=(P(("groups", "clus"), "rhs", "sub"), P(None, ("groups", "clus", "sub"))),
        check_vma=False,
    )
```

```python
import functools

import jax
import jax.numpy as jnp
from jax import lax
from jax.experimental import pallas as pl
from jax.experimental.pallas import tpu as pltpu
from jax.sharding import PartitionSpec as P

CP = 512
ROUNDS = 5

core_radius = 0.25
jitter_reach = 8
LANES = 128
AUG = 16


def shifted(value, axis, steps):
    count = lax.axis_size(axis)
    pairs = [(source, (source + steps) % count) for source in range(count)]
    return lax.ppermute(value, axis, pairs)


def moved(value, axes, target):
    counts = [lax.axis_size(axis) for axis in axes]
    pairs = []
    for major in range(counts[0]):
        for minor in range(counts[1]):
            goal = target(major, minor)
            if goal is not None:
                to_major, to_minor = goal[0] % counts[0], goal[1] % counts[1]
                pairs.append((major * counts[1] + minor, to_major * counts[1] + to_minor))
    return lax.ppermute(value, axes, pairs)


def three_parts(value):
    parts = []
    for _ in range(3):
        part = value.astype(jnp.bfloat16).astype(jnp.float32)
        parts.append(part)
        value = value - part
    return parts


def pick(index, choices):
    out = choices[0]
    for place in range(1, len(choices)):
        out = jnp.where(index == place, choices[place], out)
    return out


def prepare_kernel(sizes, *refs):
    arguments, refs = refs[:5], refs[5:]
    cot_out_ref, part_refs, small_ref = refs[0], refs[1:-7], refs[-7]
    density_ref, by_coord_ref, areas_ref, connect_ref, cot_ref, sems = refs[-6:]
    copies = []
    for at, (argument, place) in enumerate(
        zip(arguments, (density_ref, by_coord_ref, areas_ref, connect_ref, cot_ref))
    ):
        copies.append(pltpu.make_async_copy(argument, place, sems.at[at]))
        copies[-1].start()
    for copy in copies:
        copy.wait()

    clusters, rhs, row_count = density_ref.shape
    quarter = part_refs[0].shape[1]
    count = len(part_refs)
    panels, nodes_total = sizes
    device, sub_place, core = (lax.axis_index(axis) for axis in ("clus", "sub", "rhs"))

    def part_of(array, place):
        return pick(place, [array[:, at * quarter : (at + 1) * quarter] for at in range(count)])

    cot_out_ref[...] = cot_ref[...]
    first_id = clusters * panels * device + row_count * sub_place
    ids = lax.broadcasted_iota(jnp.int32, (clusters, row_count), 0) * panels
    ids = ids + lax.broadcasted_iota(jnp.int32, (clusters, row_count), 1) + first_id
    jitter = connect_ref[:, 0, :] - ids
    jitter = jnp.where(jitter > jitter_reach, jitter - nodes_total, jitter)
    jitter = jnp.where(jitter < -jitter_reach, jitter + nodes_total, jitter)
    jitter = jitter.astype(jnp.float32).astype(jnp.bfloat16)
    rows = [by_coord_ref[coord] for coord in range(3)] + [areas_ref[...], jitter]
    base = clusters * rhs
    for cluster in range(clusters):
        dens = density_ref[cluster]
        for step, part_ref in enumerate(part_refs):
            part_ref[cluster * rhs : (cluster + 1) * rhs, :] = part_of(dens, (core + step) % count)
    for at, value in enumerate(rows):
        span = slice(base + at * clusters, base + (at + 1) * clusters)
        part_refs[0][span, :] = part_of(value, core)
        if at != 3:
            at = min(at, 3)
            small_ref[at * clusters : (at + 1) * clusters, :] = value


def target_kernel(rhs_count, small_ref, *refs):
    cot_refs, (lhs_ref, aug_ref, aug32) = refs[:rhs_count], refs[rhs_count:]
    clusters, _, row_count = aug_ref.shape
    pos = [
        small_ref[coord * clusters : (coord + 1) * clusters, :].astype(jnp.float32)
        for coord in range(3)
    ]
    square = pos[0] * pos[0] + pos[1] * pos[1] + pos[2] * pos[2] + core_radius * core_radius
    ones = jnp.ones_like(square)
    aug32[...] = jnp.zeros(aug32.shape, jnp.float32)
    for row, value in enumerate([-2.0 * value for value in pos] + three_parts(square) + [ones] * 3):
        aug32[:, row, :] = value
    filled = AUG + sum(ref.shape[1] for ref in cot_refs)
    blank = jnp.zeros((LANES - filled, row_count), jnp.bfloat16)
    for cluster in range(clusters):
        aug = aug32[cluster].astype(jnp.bfloat16)
        aug_ref[cluster] = aug
        rows = [ref[cluster] for ref in cot_refs] + [aug, blank]
        lhs_ref[cluster] = jnp.concatenate(rows, axis=0).T


def step_kernel(step, length, rhs, subs, first, last, *refs):
    items, source_ref = refs[:2]
    lhs_refs, aug_refs, refs = refs[2 : 2 + subs], refs[2 + subs : 2 + 2 * subs], refs[2 + 2 * subs :]
    if not first:
        acc_in, refs = refs[0], refs[1:]
    if last:
        small_refs, refs = refs[:subs], refs[subs:]
        pot_ref, pot_out_ref, grad_ref, back_ref, acc = refs[:5]
        refs = refs[5:]
    else:
        acc, back_ref = refs[:2]
        refs = refs[2:]
    aug32, left, weight, back, raw_a, raw_b, both_a, both_b = refs
    clusters, rows, panels = acc.shape
    width = rows - AUG
    row_count = panels // subs
    quarter = source_ref.shape[1]
    base = clusters * rhs
    starts = [0] + list(range(base + 5 * clusters, source_ref.shape[0], base))

    there = [
        source_ref[base + coord * clusters : base + (coord + 1) * clusters, :].astype(jnp.float32)
        for coord in range(3)
    ]
    area = source_ref[base + 3 * clusters : base + 4 * clusters, :].astype(jnp.float32)
    square = there[0] * there[0] + there[1] * there[1] + there[2] * there[2]
    ones = jnp.ones_like(square)
    aug32[...] = jnp.zeros(aug32.shape, jnp.float32)
    for row, value in enumerate(there + [ones] * 3 + three_parts(square)):
        aug32[:, row, :] = value
    weight[...] = jnp.zeros(weight.shape, jnp.float32)
    weight[:clusters, :] = CP ** (-0.5) * area
    left[...] = jnp.zeros(left.shape, left.dtype)
    for cluster in range(clusters):
        left[cluster, width:rows, quarter:] = aug32[cluster].astype(jnp.bfloat16)
        for place, at in enumerate(starts):
            left[cluster, place * rhs : (place + 1) * rhs, :quarter] = source_ref[
                at + cluster * rhs : at + (cluster + 1) * rhs, :
            ]
    back[...] = jnp.zeros(back.shape, jnp.float32)
    if first:
        acc[...] = jnp.zeros(acc.shape, jnp.float32)
    else:
        acc[...] = acc_in[...]
    raw_b[...] = jnp.ones(raw_b.shape, jnp.float32)
    both_a[...] = jnp.zeros(both_a.shape, both_a.dtype)

    def decoded(place):
        code = items[step * length + place]
        return code // (2 * clusters), code % (2 * clusters)

    def products(place, raw):
        here, mate = decoded(place)
        mate = mate % clusters
        lhs = jnp.concatenate([ref[here] for ref in lhs_refs], axis=0)
        raw[...] = jnp.dot(lhs, left[mate], preferred_element_type=jnp.float32)

    def pointwise(place, raw, both):
        _, mate = decoded(place)
        scale = weight[pl.ds(mate, 1), :]
        for start in range(0, panels, LANES):
            span = slice(start, start + LANES)
            inverse = lax.rsqrt(raw[span, quarter:])
            kernel = scale * inverse
            both[span, :quarter] = kernel.astype(jnp.bfloat16)
            weighted = (inverse * inverse) * (kernel * raw[span, :quarter])
            both[span, quarter:] = weighted.astype(jnp.bfloat16)

    def summed(place, both):
        here, mate = decoded(place)
        mate = mate % clusters
        acc[here] += lax.dot_general(
            left[mate, :rows, :],
            both[...],
            (((1,), (1,)), ((), ())),
            preferred_element_type=jnp.float32,
        )
        aug = jnp.concatenate([ref[here] for ref in aug_refs], axis=1)
        back[mate] += jnp.dot(aug, both[:, quarter:], preferred_element_type=jnp.float32)

    @pl.loop(0, items[step * length])
    def _(pair):
        turn = 2 * pair + 1
        summed(turn, both_a)
        pointwise(turn + 1, raw_b, both_b)
        products(turn + 2, raw_a)
        summed(turn + 1, both_b)
        pointwise(turn + 2, raw_a, both_a)
        products(turn + 3, raw_b)

    for coord in range(3):
        back_ref[coord] = -0.5 * back[:, coord, :] - there[coord] * back[:, 6, :]
    if last:
        for coord in range(3):
            pos = [ref[coord * clusters : (coord + 1) * clusters, :] for ref in small_refs]
            pos = jnp.concatenate(pos, axis=1).astype(jnp.float32)
            grad_ref[coord] = acc[:, width + coord, :] - pos * acc[:, width + 3, :]
        pot_ref[...] = acc[:, :rhs, :]
        pot_out_ref[...] = acc[:, rhs:width, :].astype(jnp.bfloat16)


def run_step(step, length, items, source, targets, smalls, rhs, width, carried, last):
    lhss, augs = zip(*targets)
    clusters, _, row_count = augs[0].shape
    subs = len(targets)
    panels = subs * row_count
    quarter = source.shape[1]
    first = carried is None
    vmem = pl.BlockSpec(memory_space=pltpu.VMEM)
    smem = pl.BlockSpec(memory_space=pltpu.SMEM)
    operands = (items, source, *lhss, *augs)
    if not first:
        operands += (carried,)
    acc_shape = (clusters, width + AUG, panels)
    back_shape = jax.ShapeDtypeStruct((3, clusters, quarter), jnp.float32)
    scratch = [
        pltpu.VMEM((clusters, AUG, quarter), jnp.float32),
        pltpu.VMEM((clusters, LANES, 2 * quarter), jnp.bfloat16),
        pltpu.VMEM((clusters + 8, quarter), jnp.float32),
        pltpu.VMEM((clusters, AUG, quarter), jnp.float32),
    ]
    scratch += [pltpu.VMEM((panels, 2 * quarter), jnp.float32)] * 2
    scratch += [pltpu.VMEM((panels, 2 * quarter), jnp.bfloat16)] * 2
    if last:
        operands += tuple(smalls)
        out_shape = (
            jax.ShapeDtypeStruct((clusters, rhs, panels), jnp.float32),
            jax.ShapeDtypeStruct((clusters, width - rhs, panels), jnp.bfloat16),
            jax.ShapeDtypeStruct((3, clusters, panels), jnp.float32),
            back_shape,
        )
        scratch = [pltpu.VMEM(acc_shape, jnp.float32)] + scratch
    else:
        out_shape = (jax.ShapeDtypeStruct(acc_shape, jnp.float32), back_shape)
    pairs = (length - 6) * panels * quarter
    return pl.pallas_call(
        functools.partial(step_kernel, step, length, rhs, subs, first, last),
        out_shape=out_shape,
        in_specs=[smem] + [vmem] * (len(operands) - 1),
        out_specs=(vmem,) * len(out_shape),
        scratch_shapes=scratch,
        compiler_params=pltpu.CompilerParams(vmem_limit_bytes=20 * 1024 * 1024),
        cost_estimate=pl.CostEstimate(
            flops=2 * pairs * (2 * width + 3 * AUG), bytes_accessed=6 * 2**20, transcendentals=pairs
        ),
        name=f"near_field_{step}",
    )(*operands)


def node_kernel(grad_ref, jitter_ref, edge_ref, main_ref):
    clusters, panels = jitter_ref.shape
    wide = panels + 2 * LANES

    def spread_of(terms, jitter):
        side = jnp.zeros((terms.shape[0], LANES), jnp.float32)
        terms = 0.25 * terms
        spread = jnp.zeros((terms.shape[0], wide), jnp.float32)
        for offset in range(-jitter_reach, jitter_reach + 1):
            masked = jnp.where(jitter == offset, terms, 0.0)
            masked = jnp.concatenate([side, masked, side], axis=1)
            spread = spread + pltpu.roll(masked, offset % wide, 1)
        spread = spread + pltpu.roll(spread, 1, 1)
        return spread + pltpu.roll(spread, 32, 1)

    jitter = jitter_ref[...]
    row_at = lax.broadcasted_iota(jnp.int32, (clusters, LANES), 0)
    edge = edge_ref[...]
    edge_at = lax.broadcasted_iota(jnp.int32, edge.shape, 0)
    edge_jitter = jnp.where(edge_at < 3, edge[6:7], edge[7:8]).astype(jnp.int32)
    edge = spread_of(edge, edge_jitter)
    for coord in range(3):
        spread = spread_of(grad_ref[coord], jitter)
        below = spread[:, :LANES]
        above = spread[:, LANES + panels :]
        inner = spread[:, LANES : LANES + panels]
        before = edge[coord : coord + 1, LANES + panels :]
        after = edge[3 + coord : 4 + coord, :LANES]
        first = jnp.where(row_at == 0, before, pltpu.roll(above, 1, 0))
        last = jnp.where(row_at == clusters - 1, after, pltpu.roll(below, clusters - 1, 0))
        inner = jnp.concatenate(
            [
                inner[:, :LANES] + first,
                inner[:, LANES : panels - LANES],
                inner[:, panels - LANES :] + last,
            ],
            axis=1,
        )
        for cluster in range(clusters):
            main_ref[coord : coord + 1, cluster * panels : (cluster + 1) * panels] = inner[
                cluster : cluster + 1
            ]


def sum_kernel(*refs):
    total = refs[0][...]
    for ref in refs[1:-1]:
        total = total + ref[...].astype(jnp.float32)
    refs[-1][...] = total.astype(jnp.bfloat16)


def on_device(positions, areas, density, cotangent, matching, connect):
    clus_count = lax.axis_size("clus")
    sub_count = lax.axis_size("sub")
    rhs_count = lax.axis_size("rhs")
    device = lax.axis_index("clus")
    sub_place = lax.axis_index("sub")
    core = lax.axis_index("rhs")
    clusters, rhs, row_count = density.shape
    panels = row_count * sub_count
    quarter = row_count // rhs_count
    width = rhs * rhs_count
    vmem = pl.BlockSpec(memory_space=pltpu.VMEM)

    nodes_total = clus_count * clusters * panels

    cots = [cotangent] + [shifted(cotangent, "sub", step) for step in range(1, sub_count)]
    for step in range(1, rhs_count):
        cots += [shifted(block, "rhs", step) for block in cots[:sub_count]]

    by_coord = jnp.transpose(positions, (1, 0, 2))
    arguments = (density, by_coord, areas, connect, cotangent)
    own_cot, *parts, small = pl.pallas_call(
        functools.partial(prepare_kernel, (panels, nodes_total)),
        out_shape=(
            jax.ShapeDtypeStruct(cotangent.shape, jnp.bfloat16),
            jax.ShapeDtypeStruct((clusters * (rhs + 5), quarter), jnp.bfloat16),
            *[jax.ShapeDtypeStruct((clusters * rhs, quarter), jnp.bfloat16)] * (rhs_count - 1),
            jax.ShapeDtypeStruct((clusters * 4, row_count), jnp.bfloat16),
        ),
        in_specs=[pl.BlockSpec(memory_space=pltpu.HBM)] * len(arguments),
        out_specs=(vmem,) * (rhs_count + 2),
        scratch_shapes=[pltpu.VMEM(array.shape, array.dtype) for array in arguments]
        + [pltpu.SemaphoreType.DMA((len(arguments),))],
        compiler_params=pltpu.CompilerParams(vmem_limit_bytes=16 * 1024 * 1024),
        name="prepare",
    )(*arguments)
    cots[0] = own_cot
    arrived = [shifted(parts[0], "clus", 1)]
    for step in range(1, rhs_count):
        arrived.append(
            moved(parts[step], ("clus", "rhs"), lambda z, c, step=step: (z + 1, c + step))
        )

    per_round = 2 * ((clusters // 2 + clus_count - 2) // (clus_count - 1))
    cap = ROUNDS * per_round
    partners = lax.dynamic_slice_in_dim(matching, device * clusters, clusters, 1).reshape(-1)
    here = jnp.tile(jnp.arange(clusters, dtype=jnp.int32), ROUNDS)
    code = here * (2 * clusters) + partners % clusters
    behind = (device - partners // clusters) % clus_count
    total_items = ROUNDS * clusters
    order = jnp.arange(total_items, dtype=jnp.int32)
    rank = jnp.sum(
        ((behind[None, :] == behind[:, None]) & (order[None, :] < order[:, None])).astype(jnp.int32),
        axis=1,
    )
    steps = jnp.arange(1, clus_count, dtype=jnp.int32)
    member = behind[None, :] == steps[:, None]
    slots = jnp.arange(cap, dtype=jnp.int32)
    chosen = member[:, None, :] & (rank[None, None, :] == slots[None, :, None])
    listed = jnp.sum(jnp.where(chosen, code[None, None, :] - clusters, 0), axis=2) + clusters
    turns = (jnp.sum(member.astype(jnp.int32), axis=1) + 3) // 2
    length = cap + 6
    items = jnp.pad(listed, ((0, 0), (3, 3)), constant_values=clusters)
    items = jnp.concatenate([turns[:, None], items[:, 1:]], axis=1).reshape(-1)

    smalls = [small] + [shifted(small, "sub", step) for step in range(1, sub_count)]

    def in_order(blocks):
        return jnp.concatenate(
            [pick((sub_place - place) % sub_count, blocks) for place in range(sub_count)], axis=-1
        )

    jitter_all = in_order([block[3 * clusters :] for block in smalls]).astype(jnp.int32)
    targets = [
        pl.pallas_call(
            functools.partial(target_kernel, rhs_count),
            out_shape=(
                jax.ShapeDtypeStruct((clusters, row_count, LANES), jnp.bfloat16),
                jax.ShapeDtypeStruct((clusters, AUG, row_count), jnp.bfloat16),
            ),
            in_specs=[vmem] * (1 + rhs_count),
            out_specs=(vmem, vmem),
            scratch_shapes=[pltpu.VMEM((clusters, AUG, row_count), jnp.float32)],
            compiler_params=pltpu.CompilerParams(vmem_limit_bytes=16 * 1024 * 1024),
            name=f"targets_{place}",
        )(smalls[place], *cots[place::sub_count])
        for place in range(sub_count)
    ]

    arrived, targets = lax.optimization_barrier((arrived, targets))
    source = jnp.concatenate(arrived, axis=0)
    carried = None
    backs, jitter_rows = [], []
    for step in range(1, clus_count):
        if step > 1:
            if step > 2:
                source, backs[step - 3] = lax.optimization_barrier((source, backs[step - 3]))
            source = shifted(source, "clus", 1)
        last = step == clus_count - 1
        results = run_step(
            step - 1, length, items, source, targets, smalls, rhs, width, carried, last
        )
        if last:
            pot, pot_out, grad, back = results
        else:
            carried, back = results
        backs.append(back)
        at = clusters * (rhs + 4)
        jitter_rows.append(source[at : at + clusters])

    grad = in_order([grad[..., at * row_count : (at + 1) * row_count] for at in range(sub_count)])
    low_part = (sub_place == 0) & (core == 0)
    high_part = (sub_place == sub_count - 1) & (core == rhs_count - 1)
    uppers = [grad[:, -1, -quarter:]] + [jnp.where(high_part, back[:, -1], 0.0) for back in backs]
    lowers = [grad[:, 0, :quarter]] + [jnp.where(low_part, back[:, 0], 0.0) for back in backs]
    returned = jnp.zeros((3, clusters, quarter), jnp.float32)
    upper, lower = uppers[1], lowers[clus_count - 1]
    nothing = jnp.zeros((2, quarter), jnp.float32)
    for step in range(1, clus_count):
        rows = [
            backs[step - 1].reshape(3 * clusters, quarter),
            uppers[(step + 1) % clus_count],
            lowers[step - 1],
            nothing,
        ]
        home = shifted(jnp.concatenate(rows, axis=0), "clus", -step)
        returned = returned + home[: 3 * clusters].reshape(returned.shape)
        upper = upper + home[3 * clusters : 3 * clusters + 3]
        lower = lower + home[3 * clusters + 3 : 3 * clusters + 6]

    half = pot
    for step in range(1, rhs_count):
        arrived = shifted(pot_out[:, (step - 1) * rhs : step * rhs], "rhs", -step)
        half = half + arrived.astype(jnp.float32)

    half, grad = lax.optimization_barrier((half, grad))
    found = [half[..., :row_count]]
    for step in range(1, sub_count):
        sent = half[..., step * row_count : (step + 1) * row_count].astype(jnp.bfloat16)
        found.append(shifted(sent, "sub", -step))

    quarter_at = sub_place * rhs_count + core
    grad = grad + jnp.concatenate(
        [jnp.where(quarter_at == at, returned, 0.0) for at in range(sub_count * rhs_count)], axis=-1
    )
    share = clusters // sub_count

    blank = jnp.zeros((3, panels - quarter), jnp.float32)
    before = jnp.concatenate([blank, upper], axis=1)
    after = jnp.concatenate([lower, blank], axis=1)
    jitter_float = jitter_all.astype(jnp.float32)
    jitter_before = jnp.concatenate(
        [blank[:1], jitter_rows[0][clusters - 1 :].astype(jnp.float32)], axis=1
    )
    jitter_after = jnp.concatenate([jitter_rows[-1][:1].astype(jnp.float32), blank[:1]], axis=1)

    def edge_rows(at):
        first, end = at * share, (at + 1) * share
        inside = at < sub_count - 1
        return jnp.concatenate(
            [
                grad[:, first - 1] if at > 0 else before,
                grad[:, end] if inside else after,
                jnp.where(high_part, jitter_float[first - 1 : first] if at > 0 else jitter_before, 0.0),
                jnp.where(low_part, jitter_float[end : end + 1] if inside else jitter_after, 0.0),
            ],
            axis=0,
        ).reshape(-1, share, panels)

    def packed(place):
        return pick(
            place % sub_count,
            [
                jnp.concatenate([grad[:, at * share : (at + 1) * share], edge_rows(at)], axis=0)
                for at in range(sub_count)
            ],
        )

    summed = packed(sub_place)
    for step in range(1, sub_count):
        summed = summed + shifted(packed(sub_place + step), "sub", step)
    gathered = summed
    for step in range(1, rhs_count):
        gathered = gathered + shifted(summed, "rhs", step)
    own_jitter = pick(
        sub_place, [jitter_all[at * share : (at + 1) * share] for at in range(sub_count)]
    )
    node_grad = pl.pallas_call(
        node_kernel,
        out_shape=jax.ShapeDtypeStruct((3, share * panels), jnp.float32),
        in_specs=[vmem] * 3,
        out_specs=vmem,
        compiler_params=pltpu.CompilerParams(vmem_limit_bytes=16 * 1024 * 1024),
        cost_estimate=pl.CostEstimate(flops=2**20, bytes_accessed=2**18, transcendentals=0),
        name="node_terms",
    )(gathered[:3], own_jitter, gathered[3:].reshape(8, panels))
    potential = pl.pallas_call(
        sum_kernel,
        out_shape=jax.ShapeDtypeStruct((clusters, rhs, row_count), jnp.bfloat16),
        in_specs=[vmem] * sub_count,
        out_specs=vmem,
        compiler_params=pltpu.CompilerParams(vmem_limit_bytes=16 * 1024 * 1024),
        cost_estimate=pl.CostEstimate(flops=2**20, bytes_accessed=2**18, transcendentals=0),
        name="potential_sum",
    )(*found)
    return (potential, node_grad)


def solution(mesh):
    placed = (
        P(("groups", "clus"), None, "sub"),
        P(("groups", "clus"), "sub"),
        P(("groups", "clus"), "rhs", "sub"),
        P(("groups", "clus"), "rhs", "sub"),
        P(None, "groups"),
        P(("groups", "clus"), None, "sub"),
    )
    return jax.shard_map(
        on_device,
        mesh=mesh,
        in_specs=placed,
        out_specs=(P(("groups", "clus"), "rhs", "sub"), P(None, ("groups", "clus", "sub"))),
        check_vma=False,
    )
```

```python
import functools

import jax
import jax.numpy as jnp
from jax import lax
from jax.experimental import pallas as pl
from jax.experimental.pallas import tpu as pltpu
from jax.sharding import PartitionSpec as P

CP = 512
ROUNDS = 5

core_radius = 0.25
jitter_reach = 8
LANES = 128
AUG = 16


def shifted(value, axis, steps):
    count = lax.axis_size(axis)
    pairs = [(source, (source + steps) % count) for source in range(count)]
    return lax.ppermute(value, axis, pairs)


def moved(value, axes, target):
    counts = [lax.axis_size(axis) for axis in axes]
    pairs = []
    for major in range(counts[0]):
        for minor in range(counts[1]):
            goal = target(major, minor)
            if goal is not None:
                to_major, to_minor = goal[0] % counts[0], goal[1] % counts[1]
                pairs.append((major * counts[1] + minor, to_major * counts[1] + to_minor))
    return lax.ppermute(value, axes, pairs)


def three_parts(value):
    parts = []
    for _ in range(3):
        part = value.astype(jnp.bfloat16).astype(jnp.float32)
        parts.append(part)
        value = value - part
    return parts


def pick(index, choices):
    out = choices[0]
    for place in range(1, len(choices)):
        out = jnp.where(index == place, choices[place], out)
    return out


def prepare_kernel(sizes, *refs):
    arguments, refs = refs[:5], refs[5:]
    cot_out_ref, part_refs, small_ref = refs[0], refs[1:-7], refs[-7]
    density_ref, by_coord_ref, areas_ref, connect_ref, cot_ref, sems = refs[-6:]
    copies = []
    for at, (argument, place) in enumerate(
        zip(arguments, (density_ref, by_coord_ref, areas_ref, connect_ref, cot_ref))
    ):
        copies.append(pltpu.make_async_copy(argument, place, sems.at[at]))
        copies[-1].start()
    for copy in copies:
        copy.wait()

    clusters, rhs, row_count = density_ref.shape
    quarter = part_refs[0].shape[1]
    count = len(part_refs)
    panels, nodes_total = sizes
    device, sub_place, core = (lax.axis_index(axis) for axis in ("clus", "sub", "rhs"))

    def part_of(array, place):
        return pick(place, [array[:, at * quarter : (at + 1) * quarter] for at in range(count)])

    cot_out_ref[...] = cot_ref[...]
    first_id = clusters * panels * device + row_count * sub_place
    ids = lax.broadcasted_iota(jnp.int32, (clusters, row_count), 0) * panels
    ids = ids + lax.broadcasted_iota(jnp.int32, (clusters, row_count), 1) + first_id
    jitter = connect_ref[:, 0, :] - ids
    jitter = jnp.where(jitter > jitter_reach, jitter - nodes_total, jitter)
    jitter = jnp.where(jitter < -jitter_reach, jitter + nodes_total, jitter)
    jitter = jitter.astype(jnp.float32).astype(jnp.bfloat16)
    rows = [by_coord_ref[coord] for coord in range(3)] + [areas_ref[...], jitter]
    base = clusters * rhs
    for cluster in range(clusters):
        dens = density_ref[cluster]
        for step, part_ref in enumerate(part_refs):
            part_ref[cluster * rhs : (cluster + 1) * rhs, :] = part_of(dens, (core + step) % count)
    for at, value in enumerate(rows):
        span = slice(base + at * clusters, base + (at + 1) * clusters)
        part_refs[0][span, :] = part_of(value, core)
        if at != 3:
            at = min(at, 3)
            small_ref[at * clusters : (at + 1) * clusters, :] = value


def target_kernel(rhs_count, small_ref, *refs):
    cot_refs, (lhs_ref, aug_ref, aug32) = refs[:rhs_count], refs[rhs_count:]
    clusters, _, row_count = aug_ref.shape
    pos = [
        small_ref[coord * clusters : (coord + 1) * clusters, :].astype(jnp.float32)
        for coord in range(3)
    ]
    square = pos[0] * pos[0] + pos[1] * pos[1] + pos[2] * pos[2] + core_radius * core_radius
    ones = jnp.ones_like(square)
    aug32[...] = jnp.zeros(aug32.shape, jnp.float32)
    for row, value in enumerate([-2.0 * value for value in pos] + three_parts(square) + [ones] * 3):
        aug32[:, row, :] = value
    filled = AUG + sum(ref.shape[1] for ref in cot_refs)
    blank = jnp.zeros((LANES - filled, row_count), jnp.bfloat16)
    for cluster in range(clusters):
        aug = aug32[cluster].astype(jnp.bfloat16)
        aug_ref[cluster] = aug
        rows = [ref[cluster] for ref in cot_refs] + [aug, blank]
        lhs_ref[cluster] = jnp.concatenate(rows, axis=0).T


def step_kernel(step, length, rhs, subs, first, last, *refs):
    items, source_ref = refs[:2]
    lhs_refs, aug_refs, refs = refs[2 : 2 + subs], refs[2 + subs : 2 + 2 * subs], refs[2 + 2 * subs :]
    if not first:
        acc_in, refs = refs[0], refs[1:]
    if last:
        small_refs, refs = refs[:subs], refs[subs:]
        pot_ref, pot_out_ref, grad_ref, back_ref, acc = refs[:5]
        refs = refs[5:]
    else:
        acc, back_ref = refs[:2]
        refs = refs[2:]
    aug32, left, weight, back, raw_a, raw_b, both_a, both_b = refs
    clusters, rows, panels = acc.shape
    width = rows - AUG
    row_count = panels // subs
    quarter = source_ref.shape[1]
    base = clusters * rhs
    starts = [0] + list(range(base + 5 * clusters, source_ref.shape[0], base))

    there = [
        source_ref[base + coord * clusters : base + (coord + 1) * clusters, :].astype(jnp.float32)
        for coord in range(3)
    ]
    area = source_ref[base + 3 * clusters : base + 4 * clusters, :].astype(jnp.float32)
    square = there[0] * there[0] + there[1] * there[1] + there[2] * there[2]
    ones = jnp.ones_like(square)
    aug32[...] = jnp.zeros(aug32.shape, jnp.float32)
    for row, value in enumerate(there + [ones] * 3 + three_parts(square)):
        aug32[:, row, :] = value
    weight[...] = jnp.zeros(weight.shape, jnp.float32)
    weight[:clusters, :] = CP ** (-0.5) * area
    left[...] = jnp.zeros(left.shape, left.dtype)
    for cluster in range(clusters):
        left[cluster, width:rows, quarter:] = aug32[cluster].astype(jnp.bfloat16)
        for place, at in enumerate(starts):
            left[cluster, place * rhs : (place + 1) * rhs, :quarter] = source_ref[
                at + cluster * rhs : at + (cluster + 1) * rhs, :
            ]
    back[...] = jnp.zeros(back.shape, jnp.float32)
    if first:
        acc[...] = jnp.zeros(acc.shape, jnp.float32)
    else:
        acc[...] = acc_in[...]
    raw_b[...] = jnp.ones(raw_b.shape, jnp.float32)
    both_a[...] = jnp.zeros(both_a.shape, both_a.dtype)

    def decoded(place):
        code = items[step * length + place]
        return code // (2 * clusters), code % (2 * clusters)

    def products(place, raw):
        here, mate = decoded(place)
        mate = mate % clusters
        lhs = jnp.concatenate([ref[here] for ref in lhs_refs], axis=0)
        raw[...] = jnp.dot(lhs, left[mate], preferred_element_type=jnp.float32)

    def pointwise(place, raw, both):
        _, mate = decoded(place)
        scale = weight[pl.ds(mate, 1), :]
        for start in range(0, panels, LANES):
            span = slice(start, start + LANES)
            inverse = lax.rsqrt(raw[span, quarter:])
            kernel = scale * inverse
            both[span, :quarter] = kernel.astype(jnp.bfloat16)
            weighted = (inverse * inverse) * (kernel * raw[span, :quarter])
            both[span, quarter:] = weighted.astype(jnp.bfloat16)

    def summed(place, both):
        here, mate = decoded(place)
        mate = mate % clusters
        acc[here] += lax.dot_general(
            left[mate, :rows, :],
            both[...],
            (((1,), (1,)), ((), ())),
            preferred_element_type=jnp.float32,
        )
        aug = jnp.concatenate([ref[here] for ref in aug_refs], axis=1)
        back[mate] += jnp.dot(aug, both[:, quarter:], preferred_element_type=jnp.float32)

    @pl.loop(0, items[step * length])
    def _(pair):
        turn = 2 * pair + 1
        summed(turn, both_a)
        pointwise(turn + 1, raw_b, both_b)
        products(turn + 2, raw_a)
        summed(turn + 1, both_b)
        pointwise(turn + 2, raw_a, both_a)
        products(turn + 3, raw_b)

    for coord in range(3):
        back_ref[coord] = -0.5 * back[:, coord, :] - there[coord] * back[:, 6, :]
    if last:
        for coord in range(3):
            pos = [ref[coord * clusters : (coord + 1) * clusters, :] for ref in small_refs]
            pos = jnp.concatenate(pos, axis=1).astype(jnp.float32)
            grad_ref[coord] = acc[:, width + coord, :] - pos * acc[:, width + 3, :]
        pot_ref[...] = acc[:, :rhs, :]
        pot_out_ref[...] = acc[:, rhs:width, :].astype(jnp.bfloat16)


def run_step(step, length, items, source, targets, smalls, rhs, width, carried, last):
    lhss, augs = zip(*targets)
    clusters, _, row_count = augs[0].shape
    subs = len(targets)
    panels = subs * row_count
    quarter = source.shape[1]
    first = carried is None
    vmem = pl.BlockSpec(memory_space=pltpu.VMEM)
    smem = pl.BlockSpec(memory_space=pltpu.SMEM)
    operands = (items, source, *lhss, *augs)
    if not first:
        operands += (carried,)
    acc_shape = (clusters, width + AUG, panels)
    back_shape = jax.ShapeDtypeStruct((3, clusters, quarter), jnp.float32)
    scratch = [
        pltpu.VMEM((clusters, AUG, quarter), jnp.float32),
        pltpu.VMEM((clusters, LANES, 2 * quarter), jnp.bfloat16),
        pltpu.VMEM((clusters + 8, quarter), jnp.float32),
        pltpu.VMEM((clusters, AUG, quarter), jnp.float32),
    ]
    scratch += [pltpu.VMEM((panels, 2 * quarter), jnp.float32)] * 2
    scratch += [pltpu.VMEM((panels, 2 * quarter), jnp.bfloat16)] * 2
    if last:
        operands += tuple(smalls)
        out_shape = (
            jax.ShapeDtypeStruct((clusters, rhs, panels), jnp.float32),
            jax.ShapeDtypeStruct((clusters, width - rhs, panels), jnp.bfloat16),
            jax.ShapeDtypeStruct((3, clusters, panels), jnp.float32),
            back_shape,
        )
        scratch = [pltpu.VMEM(acc_shape, jnp.float32)] + scratch
    else:
        out_shape = (jax.ShapeDtypeStruct(acc_shape, jnp.float32), back_shape)
    pairs = (length - 6) * panels * quarter
    return pl.pallas_call(
        functools.partial(step_kernel, step, length, rhs, subs, first, last),
        out_shape=out_shape,
        in_specs=[smem] + [vmem] * (len(operands) - 1),
        out_specs=(vmem,) * len(out_shape),
        scratch_shapes=scratch,
        compiler_params=pltpu.CompilerParams(vmem_limit_bytes=20 * 1024 * 1024),
        cost_estimate=pl.CostEstimate(
            flops=2 * pairs * (2 * width + 3 * AUG), bytes_accessed=6 * 2**20, transcendentals=pairs
        ),
        name=f"near_field_{step}",
    )(*operands)


def node_kernel(grad_ref, jitter_ref, edge_ref, main_ref):
    clusters, panels = jitter_ref.shape
    wide = panels + 2 * LANES

    def spread_of(terms, jitter):
        side = jnp.zeros((terms.shape[0], LANES), jnp.float32)
        terms = 0.25 * terms
        spread = jnp.zeros((terms.shape[0], wide), jnp.float32)
        for offset in range(-jitter_reach, jitter_reach + 1):
            masked = jnp.where(jitter == offset, terms, 0.0)
            masked = jnp.concatenate([side, masked, side], axis=1)
            spread = spread + pltpu.roll(masked, offset % wide, 1)
        spread = spread + pltpu.roll(spread, 1, 1)
        return spread + pltpu.roll(spread, 32, 1)

    jitter = jitter_ref[...]
    row_at = lax.broadcasted_iota(jnp.int32, (clusters, LANES), 0)
    edge = edge_ref[...]
    edge_at = lax.broadcasted_iota(jnp.int32, edge.shape, 0)
    edge_jitter = jnp.where(edge_at < 3, edge[6:7], edge[7:8]).astype(jnp.int32)
    edge = spread_of(edge, edge_jitter)
    for coord in range(3):
        spread = spread_of(grad_ref[coord], jitter)
        below = spread[:, :LANES]
        above = spread[:, LANES + panels :]
        inner = spread[:, LANES : LANES + panels]
        before = edge[coord : coord + 1, LANES + panels :]
        after = edge[3 + coord : 4 + coord, :LANES]
        first = jnp.where(row_at == 0, before, pltpu.roll(above, 1, 0))
        last = jnp.where(row_at == clusters - 1, after, pltpu.roll(below, clusters - 1, 0))
        inner = jnp.concatenate(
            [
                inner[:, :LANES] + first,
                inner[:, LANES : panels - LANES],
                inner[:, panels - LANES :] + last,
            ],
            axis=1,
        )
        for cluster in range(clusters):
            main_ref[coord : coord + 1, cluster * panels : (cluster + 1) * panels] = inner[
                cluster : cluster + 1
            ]


def sum_kernel(*refs):
    total = refs[0][...]
    for ref in refs[1:-1]:
        total = total + ref[...].astype(jnp.float32)
    refs[-1][...] = total.astype(jnp.bfloat16)


def on_device(positions, areas, density, cotangent, matching, connect):
    clus_count = lax.axis_size("clus")
    sub_count = lax.axis_size("sub")
    rhs_count = lax.axis_size("rhs")
    device = lax.axis_index("clus")
    sub_place = lax.axis_index("sub")
    core = lax.axis_index("rhs")
    clusters, rhs, row_count = density.shape
    panels = row_count * sub_count
    quarter = row_count // rhs_count
    width = rhs * rhs_count
    vmem = pl.BlockSpec(memory_space=pltpu.VMEM)

    nodes_total = clus_count * clusters * panels

    cots = [cotangent] + [shifted(cotangent, "sub", step) for step in range(1, sub_count)]
    for step in range(1, rhs_count):
        cots += [shifted(block, "rhs", step) for block in cots[:sub_count]]

    by_coord = jnp.transpose(positions, (1, 0, 2))
    arguments = [
        pltpu.with_memory_space_constraint(array, pltpu.HBM)
        for array in (density, by_coord, areas, connect, cotangent)
    ]
    own_cot, *parts, small = pl.pallas_call(
        functools.partial(prepare_kernel, (panels, nodes_total)),
        out_shape=(
            jax.ShapeDtypeStruct(cotangent.shape, jnp.bfloat16),
            jax.ShapeDtypeStruct((clusters * (rhs + 5), quarter), jnp.bfloat16),
            *[jax.ShapeDtypeStruct((clusters * rhs, quarter), jnp.bfloat16)] * (rhs_count - 1),
            jax.ShapeDtypeStruct((clusters * 4, row_count), jnp.bfloat16),
        ),
        in_specs=[pl.BlockSpec(memory_space=pltpu.HBM)] * len(arguments),
        out_specs=(vmem,) * (rhs_count + 2),
        scratch_shapes=[pltpu.VMEM(array.shape, array.dtype) for array in arguments]
        + [pltpu.SemaphoreType.DMA((len(arguments),))],
        compiler_params=pltpu.CompilerParams(vmem_limit_bytes=16 * 1024 * 1024),
        name="prepare",
    )(*arguments)
    cots[0] = own_cot
    arrived = [shifted(parts[0], "clus", 1)]
    for step in range(1, rhs_count):
        arrived.append(
            moved(parts[step], ("clus", "rhs"), lambda z, c, step=step: (z + 1, c + step))
        )

    per_round = 2 * ((clusters // 2 + clus_count - 2) // (clus_count - 1))
    cap = ROUNDS * per_round
    partners = lax.dynamic_slice_in_dim(matching, device * clusters, clusters, 1).reshape(-1)
    here = jnp.tile(jnp.arange(clusters, dtype=jnp.int32), ROUNDS)
    code = here * (2 * clusters) + partners % clusters
    behind = (device - partners // clusters) % clus_count
    total_items = ROUNDS * clusters
    order = jnp.arange(total_items, dtype=jnp.int32)
    rank = jnp.sum(
        ((behind[None, :] == behind[:, None]) & (order[None, :] < order[:, None])).astype(jnp.int32),
        axis=1,
    )
    steps = jnp.arange(1, clus_count, dtype=jnp.int32)
    member = behind[None, :] == steps[:, None]
    slots = jnp.arange(cap, dtype=jnp.int32)
    chosen = member[:, None, :] & (rank[None, None, :] == slots[None, :, None])
    listed = jnp.sum(jnp.where(chosen, code[None, None, :] - clusters, 0), axis=2) + clusters
    turns = (jnp.sum(member.astype(jnp.int32), axis=1) + 3) // 2
    length = cap + 6
    items = jnp.pad(listed, ((0, 0), (3, 3)), constant_values=clusters)
    items = jnp.concatenate([turns[:, None], items[:, 1:]], axis=1).reshape(-1)

    smalls = [small] + [shifted(small, "sub", step) for step in range(1, sub_count)]

    def in_order(blocks):
        return jnp.concatenate(
            [pick((sub_place - place) % sub_count, blocks) for place in range(sub_count)], axis=-1
        )

    jitter_all = in_order([block[3 * clusters :] for block in smalls]).astype(jnp.int32)
    targets = [
        pl.pallas_call(
            functools.partial(target_kernel, rhs_count),
            out_shape=(
                jax.ShapeDtypeStruct((clusters, row_count, LANES), jnp.bfloat16),
                jax.ShapeDtypeStruct((clusters, AUG, row_count), jnp.bfloat16),
            ),
            in_specs=[vmem] * (1 + rhs_count),
            out_specs=(vmem, vmem),
            scratch_shapes=[pltpu.VMEM((clusters, AUG, row_count), jnp.float32)],
            compiler_params=pltpu.CompilerParams(vmem_limit_bytes=16 * 1024 * 1024),
            cost_estimate=pl.CostEstimate(flops=2**20, bytes_accessed=2**18, transcendentals=0),
            name=f"targets_{place}",
        )(smalls[place], *cots[place::sub_count])
        for place in range(sub_count)
    ]

    arrived, targets = lax.optimization_barrier((arrived, targets))
    source = jnp.concatenate(arrived, axis=0)
    carried = None
    backs, jitter_rows = [], []
    for step in range(1, clus_count):
        if step > 1:
            if step > 2:
                source, backs[step - 3] = lax.optimization_barrier((source, backs[step - 3]))
            source = shifted(source, "clus", 1)
        last = step == clus_count - 1
        results = run_step(
            step - 1, length, items, source, targets, smalls, rhs, width, carried, last
        )
        if last:
            pot, pot_out, grad, back = results
        else:
            carried, back = results
        backs.append(back)
        at = clusters * (rhs + 4)
        jitter_rows.append(source[at : at + clusters])

    grad = in_order([grad[..., at * row_count : (at + 1) * row_count] for at in range(sub_count)])
    low_part = (sub_place == 0) & (core == 0)
    high_part = (sub_place == sub_count - 1) & (core == rhs_count - 1)
    uppers = [grad[:, -1, -quarter:]] + [jnp.where(high_part, back[:, -1], 0.0) for back in backs]
    lowers = [grad[:, 0, :quarter]] + [jnp.where(low_part, back[:, 0], 0.0) for back in backs]
    nothing = jnp.zeros((2, quarter), jnp.float32)
    parcels = []
    for step in range(clus_count):
        back = backs[step - 1] if step > 0 else jnp.zeros_like(backs[0])
        parcels += [
            back.reshape(3 * clusters, quarter),
            uppers[(step + 1) % clus_count],
            lowers[(step - 1) % clus_count],
            nothing,
        ]
    rows = 3 * clusters + 8
    parcels = jnp.concatenate(parcels, axis=0).reshape(clus_count, rows, quarter)[::-1]
    parcels = jnp.concatenate([parcels, parcels], axis=0)
    parcels = lax.dynamic_slice_in_dim(parcels, clus_count - 1 - device, clus_count, 0)
    home = lax.all_to_all(parcels, "clus", split_axis=0, concat_axis=0, tiled=True)
    home = jnp.sum(home, axis=0)
    returned = home[: 3 * clusters].reshape(3, clusters, quarter)
    upper = home[3 * clusters : 3 * clusters + 3]
    lower = home[3 * clusters + 3 : 3 * clusters + 6]

    half = pot
    for step in range(1, rhs_count):
        arrived = shifted(pot_out[:, (step - 1) * rhs : step * rhs], "rhs", -step)
        half = half + arrived.astype(jnp.float32)

    half, grad = lax.optimization_barrier((half, grad))
    found = [half[..., :row_count]]
    for step in range(1, sub_count):
        sent = half[..., step * row_count : (step + 1) * row_count].astype(jnp.bfloat16)
        found.append(shifted(sent, "sub", -step))

    quarter_at = sub_place * rhs_count + core
    grad = grad + jnp.concatenate(
        [jnp.where(quarter_at == at, returned, 0.0) for at in range(sub_count * rhs_count)], axis=-1
    )
    share = clusters // sub_count

    blank = jnp.zeros((3, panels - quarter), jnp.float32)
    before = jnp.concatenate([blank, upper], axis=1)
    after = jnp.concatenate([lower, blank], axis=1)
    jitter_float = jitter_all.astype(jnp.float32)
    jitter_before = jnp.concatenate(
        [blank[:1], jitter_rows[0][clusters - 1 :].astype(jnp.float32)], axis=1
    )
    jitter_after = jnp.concatenate([jitter_rows[-1][:1].astype(jnp.float32), blank[:1]], axis=1)

    def edge_rows(at):
        first, end = at * share, (at + 1) * share
        inside = at < sub_count - 1
        return jnp.concatenate(
            [
                grad[:, first - 1] if at > 0 else before,
                grad[:, end] if inside else after,
                jnp.where(high_part, jitter_float[first - 1 : first] if at > 0 else jitter_before, 0.0),
                jnp.where(low_part, jitter_float[end : end + 1] if inside else jitter_after, 0.0),
            ],
            axis=0,
        ).reshape(-1, share, panels)

    def packed(place):
        return pick(
            place % sub_count,
            [
                jnp.concatenate([grad[:, at * share : (at + 1) * share], edge_rows(at)], axis=0)
                for at in range(sub_count)
            ],
        )

    summed = packed(sub_place)
    for step in range(1, sub_count):
        summed = summed + shifted(packed(sub_place + step), "sub", step)
    gathered = summed
    for step in range(1, rhs_count):
        gathered = gathered + shifted(summed, "rhs", step)
    own_jitter = pick(
        sub_place, [jitter_all[at * share : (at + 1) * share] for at in range(sub_count)]
    )
    node_grad = pl.pallas_call(
        node_kernel,
        out_shape=jax.ShapeDtypeStruct((3, share * panels), jnp.float32),
        in_specs=[vmem] * 3,
        out_specs=vmem,
        compiler_params=pltpu.CompilerParams(vmem_limit_bytes=16 * 1024 * 1024),
        cost_estimate=pl.CostEstimate(flops=2**20, bytes_accessed=2**18, transcendentals=0),
        name="node_terms",
    )(gathered[:3], own_jitter, gathered[3:].reshape(8, panels))
    potential = pl.pallas_call(
        sum_kernel,
        out_shape=jax.ShapeDtypeStruct((clusters, rhs, row_count), jnp.bfloat16),
        in_specs=[vmem] * sub_count,
        out_specs=vmem,
        compiler_params=pltpu.CompilerParams(vmem_limit_bytes=16 * 1024 * 1024),
        cost_estimate=pl.CostEstimate(flops=2**20, bytes_accessed=2**18, transcendentals=0),
        name="potential_sum",
    )(*found)
    return (potential, node_grad)


def solution(mesh):
    placed = (
        P(("groups", "clus"), None, "sub"),
        P(("groups", "clus"), "sub"),
        P(("groups", "clus"), "rhs", "sub"),
        P(("groups", "clus"), "rhs", "sub"),
        P(None, "groups"),
        P(("groups", "clus"), None, "sub"),
    )
    return jax.shard_map(
        on_device,
        mesh=mesh,
        in_specs=placed,
        out_specs=(P(("groups", "clus"), "rhs", "sub"), P(None, ("groups", "clus", "sub"))),
        check_vma=False,
    )
```

```python
import functools

import jax
import jax.numpy as jnp
from jax import lax
from jax.experimental import pallas as pl
from jax.experimental.pallas import tpu as pltpu
from jax.sharding import PartitionSpec as P

CP = 512
ROUNDS = 5

core_radius = 0.25
jitter_reach = 8
LANES = 128
AUG = 16


def shifted(value, axis, steps):
    count = lax.axis_size(axis)
    pairs = [(source, (source + steps) % count) for source in range(count)]
    return lax.ppermute(value, axis, pairs)


def ring_order(count):
    return [*range(0, count, 2), *reversed(range(1, count, 2))]


def round_ring(value, steps):
    order = ring_order(lax.axis_size("clus"))
    pairs = [(source, order[(at + steps) % len(order)]) for at, source in enumerate(order)]
    return lax.ppermute(value, "clus", pairs)


def moved(value, axes, target):
    counts = [lax.axis_size(axis) for axis in axes]
    pairs = []
    for major in range(counts[0]):
        for minor in range(counts[1]):
            goal = target(major, minor)
            if goal is not None:
                to_major, to_minor = goal[0] % counts[0], goal[1] % counts[1]
                pairs.append((major * counts[1] + minor, to_major * counts[1] + to_minor))
    return lax.ppermute(value, axes, pairs)


def three_parts(value):
    parts = []
    for _ in range(3):
        part = value.astype(jnp.bfloat16).astype(jnp.float32)
        parts.append(part)
        value = value - part
    return parts


def pick(index, choices):
    out = choices[0]
    for place in range(1, len(choices)):
        out = jnp.where(index == place, choices[place], out)
    return out


def prepare_kernel(sizes, *refs):
    arguments, refs = refs[:5], refs[5:]
    cot_out_ref, part_refs, small_ref = refs[0], refs[1:-7], refs[-7]
    density_ref, by_coord_ref, areas_ref, connect_ref, cot_ref, sems = refs[-6:]
    copies = []
    for at, (argument, place) in enumerate(
        zip(arguments, (density_ref, by_coord_ref, areas_ref, connect_ref, cot_ref))
    ):
        copies.append(pltpu.make_async_copy(argument, place, sems.at[at]))
        copies[-1].start()
    for copy in copies:
        copy.wait()

    clusters, rhs, row_count = density_ref.shape
    quarter = part_refs[0].shape[1]
    count = len(part_refs)
    panels, nodes_total = sizes
    device, sub_place, core = (lax.axis_index(axis) for axis in ("clus", "sub", "rhs"))

    def part_of(array, place):
        return pick(place, [array[:, at * quarter : (at + 1) * quarter] for at in range(count)])

    cot_out_ref[...] = cot_ref[...]
    first_id = clusters * panels * device + row_count * sub_place
    ids = lax.broadcasted_iota(jnp.int32, (clusters, row_count), 0) * panels
    ids = ids + lax.broadcasted_iota(jnp.int32, (clusters, row_count), 1) + first_id
    jitter = connect_ref[:, 0, :] - ids
    jitter = jnp.where(jitter > jitter_reach, jitter - nodes_total, jitter)
    jitter = jnp.where(jitter < -jitter_reach, jitter + nodes_total, jitter)
    jitter = jitter.astype(jnp.float32).astype(jnp.bfloat16)
    rows = [by_coord_ref[coord] for coord in range(3)] + [areas_ref[...], jitter]
    base = clusters * rhs
    for cluster in range(clusters):
        dens = density_ref[cluster]
        for step, part_ref in enumerate(part_refs):
            part_ref[cluster * rhs : (cluster + 1) * rhs, :] = part_of(dens, (core + step) % count)
    for at, value in enumerate(rows):
        span = slice(base + at * clusters, base + (at + 1) * clusters)
        part_refs[0][span, :] = part_of(value, core)
        if at != 3:
            at = min(at, 3)
            small_ref[at * clusters : (at + 1) * clusters, :] = value


def target_kernel(rhs_count, small_ref, *refs):
    cot_refs, (lhs_ref, aug_ref, aug32) = refs[:rhs_count], refs[rhs_count:]
    clusters, _, row_count = aug_ref.shape
    pos = [
        small_ref[coord * clusters : (coord + 1) * clusters, :].astype(jnp.float32)
        for coord in range(3)
    ]
    square = pos[0] * pos[0] + pos[1] * pos[1] + pos[2] * pos[2] + core_radius * core_radius
    ones = jnp.ones_like(square)
    aug32[...] = jnp.zeros(aug32.shape, jnp.float32)
    for row, value in enumerate([-2.0 * value for value in pos] + three_parts(square) + [ones] * 3):
        aug32[:, row, :] = value
    filled = AUG + sum(ref.shape[1] for ref in cot_refs)
    blank = jnp.zeros((LANES - filled, row_count), jnp.bfloat16)
    for cluster in range(clusters):
        aug = aug32[cluster].astype(jnp.bfloat16)
        aug_ref[cluster] = aug
        rows = [ref[cluster] for ref in cot_refs] + [aug, blank]
        lhs_ref[cluster] = jnp.concatenate(rows, axis=0).T


def step_kernel(step, length, rhs, subs, first, last, *refs):
    items, source_ref = refs[:2]
    lhs_refs, aug_refs, refs = refs[2 : 2 + subs], refs[2 + subs : 2 + 2 * subs], refs[2 + 2 * subs :]
    if not first:
        acc_in, refs = refs[0], refs[1:]
    if last:
        small_refs, refs = refs[:subs], refs[subs:]
        pot_ref, pot_out_ref, grad_ref, back_ref, acc = refs[:5]
        refs = refs[5:]
    else:
        acc, back_ref = refs[:2]
        refs = refs[2:]
    aug32, left, weight, back, raw_a, raw_b, both_a, both_b = refs
    clusters, rows, panels = acc.shape
    width = rows - AUG
    row_count = panels // subs
    quarter = source_ref.shape[1]
    base = clusters * rhs
    starts = [0] + list(range(base + 5 * clusters, source_ref.shape[0], base))

    there = [
        source_ref[base + coord * clusters : base + (coord + 1) * clusters, :].astype(jnp.float32)
        for coord in range(3)
    ]
    area = source_ref[base + 3 * clusters : base + 4 * clusters, :].astype(jnp.float32)
    square = there[0] * there[0] + there[1] * there[1] + there[2] * there[2]
    ones = jnp.ones_like(square)
    aug32[...] = jnp.zeros(aug32.shape, jnp.float32)
    for row, value in enumerate(there + [ones] * 3 + three_parts(square)):
        aug32[:, row, :] = value
    weight[...] = jnp.zeros(weight.shape, jnp.float32)
    weight[:clusters, :] = CP ** (-0.5) * area
    left[...] = jnp.zeros(left.shape, left.dtype)
    for cluster in range(clusters):
        left[cluster, width:rows, quarter:] = aug32[cluster].astype(jnp.bfloat16)
        for place, at in enumerate(starts):
            left[cluster, place * rhs : (place + 1) * rhs, :quarter] = source_ref[
                at + cluster * rhs : at + (cluster + 1) * rhs, :
            ]
    back[...] = jnp.zeros(back.shape, jnp.float32)
    if first:
        acc[...] = jnp.zeros(acc.shape, jnp.float32)
    else:
        acc[...] = acc_in[...]
    raw_b[...] = jnp.ones(raw_b.shape, jnp.float32)
    both_a[...] = jnp.zeros(both_a.shape, both_a.dtype)

    def decoded(place):
        code = items[step * length + place]
        return code // (2 * clusters), code % (2 * clusters)

    def products(place, raw):
        here, mate = decoded(place)
        mate = mate % clusters
        lhs = jnp.concatenate([ref[here] for ref in lhs_refs], axis=0)
        raw[...] = jnp.dot(lhs, left[mate], preferred_element_type=jnp.float32)

    def pointwise(place, raw, both):
        _, mate = decoded(place)
        scale = weight[pl.ds(mate, 1), :]
        for start in range(0, panels, LANES):
            span = slice(start, start + LANES)
            inverse = lax.rsqrt(raw[span, quarter:])
            kernel = scale * inverse
            both[span, :quarter] = kernel.astype(jnp.bfloat16)
            weighted = (inverse * inverse) * (kernel * raw[span, :quarter])
            both[span, quarter:] = weighted.astype(jnp.bfloat16)

    def summed(place, both):
        here, mate = decoded(place)
        mate = mate % clusters
        acc[here] += lax.dot_general(
            left[mate, :rows, :],
            both[...],
            (((1,), (1,)), ((), ())),
            preferred_element_type=jnp.float32,
        )
        aug = jnp.concatenate([ref[here] for ref in aug_refs], axis=1)
        back[mate] += jnp.dot(aug, both[:, quarter:], preferred_element_type=jnp.float32)

    @pl.loop(0, items[step * length])
    def _(pair):
        turn = 2 * pair + 1
        summed(turn, both_a)
        pointwise(turn + 1, raw_b, both_b)
        products(turn + 2, raw_a)
        summed(turn + 1, both_b)
        pointwise(turn + 2, raw_a, both_a)
        products(turn + 3, raw_b)

    for coord in range(3):
        back_ref[coord] = -0.5 * back[:, coord, :] - there[coord] * back[:, 6, :]
    if last:
        for coord in range(3):
            pos = [ref[coord * clusters : (coord + 1) * clusters, :] for ref in small_refs]
            pos = jnp.concatenate(pos, axis=1).astype(jnp.float32)
            grad_ref[coord] = acc[:, width + coord, :] - pos * acc[:, width + 3, :]
        pot_ref[...] = acc[:, :rhs, :]
        pot_out_ref[...] = acc[:, rhs:width, :].astype(jnp.bfloat16)


def run_step(step, length, items, source, targets, smalls, rhs, width, carried, last):
    lhss, augs = zip(*targets)
    clusters, _, row_count = augs[0].shape
    subs = len(targets)
    panels = subs * row_count
    quarter = source.shape[1]
    first = carried is None
    vmem = pl.BlockSpec(memory_space=pltpu.VMEM)
    smem = pl.BlockSpec(memory_space=pltpu.SMEM)
    operands = (items, source, *lhss, *augs)
    if not first:
        operands += (carried,)
    acc_shape = (clusters, width + AUG, panels)
    back_shape = jax.ShapeDtypeStruct((3, clusters, quarter), jnp.float32)
    scratch = [
        pltpu.VMEM((clusters, AUG, quarter), jnp.float32),
        pltpu.VMEM((clusters, LANES, 2 * quarter), jnp.bfloat16),
        pltpu.VMEM((clusters + 8, quarter), jnp.float32),
        pltpu.VMEM((clusters, AUG, quarter), jnp.float32),
    ]
    scratch += [pltpu.VMEM((panels, 2 * quarter), jnp.float32)] * 2
    scratch += [pltpu.VMEM((panels, 2 * quarter), jnp.bfloat16)] * 2
    if last:
        operands += tuple(smalls)
        out_shape = (
            jax.ShapeDtypeStruct((clusters, rhs, panels), jnp.float32),
            jax.ShapeDtypeStruct((clusters, width - rhs, panels), jnp.bfloat16),
            jax.ShapeDtypeStruct((3, clusters, panels), jnp.float32),
            back_shape,
        )
        scratch = [pltpu.VMEM(acc_shape, jnp.float32)] + scratch
    else:
        out_shape = (jax.ShapeDtypeStruct(acc_shape, jnp.float32), back_shape)
    pairs = (length - 6) * panels * quarter
    return pl.pallas_call(
        functools.partial(step_kernel, step, length, rhs, subs, first, last),
        out_shape=out_shape,
        in_specs=[smem] + [vmem] * (len(operands) - 1),
        out_specs=(vmem,) * len(out_shape),
        scratch_shapes=scratch,
        compiler_params=pltpu.CompilerParams(vmem_limit_bytes=20 * 1024 * 1024),
        cost_estimate=pl.CostEstimate(
            flops=2 * pairs * (2 * width + 3 * AUG), bytes_accessed=6 * 2**20, transcendentals=pairs
        ),
        name=f"near_field_{step}",
    )(*operands)


def node_kernel(grad_ref, jitter_ref, edge_ref, main_ref):
    clusters, panels = jitter_ref.shape
    wide = panels + 2 * LANES

    def spread_of(terms, jitter):
        side = jnp.zeros((terms.shape[0], LANES), jnp.float32)
        terms = 0.25 * terms
        spread = jnp.zeros((terms.shape[0], wide), jnp.float32)
        for offset in range(-jitter_reach, jitter_reach + 1):
            masked = jnp.where(jitter == offset, terms, 0.0)
            masked = jnp.concatenate([side, masked, side], axis=1)
            spread = spread + pltpu.roll(masked, offset % wide, 1)
        spread = spread + pltpu.roll(spread, 1, 1)
        return spread + pltpu.roll(spread, 32, 1)

    jitter = jitter_ref[...]
    row_at = lax.broadcasted_iota(jnp.int32, (clusters, LANES), 0)
    edge = edge_ref[...]
    edge_at = lax.broadcasted_iota(jnp.int32, edge.shape, 0)
    edge_jitter = jnp.where(edge_at < 3, edge[6:7], edge[7:8]).astype(jnp.int32)
    edge = spread_of(edge, edge_jitter)
    for coord in range(3):
        spread = spread_of(grad_ref[coord], jitter)
        below = spread[:, :LANES]
        above = spread[:, LANES + panels :]
        inner = spread[:, LANES : LANES + panels]
        before = edge[coord : coord + 1, LANES + panels :]
        after = edge[3 + coord : 4 + coord, :LANES]
        first = jnp.where(row_at == 0, before, pltpu.roll(above, 1, 0))
        last = jnp.where(row_at == clusters - 1, after, pltpu.roll(below, clusters - 1, 0))
        inner = jnp.concatenate(
            [
                inner[:, :LANES] + first,
                inner[:, LANES : panels - LANES],
                inner[:, panels - LANES :] + last,
            ],
            axis=1,
        )
        for cluster in range(clusters):
            main_ref[coord : coord + 1, cluster * panels : (cluster + 1) * panels] = inner[
                cluster : cluster + 1
            ]


def sum_kernel(*refs):
    total = refs[0][...]
    for ref in refs[1:-1]:
        total = total + ref[...].astype(jnp.float32)
    refs[-1][...] = total.astype(jnp.bfloat16)


def on_device(positions, areas, density, cotangent, matching, connect):
    clus_count = lax.axis_size("clus")
    sub_count = lax.axis_size("sub")
    rhs_count = lax.axis_size("rhs")
    device = lax.axis_index("clus")
    sub_place = lax.axis_index("sub")
    core = lax.axis_index("rhs")
    clusters, rhs, row_count = density.shape
    panels = row_count * sub_count
    quarter = row_count // rhs_count
    width = rhs * rhs_count
    vmem = pl.BlockSpec(memory_space=pltpu.VMEM)

    nodes_total = clus_count * clusters * panels

    cots = [cotangent] + [shifted(cotangent, "sub", step) for step in range(1, sub_count)]
    for step in range(1, rhs_count):
        cots += [shifted(block, "rhs", step) for block in cots[:sub_count]]

    by_coord = jnp.transpose(positions, (1, 0, 2))
    arguments = [
        pltpu.with_memory_space_constraint(array, pltpu.HBM)
        for array in (density, by_coord, areas, connect, cotangent)
    ]
    own_cot, *parts, small = pl.pallas_call(
        functools.partial(prepare_kernel, (panels, nodes_total)),
        out_shape=(
            jax.ShapeDtypeStruct(cotangent.shape, jnp.bfloat16),
            jax.ShapeDtypeStruct((clusters * (rhs + 5), quarter), jnp.bfloat16),
            *[jax.ShapeDtypeStruct((clusters * rhs, quarter), jnp.bfloat16)] * (rhs_count - 1),
            jax.ShapeDtypeStruct((clusters * 4, row_count), jnp.bfloat16),
        ),
        in_specs=[pl.BlockSpec(memory_space=pltpu.HBM)] * len(arguments),
        out_specs=(vmem,) * (rhs_count + 2),
        scratch_shapes=[pltpu.VMEM(array.shape, array.dtype) for array in arguments]
        + [pltpu.SemaphoreType.DMA((len(arguments),))],
        compiler_params=pltpu.CompilerParams(vmem_limit_bytes=16 * 1024 * 1024),
        name="prepare",
    )(*arguments)
    cots[0] = own_cot
    ring = ring_order(clus_count)
    at_place = [ring.index(index) for index in range(clus_count)]
    ring_place = pick(device, at_place)
    arrived = [round_ring(parts[0], 1)]
    for step in range(1, rhs_count):

        def goal(z, c, step=step):
            return (ring[(at_place[z] + 1) % clus_count], c + step)

        arrived.append(moved(parts[step], ("clus", "rhs"), goal))

    per_round = 2 * ((clusters // 2 + clus_count - 2) // (clus_count - 1))
    cap = ROUNDS * per_round
    partners = lax.dynamic_slice_in_dim(matching, device * clusters, clusters, 1).reshape(-1)
    here = jnp.tile(jnp.arange(clusters, dtype=jnp.int32), ROUNDS)
    code = here * (2 * clusters) + partners % clusters
    behind = (ring_place - pick(partners // clusters, at_place)) % clus_count
    total_items = ROUNDS * clusters
    order = jnp.arange(total_items, dtype=jnp.int32)
    rank = jnp.sum(
        ((behind[None, :] == behind[:, None]) & (order[None, :] < order[:, None])).astype(jnp.int32),
        axis=1,
    )
    steps = jnp.arange(1, clus_count, dtype=jnp.int32)
    member = behind[None, :] == steps[:, None]
    slots = jnp.arange(cap, dtype=jnp.int32)
    chosen = member[:, None, :] & (rank[None, None, :] == slots[None, :, None])
    listed = jnp.sum(jnp.where(chosen, code[None, None, :] - clusters, 0), axis=2) + clusters
    turns = (jnp.sum(member.astype(jnp.int32), axis=1) + 3) // 2
    length = cap + 6
    items = jnp.pad(listed, ((0, 0), (3, 3)), constant_values=clusters)
    items = jnp.concatenate([turns[:, None], items[:, 1:]], axis=1).reshape(-1)

    smalls = [small] + [shifted(small, "sub", step) for step in range(1, sub_count)]

    def in_order(blocks):
        return jnp.concatenate(
            [pick((sub_place - place) % sub_count, blocks) for place in range(sub_count)], axis=-1
        )

    jitter_all = in_order([block[3 * clusters :] for block in smalls]).astype(jnp.int32)
    targets = [
        pl.pallas_call(
            functools.partial(target_kernel, rhs_count),
            out_shape=(
                jax.ShapeDtypeStruct((clusters, row_count, LANES), jnp.bfloat16),
                jax.ShapeDtypeStruct((clusters, AUG, row_count), jnp.bfloat16),
            ),
            in_specs=[vmem] * (1 + rhs_count),
            out_specs=(vmem, vmem),
            scratch_shapes=[pltpu.VMEM((clusters, AUG, row_count), jnp.float32)],
            compiler_params=pltpu.CompilerParams(vmem_limit_bytes=16 * 1024 * 1024),
            cost_estimate=pl.CostEstimate(flops=2**20, bytes_accessed=2**18, transcendentals=0),
            name=f"targets_{place}",
        )(smalls[place], *cots[place::sub_count])
        for place in range(sub_count)
    ]

    arrived, targets = lax.optimization_barrier((arrived, targets))
    source = jnp.concatenate(arrived, axis=0)
    carried = None
    backs, jitter_rows = [], [None]
    for step in range(1, clus_count):
        if step > 1:
            if step > 2:
                source, backs[step - 3] = lax.optimization_barrier((source, backs[step - 3]))
            source = round_ring(source, 1)
        last = step == clus_count - 1
        results = run_step(
            step - 1, length, items, source, targets, smalls, rhs, width, carried, last
        )
        if last:
            pot, pot_out, grad, back = results
        else:
            carried, back = results
        backs.append(back)
        at = clusters * (rhs + 4)
        jitter_rows.append(source[at : at + clusters])

    grad = in_order([grad[..., at * row_count : (at + 1) * row_count] for at in range(sub_count)])
    low_part = (sub_place == 0) & (core == 0)
    high_part = (sub_place == sub_count - 1) & (core == rhs_count - 1)
    uppers = [grad[:, -1, -quarter:]] + [jnp.where(high_part, back[:, -1], 0.0) for back in backs]
    lowers = [grad[:, 0, :quarter]] + [jnp.where(low_part, back[:, 0], 0.0) for back in backs]

    def step_between(index, owner):
        return (at_place[index] - at_place[owner % clus_count]) % clus_count

    def needed(parts, step, offset):
        choices = []
        for index in range(clus_count):
            goal = ring[(at_place[index] - step) % clus_count]
            choices.append(parts[step_between(index, goal + offset)])
        return pick(device, choices)

    nothing = jnp.zeros((2, quarter), jnp.float32)
    returned = jnp.zeros((3, clusters, quarter), jnp.float32)
    upper, lower = needed(uppers, 0, -1), needed(lowers, 0, 1)
    for step in range(1, clus_count):
        rows = [
            backs[step - 1].reshape(3 * clusters, quarter),
            needed(uppers, step, -1),
            needed(lowers, step, 1),
            nothing,
        ]
        home = round_ring(jnp.concatenate(rows, axis=0), -step)
        returned = returned + home[: 3 * clusters].reshape(returned.shape)
        upper = upper + home[3 * clusters : 3 * clusters + 3]
        lower = lower + home[3 * clusters + 3 : 3 * clusters + 6]

    half = pot
    for step in range(1, rhs_count):
        arrived = shifted(pot_out[:, (step - 1) * rhs : step * rhs], "rhs", -step)
        half = half + arrived.astype(jnp.float32)

    half, grad = lax.optimization_barrier((half, grad))
    found = [half[..., :row_count]]
    for step in range(1, sub_count):
        sent = half[..., step * row_count : (step + 1) * row_count].astype(jnp.bfloat16)
        found.append(shifted(sent, "sub", -step))

    quarter_at = sub_place * rhs_count + core
    grad = grad + jnp.concatenate(
        [jnp.where(quarter_at == at, returned, 0.0) for at in range(sub_count * rhs_count)], axis=-1
    )
    share = clusters // sub_count

    blank = jnp.zeros((3, panels - quarter), jnp.float32)
    before = jnp.concatenate([blank, upper], axis=1)
    after = jnp.concatenate([lower, blank], axis=1)
    jitter_float = jitter_all.astype(jnp.float32)
    jitter_before = jnp.concatenate(
        [blank[:1], needed(jitter_rows, 0, -1)[clusters - 1 :].astype(jnp.float32)], axis=1
    )
    jitter_after = jnp.concatenate(
        [needed(jitter_rows, 0, 1)[:1].astype(jnp.float32), blank[:1]], axis=1
    )

    def edge_rows(at):
        first, end = at * share, (at + 1) * share
        inside = at < sub_count - 1
        return jnp.concatenate(
            [
                grad[:, first - 1] if at > 0 else before,
                grad[:, end] if inside else after,
                jnp.where(high_part, jitter_float[first - 1 : first] if at > 0 else jitter_before, 0.0),
                jnp.where(low_part, jitter_float[end : end + 1] if inside else jitter_after, 0.0),
            ],
            axis=0,
        ).reshape(-1, share, panels)

    def packed(place):
        return pick(
            place % sub_count,
            [
                jnp.concatenate([grad[:, at * share : (at + 1) * share], edge_rows(at)], axis=0)
                for at in range(sub_count)
            ],
        )

    summed = packed(sub_place)
    for step in range(1, sub_count):
        summed = summed + shifted(packed(sub_place + step), "sub", step)
    gathered = summed
    for step in range(1, rhs_count):
        gathered = gathered + shifted(summed, "rhs", step)
    own_jitter = pick(
        sub_place, [jitter_all[at * share : (at + 1) * share] for at in range(sub_count)]
    )
    node_grad = pl.pallas_call(
        node_kernel,
        out_shape=jax.ShapeDtypeStruct((3, share * panels), jnp.float32),
        in_specs=[vmem] * 3,
        out_specs=vmem,
        compiler_params=pltpu.CompilerParams(vmem_limit_bytes=16 * 1024 * 1024),
        cost_estimate=pl.CostEstimate(flops=2**20, bytes_accessed=2**18, transcendentals=0),
        name="node_terms",
    )(gathered[:3], own_jitter, gathered[3:].reshape(8, panels))
    potential = pl.pallas_call(
        sum_kernel,
        out_shape=jax.ShapeDtypeStruct((clusters, rhs, row_count), jnp.bfloat16),
        in_specs=[vmem] * sub_count,
        out_specs=vmem,
        compiler_params=pltpu.CompilerParams(vmem_limit_bytes=16 * 1024 * 1024),
        cost_estimate=pl.CostEstimate(flops=2**20, bytes_accessed=2**18, transcendentals=0),
        name="potential_sum",
    )(*found)
    return (potential, node_grad)


def solution(mesh):
    placed = (
        P(("groups", "clus"), None, "sub"),
        P(("groups", "clus"), "sub"),
        P(("groups", "clus"), "rhs", "sub"),
        P(("groups", "clus"), "rhs", "sub"),
        P(None, "groups"),
        P(("groups", "clus"), None, "sub"),
    )
    return jax.shard_map(
        on_device,
        mesh=mesh,
        in_specs=placed,
        out_specs=(P(("groups", "clus"), "rhs", "sub"), P(None, ("groups", "clus", "sub"))),
        check_vma=False,
    )
```

```python
import functools

import jax
import jax.numpy as jnp
from jax import lax
from jax.experimental import pallas as pl
from jax.experimental.pallas import tpu as pltpu
from jax.sharding import PartitionSpec as P

CP = 512
ROUNDS = 5

core_radius = 0.25
jitter_reach = 8
LANES = 128
AUG = 16


def shifted(value, axis, steps):
    count = lax.axis_size(axis)
    pairs = [(source, (source + steps) % count) for source in range(count)]
    return lax.ppermute(value, axis, pairs)


def ring_order(count):
    return [*range(0, count, 2), *reversed(range(1, count, 2))]


def round_ring(value, steps):
    order = ring_order(lax.axis_size("clus"))
    pairs = [(source, order[(at + steps) % len(order)]) for at, source in enumerate(order)]
    return lax.ppermute(value, "clus", pairs)


def moved(value, axes, target):
    counts = [lax.axis_size(axis) for axis in axes]
    pairs = []
    for major in range(counts[0]):
        for minor in range(counts[1]):
            goal = target(major, minor)
            if goal is not None:
                to_major, to_minor = goal[0] % counts[0], goal[1] % counts[1]
                pairs.append((major * counts[1] + minor, to_major * counts[1] + to_minor))
    return lax.ppermute(value, axes, pairs)


def three_parts(value):
    parts = []
    for _ in range(3):
        part = value.astype(jnp.bfloat16).astype(jnp.float32)
        parts.append(part)
        value = value - part
    return parts


def pick(index, choices):
    out = choices[0]
    for place in range(1, len(choices)):
        out = jnp.where(index == place, choices[place], out)
    return out


def fetched(arguments, places, sems):
    copies = []
    for at, (argument, place) in enumerate(zip(arguments, places)):
        copies.append(pltpu.make_async_copy(argument, place, sems.at[at]))
        copies[-1].start()
    for copy in copies:
        copy.wait()


def jitter_of(connect_ref, sizes):
    clusters, _, row_count = connect_ref.shape
    panels, nodes_total = sizes
    first_id = clusters * panels * lax.axis_index("clus") + row_count * lax.axis_index("sub")
    ids = lax.broadcasted_iota(jnp.int32, (clusters, row_count), 0) * panels
    ids = ids + lax.broadcasted_iota(jnp.int32, (clusters, row_count), 1) + first_id
    jitter = connect_ref[:, 0, :] - ids
    jitter = jnp.where(jitter > jitter_reach, jitter - nodes_total, jitter)
    jitter = jnp.where(jitter < -jitter_reach, jitter + nodes_total, jitter)
    return jitter.astype(jnp.float32).astype(jnp.bfloat16)


def prepare_kernel(sizes, *refs):
    arguments, part_refs, local_ref, scratch = refs[:5], refs[5:-7], refs[-7], refs[-6:]
    fetched(arguments, scratch[:5], scratch[5])
    density_ref, by_coord_ref, areas_ref, connect_ref, cot_ref = scratch[:5]
    clusters, rhs, _ = density_ref.shape
    quarter = part_refs[0].shape[1]
    count = len(part_refs)
    core = lax.axis_index("rhs")

    def part_of(array, place):
        return pick(place, [array[:, at * quarter : (at + 1) * quarter] for at in range(count)])

    pos = [by_coord_ref[coord] for coord in range(3)]
    jitter = jitter_of(connect_ref, sizes)
    base = clusters * rhs
    for cluster in range(clusters):
        dens = density_ref[cluster]
        span = slice(cluster * rhs, (cluster + 1) * rhs)
        local_ref[span, :] = cot_ref[cluster]
        for step, part_ref in enumerate(part_refs):
            part_ref[span, :] = part_of(dens, (core + step) % count)
    for at, value in enumerate([*pos, areas_ref[...], jitter]):
        part_refs[0][base + at * clusters : base + (at + 1) * clusters, :] = part_of(value, core)
    for at, value in enumerate([*pos, jitter]):
        local_ref[base + at * clusters : base + (at + 1) * clusters, :] = value


def target_kernel(*refs):
    local_refs, (lhs_ref, aug_ref, aug32) = refs[:-3], refs[-3:]
    clusters, _, row_count = aug_ref.shape
    rhs = local_refs[0].shape[0] // clusters - 4
    base = clusters * rhs
    pos = [
        local_refs[0][base + coord * clusters : base + (coord + 1) * clusters, :].astype(jnp.float32)
        for coord in range(3)
    ]
    square = pos[0] * pos[0] + pos[1] * pos[1] + pos[2] * pos[2] + core_radius * core_radius
    ones = jnp.ones_like(square)
    aug32[...] = jnp.zeros(aug32.shape, jnp.float32)
    for row, value in enumerate([-2.0 * value for value in pos] + three_parts(square) + [ones] * 3):
        aug32[:, row, :] = value
    blank = jnp.zeros((LANES - AUG - rhs * len(local_refs), row_count), jnp.bfloat16)
    for cluster in range(clusters):
        aug = aug32[cluster].astype(jnp.bfloat16)
        aug_ref[cluster] = aug
        rows = [ref[cluster * rhs : (cluster + 1) * rhs, :] for ref in local_refs]
        lhs_ref[cluster] = jnp.concatenate([*rows, aug, blank], axis=0).T


def step_kernel(step, length, rhs, subs, cores, first, last, *refs):
    items, refs = refs[0], refs[1:]
    source_refs, refs = refs[:cores], refs[cores:]
    source_ref = source_refs[0]
    lhs_refs, aug_refs, refs = refs[:subs], refs[subs : 2 * subs], refs[2 * subs :]
    if not first:
        acc_in, refs = refs[0], refs[1:]
    if last:
        local_refs, refs = refs[:subs], refs[subs:]
        pot_ref, pot_out_ref, grad_ref, back_ref, acc = refs[:5]
        refs = refs[5:]
    else:
        acc, back_ref = refs[:2]
        refs = refs[2:]
    aug32, left, weight, back, raw_a, raw_b, both_a, both_b = refs
    clusters, rows, panels = acc.shape
    width = rows - AUG
    row_count = panels // subs
    quarter = source_ref.shape[1]
    base = clusters * rhs

    there = [
        source_ref[base + coord * clusters : base + (coord + 1) * clusters, :].astype(jnp.float32)
        for coord in range(3)
    ]
    area = source_ref[base + 3 * clusters : base + 4 * clusters, :].astype(jnp.float32)
    square = there[0] * there[0] + there[1] * there[1] + there[2] * there[2]
    ones = jnp.ones_like(square)
    aug32[...] = jnp.zeros(aug32.shape, jnp.float32)
    for row, value in enumerate(there + [ones] * 3 + three_parts(square)):
        aug32[:, row, :] = value
    weight[...] = jnp.zeros(weight.shape, jnp.float32)
    weight[:clusters, :] = CP ** (-0.5) * area
    left[...] = jnp.zeros(left.shape, left.dtype)
    for cluster in range(clusters):
        left[cluster, width:rows, quarter:] = aug32[cluster].astype(jnp.bfloat16)
        for place, ref in enumerate(source_refs):
            left[cluster, place * rhs : (place + 1) * rhs, :quarter] = ref[
                cluster * rhs : (cluster + 1) * rhs, :
            ]
    back[...] = jnp.zeros(back.shape, jnp.float32)
    if first:
        acc[...] = jnp.zeros(acc.shape, jnp.float32)
    else:
        acc[...] = acc_in[...]
    raw_b[...] = jnp.ones(raw_b.shape, jnp.float32)
    both_a[...] = jnp.zeros(both_a.shape, both_a.dtype)

    def decoded(place):
        code = items[step * length + place]
        return code // (2 * clusters), code % (2 * clusters)

    def products(place, raw):
        here, mate = decoded(place)
        mate = mate % clusters
        lhs = jnp.concatenate([ref[here] for ref in lhs_refs], axis=0)
        raw[...] = jnp.dot(lhs, left[mate], preferred_element_type=jnp.float32)

    def pointwise(place, raw, both):
        _, mate = decoded(place)
        scale = weight[pl.ds(mate, 1), :]
        for start in range(0, panels, LANES):
            span = slice(start, start + LANES)
            inverse = lax.rsqrt(raw[span, quarter:])
            kernel = scale * inverse
            both[span, :quarter] = kernel.astype(jnp.bfloat16)
            weighted = (inverse * inverse) * (kernel * raw[span, :quarter])
            both[span, quarter:] = weighted.astype(jnp.bfloat16)

    def summed(place, both):
        here, mate = decoded(place)
        mate = mate % clusters
        acc[here] += lax.dot_general(
            left[mate, :rows, :],
            both[...],
            (((1,), (1,)), ((), ())),
            preferred_element_type=jnp.float32,
        )
        aug = jnp.concatenate([ref[here] for ref in aug_refs], axis=1)
        back[mate] += jnp.dot(aug, both[:, quarter:], preferred_element_type=jnp.float32)

    @pl.loop(0, items[step * length])
    def _(pair):
        turn = 2 * pair + 1
        summed(turn, both_a)
        pointwise(turn + 1, raw_b, both_b)
        products(turn + 2, raw_a)
        summed(turn + 1, both_b)
        pointwise(turn + 2, raw_a, both_a)
        products(turn + 3, raw_b)

    for coord in range(3):
        back_ref[coord] = -0.5 * back[:, coord, :] - there[coord] * back[:, 6, :]
    if last:
        for coord in range(3):
            span = slice(base + coord * clusters, base + (coord + 1) * clusters)
            pos = [ref[span, :] for ref in local_refs]
            pos = jnp.concatenate(pos, axis=1).astype(jnp.float32)
            grad_ref[coord] = acc[:, width + coord, :] - pos * acc[:, width + 3, :]
        pot_ref[...] = acc[:, :rhs, :]
        pot_out_ref[...] = acc[:, rhs:width, :].astype(jnp.bfloat16)


def run_step(step, length, items, sources, targets, locals_, rhs, width, carried, last):
    lhss, augs = zip(*targets)
    clusters, _, row_count = augs[0].shape
    subs = len(targets)
    panels = subs * row_count
    quarter = sources[0].shape[1]
    first = carried is None
    vmem = pl.BlockSpec(memory_space=pltpu.VMEM)
    smem = pl.BlockSpec(memory_space=pltpu.SMEM)
    operands = (items, *sources, *lhss, *augs)
    if not first:
        operands += (carried,)
    acc_shape = (clusters, width + AUG, panels)
    back_shape = jax.ShapeDtypeStruct((3, clusters, quarter), jnp.float32)
    scratch = [
        pltpu.VMEM((clusters, AUG, quarter), jnp.float32),
        pltpu.VMEM((clusters, LANES, 2 * quarter), jnp.bfloat16),
        pltpu.VMEM((clusters + 8, quarter), jnp.float32),
        pltpu.VMEM((clusters, AUG, quarter), jnp.float32),
    ]
    scratch += [pltpu.VMEM((panels, 2 * quarter), jnp.float32)] * 2
    scratch += [pltpu.VMEM((panels, 2 * quarter), jnp.bfloat16)] * 2
    if last:
        operands += tuple(locals_)
        out_shape = (
            jax.ShapeDtypeStruct((clusters, rhs, panels), jnp.float32),
            jax.ShapeDtypeStruct((clusters, width - rhs, panels), jnp.bfloat16),
            jax.ShapeDtypeStruct((3, clusters, panels), jnp.float32),
            back_shape,
        )
        scratch = [pltpu.VMEM(acc_shape, jnp.float32)] + scratch
    else:
        out_shape = (jax.ShapeDtypeStruct(acc_shape, jnp.float32), back_shape)
    pairs = (length - 6) * panels * quarter
    return pl.pallas_call(
        functools.partial(step_kernel, step, length, rhs, subs, len(sources), first, last),
        out_shape=out_shape,
        in_specs=[smem] + [vmem] * (len(operands) - 1),
        out_specs=(vmem,) * len(out_shape),
        scratch_shapes=scratch,
        compiler_params=pltpu.CompilerParams(vmem_limit_bytes=20 * 1024 * 1024),
        cost_estimate=pl.CostEstimate(
            flops=2 * pairs * (2 * width + 3 * AUG), bytes_accessed=6 * 2**20, transcendentals=pairs
        ),
        name=f"near_field_{step}",
    )(*operands)


def node_kernel(grad_ref, jitter_ref, edge_ref, main_ref):
    clusters, panels = jitter_ref.shape
    wide = panels + 2 * LANES

    def spread_of(terms, jitter):
        side = jnp.zeros((terms.shape[0], LANES), jnp.float32)
        terms = 0.25 * terms
        spread = jnp.zeros((terms.shape[0], wide), jnp.float32)
        for offset in range(-jitter_reach, jitter_reach + 1):
            masked = jnp.where(jitter == offset, terms, 0.0)
            masked = jnp.concatenate([side, masked, side], axis=1)
            spread = spread + pltpu.roll(masked, offset % wide, 1)
        spread = spread + pltpu.roll(spread, 1, 1)
        return spread + pltpu.roll(spread, 32, 1)

    jitter = jitter_ref[...]
    row_at = lax.broadcasted_iota(jnp.int32, (clusters, LANES), 0)
    edge = edge_ref[...]
    edge_at = lax.broadcasted_iota(jnp.int32, edge.shape, 0)
    edge_jitter = jnp.where(edge_at < 3, edge[6:7], edge[7:8]).astype(jnp.int32)
    edge = spread_of(edge, edge_jitter)
    for coord in range(3):
        spread = spread_of(grad_ref[coord], jitter)
        below = spread[:, :LANES]
        above = spread[:, LANES + panels :]
        inner = spread[:, LANES : LANES + panels]
        before = edge[coord : coord + 1, LANES + panels :]
        after = edge[3 + coord : 4 + coord, :LANES]
        first = jnp.where(row_at == 0, before, pltpu.roll(above, 1, 0))
        last = jnp.where(row_at == clusters - 1, after, pltpu.roll(below, clusters - 1, 0))
        inner = jnp.concatenate(
            [
                inner[:, :LANES] + first,
                inner[:, LANES : panels - LANES],
                inner[:, panels - LANES :] + last,
            ],
            axis=1,
        )
        for cluster in range(clusters):
            main_ref[coord : coord + 1, cluster * panels : (cluster + 1) * panels] = inner[
                cluster : cluster + 1
            ]


def sum_kernel(*refs):
    total = refs[0][...]
    for ref in refs[1:-1]:
        total = total + ref[...].astype(jnp.float32)
    refs[-1][...] = total.astype(jnp.bfloat16)


def on_device(positions, areas, density, cotangent, matching, connect):
    clus_count = lax.axis_size("clus")
    sub_count = lax.axis_size("sub")
    rhs_count = lax.axis_size("rhs")
    device = lax.axis_index("clus")
    sub_place = lax.axis_index("sub")
    core = lax.axis_index("rhs")
    clusters, rhs, row_count = density.shape
    panels = row_count * sub_count
    quarter = row_count // rhs_count
    width = rhs * rhs_count
    vmem = pl.BlockSpec(memory_space=pltpu.VMEM)

    nodes_total = clus_count * clusters * panels

    by_coord = jnp.transpose(positions, (1, 0, 2))
    arguments = [
        pltpu.with_memory_space_constraint(array, pltpu.HBM)
        for array in (density, by_coord, areas, connect, cotangent)
    ]
    shapes = [(clusters * (rhs + 5), quarter)] + [(clusters * rhs, quarter)] * (rhs_count - 1)
    shapes.append((clusters * (rhs + 4), row_count))
    *parts, local = pl.pallas_call(
        functools.partial(prepare_kernel, (panels, nodes_total)),
        out_shape=[jax.ShapeDtypeStruct(shape, jnp.bfloat16) for shape in shapes],
        in_specs=[pl.BlockSpec(memory_space=pltpu.HBM)] * len(arguments),
        out_specs=[vmem] * len(shapes),
        scratch_shapes=[pltpu.VMEM(array.shape, array.dtype) for array in arguments]
        + [pltpu.SemaphoreType.DMA((len(arguments),))],
        compiler_params=pltpu.CompilerParams(vmem_limit_bytes=16 * 1024 * 1024),
        name="prepare",
    )(*arguments)
    ring = ring_order(clus_count)
    at_place = [ring.index(index) for index in range(clus_count)]
    ring_place = pick(device, at_place)
    arrived = [round_ring(parts[0], 1)]
    for step in range(1, rhs_count):

        def goal(z, c, step=step):
            return (ring[(at_place[z] + 1) % clus_count], c + step)

        arrived.append(moved(parts[step], ("clus", "rhs"), goal))

    per_round = 2 * ((clusters // 2 + clus_count - 2) // (clus_count - 1))
    cap = ROUNDS * per_round
    partners = lax.dynamic_slice_in_dim(matching, device * clusters, clusters, 1).reshape(-1)
    here = jnp.tile(jnp.arange(clusters, dtype=jnp.int32), ROUNDS)
    code = here * (2 * clusters) + partners % clusters
    behind = (ring_place - pick(partners // clusters, at_place)) % clus_count
    total_items = ROUNDS * clusters
    order = jnp.arange(total_items, dtype=jnp.int32)
    rank = jnp.sum(
        ((behind[None, :] == behind[:, None]) & (order[None, :] < order[:, None])).astype(jnp.int32),
        axis=1,
    )
    steps = jnp.arange(1, clus_count, dtype=jnp.int32)
    member = behind[None, :] == steps[:, None]
    slots = jnp.arange(cap, dtype=jnp.int32)
    chosen = member[:, None, :] & (rank[None, None, :] == slots[None, :, None])
    listed = jnp.sum(jnp.where(chosen, code[None, None, :] - clusters, 0), axis=2) + clusters
    turns = (jnp.sum(member.astype(jnp.int32), axis=1) + 3) // 2
    length = cap + 6
    items = jnp.pad(listed, ((0, 0), (3, 3)), constant_values=clusters)
    items = jnp.concatenate([turns[:, None], items[:, 1:]], axis=1).reshape(-1)

    locals_ = [local] + [shifted(local, "sub", step) for step in range(1, sub_count)]
    blocks = [
        [block] + [shifted(block, "rhs", step) for step in range(1, rhs_count)] for block in locals_
    ]

    def in_order(blocks):
        return jnp.concatenate(
            [pick((sub_place - place) % sub_count, blocks) for place in range(sub_count)], axis=-1
        )

    jitter_all = in_order([block[clusters * (rhs + 3) :] for block in locals_]).astype(jnp.int32)
    targets = [
        pl.pallas_call(
            target_kernel,
            out_shape=(
                jax.ShapeDtypeStruct((clusters, row_count, LANES), jnp.bfloat16),
                jax.ShapeDtypeStruct((clusters, AUG, row_count), jnp.bfloat16),
            ),
            in_specs=[vmem] * rhs_count,
            out_specs=(vmem, vmem),
            scratch_shapes=[pltpu.VMEM((clusters, AUG, row_count), jnp.float32)],
            compiler_params=pltpu.CompilerParams(vmem_limit_bytes=16 * 1024 * 1024),
            cost_estimate=pl.CostEstimate(flops=2**20, bytes_accessed=2**18, transcendentals=0),
            name=f"targets_{place}",
        )(*blocks[place])
        for place in range(sub_count)
    ]

    arrived, targets = lax.optimization_barrier((arrived, targets))
    sources = arrived
    carried = None
    backs, jitter_rows = [], [None]
    for step in range(1, clus_count):
        if step > 1:
            if step > 2:
                sources, backs[step - 3] = lax.optimization_barrier((sources, backs[step - 3]))
            sources = [round_ring(source, 1) for source in sources]
        last = step == clus_count - 1
        results = run_step(
            step - 1, length, items, sources, targets, locals_, rhs, width, carried, last
        )
        if last:
            pot, pot_out, grad, back = results
        else:
            carried, back = results
        backs.append(back)
        at = clusters * (rhs + 4)
        jitter_rows.append(sources[0][at : at + clusters])

    grad = in_order([grad[..., at * row_count : (at + 1) * row_count] for at in range(sub_count)])
    low_part = (sub_place == 0) & (core == 0)
    high_part = (sub_place == sub_count - 1) & (core == rhs_count - 1)
    uppers = [grad[:, -1, -quarter:]] + [jnp.where(high_part, back[:, -1], 0.0) for back in backs]
    lowers = [grad[:, 0, :quarter]] + [jnp.where(low_part, back[:, 0], 0.0) for back in backs]

    def step_between(index, owner):
        return (at_place[index] - at_place[owner % clus_count]) % clus_count

    def needed(parts, step, offset):
        choices = []
        for index in range(clus_count):
            goal = ring[(at_place[index] - step) % clus_count]
            choices.append(parts[step_between(index, goal + offset)])
        return pick(device, choices)

    nothing = jnp.zeros((2, quarter), jnp.float32)
    returned = jnp.zeros((3, clusters, quarter), jnp.float32)
    upper, lower = needed(uppers, 0, -1), needed(lowers, 0, 1)
    for step in range(1, clus_count):
        rows = [
            backs[step - 1].reshape(3 * clusters, quarter),
            needed(uppers, step, -1),
            needed(lowers, step, 1),
            nothing,
        ]
        home = round_ring(jnp.concatenate(rows, axis=0), -step)
        returned = returned + home[: 3 * clusters].reshape(returned.shape)
        upper = upper + home[3 * clusters : 3 * clusters + 3]
        lower = lower + home[3 * clusters + 3 : 3 * clusters + 6]

    half = pot
    for step in range(1, rhs_count):
        arrived = shifted(pot_out[:, (step - 1) * rhs : step * rhs], "rhs", -step)
        half = half + arrived.astype(jnp.float32)

    half, grad = lax.optimization_barrier((half, grad))
    found = [half[..., :row_count]]
    for step in range(1, sub_count):
        sent = half[..., step * row_count : (step + 1) * row_count].astype(jnp.bfloat16)
        found.append(shifted(sent, "sub", -step))

    quarter_at = sub_place * rhs_count + core
    grad = grad + jnp.concatenate(
        [jnp.where(quarter_at == at, returned, 0.0) for at in range(sub_count * rhs_count)], axis=-1
    )
    share = clusters // sub_count

    blank = jnp.zeros((3, panels - quarter), jnp.float32)
    before = jnp.concatenate([blank, upper], axis=1)
    after = jnp.concatenate([lower, blank], axis=1)
    jitter_float = jitter_all.astype(jnp.float32)
    jitter_before = jnp.concatenate(
        [blank[:1], needed(jitter_rows, 0, -1)[clusters - 1 :].astype(jnp.float32)], axis=1
    )
    jitter_after = jnp.concatenate(
        [needed(jitter_rows, 0, 1)[:1].astype(jnp.float32), blank[:1]], axis=1
    )

    def edge_rows(at):
        first, end = at * share, (at + 1) * share
        inside = at < sub_count - 1
        return jnp.concatenate(
            [
                grad[:, first - 1] if at > 0 else before,
                grad[:, end] if inside else after,
                jnp.where(high_part, jitter_float[first - 1 : first] if at > 0 else jitter_before, 0.0),
                jnp.where(low_part, jitter_float[end : end + 1] if inside else jitter_after, 0.0),
            ],
            axis=0,
        ).reshape(-1, share, panels)

    def packed(place):
        return pick(
            place % sub_count,
            [
                jnp.concatenate([grad[:, at * share : (at + 1) * share], edge_rows(at)], axis=0)
                for at in range(sub_count)
            ],
        )

    summed = packed(sub_place)
    for step in range(1, sub_count):
        summed = summed + shifted(packed(sub_place + step), "sub", step)
    gathered = summed
    for step in range(1, rhs_count):
        gathered = gathered + shifted(summed, "rhs", step)
    own_jitter = pick(
        sub_place, [jitter_all[at * share : (at + 1) * share] for at in range(sub_count)]
    )
    node_grad = pl.pallas_call(
        node_kernel,
        out_shape=jax.ShapeDtypeStruct((3, share * panels), jnp.float32),
        in_specs=[vmem] * 3,
        out_specs=vmem,
        compiler_params=pltpu.CompilerParams(vmem_limit_bytes=16 * 1024 * 1024),
        cost_estimate=pl.CostEstimate(flops=2**20, bytes_accessed=2**18, transcendentals=0),
        name="node_terms",
    )(gathered[:3], own_jitter, gathered[3:].reshape(8, panels))
    potential = pl.pallas_call(
        sum_kernel,
        out_shape=jax.ShapeDtypeStruct((clusters, rhs, row_count), jnp.bfloat16),
        in_specs=[vmem] * sub_count,
        out_specs=vmem,
        compiler_params=pltpu.CompilerParams(vmem_limit_bytes=16 * 1024 * 1024),
        cost_estimate=pl.CostEstimate(flops=2**20, bytes_accessed=2**18, transcendentals=0),
        name="potential_sum",
    )(*found)
    return (potential, node_grad)


def solution(mesh):
    placed = (
        P(("groups", "clus"), None, "sub"),
        P(("groups", "clus"), "sub"),
        P(("groups", "clus"), "rhs", "sub"),
        P(("groups", "clus"), "rhs", "sub"),
        P(None, "groups"),
        P(("groups", "clus"), None, "sub"),
    )
    return jax.shard_map(
        on_device,
        mesh=mesh,
        in_specs=placed,
        out_specs=(P(("groups", "clus"), "rhs", "sub"), P(None, ("groups", "clus", "sub"))),
        check_vma=False,
    )
```

```python
import functools

import jax
import jax.numpy as jnp
from jax import lax
from jax.experimental import pallas as pl
from jax.experimental.pallas import tpu as pltpu
from jax.sharding import PartitionSpec as P

CP = 512
ROUNDS = 5

core_radius = 0.25
jitter_reach = 8
LANES = 128
AUG = 16


def shifted(value, axis, steps):
    count = lax.axis_size(axis)
    pairs = [(source, (source + steps) % count) for source in range(count)]
    return lax.ppermute(value, axis, pairs)


def ring_order(count):
    return [*range(0, count, 2), *reversed(range(1, count, 2))]


def round_ring(value, steps):
    order = ring_order(lax.axis_size("clus"))
    pairs = [(source, order[(at + steps) % len(order)]) for at, source in enumerate(order)]
    return lax.ppermute(value, "clus", pairs)


def moved(value, axes, target):
    counts = [lax.axis_size(axis) for axis in axes]
    pairs = []
    for major in range(counts[0]):
        for minor in range(counts[1]):
            goal = target(major, minor)
            if goal is not None:
                to_major, to_minor = goal[0] % counts[0], goal[1] % counts[1]
                pairs.append((major * counts[1] + minor, to_major * counts[1] + to_minor))
    return lax.ppermute(value, axes, pairs)


def three_parts(value):
    parts = []
    for _ in range(3):
        part = value.astype(jnp.bfloat16).astype(jnp.float32)
        parts.append(part)
        value = value - part
    return parts


def pick(index, choices):
    out = choices[0]
    for place in range(1, len(choices)):
        out = jnp.where(index == place, choices[place], out)
    return out


def fetched(arguments, places, sems):
    copies = []
    for at, (argument, place) in enumerate(zip(arguments, places)):
        copies.append(pltpu.make_async_copy(argument, place, sems.at[at]))
        copies[-1].start()
    for copy in copies:
        copy.wait()


def jitter_of(connect_ref, sizes):
    clusters, _, row_count = connect_ref.shape
    panels, nodes_total = sizes
    first_id = clusters * panels * lax.axis_index("clus") + row_count * lax.axis_index("sub")
    ids = lax.broadcasted_iota(jnp.int32, (clusters, row_count), 0) * panels
    ids = ids + lax.broadcasted_iota(jnp.int32, (clusters, row_count), 1) + first_id
    jitter = connect_ref[:, 0, :] - ids
    jitter = jnp.where(jitter > jitter_reach, jitter - nodes_total, jitter)
    jitter = jnp.where(jitter < -jitter_reach, jitter + nodes_total, jitter)
    return jitter.astype(jnp.float32).astype(jnp.bfloat16)


def prepare_kernel(sizes, *refs):
    arguments, part_refs, local_ref, scratch = refs[:5], refs[5:-7], refs[-7], refs[-6:]
    fetched(arguments, scratch[:5], scratch[5])
    density_ref, by_coord_ref, areas_ref, connect_ref, cot_ref = scratch[:5]
    clusters, rhs, _ = density_ref.shape
    quarter = part_refs[0].shape[1]
    count = len(part_refs)
    core = lax.axis_index("rhs")

    def part_of(array, place):
        return pick(place, [array[:, at * quarter : (at + 1) * quarter] for at in range(count)])

    pos = [by_coord_ref[coord] for coord in range(3)]
    jitter = jitter_of(connect_ref, sizes)
    base = clusters * rhs
    for cluster in range(clusters):
        dens = density_ref[cluster]
        span = slice(cluster * rhs, (cluster + 1) * rhs)
        local_ref[span, :] = cot_ref[cluster]
        for step, part_ref in enumerate(part_refs):
            part_ref[span, :] = part_of(dens, (core + step) % count)
    for at, value in enumerate([*pos, areas_ref[...], jitter]):
        part_refs[0][base + at * clusters : base + (at + 1) * clusters, :] = part_of(value, core)
    for at, value in enumerate([*pos, jitter]):
        local_ref[base + at * clusters : base + (at + 1) * clusters, :] = value


def target_kernel(*refs):
    local_refs, (lhs_ref, aug_ref, aug32) = refs[:-3], refs[-3:]
    clusters, _, row_count = aug_ref.shape
    rhs = local_refs[0].shape[0] // clusters - 4
    base = clusters * rhs
    pos = [
        local_refs[0][base + coord * clusters : base + (coord + 1) * clusters, :].astype(jnp.float32)
        for coord in range(3)
    ]
    square = pos[0] * pos[0] + pos[1] * pos[1] + pos[2] * pos[2] + core_radius * core_radius
    ones = jnp.ones_like(square)
    aug32[...] = jnp.zeros(aug32.shape, jnp.float32)
    for row, value in enumerate([-2.0 * value for value in pos] + three_parts(square) + [ones] * 3):
        aug32[:, row, :] = value
    blank = jnp.zeros((LANES - AUG - rhs * len(local_refs), row_count), jnp.bfloat16)
    for cluster in range(clusters):
        aug = aug32[cluster].astype(jnp.bfloat16)
        aug_ref[cluster] = aug
        rows = [ref[cluster * rhs : (cluster + 1) * rhs, :] for ref in local_refs]
        lhs_ref[cluster] = jnp.concatenate([*rows, aug, blank], axis=0).T


def step_kernel(step, length, rhs, subs, first, last, *refs):
    items, source_ref, refs = refs[0], refs[1], refs[2:]
    lhs_refs, aug_refs, refs = refs[:subs], refs[subs : 2 * subs], refs[2 * subs :]
    if not first:
        acc_in, refs = refs[0], refs[1:]
    if last:
        local_refs, refs = refs[:subs], refs[subs:]
        pot_ref, pot_out_ref, grad_ref, back_ref, acc = refs[:5]
        refs = refs[5:]
    else:
        acc, back_ref = refs[:2]
        refs = refs[2:]
    aug32, left, weight, back, raw_a, raw_b, both_a, both_b = refs
    clusters, rows, panels = acc.shape
    width = rows - AUG
    row_count = panels // subs
    quarter = source_ref.shape[1]
    base = clusters * rhs

    starts = [0] + list(range(base + 5 * clusters, source_ref.shape[0], base))

    there = [
        source_ref[base + coord * clusters : base + (coord + 1) * clusters, :].astype(jnp.float32)
        for coord in range(3)
    ]
    area = source_ref[base + 3 * clusters : base + 4 * clusters, :].astype(jnp.float32)
    square = there[0] * there[0] + there[1] * there[1] + there[2] * there[2]
    ones = jnp.ones_like(square)
    aug32[...] = jnp.zeros(aug32.shape, jnp.float32)
    for row, value in enumerate(there + [ones] * 3 + three_parts(square)):
        aug32[:, row, :] = value
    weight[...] = jnp.zeros(weight.shape, jnp.float32)
    weight[:clusters, :] = CP ** (-0.5) * area
    left[...] = jnp.zeros(left.shape, left.dtype)
    for cluster in range(clusters):
        left[cluster, width:rows, quarter:] = aug32[cluster].astype(jnp.bfloat16)
        for place, at in enumerate(starts):
            left[cluster, place * rhs : (place + 1) * rhs, :quarter] = source_ref[
                at + cluster * rhs : at + (cluster + 1) * rhs, :
            ]
    back[...] = jnp.zeros(back.shape, jnp.float32)
    if first:
        acc[...] = jnp.zeros(acc.shape, jnp.float32)
    else:
        acc[...] = acc_in[...]
    raw_b[...] = jnp.ones(raw_b.shape, jnp.float32)
    both_a[...] = jnp.zeros(both_a.shape, both_a.dtype)

    def decoded(place):
        code = items[step * length + place]
        return code // (2 * clusters), code % (2 * clusters)

    def products(place, raw):
        here, mate = decoded(place)
        mate = mate % clusters
        lhs = jnp.concatenate([ref[here] for ref in lhs_refs], axis=0)
        raw[...] = jnp.dot(lhs, left[mate], preferred_element_type=jnp.float32)

    def pointwise(place, raw, both):
        _, mate = decoded(place)
        scale = weight[pl.ds(mate, 1), :]
        for start in range(0, panels, LANES):
            span = slice(start, start + LANES)
            inverse = lax.rsqrt(raw[span, quarter:])
            kernel = scale * inverse
            both[span, :quarter] = kernel.astype(jnp.bfloat16)
            weighted = (inverse * inverse) * (kernel * raw[span, :quarter])
            both[span, quarter:] = weighted.astype(jnp.bfloat16)

    def summed(place, both):
        here, mate = decoded(place)
        mate = mate % clusters
        acc[here] += lax.dot_general(
            left[mate, :rows, :],
            both[...],
            (((1,), (1,)), ((), ())),
            preferred_element_type=jnp.float32,
        )
        aug = jnp.concatenate([ref[here] for ref in aug_refs], axis=1)
        back[mate] += jnp.dot(aug, both[:, quarter:], preferred_element_type=jnp.float32)

    @pl.loop(0, items[step * length])
    def _(pair):
        turn = 2 * pair + 1
        summed(turn, both_a)
        pointwise(turn + 1, raw_b, both_b)
        products(turn + 2, raw_a)
        summed(turn + 1, both_b)
        pointwise(turn + 2, raw_a, both_a)
        products(turn + 3, raw_b)

    for coord in range(3):
        back_ref[coord] = -0.5 * back[:, coord, :] - there[coord] * back[:, 6, :]
    if last:
        for coord in range(3):
            span = slice(base + coord * clusters, base + (coord + 1) * clusters)
            pos = [ref[span, :] for ref in local_refs]
            pos = jnp.concatenate(pos, axis=1).astype(jnp.float32)
            grad_ref[coord] = acc[:, width + coord, :] - pos * acc[:, width + 3, :]
        pot_ref[...] = acc[:, :rhs, :]
        pot_out_ref[...] = acc[:, rhs:width, :].astype(jnp.bfloat16)


def run_step(step, length, items, source, targets, locals_, rhs, width, carried, last):
    lhss, augs = zip(*targets)
    clusters, _, row_count = augs[0].shape
    subs = len(targets)
    panels = subs * row_count
    quarter = source.shape[1]
    first = carried is None
    vmem = pl.BlockSpec(memory_space=pltpu.VMEM)
    smem = pl.BlockSpec(memory_space=pltpu.SMEM)
    operands = (items, source, *lhss, *augs)
    if not first:
        operands += (carried,)
    acc_shape = (clusters, width + AUG, panels)
    back_shape = jax.ShapeDtypeStruct((3, clusters, quarter), jnp.float32)
    scratch = [
        pltpu.VMEM((clusters, AUG, quarter), jnp.float32),
        pltpu.VMEM((clusters, LANES, 2 * quarter), jnp.bfloat16),
        pltpu.VMEM((clusters + 8, quarter), jnp.float32),
        pltpu.VMEM((clusters, AUG, quarter), jnp.float32),
    ]
    scratch += [pltpu.VMEM((panels, 2 * quarter), jnp.float32)] * 2
    scratch += [pltpu.VMEM((panels, 2 * quarter), jnp.bfloat16)] * 2
    if last:
        operands += tuple(locals_)
        out_shape = (
            jax.ShapeDtypeStruct((clusters, rhs, panels), jnp.float32),
            jax.ShapeDtypeStruct((clusters, width - rhs, panels), jnp.bfloat16),
            jax.ShapeDtypeStruct((3, clusters, panels), jnp.float32),
            back_shape,
        )
        scratch = [pltpu.VMEM(acc_shape, jnp.float32)] + scratch
    else:
        out_shape = (jax.ShapeDtypeStruct(acc_shape, jnp.float32), back_shape)
    pairs = (length - 6) * panels * quarter
    return pl.pallas_call(
        functools.partial(step_kernel, step, length, rhs, subs, first, last),
        out_shape=out_shape,
        in_specs=[smem] + [vmem] * (len(operands) - 1),
        out_specs=(vmem,) * len(out_shape),
        scratch_shapes=scratch,
        compiler_params=pltpu.CompilerParams(vmem_limit_bytes=20 * 1024 * 1024),
        cost_estimate=pl.CostEstimate(
            flops=2 * pairs * (2 * width + 3 * AUG), bytes_accessed=6 * 2**20, transcendentals=pairs
        ),
        name=f"near_field_{step}",
    )(*operands)


def node_kernel(grad_ref, jitter_ref, edge_ref, main_ref):
    clusters, panels = jitter_ref.shape
    wide = panels + 2 * LANES

    def spread_of(terms, jitter):
        side = jnp.zeros((terms.shape[0], LANES), jnp.float32)
        terms = 0.25 * terms
        spread = jnp.zeros((terms.shape[0], wide), jnp.float32)
        for offset in range(-jitter_reach, jitter_reach + 1):
            masked = jnp.where(jitter == offset, terms, 0.0)
            masked = jnp.concatenate([side, masked, side], axis=1)
            spread = spread + pltpu.roll(masked, offset % wide, 1)
        spread = spread + pltpu.roll(spread, 1, 1)
        return spread + pltpu.roll(spread, 32, 1)

    jitter = jitter_ref[...]
    row_at = lax.broadcasted_iota(jnp.int32, (clusters, LANES), 0)
    edge = edge_ref[...]
    edge_at = lax.broadcasted_iota(jnp.int32, edge.shape, 0)
    edge_jitter = jnp.where(edge_at < 3, edge[6:7], edge[7:8]).astype(jnp.int32)
    edge = spread_of(edge, edge_jitter)
    for coord in range(3):
        spread = spread_of(grad_ref[coord], jitter)
        below = spread[:, :LANES]
        above = spread[:, LANES + panels :]
        inner = spread[:, LANES : LANES + panels]
        before = edge[coord : coord + 1, LANES + panels :]
        after = edge[3 + coord : 4 + coord, :LANES]
        first = jnp.where(row_at == 0, before, pltpu.roll(above, 1, 0))
        last = jnp.where(row_at == clusters - 1, after, pltpu.roll(below, clusters - 1, 0))
        inner = jnp.concatenate(
            [
                inner[:, :LANES] + first,
                inner[:, LANES : panels - LANES],
                inner[:, panels - LANES :] + last,
            ],
            axis=1,
        )
        for cluster in range(clusters):
            main_ref[coord : coord + 1, cluster * panels : (cluster + 1) * panels] = inner[
                cluster : cluster + 1
            ]


def sum_kernel(*refs):
    total = refs[0][...]
    for ref in refs[1:-1]:
        total = total + ref[...].astype(jnp.float32)
    refs[-1][...] = total.astype(jnp.bfloat16)


def on_device(positions, areas, density, cotangent, matching, connect):
    clus_count = lax.axis_size("clus")
    sub_count = lax.axis_size("sub")
    rhs_count = lax.axis_size("rhs")
    device = lax.axis_index("clus")
    sub_place = lax.axis_index("sub")
    core = lax.axis_index("rhs")
    clusters, rhs, row_count = density.shape
    panels = row_count * sub_count
    quarter = row_count // rhs_count
    width = rhs * rhs_count
    vmem = pl.BlockSpec(memory_space=pltpu.VMEM)

    nodes_total = clus_count * clusters * panels

    by_coord = jnp.transpose(positions, (1, 0, 2))
    arguments = [
        pltpu.with_memory_space_constraint(array, pltpu.HBM)
        for array in (density, by_coord, areas, connect, cotangent)
    ]
    shapes = [(clusters * (rhs + 5), quarter)] + [(clusters * rhs, quarter)] * (rhs_count - 1)
    shapes.append((clusters * (rhs + 4), row_count))
    *parts, local = pl.pallas_call(
        functools.partial(prepare_kernel, (panels, nodes_total)),
        out_shape=[jax.ShapeDtypeStruct(shape, jnp.bfloat16) for shape in shapes],
        in_specs=[pl.BlockSpec(memory_space=pltpu.HBM)] * len(arguments),
        out_specs=[vmem] * len(shapes),
        scratch_shapes=[pltpu.VMEM(array.shape, array.dtype) for array in arguments]
        + [pltpu.SemaphoreType.DMA((len(arguments),))],
        compiler_params=pltpu.CompilerParams(vmem_limit_bytes=16 * 1024 * 1024),
        name="prepare",
    )(*arguments)
    ring = ring_order(clus_count)
    at_place = [ring.index(index) for index in range(clus_count)]
    ring_place = pick(device, at_place)

    def own_parts(parts, steps):
        arrived = [round_ring(parts[0], steps)]
        for step in range(1, rhs_count):

            def goal(z, c, step=step):
                return (ring[(at_place[z] + steps) % clus_count], c + step)

            arrived.append(moved(parts[step], ("clus", "rhs"), goal))
        return arrived

    arrived = own_parts(parts, 1)

    per_round = 2 * ((clusters // 2 + clus_count - 2) // (clus_count - 1))
    cap = ROUNDS * per_round
    partners = lax.dynamic_slice_in_dim(matching, device * clusters, clusters, 1).reshape(-1)
    here = jnp.tile(jnp.arange(clusters, dtype=jnp.int32), ROUNDS)
    code = here * (2 * clusters) + partners % clusters
    behind = (ring_place - pick(partners // clusters, at_place)) % clus_count
    total_items = ROUNDS * clusters
    order = jnp.arange(total_items, dtype=jnp.int32)
    rank = jnp.sum(
        ((behind[None, :] == behind[:, None]) & (order[None, :] < order[:, None])).astype(jnp.int32),
        axis=1,
    )
    steps = jnp.arange(1, clus_count, dtype=jnp.int32)
    member = behind[None, :] == steps[:, None]
    slots = jnp.arange(cap, dtype=jnp.int32)
    chosen = member[:, None, :] & (rank[None, None, :] == slots[None, :, None])
    listed = jnp.sum(jnp.where(chosen, code[None, None, :] - clusters, 0), axis=2) + clusters
    turns = (jnp.sum(member.astype(jnp.int32), axis=1) + 3) // 2
    length = cap + 6
    items = jnp.pad(listed, ((0, 0), (3, 3)), constant_values=clusters)
    items = jnp.concatenate([turns[:, None], items[:, 1:]], axis=1).reshape(-1)

    locals_ = [local] + [shifted(local, "sub", step) for step in range(1, sub_count)]
    blocks = [
        [block] + [shifted(block, "rhs", step) for step in range(1, rhs_count)] for block in locals_
    ]

    def in_order(blocks):
        return jnp.concatenate(
            [pick((sub_place - place) % sub_count, blocks) for place in range(sub_count)], axis=-1
        )

    jitter_all = in_order([block[clusters * (rhs + 3) :] for block in locals_]).astype(jnp.int32)
    targets = [
        pl.pallas_call(
            target_kernel,
            out_shape=(
                jax.ShapeDtypeStruct((clusters, row_count, LANES), jnp.bfloat16),
                jax.ShapeDtypeStruct((clusters, AUG, row_count), jnp.bfloat16),
            ),
            in_specs=[vmem] * rhs_count,
            out_specs=(vmem, vmem),
            scratch_shapes=[pltpu.VMEM((clusters, AUG, row_count), jnp.float32)],
            compiler_params=pltpu.CompilerParams(vmem_limit_bytes=16 * 1024 * 1024),
            cost_estimate=pl.CostEstimate(flops=2**20, bytes_accessed=2**18, transcendentals=0),
            name=f"targets_{place}",
        )(*blocks[place])
        for place in range(sub_count)
    ]

    arrived, targets = lax.optimization_barrier((arrived, targets))
    source = jnp.concatenate(arrived, axis=0)
    source, parts = lax.optimization_barrier((source, parts))
    from_next = own_parts(parts, -1) if clus_count > 2 else None
    carried = None
    backs, jitter_rows = [], [None]
    for step in range(1, clus_count):
        if 1 < step < clus_count - 1:
            if step > 2:
                source, backs[step - 3] = lax.optimization_barrier((source, backs[step - 3]))
            source = round_ring(source, 1)
        elif step > 1:
            from_next, backs[-1] = lax.optimization_barrier((from_next, backs[-1]))
            source = jnp.concatenate(from_next, axis=0)
        last = step == clus_count - 1
        results = run_step(
            step - 1, length, items, source, targets, locals_, rhs, width, carried, last
        )
        if last:
            pot, pot_out, grad, back = results
        else:
            carried, back = results
        backs.append(back)
        at = clusters * (rhs + 4)
        jitter_rows.append(source[at : at + clusters])

    grad = in_order([grad[..., at * row_count : (at + 1) * row_count] for at in range(sub_count)])
    low_part = (sub_place == 0) & (core == 0)
    high_part = (sub_place == sub_count - 1) & (core == rhs_count - 1)
    uppers = [grad[:, -1, -quarter:]] + [jnp.where(high_part, back[:, -1], 0.0) for back in backs]
    lowers = [grad[:, 0, :quarter]] + [jnp.where(low_part, back[:, 0], 0.0) for back in backs]

    def step_between(index, owner):
        return (at_place[index] - at_place[owner % clus_count]) % clus_count

    def needed(parts, step, offset):
        choices = []
        for index in range(clus_count):
            goal = ring[(at_place[index] - step) % clus_count]
            choices.append(parts[step_between(index, goal + offset)])
        return pick(device, choices)

    nothing = jnp.zeros((2, quarter), jnp.float32)
    returned = jnp.zeros((3, clusters, quarter), jnp.float32)
    upper, lower = needed(uppers, 0, -1), needed(lowers, 0, 1)
    for step in range(1, clus_count):
        rows = [
            backs[step - 1].reshape(3 * clusters, quarter),
            needed(uppers, step, -1),
            needed(lowers, step, 1),
            nothing,
        ]
        home = round_ring(jnp.concatenate(rows, axis=0), -step)
        returned = returned + home[: 3 * clusters].reshape(returned.shape)
        upper = upper + home[3 * clusters : 3 * clusters + 3]
        lower = lower + home[3 * clusters + 3 : 3 * clusters + 6]

    half = pot
    for step in range(1, rhs_count):
        arrived = shifted(pot_out[:, (step - 1) * rhs : step * rhs], "rhs", -step)
        half = half + arrived.astype(jnp.float32)

    half, grad = lax.optimization_barrier((half, grad))
    found = [half[..., :row_count]]
    for step in range(1, sub_count):
        sent = half[..., step * row_count : (step + 1) * row_count].astype(jnp.bfloat16)
        found.append(shifted(sent, "sub", -step))

    quarter_at = sub_place * rhs_count + core
    grad = grad + jnp.concatenate(
        [jnp.where(quarter_at == at, returned, 0.0) for at in range(sub_count * rhs_count)], axis=-1
    )
    share = clusters // sub_count

    blank = jnp.zeros((3, panels - quarter), jnp.float32)
    before = jnp.concatenate([blank, upper], axis=1)
    after = jnp.concatenate([lower, blank], axis=1)
    jitter_float = jitter_all.astype(jnp.float32)
    jitter_before = jnp.concatenate(
        [blank[:1], needed(jitter_rows, 0, -1)[clusters - 1 :].astype(jnp.float32)], axis=1
    )
    jitter_after = jnp.concatenate(
        [needed(jitter_rows, 0, 1)[:1].astype(jnp.float32), blank[:1]], axis=1
    )

    def edge_rows(at):
        first, end = at * share, (at + 1) * share
        inside = at < sub_count - 1
        return jnp.concatenate(
            [
                grad[:, first - 1] if at > 0 else before,
                grad[:, end] if inside else after,
                jnp.where(high_part, jitter_float[first - 1 : first] if at > 0 else jitter_before, 0.0),
                jnp.where(low_part, jitter_float[end : end + 1] if inside else jitter_after, 0.0),
            ],
            axis=0,
        ).reshape(-1, share, panels)

    def packed(place):
        return pick(
            place % sub_count,
            [
                jnp.concatenate([grad[:, at * share : (at + 1) * share], edge_rows(at)], axis=0)
                for at in range(sub_count)
            ],
        )

    summed = packed(sub_place)
    for step in range(1, sub_count):
        summed = summed + shifted(packed(sub_place + step), "sub", step)
    gathered = summed
    for step in range(1, rhs_count):
        gathered = gathered + shifted(summed, "rhs", step)
    own_jitter = pick(
        sub_place, [jitter_all[at * share : (at + 1) * share] for at in range(sub_count)]
    )
    node_grad = pl.pallas_call(
        node_kernel,
        out_shape=jax.ShapeDtypeStruct((3, share * panels), jnp.float32),
        in_specs=[vmem] * 3,
        out_specs=vmem,
        compiler_params=pltpu.CompilerParams(vmem_limit_bytes=16 * 1024 * 1024),
        cost_estimate=pl.CostEstimate(flops=2**20, bytes_accessed=2**18, transcendentals=0),
        name="node_terms",
    )(gathered[:3], own_jitter, gathered[3:].reshape(8, panels))
    potential = pl.pallas_call(
        sum_kernel,
        out_shape=jax.ShapeDtypeStruct((clusters, rhs, row_count), jnp.bfloat16),
        in_specs=[vmem] * sub_count,
        out_specs=vmem,
        compiler_params=pltpu.CompilerParams(vmem_limit_bytes=16 * 1024 * 1024),
        cost_estimate=pl.CostEstimate(flops=2**20, bytes_accessed=2**18, transcendentals=0),
        name="potential_sum",
    )(*found)
    return (potential, node_grad)


def solution(mesh):
    placed = (
        P(("groups", "clus"), None, "sub"),
        P(("groups", "clus"), "sub"),
        P(("groups", "clus"), "rhs", "sub"),
        P(("groups", "clus"), "rhs", "sub"),
        P(None, "groups"),
        P(("groups", "clus"), None, "sub"),
    )
    return jax.shard_map(
        on_device,
        mesh=mesh,
        in_specs=placed,
        out_specs=(P(("groups", "clus"), "rhs", "sub"), P(None, ("groups", "clus", "sub"))),
        check_vma=False,
    )
```

```python
import functools

import jax
import jax.numpy as jnp
from jax import lax
from jax.experimental import pallas as pl
from jax.experimental.pallas import tpu as pltpu
from jax.sharding import PartitionSpec as P

CP = 512
ROUNDS = 5

core_radius = 0.25
jitter_reach = 8
LANES = 128
AUG = 16


def shifted(value, axis, steps):
    count = lax.axis_size(axis)
    pairs = [(source, (source + steps) % count) for source in range(count)]
    return lax.ppermute(value, axis, pairs)


def ring_order(count):
    return [*range(0, count, 2), *reversed(range(1, count, 2))]


def round_ring(value, steps):
    order = ring_order(lax.axis_size("clus"))
    pairs = [(source, order[(at + steps) % len(order)]) for at, source in enumerate(order)]
    return lax.ppermute(value, "clus", pairs)


def moved(value, axes, target):
    counts = [lax.axis_size(axis) for axis in axes]
    pairs = []
    for major in range(counts[0]):
        for minor in range(counts[1]):
            goal = target(major, minor)
            if goal is not None:
                to_major, to_minor = goal[0] % counts[0], goal[1] % counts[1]
                pairs.append((major * counts[1] + minor, to_major * counts[1] + to_minor))
    return lax.ppermute(value, axes, pairs)


def three_parts(value):
    parts = []
    for _ in range(3):
        part = value.astype(jnp.bfloat16).astype(jnp.float32)
        parts.append(part)
        value = value - part
    return parts


def pick(index, choices):
    out = choices[0]
    for place in range(1, len(choices)):
        out = jnp.where(index == place, choices[place], out)
    return out


def fetched(arguments, places, sems):
    copies = []
    for at, (argument, place) in enumerate(zip(arguments, places)):
        copies.append(pltpu.make_async_copy(argument, place, sems.at[at]))
        copies[-1].start()
    for copy in copies:
        copy.wait()


def jitter_of(connect_ref, sizes):
    clusters, _, row_count = connect_ref.shape
    panels, nodes_total = sizes
    first_id = clusters * panels * lax.axis_index("clus") + row_count * lax.axis_index("sub")
    ids = lax.broadcasted_iota(jnp.int32, (clusters, row_count), 0) * panels
    ids = ids + lax.broadcasted_iota(jnp.int32, (clusters, row_count), 1) + first_id
    jitter = connect_ref[:, 0, :] - ids
    jitter = jnp.where(jitter > jitter_reach, jitter - nodes_total, jitter)
    jitter = jnp.where(jitter < -jitter_reach, jitter + nodes_total, jitter)
    return jitter.astype(jnp.float32).astype(jnp.bfloat16)


def prepare_kernel(sizes, *refs):
    arguments, part_refs, local_ref, scratch = refs[:5], refs[5:-7], refs[-7], refs[-6:]
    fetched(arguments, scratch[:5], scratch[5])
    density_ref, by_coord_ref, areas_ref, connect_ref, cot_ref = scratch[:5]
    clusters, rhs, _ = density_ref.shape
    quarter = part_refs[0].shape[1]
    count = len(part_refs)
    core = lax.axis_index("rhs")

    def part_of(array, place):
        return pick(place, [array[:, at * quarter : (at + 1) * quarter] for at in range(count)])

    pos = [by_coord_ref[coord] for coord in range(3)]
    jitter = jitter_of(connect_ref, sizes)
    base = clusters * rhs
    for cluster in range(clusters):
        dens = density_ref[cluster]
        span = slice(cluster * rhs, (cluster + 1) * rhs)
        local_ref[span, :] = cot_ref[cluster]
        for step, part_ref in enumerate(part_refs):
            part_ref[span, :] = part_of(dens, (core + step) % count)
    for at, value in enumerate([*pos, areas_ref[...], jitter]):
        part_refs[0][base + at * clusters : base + (at + 1) * clusters, :] = part_of(value, core)
    for at, value in enumerate([*pos, jitter]):
        local_ref[base + at * clusters : base + (at + 1) * clusters, :] = value


def target_kernel(*refs):
    local_refs, (lhs_ref, aug_ref, aug32) = refs[:-3], refs[-3:]
    clusters, _, row_count = aug_ref.shape
    rhs = local_refs[0].shape[0] // clusters - 4
    base = clusters * rhs
    pos = [
        local_refs[0][base + coord * clusters : base + (coord + 1) * clusters, :].astype(jnp.float32)
        for coord in range(3)
    ]
    square = pos[0] * pos[0] + pos[1] * pos[1] + pos[2] * pos[2] + core_radius * core_radius
    ones = jnp.ones_like(square)
    aug32[...] = jnp.zeros(aug32.shape, jnp.float32)
    for row, value in enumerate([-2.0 * value for value in pos] + three_parts(square) + [ones] * 3):
        aug32[:, row, :] = value
    blank = jnp.zeros((LANES - AUG - rhs * len(local_refs), row_count), jnp.bfloat16)
    for cluster in range(clusters):
        aug = aug32[cluster].astype(jnp.bfloat16)
        aug_ref[cluster] = aug
        rows = [ref[cluster * rhs : (cluster + 1) * rhs, :] for ref in local_refs]
        lhs_ref[cluster] = jnp.concatenate([*rows, aug, blank], axis=0).T


def step_kernel(step, length, rhs, subs, first, last, *refs):
    items, source_ref, refs = refs[0], refs[1], refs[2:]
    lhs_refs, aug_refs, refs = refs[:subs], refs[subs : 2 * subs], refs[2 * subs :]
    if not first:
        acc_in, refs = refs[0], refs[1:]
    if last:
        local_refs, refs = refs[:subs], refs[subs:]
        pot_ref, pot_out_ref, grad_ref, back_ref, acc = refs[:5]
        refs = refs[5:]
    else:
        acc, back_ref = refs[:2]
        refs = refs[2:]
    aug32, left, weight, back, both_a, both_b = refs
    clusters, rows, panels = acc.shape
    width = rows - AUG
    row_count = panels // subs
    quarter = source_ref.shape[1]
    base = clusters * rhs

    starts = [0] + list(range(base + 5 * clusters, source_ref.shape[0], base))

    there = [
        source_ref[base + coord * clusters : base + (coord + 1) * clusters, :].astype(jnp.float32)
        for coord in range(3)
    ]
    area = source_ref[base + 3 * clusters : base + 4 * clusters, :].astype(jnp.float32)
    square = there[0] * there[0] + there[1] * there[1] + there[2] * there[2]
    ones = jnp.ones_like(square)
    aug32[...] = jnp.zeros(aug32.shape, jnp.float32)
    for row, value in enumerate(there + [ones] * 3 + three_parts(square)):
        aug32[:, row, :] = value
    weight[...] = jnp.zeros(weight.shape, jnp.float32)
    weight[:clusters, :] = CP ** (-0.5) * area
    left[...] = jnp.zeros(left.shape, left.dtype)
    for cluster in range(clusters):
        left[cluster, width:rows, quarter:] = aug32[cluster].astype(jnp.bfloat16)
        for place, at in enumerate(starts):
            left[cluster, place * rhs : (place + 1) * rhs, :quarter] = source_ref[
                at + cluster * rhs : at + (cluster + 1) * rhs, :
            ]
    back[...] = jnp.zeros(back.shape, jnp.float32)
    if first:
        acc[...] = jnp.zeros(acc.shape, jnp.float32)
    else:
        acc[...] = acc_in[...]
    both_a[...] = jnp.zeros(both_a.shape, both_a.dtype)

    def decoded(place):
        code = items[step * length + place]
        return code // (2 * clusters), code % (2 * clusters)

    def formed(place, both):
        here, mate = decoded(place)
        scale = weight[pl.ds(mate, 1), :]
        mate = mate % clusters
        lhs = jnp.concatenate([ref[here] for ref in lhs_refs], axis=0)
        raw = jnp.dot(lhs, left[mate], preferred_element_type=jnp.float32)
        for start in range(0, panels, LANES):
            span = slice(start, start + LANES)
            inverse = lax.rsqrt(raw[span, quarter:])
            kernel = scale * inverse
            both[span, :quarter] = kernel.astype(jnp.bfloat16)
            weighted = (inverse * inverse) * (kernel * raw[span, :quarter])
            both[span, quarter:] = weighted.astype(jnp.bfloat16)

    def summed(place, both):
        here, mate = decoded(place)
        mate = mate % clusters
        acc[here] += lax.dot_general(
            left[mate, :rows, :],
            both[...],
            (((1,), (1,)), ((), ())),
            preferred_element_type=jnp.float32,
        )
        aug = jnp.concatenate([ref[here] for ref in aug_refs], axis=1)
        back[mate] += jnp.dot(aug, both[:, quarter:], preferred_element_type=jnp.float32)

    @pl.loop(0, items[step * length])
    def _(pair):
        turn = 2 * pair + 1
        summed(turn, both_a)
        formed(turn + 1, both_b)
        summed(turn + 1, both_b)
        formed(turn + 2, both_a)

    for coord in range(3):
        back_ref[coord] = -0.5 * back[:, coord, :] - there[coord] * back[:, 6, :]
    if last:
        for coord in range(3):
            span = slice(base + coord * clusters, base + (coord + 1) * clusters)
            pos = [ref[span, :] for ref in local_refs]
            pos = jnp.concatenate(pos, axis=1).astype(jnp.float32)
            grad_ref[coord] = acc[:, width + coord, :] - pos * acc[:, width + 3, :]
        pot_ref[...] = acc[:, :rhs, :]
        pot_out_ref[...] = acc[:, rhs:width, :].astype(jnp.bfloat16)


def run_step(step, length, items, source, targets, locals_, rhs, width, carried, last):
    lhss, augs = zip(*targets)
    clusters, _, row_count = augs[0].shape
    subs = len(targets)
    panels = subs * row_count
    quarter = source.shape[1]
    first = carried is None
    vmem = pl.BlockSpec(memory_space=pltpu.VMEM)
    smem = pl.BlockSpec(memory_space=pltpu.SMEM)
    operands = (items, source, *lhss, *augs)
    if not first:
        operands += (carried,)
    acc_shape = (clusters, width + AUG, panels)
    back_shape = jax.ShapeDtypeStruct((3, clusters, quarter), jnp.float32)
    scratch = [
        pltpu.VMEM((clusters, AUG, quarter), jnp.float32),
        pltpu.VMEM((clusters, LANES, 2 * quarter), jnp.bfloat16),
        pltpu.VMEM((clusters + 8, quarter), jnp.float32),
        pltpu.VMEM((clusters, AUG, quarter), jnp.float32),
    ]
    scratch += [pltpu.VMEM((panels, 2 * quarter), jnp.bfloat16)] * 2
    if last:
        operands += tuple(locals_)
        out_shape = (
            jax.ShapeDtypeStruct((clusters, rhs, panels), jnp.float32),
            jax.ShapeDtypeStruct((clusters, width - rhs, panels), jnp.bfloat16),
            jax.ShapeDtypeStruct((3, clusters, panels), jnp.float32),
            back_shape,
        )
        scratch = [pltpu.VMEM(acc_shape, jnp.float32)] + scratch
    else:
        out_shape = (jax.ShapeDtypeStruct(acc_shape, jnp.float32), back_shape)
    pairs = (length - 6) * panels * quarter
    return pl.pallas_call(
        functools.partial(step_kernel, step, length, rhs, subs, first, last),
        out_shape=out_shape,
        in_specs=[smem] + [vmem] * (len(operands) - 1),
        out_specs=(vmem,) * len(out_shape),
        scratch_shapes=scratch,
        compiler_params=pltpu.CompilerParams(vmem_limit_bytes=20 * 1024 * 1024),
        cost_estimate=pl.CostEstimate(
            flops=2 * pairs * (2 * width + 3 * AUG), bytes_accessed=6 * 2**20, transcendentals=pairs
        ),
        name=f"near_field_{step}",
    )(*operands)


def node_kernel(grad_ref, jitter_ref, edge_ref, main_ref):
    clusters, panels = jitter_ref.shape
    wide = panels + 2 * LANES

    def spread_of(terms, jitter):
        side = jnp.zeros((terms.shape[0], LANES), jnp.float32)
        terms = 0.25 * terms
        spread = jnp.zeros((terms.shape[0], wide), jnp.float32)
        for offset in range(-jitter_reach, jitter_reach + 1):
            masked = jnp.where(jitter == offset, terms, 0.0)
            masked = jnp.concatenate([side, masked, side], axis=1)
            spread = spread + pltpu.roll(masked, offset % wide, 1)
        spread = spread + pltpu.roll(spread, 1, 1)
        return spread + pltpu.roll(spread, 32, 1)

    jitter = jitter_ref[...]
    row_at = lax.broadcasted_iota(jnp.int32, (clusters, LANES), 0)
    edge = edge_ref[...]
    edge_at = lax.broadcasted_iota(jnp.int32, edge.shape, 0)
    edge_jitter = jnp.where(edge_at < 3, edge[6:7], edge[7:8]).astype(jnp.int32)
    edge = spread_of(edge, edge_jitter)
    for coord in range(3):
        spread = spread_of(grad_ref[coord], jitter)
        below = spread[:, :LANES]
        above = spread[:, LANES + panels :]
        inner = spread[:, LANES : LANES + panels]
        before = edge[coord : coord + 1, LANES + panels :]
        after = edge[3 + coord : 4 + coord, :LANES]
        first = jnp.where(row_at == 0, before, pltpu.roll(above, 1, 0))
        last = jnp.where(row_at == clusters - 1, after, pltpu.roll(below, clusters - 1, 0))
        inner = jnp.concatenate(
            [
                inner[:, :LANES] + first,
                inner[:, LANES : panels - LANES],
                inner[:, panels - LANES :] + last,
            ],
            axis=1,
        )
        for cluster in range(clusters):
            main_ref[coord : coord + 1, cluster * panels : (cluster + 1) * panels] = inner[
                cluster : cluster + 1
            ]


def sum_kernel(*refs):
    total = refs[0][...]
    for ref in refs[1:-1]:
        total = total + ref[...].astype(jnp.float32)
    refs[-1][...] = total.astype(jnp.bfloat16)


def on_device(positions, areas, density, cotangent, matching, connect):
    clus_count = lax.axis_size("clus")
    sub_count = lax.axis_size("sub")
    rhs_count = lax.axis_size("rhs")
    device = lax.axis_index("clus")
    sub_place = lax.axis_index("sub")
    core = lax.axis_index("rhs")
    clusters, rhs, row_count = density.shape
    panels = row_count * sub_count
    quarter = row_count // rhs_count
    width = rhs * rhs_count
    vmem = pl.BlockSpec(memory_space=pltpu.VMEM)

    nodes_total = clus_count * clusters * panels

    by_coord = jnp.transpose(positions, (1, 0, 2))
    arguments = [
        pltpu.with_memory_space_constraint(array, pltpu.HBM)
        for array in (density, by_coord, areas, connect, cotangent)
    ]
    shapes = [(clusters * (rhs + 5), quarter)] + [(clusters * rhs, quarter)] * (rhs_count - 1)
    shapes.append((clusters * (rhs + 4), row_count))
    *parts, local = pl.pallas_call(
        functools.partial(prepare_kernel, (panels, nodes_total)),
        out_shape=[jax.ShapeDtypeStruct(shape, jnp.bfloat16) for shape in shapes],
        in_specs=[pl.BlockSpec(memory_space=pltpu.HBM)] * len(arguments),
        out_specs=[vmem] * len(shapes),
        scratch_shapes=[pltpu.VMEM(array.shape, array.dtype) for array in arguments]
        + [pltpu.SemaphoreType.DMA((len(arguments),))],
        compiler_params=pltpu.CompilerParams(vmem_limit_bytes=16 * 1024 * 1024),
        name="prepare",
    )(*arguments)
    ring = ring_order(clus_count)
    at_place = [ring.index(index) for index in range(clus_count)]
    ring_place = pick(device, at_place)

    def own_parts(parts, steps):
        arrived = [round_ring(parts[0], steps)]
        for step in range(1, rhs_count):

            def goal(z, c, step=step):
                return (ring[(at_place[z] + steps) % clus_count], c + step)

            arrived.append(moved(parts[step], ("clus", "rhs"), goal))
        return arrived

    arrived = own_parts(parts, 1)

    per_round = 2 * ((clusters // 2 + clus_count - 2) // (clus_count - 1))
    cap = ROUNDS * per_round
    partners = lax.dynamic_slice_in_dim(matching, device * clusters, clusters, 1).reshape(-1)
    here = jnp.tile(jnp.arange(clusters, dtype=jnp.int32), ROUNDS)
    code = here * (2 * clusters) + partners % clusters
    behind = (ring_place - pick(partners // clusters, at_place)) % clus_count
    total_items = ROUNDS * clusters
    order = jnp.arange(total_items, dtype=jnp.int32)
    rank = jnp.sum(
        ((behind[None, :] == behind[:, None]) & (order[None, :] < order[:, None])).astype(jnp.int32),
        axis=1,
    )
    steps = jnp.arange(1, clus_count, dtype=jnp.int32)
    member = behind[None, :] == steps[:, None]
    slots = jnp.arange(cap, dtype=jnp.int32)
    chosen = member[:, None, :] & (rank[None, None, :] == slots[None, :, None])
    listed = jnp.sum(jnp.where(chosen, code[None, None, :] - clusters, 0), axis=2) + clusters
    turns = (jnp.sum(member.astype(jnp.int32), axis=1) + 2) // 2
    length = cap + 6
    items = jnp.pad(listed, ((0, 0), (2, 4)), constant_values=clusters)
    items = jnp.concatenate([turns[:, None], items[:, 1:]], axis=1).reshape(-1)

    locals_ = [local] + [shifted(local, "sub", step) for step in range(1, sub_count)]
    blocks = [
        [block] + [shifted(block, "rhs", step) for step in range(1, rhs_count)] for block in locals_
    ]

    def in_order(blocks):
        return jnp.concatenate(
            [pick((sub_place - place) % sub_count, blocks) for place in range(sub_count)], axis=-1
        )

    jitter_all = in_order([block[clusters * (rhs + 3) :] for block in locals_]).astype(jnp.int32)
    targets = [
        pl.pallas_call(
            target_kernel,
            out_shape=(
                jax.ShapeDtypeStruct((clusters, row_count, LANES), jnp.bfloat16),
                jax.ShapeDtypeStruct((clusters, AUG, row_count), jnp.bfloat16),
            ),
            in_specs=[vmem] * rhs_count,
            out_specs=(vmem, vmem),
            scratch_shapes=[pltpu.VMEM((clusters, AUG, row_count), jnp.float32)],
            compiler_params=pltpu.CompilerParams(vmem_limit_bytes=16 * 1024 * 1024),
            cost_estimate=pl.CostEstimate(flops=2**20, bytes_accessed=2**18, transcendentals=0),
            name=f"targets_{place}",
        )(*blocks[place])
        for place in range(sub_count)
    ]

    arrived, targets = lax.optimization_barrier((arrived, targets))
    source = jnp.concatenate(arrived, axis=0)
    source, parts = lax.optimization_barrier((source, parts))
    from_next = own_parts(parts, -1) if clus_count > 2 else None
    carried = None
    backs, jitter_rows = [], [None]
    for step in range(1, clus_count):
        if 1 < step < clus_count - 1:
            if step > 2:
                source, backs[step - 3] = lax.optimization_barrier((source, backs[step - 3]))
            source = round_ring(source, 1)
        elif step > 1:
            from_next, backs[-1] = lax.optimization_barrier((from_next, backs[-1]))
            source = jnp.concatenate(from_next, axis=0)
        last = step == clus_count - 1
        results = run_step(
            step - 1, length, items, source, targets, locals_, rhs, width, carried, last
        )
        if last:
            pot, pot_out, grad, back = results
        else:
            carried, back = results
        backs.append(back)
        at = clusters * (rhs + 4)
        jitter_rows.append(source[at : at + clusters])

    grad = in_order([grad[..., at * row_count : (at + 1) * row_count] for at in range(sub_count)])
    low_part = (sub_place == 0) & (core == 0)
    high_part = (sub_place == sub_count - 1) & (core == rhs_count - 1)
    uppers = [grad[:, -1, -quarter:]] + [jnp.where(high_part, back[:, -1], 0.0) for back in backs]
    lowers = [grad[:, 0, :quarter]] + [jnp.where(low_part, back[:, 0], 0.0) for back in backs]

    def step_between(index, owner):
        return (at_place[index] - at_place[owner % clus_count]) % clus_count

    def needed(parts, step, offset):
        choices = []
        for index in range(clus_count):
            goal = ring[(at_place[index] - step) % clus_count]
            choices.append(parts[step_between(index, goal + offset)])
        return pick(device, choices)

    nothing = jnp.zeros((2, quarter), jnp.float32)
    returned = jnp.zeros((3, clusters, quarter), jnp.float32)
    upper, lower = needed(uppers, 0, -1), needed(lowers, 0, 1)
    for step in range(1, clus_count):
        rows = [
            backs[step - 1].reshape(3 * clusters, quarter),
            needed(uppers, step, -1),
            needed(lowers, step, 1),
            nothing,
        ]
        home = round_ring(jnp.concatenate(rows, axis=0), -step)
        returned = returned + home[: 3 * clusters].reshape(returned.shape)
        upper = upper + home[3 * clusters : 3 * clusters + 3]
        lower = lower + home[3 * clusters + 3 : 3 * clusters + 6]

    half = pot
    for step in range(1, rhs_count):
        arrived = shifted(pot_out[:, (step - 1) * rhs : step * rhs], "rhs", -step)
        half = half + arrived.astype(jnp.float32)

    half, grad = lax.optimization_barrier((half, grad))
    found = [half[..., :row_count]]
    for step in range(1, sub_count):
        sent = half[..., step * row_count : (step + 1) * row_count].astype(jnp.bfloat16)
        found.append(shifted(sent, "sub", -step))

    quarter_at = sub_place * rhs_count + core
    grad = grad + jnp.concatenate(
        [jnp.where(quarter_at == at, returned, 0.0) for at in range(sub_count * rhs_count)], axis=-1
    )
    share = clusters // sub_count

    blank = jnp.zeros((3, panels - quarter), jnp.float32)
    before = jnp.concatenate([blank, upper], axis=1)
    after = jnp.concatenate([lower, blank], axis=1)
    jitter_float = jitter_all.astype(jnp.float32)
    jitter_before = jnp.concatenate(
        [blank[:1], needed(jitter_rows, 0, -1)[clusters - 1 :].astype(jnp.float32)], axis=1
    )
    jitter_after = jnp.concatenate(
        [needed(jitter_rows, 0, 1)[:1].astype(jnp.float32), blank[:1]], axis=1
    )

    def edge_rows(at):
        first, end = at * share, (at + 1) * share
        inside = at < sub_count - 1
        return jnp.concatenate(
            [
                grad[:, first - 1] if at > 0 else before,
                grad[:, end] if inside else after,
                jnp.where(high_part, jitter_float[first - 1 : first] if at > 0 else jitter_before, 0.0),
                jnp.where(low_part, jitter_float[end : end + 1] if inside else jitter_after, 0.0),
            ],
            axis=0,
        ).reshape(-1, share, panels)

    def packed(place):
        return pick(
            place % sub_count,
            [
                jnp.concatenate([grad[:, at * share : (at + 1) * share], edge_rows(at)], axis=0)
                for at in range(sub_count)
            ],
        )

    summed = packed(sub_place)
    for step in range(1, sub_count):
        summed = summed + shifted(packed(sub_place + step), "sub", step)
    gathered = summed
    for step in range(1, rhs_count):
        gathered = gathered + shifted(summed, "rhs", step)
    own_jitter = pick(
        sub_place, [jitter_all[at * share : (at + 1) * share] for at in range(sub_count)]
    )
    node_grad = pl.pallas_call(
        node_kernel,
        out_shape=jax.ShapeDtypeStruct((3, share * panels), jnp.float32),
        in_specs=[vmem] * 3,
        out_specs=vmem,
        compiler_params=pltpu.CompilerParams(vmem_limit_bytes=16 * 1024 * 1024),
        cost_estimate=pl.CostEstimate(flops=2**20, bytes_accessed=2**18, transcendentals=0),
        name="node_terms",
    )(gathered[:3], own_jitter, gathered[3:].reshape(8, panels))
    potential = pl.pallas_call(
        sum_kernel,
        out_shape=jax.ShapeDtypeStruct((clusters, rhs, row_count), jnp.bfloat16),
        in_specs=[vmem] * sub_count,
        out_specs=vmem,
        compiler_params=pltpu.CompilerParams(vmem_limit_bytes=16 * 1024 * 1024),
        cost_estimate=pl.CostEstimate(flops=2**20, bytes_accessed=2**18, transcendentals=0),
        name="potential_sum",
    )(*found)
    return (potential, node_grad)


def solution(mesh):
    placed = (
        P(("groups", "clus"), None, "sub"),
        P(("groups", "clus"), "sub"),
        P(("groups", "clus"), "rhs", "sub"),
        P(("groups", "clus"), "rhs", "sub"),
        P(None, "groups"),
        P(("groups", "clus"), None, "sub"),
    )
    return jax.shard_map(
        on_device,
        mesh=mesh,
        in_specs=placed,
        out_specs=(P(("groups", "clus"), "rhs", "sub"), P(None, ("groups", "clus", "sub"))),
        check_vma=False,
    )
```

```python
import functools

import jax
import jax.numpy as jnp
from jax import lax
from jax.experimental import pallas as pl
from jax.experimental.pallas import tpu as pltpu
from jax.sharding import PartitionSpec as P

CP = 512
ROUNDS = 5

core_radius = 0.25
jitter_reach = 8
LANES = 128
AUG = 16
HALF_ROOT = -0.7213475204444817


def shifted(value, axis, steps):
    count = lax.axis_size(axis)
    pairs = [(source, (source + steps) % count) for source in range(count)]
    return lax.ppermute(value, axis, pairs)


def ring_order(count):
    return [*range(0, count, 2), *reversed(range(1, count, 2))]


def round_ring(value, steps):
    order = ring_order(lax.axis_size("clus"))
    pairs = [(source, order[(at + steps) % len(order)]) for at, source in enumerate(order)]
    return lax.ppermute(value, "clus", pairs)


def moved(value, axes, target):
    counts = [lax.axis_size(axis) for axis in axes]
    pairs = []
    for major in range(counts[0]):
        for minor in range(counts[1]):
            goal = target(major, minor)
            if goal is not None:
                to_major, to_minor = goal[0] % counts[0], goal[1] % counts[1]
                pairs.append((major * counts[1] + minor, to_major * counts[1] + to_minor))
    return lax.ppermute(value, axes, pairs)


def three_parts(value):
    parts = []
    for _ in range(3):
        part = value.astype(jnp.bfloat16).astype(jnp.float32)
        parts.append(part)
        value = value - part
    return parts


def pick(index, choices):
    out = choices[0]
    for place in range(1, len(choices)):
        out = jnp.where(index == place, choices[place], out)
    return out


def fetched(arguments, places, sems):
    copies = []
    for at, (argument, place) in enumerate(zip(arguments, places)):
        copies.append(pltpu.make_async_copy(argument, place, sems.at[at]))
        copies[-1].start()
    for copy in copies:
        copy.wait()


def jitter_of(connect_ref, sizes):
    clusters, _, row_count = connect_ref.shape
    panels, nodes_total = sizes
    first_id = clusters * panels * lax.axis_index("clus") + row_count * lax.axis_index("sub")
    ids = lax.broadcasted_iota(jnp.int32, (clusters, row_count), 0) * panels
    ids = ids + lax.broadcasted_iota(jnp.int32, (clusters, row_count), 1) + first_id
    jitter = connect_ref[:, 0, :] - ids
    jitter = jnp.where(jitter > jitter_reach, jitter - nodes_total, jitter)
    jitter = jnp.where(jitter < -jitter_reach, jitter + nodes_total, jitter)
    return jitter.astype(jnp.float32).astype(jnp.bfloat16)


def prepare_kernel(sizes, *refs):
    arguments, part_refs, local_ref, scratch = refs[:5], refs[5:-7], refs[-7], refs[-6:]
    fetched(arguments, scratch[:5], scratch[5])
    density_ref, by_coord_ref, areas_ref, connect_ref, cot_ref = scratch[:5]
    clusters, rhs, _ = density_ref.shape
    quarter = part_refs[0].shape[1]
    count = len(part_refs)
    core = lax.axis_index("rhs")

    def part_of(array, place):
        return pick(place, [array[:, at * quarter : (at + 1) * quarter] for at in range(count)])

    pos = [by_coord_ref[coord] for coord in range(3)]
    jitter = jitter_of(connect_ref, sizes)
    base = clusters * rhs
    for cluster in range(clusters):
        dens = density_ref[cluster]
        span = slice(cluster * rhs, (cluster + 1) * rhs)
        local_ref[span, :] = cot_ref[cluster]
        for step, part_ref in enumerate(part_refs):
            part_ref[span, :] = part_of(dens, (core + step) % count)
    for at, value in enumerate([*pos, areas_ref[...], jitter]):
        part_refs[0][base + at * clusters : base + (at + 1) * clusters, :] = part_of(value, core)
    for at, value in enumerate([*pos, jitter]):
        local_ref[base + at * clusters : base + (at + 1) * clusters, :] = value


def target_kernel(*refs):
    local_refs, (lhs_ref, aug_ref, aug32) = refs[:-3], refs[-3:]
    clusters, _, row_count = aug_ref.shape
    rhs = local_refs[0].shape[0] // clusters - 4
    base = clusters * rhs
    pos = [
        local_refs[0][base + coord * clusters : base + (coord + 1) * clusters, :].astype(jnp.float32)
        for coord in range(3)
    ]
    square = pos[0] * pos[0] + pos[1] * pos[1] + pos[2] * pos[2] + core_radius * core_radius
    ones = jnp.ones_like(square)
    aug32[...] = jnp.zeros(aug32.shape, jnp.float32)
    for row, value in enumerate([-2.0 * value for value in pos] + three_parts(square) + [ones] * 3):
        aug32[:, row, :] = value
    blank = jnp.zeros((LANES - AUG - rhs * len(local_refs), row_count), jnp.bfloat16)
    for cluster in range(clusters):
        aug = aug32[cluster].astype(jnp.bfloat16)
        aug_ref[cluster] = aug
        rows = [ref[cluster * rhs : (cluster + 1) * rhs, :] for ref in local_refs]
        lhs_ref[cluster] = jnp.concatenate([*rows, aug, blank], axis=0).T


def step_kernel(step, length, rhs, subs, first, last, *refs):
    items, source_ref, refs = refs[0], refs[1], refs[2:]
    lhs_refs, aug_refs, refs = refs[:subs], refs[subs : 2 * subs], refs[2 * subs :]
    if not first:
        acc_in, refs = refs[0], refs[1:]
    if last:
        local_refs, refs = refs[:subs], refs[subs:]
        pot_ref, pot_out_ref, grad_ref, back_ref, acc = refs[:5]
        refs = refs[5:]
    else:
        acc, back_ref = refs[:2]
        refs = refs[2:]
    aug32, left, weight, back, raw_a, raw_b, both_a, both_b = refs
    clusters, rows, panels = acc.shape
    width = rows - AUG
    row_count = panels // subs
    quarter = source_ref.shape[1]
    base = clusters * rhs

    starts = [0] + list(range(base + 5 * clusters, source_ref.shape[0], base))

    there = [
        source_ref[base + coord * clusters : base + (coord + 1) * clusters, :].astype(jnp.float32)
        for coord in range(3)
    ]
    area = source_ref[base + 3 * clusters : base + 4 * clusters, :].astype(jnp.float32)
    square = there[0] * there[0] + there[1] * there[1] + there[2] * there[2]
    ones = jnp.ones_like(square)
    aug32[...] = jnp.zeros(aug32.shape, jnp.float32)
    for row, value in enumerate(there + [ones] * 3 + three_parts(square)):
        aug32[:, row, :] = value
    weight[...] = jnp.zeros(weight.shape, jnp.float32)
    weight[:clusters, :] = CP ** (-0.5) * area
    left[...] = jnp.zeros(left.shape, left.dtype)
    for cluster in range(clusters):
        left[cluster, width:rows, quarter:] = aug32[cluster].astype(jnp.bfloat16)
        for place, at in enumerate(starts):
            left[cluster, place * rhs : (place + 1) * rhs, :quarter] = source_ref[
                at + cluster * rhs : at + (cluster + 1) * rhs, :
            ]
    back[...] = jnp.zeros(back.shape, jnp.float32)
    if first:
        acc[...] = jnp.zeros(acc.shape, jnp.float32)
    else:
        acc[...] = acc_in[...]
    raw_b[...] = jnp.ones(raw_b.shape, jnp.float32)
    both_a[...] = jnp.zeros(both_a.shape, both_a.dtype)

    def decoded(place):
        code = items[step * length + place]
        return code // (2 * clusters), code % (2 * clusters)

    def products(place, raw):
        here, mate = decoded(place)
        mate = mate % clusters
        lhs = jnp.concatenate([ref[here] for ref in lhs_refs], axis=0)
        raw[...] = jnp.dot(lhs, left[mate], preferred_element_type=jnp.float32)

    def pointwise(place, raw, both):
        _, mate = decoded(place)
        scale = weight[pl.ds(mate, 1), :]
        for start in range(0, panels, LANES):
            span = slice(start, start + LANES)
            inverse = lax.exp2(HALF_ROOT * lax.log(raw[span, quarter:]))
            kernel = scale * inverse
            both[span, :quarter] = kernel.astype(jnp.bfloat16)
            weighted = (inverse * inverse) * (kernel * raw[span, :quarter])
            both[span, quarter:] = weighted.astype(jnp.bfloat16)

    def summed(place, both):
        here, mate = decoded(place)
        mate = mate % clusters
        acc[here] += lax.dot_general(
            left[mate, :rows, :],
            both[...],
            (((1,), (1,)), ((), ())),
            preferred_element_type=jnp.float32,
        )
        aug = jnp.concatenate([ref[here] for ref in aug_refs], axis=1)
        back[mate] += jnp.dot(aug, both[:, quarter:], preferred_element_type=jnp.float32)

    @pl.loop(0, items[step * length])
    def _(pair):
        turn = 2 * pair + 1
        summed(turn, both_a)
        pointwise(turn + 1, raw_b, both_b)
        products(turn + 2, raw_a)
        summed(turn + 1, both_b)
        pointwise(turn + 2, raw_a, both_a)
        products(turn + 3, raw_b)

    for coord in range(3):
        back_ref[coord] = -0.5 * back[:, coord, :] - there[coord] * back[:, 6, :]
    if last:
        for coord in range(3):
            span = slice(base + coord * clusters, base + (coord + 1) * clusters)
            pos = [ref[span, :] for ref in local_refs]
            pos = jnp.concatenate(pos, axis=1).astype(jnp.float32)
            grad_ref[coord] = acc[:, width + coord, :] - pos * acc[:, width + 3, :]
        pot_ref[...] = acc[:, :rhs, :]
        pot_out_ref[...] = acc[:, rhs:width, :].astype(jnp.bfloat16)


def run_step(step, length, items, source, targets, locals_, rhs, width, carried, last):
    lhss, augs = zip(*targets)
    clusters, _, row_count = augs[0].shape
    subs = len(targets)
    panels = subs * row_count
    quarter = source.shape[1]
    first = carried is None
    vmem = pl.BlockSpec(memory_space=pltpu.VMEM)
    smem = pl.BlockSpec(memory_space=pltpu.SMEM)
    operands = (items, source, *lhss, *augs)
    if not first:
        operands += (carried,)
    acc_shape = (clusters, width + AUG, panels)
    back_shape = jax.ShapeDtypeStruct((3, clusters, quarter), jnp.float32)
    scratch = [
        pltpu.VMEM((clusters, AUG, quarter), jnp.float32),
        pltpu.VMEM((clusters, LANES, 2 * quarter), jnp.bfloat16),
        pltpu.VMEM((clusters + 8, quarter), jnp.float32),
        pltpu.VMEM((clusters, AUG, quarter), jnp.float32),
    ]
    scratch += [pltpu.VMEM((panels, 2 * quarter), jnp.float32)] * 2
    scratch += [pltpu.VMEM((panels, 2 * quarter), jnp.bfloat16)] * 2
    if last:
        operands += tuple(locals_)
        out_shape = (
            jax.ShapeDtypeStruct((clusters, rhs, panels), jnp.float32),
            jax.ShapeDtypeStruct((clusters, width - rhs, panels), jnp.bfloat16),
            jax.ShapeDtypeStruct((3, clusters, panels), jnp.float32),
            back_shape,
        )
        scratch = [pltpu.VMEM(acc_shape, jnp.float32)] + scratch
    else:
        out_shape = (jax.ShapeDtypeStruct(acc_shape, jnp.float32), back_shape)
    pairs = (length - 6) * panels * quarter
    return pl.pallas_call(
        functools.partial(step_kernel, step, length, rhs, subs, first, last),
        out_shape=out_shape,
        in_specs=[smem] + [vmem] * (len(operands) - 1),
        out_specs=(vmem,) * len(out_shape),
        scratch_shapes=scratch,
        compiler_params=pltpu.CompilerParams(vmem_limit_bytes=20 * 1024 * 1024),
        cost_estimate=pl.CostEstimate(
            flops=2 * pairs * (2 * width + 3 * AUG), bytes_accessed=6 * 2**20, transcendentals=pairs
        ),
        name=f"near_field_{step}",
    )(*operands)


def node_kernel(grad_ref, jitter_ref, edge_ref, main_ref):
    clusters, panels = jitter_ref.shape
    wide = panels + 2 * LANES

    def spread_of(terms, jitter):
        side = jnp.zeros((terms.shape[0], LANES), jnp.float32)
        terms = 0.25 * terms
        spread = jnp.zeros((terms.shape[0], wide), jnp.float32)
        for offset in range(-jitter_reach, jitter_reach + 1):
            masked = jnp.where(jitter == offset, terms, 0.0)
            masked = jnp.concatenate([side, masked, side], axis=1)
            spread = spread + pltpu.roll(masked, offset % wide, 1)
        spread = spread + pltpu.roll(spread, 1, 1)
        return spread + pltpu.roll(spread, 32, 1)

    jitter = jitter_ref[...]
    row_at = lax.broadcasted_iota(jnp.int32, (clusters, LANES), 0)
    edge = edge_ref[...]
    edge_at = lax.broadcasted_iota(jnp.int32, edge.shape, 0)
    edge_jitter = jnp.where(edge_at < 3, edge[6:7], edge[7:8]).astype(jnp.int32)
    edge = spread_of(edge, edge_jitter)
    for coord in range(3):
        spread = spread_of(grad_ref[coord], jitter)
        below = spread[:, :LANES]
        above = spread[:, LANES + panels :]
        inner = spread[:, LANES : LANES + panels]
        before = edge[coord : coord + 1, LANES + panels :]
        after = edge[3 + coord : 4 + coord, :LANES]
        first = jnp.where(row_at == 0, before, pltpu.roll(above, 1, 0))
        last = jnp.where(row_at == clusters - 1, after, pltpu.roll(below, clusters - 1, 0))
        inner = jnp.concatenate(
            [
                inner[:, :LANES] + first,
                inner[:, LANES : panels - LANES],
                inner[:, panels - LANES :] + last,
            ],
            axis=1,
        )
        for cluster in range(clusters):
            main_ref[coord : coord + 1, cluster * panels : (cluster + 1) * panels] = inner[
                cluster : cluster + 1
            ]


def sum_kernel(*refs):
    total = refs[0][...]
    for ref in refs[1:-1]:
        total = total + ref[...].astype(jnp.float32)
    refs[-1][...] = total.astype(jnp.bfloat16)


def on_device(positions, areas, density, cotangent, matching, connect):
    clus_count = lax.axis_size("clus")
    sub_count = lax.axis_size("sub")
    rhs_count = lax.axis_size("rhs")
    device = lax.axis_index("clus")
    sub_place = lax.axis_index("sub")
    core = lax.axis_index("rhs")
    clusters, rhs, row_count = density.shape
    panels = row_count * sub_count
    quarter = row_count // rhs_count
    width = rhs * rhs_count
    vmem = pl.BlockSpec(memory_space=pltpu.VMEM)

    nodes_total = clus_count * clusters * panels

    by_coord = jnp.transpose(positions, (1, 0, 2))
    arguments = [
        pltpu.with_memory_space_constraint(array, pltpu.HBM)
        for array in (density, by_coord, areas, connect, cotangent)
    ]
    shapes = [(clusters * (rhs + 5), quarter)] + [(clusters * rhs, quarter)] * (rhs_count - 1)
    shapes.append((clusters * (rhs + 4), row_count))
    *parts, local = pl.pallas_call(
        functools.partial(prepare_kernel, (panels, nodes_total)),
        out_shape=[jax.ShapeDtypeStruct(shape, jnp.bfloat16) for shape in shapes],
        in_specs=[pl.BlockSpec(memory_space=pltpu.HBM)] * len(arguments),
        out_specs=[vmem] * len(shapes),
        scratch_shapes=[pltpu.VMEM(array.shape, array.dtype) for array in arguments]
        + [pltpu.SemaphoreType.DMA((len(arguments),))],
        compiler_params=pltpu.CompilerParams(vmem_limit_bytes=16 * 1024 * 1024),
        name="prepare",
    )(*arguments)
    ring = ring_order(clus_count)
    at_place = [ring.index(index) for index in range(clus_count)]
    ring_place = pick(device, at_place)

    def own_parts(parts, steps):
        arrived = [round_ring(parts[0], steps)]
        for step in range(1, rhs_count):

            def goal(z, c, step=step):
                return (ring[(at_place[z] + steps) % clus_count], c + step)

            arrived.append(moved(parts[step], ("clus", "rhs"), goal))
        return arrived

    arrived = own_parts(parts, 1)

    per_round = 2 * ((clusters // 2 + clus_count - 2) // (clus_count - 1))
    cap = ROUNDS * per_round
    partners = lax.dynamic_slice_in_dim(matching, device * clusters, clusters, 1).reshape(-1)
    here = jnp.tile(jnp.arange(clusters, dtype=jnp.int32), ROUNDS)
    code = here * (2 * clusters) + partners % clusters
    behind = (ring_place - pick(partners // clusters, at_place)) % clus_count
    total_items = ROUNDS * clusters
    order = jnp.arange(total_items, dtype=jnp.int32)
    rank = jnp.sum(
        ((behind[None, :] == behind[:, None]) & (order[None, :] < order[:, None])).astype(jnp.int32),
        axis=1,
    )
    steps = jnp.arange(1, clus_count, dtype=jnp.int32)
    member = behind[None, :] == steps[:, None]
    slots = jnp.arange(cap, dtype=jnp.int32)
    chosen = member[:, None, :] & (rank[None, None, :] == slots[None, :, None])
    listed = jnp.sum(jnp.where(chosen, code[None, None, :] - clusters, 0), axis=2) + clusters
    turns = (jnp.sum(member.astype(jnp.int32), axis=1) + 3) // 2
    length = cap + 6
    items = jnp.pad(listed, ((0, 0), (3, 3)), constant_values=clusters)
    items = jnp.concatenate([turns[:, None], items[:, 1:]], axis=1).reshape(-1)

    locals_ = [local] + [shifted(local, "sub", step) for step in range(1, sub_count)]
    blocks = [
        [block] + [shifted(block, "rhs", step) for step in range(1, rhs_count)] for block in locals_
    ]

    def in_order(blocks):
        return jnp.concatenate(
            [pick((sub_place - place) % sub_count, blocks) for place in range(sub_count)], axis=-1
        )

    jitter_all = in_order([block[clusters * (rhs + 3) :] for block in locals_]).astype(jnp.int32)
    targets = [
        pl.pallas_call(
            target_kernel,
            out_shape=(
                jax.ShapeDtypeStruct((clusters, row_count, LANES), jnp.bfloat16),
                jax.ShapeDtypeStruct((clusters, AUG, row_count), jnp.bfloat16),
            ),
            in_specs=[vmem] * rhs_count,
            out_specs=(vmem, vmem),
            scratch_shapes=[pltpu.VMEM((clusters, AUG, row_count), jnp.float32)],
            compiler_params=pltpu.CompilerParams(vmem_limit_bytes=16 * 1024 * 1024),
            cost_estimate=pl.CostEstimate(flops=2**20, bytes_accessed=2**18, transcendentals=0),
            name=f"targets_{place}",
        )(*blocks[place])
        for place in range(sub_count)
    ]

    arrived, targets = lax.optimization_barrier((arrived, targets))
    source = jnp.concatenate(arrived, axis=0)
    source, parts = lax.optimization_barrier((source, parts))
    from_next = own_parts(parts, -1) if clus_count > 2 else None
    carried = None
    backs, jitter_rows = [], [None]
    for step in range(1, clus_count):
        if 1 < step < clus_count - 1:
            if step > 2:
                source, backs[step - 3] = lax.optimization_barrier((source, backs[step - 3]))
            source = round_ring(source, 1)
        elif step > 1:
            from_next, backs[-1] = lax.optimization_barrier((from_next, backs[-1]))
            source = jnp.concatenate(from_next, axis=0)
        last = step == clus_count - 1
        results = run_step(
            step - 1, length, items, source, targets, locals_, rhs, width, carried, last
        )
        if last:
            pot, pot_out, grad, back = results
        else:
            carried, back = results
        backs.append(back)
        at = clusters * (rhs + 4)
        jitter_rows.append(source[at : at + clusters])

    grad = in_order([grad[..., at * row_count : (at + 1) * row_count] for at in range(sub_count)])
    low_part = (sub_place == 0) & (core == 0)
    high_part = (sub_place == sub_count - 1) & (core == rhs_count - 1)
    uppers = [grad[:, -1, -quarter:]] + [jnp.where(high_part, back[:, -1], 0.0) for back in backs]
    lowers = [grad[:, 0, :quarter]] + [jnp.where(low_part, back[:, 0], 0.0) for back in backs]

    def step_between(index, owner):
        return (at_place[index] - at_place[owner % clus_count]) % clus_count

    def needed(parts, step, offset):
        choices = []
        for index in range(clus_count):
            goal = ring[(at_place[index] - step) % clus_count]
            choices.append(parts[step_between(index, goal + offset)])
        return pick(device, choices)

    nothing = jnp.zeros((2, quarter), jnp.float32)
    returned = jnp.zeros((3, clusters, quarter), jnp.float32)
    upper, lower = needed(uppers, 0, -1), needed(lowers, 0, 1)
    for step in range(1, clus_count):
        rows = [
            backs[step - 1].reshape(3 * clusters, quarter),
            needed(uppers, step, -1),
            needed(lowers, step, 1),
            nothing,
        ]
        home = round_ring(jnp.concatenate(rows, axis=0), -step)
        returned = returned + home[: 3 * clusters].reshape(returned.shape)
        upper = upper + home[3 * clusters : 3 * clusters + 3]
        lower = lower + home[3 * clusters + 3 : 3 * clusters + 6]

    half = pot
    for step in range(1, rhs_count):
        arrived = shifted(pot_out[:, (step - 1) * rhs : step * rhs], "rhs", -step)
        half = half + arrived.astype(jnp.float32)

    half, grad = lax.optimization_barrier((half, grad))
    found = [half[..., :row_count]]
    for step in range(1, sub_count):
        sent = half[..., step * row_count : (step + 1) * row_count].astype(jnp.bfloat16)
        found.append(shifted(sent, "sub", -step))

    quarter_at = sub_place * rhs_count + core
    grad = grad + jnp.concatenate(
        [jnp.where(quarter_at == at, returned, 0.0) for at in range(sub_count * rhs_count)], axis=-1
    )
    share = clusters // sub_count

    blank = jnp.zeros((3, panels - quarter), jnp.float32)
    before = jnp.concatenate([blank, upper], axis=1)
    after = jnp.concatenate([lower, blank], axis=1)
    jitter_float = jitter_all.astype(jnp.float32)
    jitter_before = jnp.concatenate(
        [blank[:1], needed(jitter_rows, 0, -1)[clusters - 1 :].astype(jnp.float32)], axis=1
    )
    jitter_after = jnp.concatenate(
        [needed(jitter_rows, 0, 1)[:1].astype(jnp.float32), blank[:1]], axis=1
    )

    def edge_rows(at):
        first, end = at * share, (at + 1) * share
        inside = at < sub_count - 1
        return jnp.concatenate(
            [
                grad[:, first - 1] if at > 0 else before,
                grad[:, end] if inside else after,
                jnp.where(high_part, jitter_float[first - 1 : first] if at > 0 else jitter_before, 0.0),
                jnp.where(low_part, jitter_float[end : end + 1] if inside else jitter_after, 0.0),
            ],
            axis=0,
        ).reshape(-1, share, panels)

    def packed(place):
        return pick(
            place % sub_count,
            [
                jnp.concatenate([grad[:, at * share : (at + 1) * share], edge_rows(at)], axis=0)
                for at in range(sub_count)
            ],
        )

    summed = packed(sub_place)
    for step in range(1, sub_count):
        summed = summed + shifted(packed(sub_place + step), "sub", step)
    gathered = summed
    for step in range(1, rhs_count):
        gathered = gathered + shifted(summed, "rhs", step)
    own_jitter = pick(
        sub_place, [jitter_all[at * share : (at + 1) * share] for at in range(sub_count)]
    )
    node_grad = pl.pallas_call(
        node_kernel,
        out_shape=jax.ShapeDtypeStruct((3, share * panels), jnp.float32),
        in_specs=[vmem] * 3,
        out_specs=vmem,
        compiler_params=pltpu.CompilerParams(vmem_limit_bytes=16 * 1024 * 1024),
        cost_estimate=pl.CostEstimate(flops=2**20, bytes_accessed=2**18, transcendentals=0),
        name="node_terms",
    )(gathered[:3], own_jitter, gathered[3:].reshape(8, panels))
    potential = pl.pallas_call(
        sum_kernel,
        out_shape=jax.ShapeDtypeStruct((clusters, rhs, row_count), jnp.bfloat16),
        in_specs=[vmem] * sub_count,
        out_specs=vmem,
        compiler_params=pltpu.CompilerParams(vmem_limit_bytes=16 * 1024 * 1024),
        cost_estimate=pl.CostEstimate(flops=2**20, bytes_accessed=2**18, transcendentals=0),
        name="potential_sum",
    )(*found)
    return (potential, node_grad)


def solution(mesh):
    placed = (
        P(("groups", "clus"), None, "sub"),
        P(("groups", "clus"), "sub"),
        P(("groups", "clus"), "rhs", "sub"),
        P(("groups", "clus"), "rhs", "sub"),
        P(None, "groups"),
        P(("groups", "clus"), None, "sub"),
    )
    return jax.shard_map(
        on_device,
        mesh=mesh,
        in_specs=placed,
        out_specs=(P(("groups", "clus"), "rhs", "sub"), P(None, ("groups", "clus", "sub"))),
        check_vma=False,
    )
```

```python
import functools

import jax
import jax.numpy as jnp
from jax import lax
from jax.experimental import pallas as pl
from jax.experimental.pallas import tpu as pltpu
from jax.sharding import PartitionSpec as P

CP = 512
ROUNDS = 5

core_radius = 0.25
jitter_reach = 8
LANES = 128
AUG = 16


def shifted(value, axis, steps):
    count = lax.axis_size(axis)
    pairs = [(source, (source + steps) % count) for source in range(count)]
    return lax.ppermute(value, axis, pairs)


def ring_order(count):
    return [*range(0, count, 2), *reversed(range(1, count, 2))]


def round_ring(value, steps):
    order = ring_order(lax.axis_size("clus"))
    pairs = [(source, order[(at + steps) % len(order)]) for at, source in enumerate(order)]
    return lax.ppermute(value, "clus", pairs)


def moved(value, axes, target):
    counts = [lax.axis_size(axis) for axis in axes]
    pairs = []
    for major in range(counts[0]):
        for minor in range(counts[1]):
            goal = target(major, minor)
            if goal is not None:
                to_major, to_minor = goal[0] % counts[0], goal[1] % counts[1]
                pairs.append((major * counts[1] + minor, to_major * counts[1] + to_minor))
    return lax.ppermute(value, axes, pairs)


def three_parts(value):
    parts = []
    for _ in range(3):
        part = value.astype(jnp.bfloat16).astype(jnp.float32)
        parts.append(part)
        value = value - part
    return parts


def pick(index, choices):
    out = choices[0]
    for place in range(1, len(choices)):
        out = jnp.where(index == place, choices[place], out)
    return out


def fetched(arguments, places, sems):
    copies = []
    for at, (argument, place) in enumerate(zip(arguments, places)):
        copies.append(pltpu.make_async_copy(argument, place, sems.at[at]))
        copies[-1].start()
    for copy in copies:
        copy.wait()


def jitter_of(connect_ref, sizes):
    clusters, _, row_count = connect_ref.shape
    panels, nodes_total = sizes
    first_id = clusters * panels * lax.axis_index("clus") + row_count * lax.axis_index("sub")
    ids = lax.broadcasted_iota(jnp.int32, (clusters, row_count), 0) * panels
    ids = ids + lax.broadcasted_iota(jnp.int32, (clusters, row_count), 1) + first_id
    jitter = connect_ref[:, 0, :] - ids
    jitter = jnp.where(jitter > jitter_reach, jitter - nodes_total, jitter)
    jitter = jnp.where(jitter < -jitter_reach, jitter + nodes_total, jitter)
    return jitter.astype(jnp.float32).astype(jnp.bfloat16)


def prepare_kernel(sizes, *refs):
    arguments, part_refs, local_ref, scratch = refs[:5], refs[5:-7], refs[-7], refs[-6:]
    fetched(arguments, scratch[:5], scratch[5])
    density_ref, by_coord_ref, areas_ref, connect_ref, cot_ref = scratch[:5]
    clusters, rhs, _ = density_ref.shape
    quarter = part_refs[0].shape[1]
    count = len(part_refs)
    core = lax.axis_index("rhs")

    def part_of(array, place):
        return pick(place, [array[:, at * quarter : (at + 1) * quarter] for at in range(count)])

    pos = [by_coord_ref[coord] for coord in range(3)]
    jitter = jitter_of(connect_ref, sizes)
    base = clusters * rhs
    for cluster in range(clusters):
        dens = density_ref[cluster]
        span = slice(cluster * rhs, (cluster + 1) * rhs)
        local_ref[span, :] = cot_ref[cluster]
        for step, part_ref in enumerate(part_refs):
            part_ref[span, :] = part_of(dens, (core + step) % count)
    for at, value in enumerate([*pos, areas_ref[...], jitter]):
        part_refs[0][base + at * clusters : base + (at + 1) * clusters, :] = part_of(value, core)
    for at, value in enumerate([*pos, jitter]):
        local_ref[base + at * clusters : base + (at + 1) * clusters, :] = value


def target_kernel(*refs):
    local_refs, (lhs_ref, aug_ref, aug32) = refs[:-3], refs[-3:]
    clusters, _, row_count = aug_ref.shape
    rhs = local_refs[0].shape[0] // clusters - 4
    base = clusters * rhs
    pos = [
        local_refs[0][base + coord * clusters : base + (coord + 1) * clusters, :].astype(jnp.float32)
        for coord in range(3)
    ]
    square = pos[0] * pos[0] + pos[1] * pos[1] + pos[2] * pos[2] + core_radius * core_radius
    ones = jnp.ones_like(square)
    aug32[...] = jnp.zeros(aug32.shape, jnp.float32)
    for row, value in enumerate([-2.0 * value for value in pos] + three_parts(square) + [ones] * 3):
        aug32[:, row, :] = value
    blank = jnp.zeros((LANES - AUG - rhs * len(local_refs), row_count), jnp.bfloat16)
    for cluster in range(clusters):
        aug = aug32[cluster].astype(jnp.bfloat16)
        aug_ref[cluster] = aug
        rows = [ref[cluster * rhs : (cluster + 1) * rhs, :] for ref in local_refs]
        lhs_ref[cluster] = jnp.concatenate([*rows, aug, blank], axis=0).T


def step_kernel(step, length, rhs, subs, first, last, *refs):
    items, source_ref, refs = refs[0], refs[1], refs[2:]
    lhs_refs, aug_refs, refs = refs[:subs], refs[subs : 2 * subs], refs[2 * subs :]
    if not first:
        acc_in, refs = refs[0], refs[1:]
    if last:
        local_refs, refs = refs[:subs], refs[subs:]
        pot_ref, pot_out_ref, grad_ref, back_ref, acc = refs[:5]
        refs = refs[5:]
    else:
        acc, back_ref = refs[:2]
        refs = refs[2:]
    aug32, left_a, left_b, weight, back, raw_a, raw_b, both = refs
    clusters, rows, panels = acc.shape
    width = rows - AUG
    row_count = panels // subs
    quarter = source_ref.shape[1]
    base = clusters * rhs

    starts = [0] + list(range(base + 5 * clusters, source_ref.shape[0], base))

    there = [
        source_ref[base + coord * clusters : base + (coord + 1) * clusters, :].astype(jnp.float32)
        for coord in range(3)
    ]
    area = source_ref[base + 3 * clusters : base + 4 * clusters, :].astype(jnp.float32)
    square = there[0] * there[0] + there[1] * there[1] + there[2] * there[2]
    ones = jnp.ones_like(square)
    aug32[...] = jnp.zeros(aug32.shape, jnp.float32)
    for row, value in enumerate(there + [ones] * 3 + three_parts(square)):
        aug32[:, row, :] = value
    weight[...] = jnp.zeros(weight.shape, jnp.float32)
    weight[:clusters, :] = CP ** (-0.5) * area
    left_a[...] = jnp.zeros(left_a.shape, left_a.dtype)
    left_b[...] = jnp.zeros(left_b.shape, left_b.dtype)
    for cluster in range(clusters):
        distance_rows = aug32[cluster].astype(jnp.bfloat16)
        left_a[cluster, width:rows, quarter:] = distance_rows
        left_b[cluster, width:rows, :quarter] = distance_rows
        for place, at in enumerate(starts):
            span = slice(place * rhs, (place + 1) * rhs)
            dens = source_ref[at + cluster * rhs : at + (cluster + 1) * rhs, :]
            left_a[cluster, span, :quarter] = dens
            left_b[cluster, span, quarter:] = dens
    back[...] = jnp.zeros(back.shape, jnp.float32)
    if first:
        acc[...] = jnp.zeros(acc.shape, jnp.float32)
    else:
        acc[...] = acc_in[...]
    raw_b[...] = jnp.ones(raw_b.shape, jnp.float32)
    both[:, : 2 * quarter] = jnp.zeros((panels, 2 * quarter), both.dtype)

    halves = [slice(at * quarter, (at + 1) * quarter) for at in range(4)]

    def decoded(place):
        code = items[step * length + place]
        return code // (2 * clusters), code % (2 * clusters)

    def products(place, left, raw):
        here, mate = decoded(place)
        lhs = jnp.concatenate([ref[here] for ref in lhs_refs], axis=0)
        raw[...] = jnp.dot(lhs, left[mate % clusters], preferred_element_type=jnp.float32)

    def pointwise(place, raw, raw_halves, both_halves):
        _, mate = decoded(place)
        scale = weight[pl.ds(mate, 1), :]
        for start in range(0, panels, LANES):
            span = slice(start, start + LANES)
            inverse = lax.rsqrt(raw[span, raw_halves[1]])
            kernel = scale * inverse
            both[span, both_halves[0]] = kernel.astype(jnp.bfloat16)
            weighted = (inverse * inverse) * (kernel * raw[span, raw_halves[0]])
            both[span, both_halves[1]] = weighted.astype(jnp.bfloat16)

    def summed(place, left, columns):
        here, mate = decoded(place)
        acc[here] += lax.dot_general(
            left[mate % clusters, :rows, :],
            both[:, columns],
            (((1,), (1,)), ((), ())),
            preferred_element_type=jnp.float32,
        )

    def source_sums(place):
        (here_a, mate_a), (here_b, mate_b) = decoded(place), decoded(place + 1)
        aug = jnp.concatenate(
            [
                jnp.concatenate([ref[here] for ref in aug_refs], axis=1)
                for here in (here_a, here_b)
            ],
            axis=0,
        )
        sums = jnp.dot(aug, both[:, quarter : 3 * quarter], preferred_element_type=jnp.float32)
        back[mate_a % clusters] += sums[:AUG, :quarter]
        back[mate_b % clusters] += sums[AUG:, quarter:]

    forward, backward = (halves[0], halves[1]), (halves[1], halves[0])
    columns_a, columns_b = slice(0, 2 * quarter), slice(2 * quarter, 4 * quarter)

    @pl.loop(0, items[step * length])
    def _(pair):
        turn = 2 * pair + 1
        summed(turn, left_a, columns_a)
        pointwise(turn + 1, raw_b, backward, (halves[3], halves[2]))
        products(turn + 2, left_a, raw_a)
        source_sums(turn)
        summed(turn + 1, left_b, columns_b)
        pointwise(turn + 2, raw_a, forward, (halves[0], halves[1]))
        products(turn + 3, left_b, raw_b)

    for coord in range(3):
        back_ref[coord] = -0.5 * back[:, coord, :] - there[coord] * back[:, 6, :]
    if last:
        for coord in range(3):
            span = slice(base + coord * clusters, base + (coord + 1) * clusters)
            pos = [ref[span, :] for ref in local_refs]
            pos = jnp.concatenate(pos, axis=1).astype(jnp.float32)
            grad_ref[coord] = acc[:, width + coord, :] - pos * acc[:, width + 3, :]
        pot_ref[...] = acc[:, :rhs, :]
        pot_out_ref[...] = acc[:, rhs:width, :].astype(jnp.bfloat16)


def run_step(step, length, items, source, targets, locals_, rhs, width, carried, last):
    lhss, augs = zip(*targets)
    clusters, _, row_count = augs[0].shape
    subs = len(targets)
    panels = subs * row_count
    quarter = source.shape[1]
    first = carried is None
    vmem = pl.BlockSpec(memory_space=pltpu.VMEM)
    smem = pl.BlockSpec(memory_space=pltpu.SMEM)
    operands = (items, source, *lhss, *augs)
    if not first:
        operands += (carried,)
    acc_shape = (clusters, width + AUG, panels)
    back_shape = jax.ShapeDtypeStruct((3, clusters, quarter), jnp.float32)
    scratch = [
        pltpu.VMEM((clusters, AUG, quarter), jnp.float32),
        pltpu.VMEM((clusters, LANES, 2 * quarter), jnp.bfloat16),
        pltpu.VMEM((clusters, LANES, 2 * quarter), jnp.bfloat16),
        pltpu.VMEM((clusters + 8, quarter), jnp.float32),
        pltpu.VMEM((clusters, AUG, quarter), jnp.float32),
    ]
    scratch += [pltpu.VMEM((panels, 2 * quarter), jnp.float32)] * 2
    scratch += [pltpu.VMEM((panels, 4 * quarter), jnp.bfloat16)]
    if last:
        operands += tuple(locals_)
        out_shape = (
            jax.ShapeDtypeStruct((clusters, rhs, panels), jnp.float32),
            jax.ShapeDtypeStruct((clusters, width - rhs, panels), jnp.bfloat16),
            jax.ShapeDtypeStruct((3, clusters, panels), jnp.float32),
            back_shape,
        )
        scratch = [pltpu.VMEM(acc_shape, jnp.float32)] + scratch
    else:
        out_shape = (jax.ShapeDtypeStruct(acc_shape, jnp.float32), back_shape)
    pairs = (length - 6) * panels * quarter
    return pl.pallas_call(
        functools.partial(step_kernel, step, length, rhs, subs, first, last),
        out_shape=out_shape,
        in_specs=[smem] + [vmem] * (len(operands) - 1),
        out_specs=(vmem,) * len(out_shape),
        scratch_shapes=scratch,
        compiler_params=pltpu.CompilerParams(vmem_limit_bytes=20 * 1024 * 1024),
        cost_estimate=pl.CostEstimate(
            flops=2 * pairs * (2 * width + 3 * AUG), bytes_accessed=6 * 2**20, transcendentals=pairs
        ),
        name=f"near_field_{step}",
    )(*operands)


def node_kernel(grad_ref, jitter_ref, edge_ref, main_ref):
    clusters, panels = jitter_ref.shape
    wide = panels + 2 * LANES

    def spread_of(terms, jitter):
        side = jnp.zeros((terms.shape[0], LANES), jnp.float32)
        terms = 0.25 * terms
        spread = jnp.zeros((terms.shape[0], wide), jnp.float32)
        for offset in range(-jitter_reach, jitter_reach + 1):
            masked = jnp.where(jitter == offset, terms, 0.0)
            masked = jnp.concatenate([side, masked, side], axis=1)
            spread = spread + pltpu.roll(masked, offset % wide, 1)
        spread = spread + pltpu.roll(spread, 1, 1)
        return spread + pltpu.roll(spread, 32, 1)

    jitter = jitter_ref[...]
    row_at = lax.broadcasted_iota(jnp.int32, (clusters, LANES), 0)
    edge = edge_ref[...]
    edge_at = lax.broadcasted_iota(jnp.int32, edge.shape, 0)
    edge_jitter = jnp.where(edge_at < 3, edge[6:7], edge[7:8]).astype(jnp.int32)
    edge = spread_of(edge, edge_jitter)
    for coord in range(3):
        spread = spread_of(grad_ref[coord], jitter)
        below = spread[:, :LANES]
        above = spread[:, LANES + panels :]
        inner = spread[:, LANES : LANES + panels]
        before = edge[coord : coord + 1, LANES + panels :]
        after = edge[3 + coord : 4 + coord, :LANES]
        first = jnp.where(row_at == 0, before, pltpu.roll(above, 1, 0))
        last = jnp.where(row_at == clusters - 1, after, pltpu.roll(below, clusters - 1, 0))
        inner = jnp.concatenate(
            [
                inner[:, :LANES] + first,
                inner[:, LANES : panels - LANES],
                inner[:, panels - LANES :] + last,
            ],
            axis=1,
        )
        for cluster in range(clusters):
            main_ref[coord : coord + 1, cluster * panels : (cluster + 1) * panels] = inner[
                cluster : cluster + 1
            ]


def sum_kernel(*refs):
    total = refs[0][...]
    for ref in refs[1:-1]:
        total = total + ref[...].astype(jnp.float32)
    refs[-1][...] = total.astype(jnp.bfloat16)


def on_device(positions, areas, density, cotangent, matching, connect):
    clus_count = lax.axis_size("clus")
    sub_count = lax.axis_size("sub")
    rhs_count = lax.axis_size("rhs")
    device = lax.axis_index("clus")
    sub_place = lax.axis_index("sub")
    core = lax.axis_index("rhs")
    clusters, rhs, row_count = density.shape
    panels = row_count * sub_count
    quarter = row_count // rhs_count
    width = rhs * rhs_count
    vmem = pl.BlockSpec(memory_space=pltpu.VMEM)

    nodes_total = clus_count * clusters * panels

    by_coord = jnp.transpose(positions, (1, 0, 2))
    arguments = [
        pltpu.with_memory_space_constraint(array, pltpu.HBM)
        for array in (density, by_coord, areas, connect, cotangent)
    ]
    shapes = [(clusters * (rhs + 5), quarter)] + [(clusters * rhs, quarter)] * (rhs_count - 1)
    shapes.append((clusters * (rhs + 4), row_count))
    *parts, local = pl.pallas_call(
        functools.partial(prepare_kernel, (panels, nodes_total)),
        out_shape=[jax.ShapeDtypeStruct(shape, jnp.bfloat16) for shape in shapes],
        in_specs=[pl.BlockSpec(memory_space=pltpu.HBM)] * len(arguments),
        out_specs=[vmem] * len(shapes),
        scratch_shapes=[pltpu.VMEM(array.shape, array.dtype) for array in arguments]
        + [pltpu.SemaphoreType.DMA((len(arguments),))],
        compiler_params=pltpu.CompilerParams(vmem_limit_bytes=16 * 1024 * 1024),
        name="prepare",
    )(*arguments)
    ring = ring_order(clus_count)
    at_place = [ring.index(index) for index in range(clus_count)]
    ring_place = pick(device, at_place)

    def own_parts(parts, steps):
        arrived = [round_ring(parts[0], steps)]
        for step in range(1, rhs_count):

            def goal(z, c, step=step):
                return (ring[(at_place[z] + steps) % clus_count], c + step)

            arrived.append(moved(parts[step], ("clus", "rhs"), goal))
        return arrived

    arrived = own_parts(parts, 1)

    per_round = 2 * ((clusters // 2 + clus_count - 2) // (clus_count - 1))
    cap = ROUNDS * per_round
    partners = lax.dynamic_slice_in_dim(matching, device * clusters, clusters, 1).reshape(-1)
    here = jnp.tile(jnp.arange(clusters, dtype=jnp.int32), ROUNDS)
    code = here * (2 * clusters) + partners % clusters
    behind = (ring_place - pick(partners // clusters, at_place)) % clus_count
    total_items = ROUNDS * clusters
    order = jnp.arange(total_items, dtype=jnp.int32)
    rank = jnp.sum(
        ((behind[None, :] == behind[:, None]) & (order[None, :] < order[:, None])).astype(jnp.int32),
        axis=1,
    )
    steps = jnp.arange(1, clus_count, dtype=jnp.int32)
    member = behind[None, :] == steps[:, None]
    slots = jnp.arange(cap, dtype=jnp.int32)
    chosen = member[:, None, :] & (rank[None, None, :] == slots[None, :, None])
    listed = jnp.sum(jnp.where(chosen, code[None, None, :] - clusters, 0), axis=2) + clusters
    turns = (jnp.sum(member.astype(jnp.int32), axis=1) + 3) // 2
    length = cap + 6
    items = jnp.pad(listed, ((0, 0), (3, 3)), constant_values=clusters)
    items = jnp.concatenate([turns[:, None], items[:, 1:]], axis=1).reshape(-1)

    locals_ = [local] + [shifted(local, "sub", step) for step in range(1, sub_count)]
    blocks = [
        [block] + [shifted(block, "rhs", step) for step in range(1, rhs_count)] for block in locals_
    ]

    def in_order(blocks):
        return jnp.concatenate(
            [pick((sub_place - place) % sub_count, blocks) for place in range(sub_count)], axis=-1
        )

    jitter_all = in_order([block[clusters * (rhs + 3) :] for block in locals_]).astype(jnp.int32)
    targets = [
        pl.pallas_call(
            target_kernel,
            out_shape=(
                jax.ShapeDtypeStruct((clusters, row_count, LANES), jnp.bfloat16),
                jax.ShapeDtypeStruct((clusters, AUG, row_count), jnp.bfloat16),
            ),
            in_specs=[vmem] * rhs_count,
            out_specs=(vmem, vmem),
            scratch_shapes=[pltpu.VMEM((clusters, AUG, row_count), jnp.float32)],
            compiler_params=pltpu.CompilerParams(vmem_limit_bytes=16 * 1024 * 1024),
            cost_estimate=pl.CostEstimate(flops=2**20, bytes_accessed=2**18, transcendentals=0),
            name=f"targets_{place}",
        )(*blocks[place])
        for place in range(sub_count)
    ]

    arrived, targets = lax.optimization_barrier((arrived, targets))
    source = jnp.concatenate(arrived, axis=0)
    source, parts = lax.optimization_barrier((source, parts))
    from_next = own_parts(parts, -1) if clus_count > 2 else None
    carried = None
    backs, jitter_rows = [], [None]
    for step in range(1, clus_count):
        if 1 < step < clus_count - 1:
            if step > 2:
                source, backs[step - 3] = lax.optimization_barrier((source, backs[step - 3]))
            source = round_ring(source, 1)
        elif step > 1:
            from_next, backs[-1] = lax.optimization_barrier((from_next, backs[-1]))
            source = jnp.concatenate(from_next, axis=0)
        last = step == clus_count - 1
        results = run_step(
            step - 1, length, items, source, targets, locals_, rhs, width, carried, last
        )
        if last:
            pot, pot_out, grad, back = results
        else:
            carried, back = results
        backs.append(back)
        at = clusters * (rhs + 4)
        jitter_rows.append(source[at : at + clusters])

    grad = in_order([grad[..., at * row_count : (at + 1) * row_count] for at in range(sub_count)])
    low_part = (sub_place == 0) & (core == 0)
    high_part = (sub_place == sub_count - 1) & (core == rhs_count - 1)
    uppers = [grad[:, -1, -quarter:]] + [jnp.where(high_part, back[:, -1], 0.0) for back in backs]
    lowers = [grad[:, 0, :quarter]] + [jnp.where(low_part, back[:, 0], 0.0) for back in backs]

    def step_between(index, owner):
        return (at_place[index] - at_place[owner % clus_count]) % clus_count

    def needed(parts, step, offset):
        choices = []
        for index in range(clus_count):
            goal = ring[(at_place[index] - step) % clus_count]
            choices.append(parts[step_between(index, goal + offset)])
        return pick(device, choices)

    nothing = jnp.zeros((2, quarter), jnp.float32)
    returned = jnp.zeros((3, clusters, quarter), jnp.float32)
    upper, lower = needed(uppers, 0, -1), needed(lowers, 0, 1)
    for step in range(1, clus_count):
        rows = [
            backs[step - 1].reshape(3 * clusters, quarter),
            needed(uppers, step, -1),
            needed(lowers, step, 1),
            nothing,
        ]
        home = round_ring(jnp.concatenate(rows, axis=0), -step)
        returned = returned + home[: 3 * clusters].reshape(returned.shape)
        upper = upper + home[3 * clusters : 3 * clusters + 3]
        lower = lower + home[3 * clusters + 3 : 3 * clusters + 6]

    half = pot
    for step in range(1, rhs_count):
        arrived = shifted(pot_out[:, (step - 1) * rhs : step * rhs], "rhs", -step)
        half = half + arrived.astype(jnp.float32)

    half, grad = lax.optimization_barrier((half, grad))
    found = [half[..., :row_count]]
    for step in range(1, sub_count):
        sent = half[..., step * row_count : (step + 1) * row_count].astype(jnp.bfloat16)
        found.append(shifted(sent, "sub", -step))

    quarter_at = sub_place * rhs_count + core
    grad = grad + jnp.concatenate(
        [jnp.where(quarter_at == at, returned, 0.0) for at in range(sub_count * rhs_count)], axis=-1
    )
    share = clusters // sub_count

    blank = jnp.zeros((3, panels - quarter), jnp.float32)
    before = jnp.concatenate([blank, upper], axis=1)
    after = jnp.concatenate([lower, blank], axis=1)
    jitter_float = jitter_all.astype(jnp.float32)
    jitter_before = jnp.concatenate(
        [blank[:1], needed(jitter_rows, 0, -1)[clusters - 1 :].astype(jnp.float32)], axis=1
    )
    jitter_after = jnp.concatenate(
        [needed(jitter_rows, 0, 1)[:1].astype(jnp.float32), blank[:1]], axis=1
    )

    def edge_rows(at):
        first, end = at * share, (at + 1) * share
        inside = at < sub_count - 1
        return jnp.concatenate(
            [
                grad[:, first - 1] if at > 0 else before,
                grad[:, end] if inside else after,
                jnp.where(high_part, jitter_float[first - 1 : first] if at > 0 else jitter_before, 0.0),
                jnp.where(low_part, jitter_float[end : end + 1] if inside else jitter_after, 0.0),
            ],
            axis=0,
        ).reshape(-1, share, panels)

    def packed(place):
        return pick(
            place % sub_count,
            [
                jnp.concatenate([grad[:, at * share : (at + 1) * share], edge_rows(at)], axis=0)
                for at in range(sub_count)
            ],
        )

    summed = packed(sub_place)
    for step in range(1, sub_count):
        summed = summed + shifted(packed(sub_place + step), "sub", step)
    gathered = summed
    for step in range(1, rhs_count):
        gathered = gathered + shifted(summed, "rhs", step)
    own_jitter = pick(
        sub_place, [jitter_all[at * share : (at + 1) * share] for at in range(sub_count)]
    )
    node_grad = pl.pallas_call(
        node_kernel,
        out_shape=jax.ShapeDtypeStruct((3, share * panels), jnp.float32),
        in_specs=[vmem] * 3,
        out_specs=vmem,
        compiler_params=pltpu.CompilerParams(vmem_limit_bytes=16 * 1024 * 1024),
        cost_estimate=pl.CostEstimate(flops=2**20, bytes_accessed=2**18, transcendentals=0),
        name="node_terms",
    )(gathered[:3], own_jitter, gathered[3:].reshape(8, panels))
    potential = pl.pallas_call(
        sum_kernel,
        out_shape=jax.ShapeDtypeStruct((clusters, rhs, row_count), jnp.bfloat16),
        in_specs=[vmem] * sub_count,
        out_specs=vmem,
        compiler_params=pltpu.CompilerParams(vmem_limit_bytes=16 * 1024 * 1024),
        cost_estimate=pl.CostEstimate(flops=2**20, bytes_accessed=2**18, transcendentals=0),
        name="potential_sum",
    )(*found)
    return (potential, node_grad)


def solution(mesh):
    placed = (
        P(("groups", "clus"), None, "sub"),
        P(("groups", "clus"), "sub"),
        P(("groups", "clus"), "rhs", "sub"),
        P(("groups", "clus"), "rhs", "sub"),
        P(None, "groups"),
        P(("groups", "clus"), None, "sub"),
    )
    return jax.shard_map(
        on_device,
        mesh=mesh,
        in_specs=placed,
        out_specs=(P(("groups", "clus"), "rhs", "sub"), P(None, ("groups", "clus", "sub"))),
        check_vma=False,
    )
```

```python
import functools

import jax
import jax.numpy as jnp
from jax import lax
from jax.experimental import pallas as pl
from jax.experimental.pallas import tpu as pltpu
from jax.sharding import PartitionSpec as P

CP = 512
ROUNDS = 5

core_radius = 0.25
jitter_reach = 8
LANES = 128
AUG = 16


def shifted(value, axis, steps):
    count = lax.axis_size(axis)
    pairs = [(source, (source + steps) % count) for source in range(count)]
    return lax.ppermute(value, axis, pairs)


def ring_order(count):
    return [*range(0, count, 2), *reversed(range(1, count, 2))]


def round_ring(value, steps):
    order = ring_order(lax.axis_size("clus"))
    pairs = [(source, order[(at + steps) % len(order)]) for at, source in enumerate(order)]
    return lax.ppermute(value, "clus", pairs)


def moved(value, axes, target):
    counts = [lax.axis_size(axis) for axis in axes]
    pairs = []
    for major in range(counts[0]):
        for minor in range(counts[1]):
            goal = target(major, minor)
            if goal is not None:
                to_major, to_minor = goal[0] % counts[0], goal[1] % counts[1]
                pairs.append((major * counts[1] + minor, to_major * counts[1] + to_minor))
    return lax.ppermute(value, axes, pairs)


def three_parts(value):
    parts = []
    for _ in range(3):
        part = value.astype(jnp.bfloat16).astype(jnp.float32)
        parts.append(part)
        value = value - part
    return parts


def pick(index, choices):
    out = choices[0]
    for place in range(1, len(choices)):
        out = jnp.where(index == place, choices[place], out)
    return out


def fetched(arguments, places, sems):
    copies = []
    for at, (argument, place) in enumerate(zip(arguments, places)):
        copies.append(pltpu.make_async_copy(argument, place, sems.at[at]))
        copies[-1].start()
    for copy in copies:
        copy.wait()


def jitter_of(connect_ref, sizes):
    clusters, _, row_count = connect_ref.shape
    panels, nodes_total = sizes
    first_id = clusters * panels * lax.axis_index("clus") + row_count * lax.axis_index("sub")
    ids = lax.broadcasted_iota(jnp.int32, (clusters, row_count), 0) * panels
    ids = ids + lax.broadcasted_iota(jnp.int32, (clusters, row_count), 1) + first_id
    jitter = connect_ref[:, 0, :] - ids
    jitter = jnp.where(jitter > jitter_reach, jitter - nodes_total, jitter)
    jitter = jnp.where(jitter < -jitter_reach, jitter + nodes_total, jitter)
    return jitter.astype(jnp.float32).astype(jnp.bfloat16)


def prepare_kernel(sizes, *refs):
    arguments, part_refs, local_ref, scratch = refs[:5], refs[5:-7], refs[-7], refs[-6:]
    fetched(arguments, scratch[:5], scratch[5])
    density_ref, by_coord_ref, areas_ref, connect_ref, cot_ref = scratch[:5]
    clusters, rhs, _ = density_ref.shape
    quarter = part_refs[0].shape[1]
    count = len(part_refs)
    core = lax.axis_index("rhs")

    def part_of(array, place):
        return pick(place, [array[:, at * quarter : (at + 1) * quarter] for at in range(count)])

    pos = [by_coord_ref[coord] for coord in range(3)]
    jitter = jitter_of(connect_ref, sizes)
    base = clusters * rhs
    for cluster in range(clusters):
        dens = density_ref[cluster]
        span = slice(cluster * rhs, (cluster + 1) * rhs)
        local_ref[span, :] = cot_ref[cluster]
        for step, part_ref in enumerate(part_refs):
            part_ref[span, :] = part_of(dens, (core + step) % count)
    for at, value in enumerate([*pos, areas_ref[...], jitter]):
        part_refs[0][base + at * clusters : base + (at + 1) * clusters, :] = part_of(value, core)
    for at, value in enumerate([*pos, jitter]):
        local_ref[base + at * clusters : base + (at + 1) * clusters, :] = value


def target_kernel(*refs):
    local_refs, (lhs_ref, aug_ref, aug32) = refs[:-3], refs[-3:]
    clusters, _, row_count = aug_ref.shape
    rhs = local_refs[0].shape[0] // clusters - 4
    base = clusters * rhs
    pos = [
        local_refs[0][base + coord * clusters : base + (coord + 1) * clusters, :].astype(jnp.float32)
        for coord in range(3)
    ]
    square = pos[0] * pos[0] + pos[1] * pos[1] + pos[2] * pos[2] + core_radius * core_radius
    ones = jnp.ones_like(square)
    aug32[...] = jnp.zeros(aug32.shape, jnp.float32)
    for row, value in enumerate([-2.0 * value for value in pos] + three_parts(square) + [ones] * 3):
        aug32[:, row, :] = value
    blank = jnp.zeros((LANES - AUG - rhs * len(local_refs), row_count), jnp.bfloat16)
    for cluster in range(clusters):
        aug = aug32[cluster].astype(jnp.bfloat16)
        aug_ref[cluster] = aug
        rows = [ref[cluster * rhs : (cluster + 1) * rhs, :] for ref in local_refs]
        lhs_ref[cluster] = jnp.concatenate([*rows, aug, blank], axis=0).T


def step_kernel(step, length, rhs, subs, first, last, *refs):
    items, source_ref, refs = refs[0], refs[1], refs[2:]
    lhs_refs, aug_refs, refs = refs[:subs], refs[subs : 2 * subs], refs[2 * subs :]
    if not first:
        acc_in, refs = refs[0], refs[1:]
    if last:
        local_refs, refs = refs[:subs], refs[subs:]
        pot_ref, pot_out_ref, grad_ref, back_ref, acc = refs[:5]
        refs = refs[5:]
    else:
        acc, back_ref = refs[:2]
        refs = refs[2:]
    aug32, left_a, left_b, weight, back, raw_a, raw_b, both = refs
    clusters, rows, panels = acc.shape
    width = rows - AUG
    row_count = panels // subs
    quarter = source_ref.shape[1]
    base = clusters * rhs

    starts = [0] + list(range(base + 5 * clusters, source_ref.shape[0], base))

    there = [
        source_ref[base + coord * clusters : base + (coord + 1) * clusters, :].astype(jnp.float32)
        for coord in range(3)
    ]
    area = source_ref[base + 3 * clusters : base + 4 * clusters, :].astype(jnp.float32)
    square = there[0] * there[0] + there[1] * there[1] + there[2] * there[2]
    ones = jnp.ones_like(square)
    aug32[...] = jnp.zeros(aug32.shape, jnp.float32)
    for row, value in enumerate(there + [ones] * 3 + three_parts(square)):
        aug32[:, row, :] = value
    weight[...] = jnp.zeros(weight.shape, jnp.float32)
    weight[:clusters, :] = CP ** (-0.5) * area
    left_a[...] = jnp.zeros(left_a.shape, left_a.dtype)
    left_b[...] = jnp.zeros(left_b.shape, left_b.dtype)
    for cluster in range(clusters):
        distance_rows = aug32[cluster].astype(jnp.bfloat16)
        left_a[cluster, width:rows, quarter:] = distance_rows
        left_b[cluster, width:rows, :quarter] = distance_rows
        for place, at in enumerate(starts):
            span = slice(place * rhs, (place + 1) * rhs)
            dens = source_ref[at + cluster * rhs : at + (cluster + 1) * rhs, :]
            left_a[cluster, span, :quarter] = dens
            left_b[cluster, span, quarter:] = dens
    back[...] = jnp.zeros(back.shape, jnp.float32)
    if first:
        acc[...] = jnp.zeros(acc.shape, jnp.float32)
    else:
        acc[...] = acc_in[...]
    raw_b[...] = jnp.ones(raw_b.shape, jnp.float32)
    both[:, : 2 * quarter] = jnp.zeros((panels, 2 * quarter), both.dtype)

    halves = [slice(at * quarter, (at + 1) * quarter) for at in range(4)]

    def decoded(place):
        code = items[step * length + place]
        return code // (2 * clusters), code % (2 * clusters)

    def products(place, left, raw):
        here, mate = decoded(place)
        lhs = jnp.concatenate([ref[here] for ref in lhs_refs], axis=0)
        raw[...] = jnp.dot(lhs, left[mate % clusters], preferred_element_type=jnp.float32)

    def pointwise(place, raw, raw_halves, both_halves):
        _, mate = decoded(place)
        scale = weight[pl.ds(mate, 1), :]
        for start in range(0, panels, LANES):
            span = slice(start, start + LANES)
            inverse = lax.rsqrt(raw[span, raw_halves[1]])
            kernel = scale * inverse
            both[span, both_halves[0]] = kernel.astype(jnp.bfloat16)
            weighted = (inverse * inverse) * (kernel * raw[span, raw_halves[0]])
            both[span, both_halves[1]] = weighted.astype(jnp.bfloat16)

    def summed(place, left, columns):
        here, mate = decoded(place)
        acc[here] += lax.dot_general(
            left[mate % clusters, :rows, :],
            both[:, columns],
            (((1,), (1,)), ((), ())),
            preferred_element_type=jnp.float32,
        )

    def source_sums(place):
        (here_a, mate_a), (here_b, mate_b) = decoded(place), decoded(place + 1)
        aug = jnp.concatenate(
            [
                jnp.concatenate([ref[here] for ref in aug_refs], axis=1)
                for here in (here_a, here_b)
            ],
            axis=0,
        )
        sums = jnp.dot(aug, both[:, quarter : 3 * quarter], preferred_element_type=jnp.float32)
        back[mate_a % clusters] += sums[:AUG, :quarter]
        back[mate_b % clusters] += sums[AUG:, quarter:]

    forward, backward = (halves[0], halves[1]), (halves[1], halves[0])
    columns_a, columns_b = slice(0, 2 * quarter), slice(2 * quarter, 4 * quarter)

    @pl.loop(0, items[step * length])
    def _(four):
        for turn in (4 * four + 1, 4 * four + 3):
            summed(turn, left_a, columns_a)
            pointwise(turn + 1, raw_b, backward, (halves[3], halves[2]))
            products(turn + 2, left_a, raw_a)
            source_sums(turn)
            summed(turn + 1, left_b, columns_b)
            pointwise(turn + 2, raw_a, forward, (halves[0], halves[1]))
            products(turn + 3, left_b, raw_b)

    for coord in range(3):
        back_ref[coord] = -0.5 * back[:, coord, :] - there[coord] * back[:, 6, :]
    if last:
        for coord in range(3):
            span = slice(base + coord * clusters, base + (coord + 1) * clusters)
            pos = [ref[span, :] for ref in local_refs]
            pos = jnp.concatenate(pos, axis=1).astype(jnp.float32)
            grad_ref[coord] = acc[:, width + coord, :] - pos * acc[:, width + 3, :]
        pot_ref[...] = acc[:, :rhs, :]
        pot_out_ref[...] = acc[:, rhs:width, :].astype(jnp.bfloat16)


def run_step(step, length, items, source, targets, locals_, rhs, width, carried, last):
    lhss, augs = zip(*targets)
    clusters, _, row_count = augs[0].shape
    subs = len(targets)
    panels = subs * row_count
    quarter = source.shape[1]
    first = carried is None
    vmem = pl.BlockSpec(memory_space=pltpu.VMEM)
    smem = pl.BlockSpec(memory_space=pltpu.SMEM)
    operands = (items, source, *lhss, *augs)
    if not first:
        operands += (carried,)
    acc_shape = (clusters, width + AUG, panels)
    back_shape = jax.ShapeDtypeStruct((3, clusters, quarter), jnp.float32)
    scratch = [
        pltpu.VMEM((clusters, AUG, quarter), jnp.float32),
        pltpu.VMEM((clusters, LANES, 2 * quarter), jnp.bfloat16),
        pltpu.VMEM((clusters, LANES, 2 * quarter), jnp.bfloat16),
        pltpu.VMEM((clusters + 8, quarter), jnp.float32),
        pltpu.VMEM((clusters, AUG, quarter), jnp.float32),
    ]
    scratch += [pltpu.VMEM((panels, 2 * quarter), jnp.float32)] * 2
    scratch += [pltpu.VMEM((panels, 4 * quarter), jnp.bfloat16)]
    if last:
        operands += tuple(locals_)
        out_shape = (
            jax.ShapeDtypeStruct((clusters, rhs, panels), jnp.float32),
            jax.ShapeDtypeStruct((clusters, width - rhs, panels), jnp.bfloat16),
            jax.ShapeDtypeStruct((3, clusters, panels), jnp.float32),
            back_shape,
        )
        scratch = [pltpu.VMEM(acc_shape, jnp.float32)] + scratch
    else:
        out_shape = (jax.ShapeDtypeStruct(acc_shape, jnp.float32), back_shape)
    pairs = (length - 10) * panels * quarter
    return pl.pallas_call(
        functools.partial(step_kernel, step, length, rhs, subs, first, last),
        out_shape=out_shape,
        in_specs=[smem] + [vmem] * (len(operands) - 1),
        out_specs=(vmem,) * len(out_shape),
        scratch_shapes=scratch,
        compiler_params=pltpu.CompilerParams(vmem_limit_bytes=20 * 1024 * 1024),
        cost_estimate=pl.CostEstimate(
            flops=2 * pairs * (2 * width + 3 * AUG), bytes_accessed=6 * 2**20, transcendentals=pairs
        ),
        name=f"near_field_{step}",
    )(*operands)


def node_kernel(grad_ref, jitter_ref, edge_ref, main_ref):
    clusters, panels = jitter_ref.shape
    wide = panels + 2 * LANES

    def spread_of(terms, jitter):
        side = jnp.zeros((terms.shape[0], LANES), jnp.float32)
        terms = 0.25 * terms
        spread = jnp.zeros((terms.shape[0], wide), jnp.float32)
        for offset in range(-jitter_reach, jitter_reach + 1):
            masked = jnp.where(jitter == offset, terms, 0.0)
            masked = jnp.concatenate([side, masked, side], axis=1)
            spread = spread + pltpu.roll(masked, offset % wide, 1)
        spread = spread + pltpu.roll(spread, 1, 1)
        return spread + pltpu.roll(spread, 32, 1)

    jitter = jitter_ref[...]
    row_at = lax.broadcasted_iota(jnp.int32, (clusters, LANES), 0)
    edge = edge_ref[...]
    edge_at = lax.broadcasted_iota(jnp.int32, edge.shape, 0)
    edge_jitter = jnp.where(edge_at < 3, edge[6:7], edge[7:8]).astype(jnp.int32)
    edge = spread_of(edge, edge_jitter)
    for coord in range(3):
        spread = spread_of(grad_ref[coord], jitter)
        below = spread[:, :LANES]
        above = spread[:, LANES + panels :]
        inner = spread[:, LANES : LANES + panels]
        before = edge[coord : coord + 1, LANES + panels :]
        after = edge[3 + coord : 4 + coord, :LANES]
        first = jnp.where(row_at == 0, before, pltpu.roll(above, 1, 0))
        last = jnp.where(row_at == clusters - 1, after, pltpu.roll(below, clusters - 1, 0))
        inner = jnp.concatenate(
            [
                inner[:, :LANES] + first,
                inner[:, LANES : panels - LANES],
                inner[:, panels - LANES :] + last,
            ],
            axis=1,
        )
        for cluster in range(clusters):
            main_ref[coord : coord + 1, cluster * panels : (cluster + 1) * panels] = inner[
                cluster : cluster + 1
            ]


def sum_kernel(*refs):
    total = refs[0][...]
    for ref in refs[1:-1]:
        total = total + ref[...].astype(jnp.float32)
    refs[-1][...] = total.astype(jnp.bfloat16)


def on_device(positions, areas, density, cotangent, matching, connect):
    clus_count = lax.axis_size("clus")
    sub_count = lax.axis_size("sub")
    rhs_count = lax.axis_size("rhs")
    device = lax.axis_index("clus")
    sub_place = lax.axis_index("sub")
    core = lax.axis_index("rhs")
    clusters, rhs, row_count = density.shape
    panels = row_count * sub_count
    quarter = row_count // rhs_count
    width = rhs * rhs_count
    vmem = pl.BlockSpec(memory_space=pltpu.VMEM)

    nodes_total = clus_count * clusters * panels

    by_coord = jnp.transpose(positions, (1, 0, 2))
    arguments = [
        pltpu.with_memory_space_constraint(array, pltpu.HBM)
        for array in (density, by_coord, areas, connect, cotangent)
    ]
    shapes = [(clusters * (rhs + 5), quarter)] + [(clusters * rhs, quarter)] * (rhs_count - 1)
    shapes.append((clusters * (rhs + 4), row_count))
    *parts, local = pl.pallas_call(
        functools.partial(prepare_kernel, (panels, nodes_total)),
        out_shape=[jax.ShapeDtypeStruct(shape, jnp.bfloat16) for shape in shapes],
        in_specs=[pl.BlockSpec(memory_space=pltpu.HBM)] * len(arguments),
        out_specs=[vmem] * len(shapes),
        scratch_shapes=[pltpu.VMEM(array.shape, array.dtype) for array in arguments]
        + [pltpu.SemaphoreType.DMA((len(arguments),))],
        compiler_params=pltpu.CompilerParams(vmem_limit_bytes=16 * 1024 * 1024),
        name="prepare",
    )(*arguments)
    ring = ring_order(clus_count)
    at_place = [ring.index(index) for index in range(clus_count)]
    ring_place = pick(device, at_place)

    def own_parts(parts, steps):
        arrived = [round_ring(parts[0], steps)]
        for step in range(1, rhs_count):

            def goal(z, c, step=step):
                return (ring[(at_place[z] + steps) % clus_count], c + step)

            arrived.append(moved(parts[step], ("clus", "rhs"), goal))
        return arrived

    arrived = own_parts(parts, 1)

    per_round = 2 * ((clusters // 2 + clus_count - 2) // (clus_count - 1))
    cap = ROUNDS * per_round
    partners = lax.dynamic_slice_in_dim(matching, device * clusters, clusters, 1).reshape(-1)
    here = jnp.tile(jnp.arange(clusters, dtype=jnp.int32), ROUNDS)
    code = here * (2 * clusters) + partners % clusters
    behind = (ring_place - pick(partners // clusters, at_place)) % clus_count
    total_items = ROUNDS * clusters
    order = jnp.arange(total_items, dtype=jnp.int32)
    rank = jnp.sum(
        ((behind[None, :] == behind[:, None]) & (order[None, :] < order[:, None])).astype(jnp.int32),
        axis=1,
    )
    steps = jnp.arange(1, clus_count, dtype=jnp.int32)
    member = behind[None, :] == steps[:, None]
    slots = jnp.arange(cap, dtype=jnp.int32)
    chosen = member[:, None, :] & (rank[None, None, :] == slots[None, :, None])
    listed = jnp.sum(jnp.where(chosen, code[None, None, :] - clusters, 0), axis=2) + clusters
    fours = (jnp.sum(member.astype(jnp.int32), axis=1) + 5) // 4
    length = cap + 10
    items = jnp.pad(listed, ((0, 0), (3, 7)), constant_values=clusters)
    items = jnp.concatenate([fours[:, None], items[:, 1:]], axis=1).reshape(-1)

    locals_ = [local] + [shifted(local, "sub", step) for step in range(1, sub_count)]
    blocks = [
        [block] + [shifted(block, "rhs", step) for step in range(1, rhs_count)] for block in locals_
    ]

    def in_order(blocks):
        return jnp.concatenate(
            [pick((sub_place - place) % sub_count, blocks) for place in range(sub_count)], axis=-1
        )

    jitter_all = in_order([block[clusters * (rhs + 3) :] for block in locals_]).astype(jnp.int32)
    targets = [
        pl.pallas_call(
            target_kernel,
            out_shape=(
                jax.ShapeDtypeStruct((clusters, row_count, LANES), jnp.bfloat16),
                jax.ShapeDtypeStruct((clusters, AUG, row_count), jnp.bfloat16),
            ),
            in_specs=[vmem] * rhs_count,
            out_specs=(vmem, vmem),
            scratch_shapes=[pltpu.VMEM((clusters, AUG, row_count), jnp.float32)],
            compiler_params=pltpu.CompilerParams(vmem_limit_bytes=16 * 1024 * 1024),
            cost_estimate=pl.CostEstimate(flops=2**20, bytes_accessed=2**18, transcendentals=0),
            name=f"targets_{place}",
        )(*blocks[place])
        for place in range(sub_count)
    ]

    arrived, targets = lax.optimization_barrier((arrived, targets))
    source = jnp.concatenate(arrived, axis=0)
    source, parts = lax.optimization_barrier((source, parts))
    from_next = own_parts(parts, -1) if clus_count > 2 else None
    carried = None
    backs, jitter_rows = [], [None]
    for step in range(1, clus_count):
        if 1 < step < clus_count - 1:
            if step > 2:
                source, backs[step - 3] = lax.optimization_barrier((source, backs[step - 3]))
            source = round_ring(source, 1)
        elif step > 1:
            from_next, backs[-1] = lax.optimization_barrier((from_next, backs[-1]))
            source = jnp.concatenate(from_next, axis=0)
        last = step == clus_count - 1
        results = run_step(
            step - 1, length, items, source, targets, locals_, rhs, width, carried, last
        )
        if last:
            pot, pot_out, grad, back = results
        else:
            carried, back = results
        backs.append(back)
        at = clusters * (rhs + 4)
        jitter_rows.append(source[at : at + clusters])

    grad = in_order([grad[..., at * row_count : (at + 1) * row_count] for at in range(sub_count)])
    low_part = (sub_place == 0) & (core == 0)
    high_part = (sub_place == sub_count - 1) & (core == rhs_count - 1)
    uppers = [grad[:, -1, -quarter:]] + [jnp.where(high_part, back[:, -1], 0.0) for back in backs]
    lowers = [grad[:, 0, :quarter]] + [jnp.where(low_part, back[:, 0], 0.0) for back in backs]

    def step_between(index, owner):
        return (at_place[index] - at_place[owner % clus_count]) % clus_count

    def needed(parts, step, offset):
        choices = []
        for index in range(clus_count):
            goal = ring[(at_place[index] - step) % clus_count]
            choices.append(parts[step_between(index, goal + offset)])
        return pick(device, choices)

    nothing = jnp.zeros((2, quarter), jnp.float32)
    returned = jnp.zeros((3, clusters, quarter), jnp.float32)
    upper, lower = needed(uppers, 0, -1), needed(lowers, 0, 1)
    for step in range(1, clus_count):
        rows = [
            backs[step - 1].reshape(3 * clusters, quarter),
            needed(uppers, step, -1),
            needed(lowers, step, 1),
            nothing,
        ]
        home = round_ring(jnp.concatenate(rows, axis=0), -step)
        returned = returned + home[: 3 * clusters].reshape(returned.shape)
        upper = upper + home[3 * clusters : 3 * clusters + 3]
        lower = lower + home[3 * clusters + 3 : 3 * clusters + 6]

    half = pot
    for step in range(1, rhs_count):
        arrived = shifted(pot_out[:, (step - 1) * rhs : step * rhs], "rhs", -step)
        half = half + arrived.astype(jnp.float32)

    half, grad = lax.optimization_barrier((half, grad))
    found = [half[..., :row_count]]
    for step in range(1, sub_count):
        sent = half[..., step * row_count : (step + 1) * row_count].astype(jnp.bfloat16)
        found.append(shifted(sent, "sub", -step))

    quarter_at = sub_place * rhs_count + core
    grad = grad + jnp.concatenate(
        [jnp.where(quarter_at == at, returned, 0.0) for at in range(sub_count * rhs_count)], axis=-1
    )
    share = clusters // sub_count

    blank = jnp.zeros((3, panels - quarter), jnp.float32)
    before = jnp.concatenate([blank, upper], axis=1)
    after = jnp.concatenate([lower, blank], axis=1)
    jitter_float = jitter_all.astype(jnp.float32)
    jitter_before = jnp.concatenate(
        [blank[:1], needed(jitter_rows, 0, -1)[clusters - 1 :].astype(jnp.float32)], axis=1
    )
    jitter_after = jnp.concatenate(
        [needed(jitter_rows, 0, 1)[:1].astype(jnp.float32), blank[:1]], axis=1
    )

    def edge_rows(at):
        first, end = at * share, (at + 1) * share
        inside = at < sub_count - 1
        return jnp.concatenate(
            [
                grad[:, first - 1] if at > 0 else before,
                grad[:, end] if inside else after,
                jnp.where(high_part, jitter_float[first - 1 : first] if at > 0 else jitter_before, 0.0),
                jnp.where(low_part, jitter_float[end : end + 1] if inside else jitter_after, 0.0),
            ],
            axis=0,
        ).reshape(-1, share, panels)

    def packed(place):
        return pick(
            place % sub_count,
            [
                jnp.concatenate([grad[:, at * share : (at + 1) * share], edge_rows(at)], axis=0)
                for at in range(sub_count)
            ],
        )

    summed = packed(sub_place)
    for step in range(1, sub_count):
        summed = summed + shifted(packed(sub_place + step), "sub", step)
    gathered = summed
    for step in range(1, rhs_count):
        gathered = gathered + shifted(summed, "rhs", step)
    own_jitter = pick(
        sub_place, [jitter_all[at * share : (at + 1) * share] for at in range(sub_count)]
    )
    node_grad = pl.pallas_call(
        node_kernel,
        out_shape=jax.ShapeDtypeStruct((3, share * panels), jnp.float32),
        in_specs=[vmem] * 3,
        out_specs=vmem,
        compiler_params=pltpu.CompilerParams(vmem_limit_bytes=16 * 1024 * 1024),
        cost_estimate=pl.CostEstimate(flops=2**20, bytes_accessed=2**18, transcendentals=0),
        name="node_terms",
    )(gathered[:3], own_jitter, gathered[3:].reshape(8, panels))
    potential = pl.pallas_call(
        sum_kernel,
        out_shape=jax.ShapeDtypeStruct((clusters, rhs, row_count), jnp.bfloat16),
        in_specs=[vmem] * sub_count,
        out_specs=vmem,
        compiler_params=pltpu.CompilerParams(vmem_limit_bytes=16 * 1024 * 1024),
        cost_estimate=pl.CostEstimate(flops=2**20, bytes_accessed=2**18, transcendentals=0),
        name="potential_sum",
    )(*found)
    return (potential, node_grad)


def solution(mesh):
    placed = (
        P(("groups", "clus"), None, "sub"),
        P(("groups", "clus"), "sub"),
        P(("groups", "clus"), "rhs", "sub"),
        P(("groups", "clus"), "rhs", "sub"),
        P(None, "groups"),
        P(("groups", "clus"), None, "sub"),
    )
    return jax.shard_map(
        on_device,
        mesh=mesh,
        in_specs=placed,
        out_specs=(P(("groups", "clus"), "rhs", "sub"), P(None, ("groups", "clus", "sub"))),
        check_vma=False,
    )
```

```python
import functools

import jax
import jax.numpy as jnp
from jax import lax
from jax.experimental import pallas as pl
from jax.experimental.pallas import tpu as pltpu
from jax.sharding import PartitionSpec as P

CP = 512
ROUNDS = 5

core_radius = 0.25
jitter_reach = 8
LANES = 128
AUG = 16


def shifted(value, axis, steps):
    count = lax.axis_size(axis)
    pairs = [(source, (source + steps) % count) for source in range(count)]
    return lax.ppermute(value, axis, pairs)


def ring_order(count):
    return [*range(0, count, 2), *reversed(range(1, count, 2))]


def round_ring(value, steps):
    order = ring_order(lax.axis_size("clus"))
    pairs = [(source, order[(at + steps) % len(order)]) for at, source in enumerate(order)]
    return lax.ppermute(value, "clus", pairs)


def moved(value, axes, target):
    counts = [lax.axis_size(axis) for axis in axes]
    pairs = []
    for major in range(counts[0]):
        for minor in range(counts[1]):
            goal = target(major, minor)
            if goal is not None:
                to_major, to_minor = goal[0] % counts[0], goal[1] % counts[1]
                pairs.append((major * counts[1] + minor, to_major * counts[1] + to_minor))
    return lax.ppermute(value, axes, pairs)


def three_parts(value):
    parts = []
    for _ in range(3):
        part = value.astype(jnp.bfloat16).astype(jnp.float32)
        parts.append(part)
        value = value - part
    return parts


def pick(index, choices):
    out = choices[0]
    for place in range(1, len(choices)):
        out = jnp.where(index == place, choices[place], out)
    return out


def fetched(arguments, places, sems):
    copies = []
    for at, (argument, place) in enumerate(zip(arguments, places)):
        copies.append(pltpu.make_async_copy(argument, place, sems.at[at]))
        copies[-1].start()
    for copy in copies:
        copy.wait()


def jitter_of(connect_ref, sizes):
    clusters, _, row_count = connect_ref.shape
    panels, nodes_total = sizes
    first_id = clusters * panels * lax.axis_index("clus") + row_count * lax.axis_index("sub")
    ids = lax.broadcasted_iota(jnp.int32, (clusters, row_count), 0) * panels
    ids = ids + lax.broadcasted_iota(jnp.int32, (clusters, row_count), 1) + first_id
    jitter = connect_ref[:, 0, :] - ids
    jitter = jnp.where(jitter > jitter_reach, jitter - nodes_total, jitter)
    jitter = jnp.where(jitter < -jitter_reach, jitter + nodes_total, jitter)
    return jitter.astype(jnp.float32).astype(jnp.bfloat16)


def prepare_kernel(sizes, *refs):
    arguments, part_refs, local_ref, scratch = refs[:5], refs[5:-7], refs[-7], refs[-6:]
    fetched(arguments, scratch[:5], scratch[5])
    density_ref, by_coord_ref, areas_ref, connect_ref, cot_ref = scratch[:5]
    clusters, rhs, _ = density_ref.shape
    quarter = part_refs[0].shape[1]
    count = len(part_refs)
    core = lax.axis_index("rhs")

    def part_of(array, place):
        return pick(place, [array[:, at * quarter : (at + 1) * quarter] for at in range(count)])

    pos = [by_coord_ref[coord] for coord in range(3)]
    jitter = jitter_of(connect_ref, sizes)
    base = clusters * rhs
    for cluster in range(clusters):
        dens = density_ref[cluster]
        span = slice(cluster * rhs, (cluster + 1) * rhs)
        local_ref[span, :] = cot_ref[cluster]
        for step, part_ref in enumerate(part_refs):
            part_ref[span, :] = part_of(dens, (core + step) % count)
    for at, value in enumerate([*pos, areas_ref[...], jitter]):
        part_refs[0][base + at * clusters : base + (at + 1) * clusters, :] = part_of(value, core)
    for at, value in enumerate([*pos, jitter]):
        local_ref[base + at * clusters : base + (at + 1) * clusters, :] = value


def target_kernel(*refs):
    local_refs, (lhs_ref, aug_ref, aug32) = refs[:-3], refs[-3:]
    clusters, _, row_count = aug_ref.shape
    rhs = local_refs[0].shape[0] // clusters - 4
    base = clusters * rhs
    pos = [
        local_refs[0][base + coord * clusters : base + (coord + 1) * clusters, :].astype(jnp.float32)
        for coord in range(3)
    ]
    square = pos[0] * pos[0] + pos[1] * pos[1] + pos[2] * pos[2] + core_radius * core_radius
    ones = jnp.ones_like(square)
    aug32[...] = jnp.zeros(aug32.shape, jnp.float32)
    for row, value in enumerate([-2.0 * value for value in pos] + three_parts(square) + [ones] * 3):
        aug32[:, row, :] = value
    blank = jnp.zeros((LANES - AUG - rhs * len(local_refs), row_count), jnp.bfloat16)
    for cluster in range(clusters):
        aug = aug32[cluster].astype(jnp.bfloat16)
        aug_ref[cluster] = aug
        rows = [ref[cluster * rhs : (cluster + 1) * rhs, :] for ref in local_refs]
        lhs_ref[cluster] = jnp.concatenate([*rows, aug, blank], axis=0).T


def step_kernel(step, length, rhs, subs, first, last, *refs):
    items, source_ref, refs = refs[0], refs[1], refs[2:]
    lhs_refs, aug_refs, refs = refs[:subs], refs[subs : 2 * subs], refs[2 * subs :]
    if not first:
        acc_in, refs = refs[0], refs[1:]
    if last:
        local_refs, refs = refs[:subs], refs[subs:]
        pot_ref, pot_out_ref, grad_ref, back_ref, acc = refs[:5]
        refs = refs[5:]
    else:
        acc, back_ref = refs[:2]
        refs = refs[2:]
    aug32, left_a, left_b, weight, back, raw_a, raw_b, both = refs
    clusters, rows, panels = acc.shape
    width = rows - AUG
    row_count = panels // subs
    quarter = source_ref.shape[1]
    base = clusters * rhs

    starts = [0] + list(range(base + 5 * clusters, source_ref.shape[0], base))

    there = [
        source_ref[base + coord * clusters : base + (coord + 1) * clusters, :].astype(jnp.float32)
        for coord in range(3)
    ]
    area = source_ref[base + 3 * clusters : base + 4 * clusters, :].astype(jnp.float32)
    square = there[0] * there[0] + there[1] * there[1] + there[2] * there[2]
    ones = jnp.ones_like(square)
    aug32[...] = jnp.zeros(aug32.shape, jnp.float32)
    for row, value in enumerate(there + [ones] * 3 + three_parts(square)):
        aug32[:, row, :] = value
    weight[...] = jnp.zeros(weight.shape, jnp.float32)
    weight[:clusters, :] = CP ** (-0.5) * area
    left_a[...] = jnp.zeros(left_a.shape, left_a.dtype)
    left_b[...] = jnp.zeros(left_b.shape, left_b.dtype)
    for cluster in range(clusters):
        distance_rows = aug32[cluster].astype(jnp.bfloat16)
        left_a[cluster, width:rows, quarter:] = distance_rows
        left_b[cluster, width:rows, :quarter] = distance_rows
        for place, at in enumerate(starts):
            span = slice(place * rhs, (place + 1) * rhs)
            dens = source_ref[at + cluster * rhs : at + (cluster + 1) * rhs, :]
            left_a[cluster, span, :quarter] = dens
            left_b[cluster, span, quarter:] = dens
    back[...] = jnp.zeros(back.shape, jnp.float32)
    if first:
        acc[...] = jnp.zeros(acc.shape, jnp.float32)
    else:
        acc[...] = acc_in[...]
    raw_b[...] = jnp.ones(raw_b.shape, jnp.float32)
    both[:, : 2 * quarter] = jnp.zeros((panels, 2 * quarter), both.dtype)

    halves = [slice(at * quarter, (at + 1) * quarter) for at in range(4)]

    def decoded(place):
        code = items[step * length + place]
        return code // (2 * clusters), code % (2 * clusters)

    part = max(2 * LANES, panels // 2)
    spans = [slice(start, start + part) for start in range(0, panels, part)]

    def products(place, left, raw, span):
        here, mate = decoded(place)
        lhs = jnp.concatenate([ref[here] for ref in lhs_refs], axis=0)[span]
        raw[span, :] = jnp.dot(lhs, left[mate % clusters], preferred_element_type=jnp.float32)

    def pointwise(place, raw, raw_halves, both_halves, span):
        _, mate = decoded(place)
        scale = weight[pl.ds(mate, 1), :]
        for start in range(span.start, span.stop, LANES):
            piece = slice(start, start + LANES)
            inverse = lax.rsqrt(raw[piece, raw_halves[1]])
            kernel = scale * inverse
            both[piece, both_halves[0]] = kernel.astype(jnp.bfloat16)
            weighted = (inverse * inverse) * (kernel * raw[piece, raw_halves[0]])
            both[piece, both_halves[1]] = weighted.astype(jnp.bfloat16)

    def summed(place, left, columns, span):
        here, mate = decoded(place)
        acc[here, :, span] += lax.dot_general(
            left[mate % clusters, :rows, :],
            both[span, columns],
            (((1,), (1,)), ((), ())),
            preferred_element_type=jnp.float32,
        )

    def source_sums(place):
        (here_a, mate_a), (here_b, mate_b) = decoded(place), decoded(place + 1)
        aug = jnp.concatenate(
            [
                jnp.concatenate([ref[here] for ref in aug_refs], axis=1)
                for here in (here_a, here_b)
            ],
            axis=0,
        )
        sums = jnp.dot(aug, both[:, quarter : 3 * quarter], preferred_element_type=jnp.float32)
        back[mate_a % clusters] += sums[:AUG, :quarter]
        back[mate_b % clusters] += sums[AUG:, quarter:]

    forward, backward = (halves[0], halves[1]), (halves[1], halves[0])
    columns_a, columns_b = slice(0, 2 * quarter), slice(2 * quarter, 4 * quarter)

    @pl.loop(0, items[step * length])
    def _(pair):
        turn = 2 * pair + 1
        for span in spans:
            summed(turn, left_a, columns_a, span)
            pointwise(turn + 1, raw_b, backward, (halves[3], halves[2]), span)
            products(turn + 2, left_a, raw_a, span)
        source_sums(turn)
        for span in spans:
            summed(turn + 1, left_b, columns_b, span)
            pointwise(turn + 2, raw_a, forward, (halves[0], halves[1]), span)
            products(turn + 3, left_b, raw_b, span)

    for coord in range(3):
        back_ref[coord] = -0.5 * back[:, coord, :] - there[coord] * back[:, 6, :]
    if last:
        for coord in range(3):
            span = slice(base + coord * clusters, base + (coord + 1) * clusters)
            pos = [ref[span, :] for ref in local_refs]
            pos = jnp.concatenate(pos, axis=1).astype(jnp.float32)
            grad_ref[coord] = acc[:, width + coord, :] - pos * acc[:, width + 3, :]
        pot_ref[...] = acc[:, :rhs, :]
        pot_out_ref[...] = acc[:, rhs:width, :].astype(jnp.bfloat16)


def run_step(step, length, items, source, targets, locals_, rhs, width, carried, last):
    lhss, augs = zip(*targets)
    clusters, _, row_count = augs[0].shape
    subs = len(targets)
    panels = subs * row_count
    quarter = source.shape[1]
    first = carried is None
    vmem = pl.BlockSpec(memory_space=pltpu.VMEM)
    smem = pl.BlockSpec(memory_space=pltpu.SMEM)
    operands = (items, source, *lhss, *augs)
    if not first:
        operands += (carried,)
    acc_shape = (clusters, width + AUG, panels)
    back_shape = jax.ShapeDtypeStruct((3, clusters, quarter), jnp.float32)
    scratch = [
        pltpu.VMEM((clusters, AUG, quarter), jnp.float32),
        pltpu.VMEM((clusters, LANES, 2 * quarter), jnp.bfloat16),
        pltpu.VMEM((clusters, LANES, 2 * quarter), jnp.bfloat16),
        pltpu.VMEM((clusters + 8, quarter), jnp.float32),
        pltpu.VMEM((clusters, AUG, quarter), jnp.float32),
    ]
    scratch += [pltpu.VMEM((panels, 2 * quarter), jnp.float32)] * 2
    scratch += [pltpu.VMEM((panels, 4 * quarter), jnp.bfloat16)]
    if last:
        operands += tuple(locals_)
        out_shape = (
            jax.ShapeDtypeStruct((clusters, rhs, panels), jnp.float32),
            jax.ShapeDtypeStruct((clusters, width - rhs, panels), jnp.bfloat16),
            jax.ShapeDtypeStruct((3, clusters, panels), jnp.float32),
            back_shape,
        )
        scratch = [pltpu.VMEM(acc_shape, jnp.float32)] + scratch
    else:
        out_shape = (jax.ShapeDtypeStruct(acc_shape, jnp.float32), back_shape)
    pairs = (length - 6) * panels * quarter
    return pl.pallas_call(
        functools.partial(step_kernel, step, length, rhs, subs, first, last),
        out_shape=out_shape,
        in_specs=[smem] + [vmem] * (len(operands) - 1),
        out_specs=(vmem,) * len(out_shape),
        scratch_shapes=scratch,
        compiler_params=pltpu.CompilerParams(vmem_limit_bytes=20 * 1024 * 1024),
        cost_estimate=pl.CostEstimate(
            flops=2 * pairs * (2 * width + 3 * AUG), bytes_accessed=6 * 2**20, transcendentals=pairs
        ),
        name=f"near_field_{step}",
    )(*operands)


def node_kernel(grad_ref, jitter_ref, edge_ref, main_ref):
    clusters, panels = jitter_ref.shape
    wide = panels + 2 * LANES

    def spread_of(terms, jitter):
        side = jnp.zeros((terms.shape[0], LANES), jnp.float32)
        terms = 0.25 * terms
        spread = jnp.zeros((terms.shape[0], wide), jnp.float32)
        for offset in range(-jitter_reach, jitter_reach + 1):
            masked = jnp.where(jitter == offset, terms, 0.0)
            masked = jnp.concatenate([side, masked, side], axis=1)
            spread = spread + pltpu.roll(masked, offset % wide, 1)
        spread = spread + pltpu.roll(spread, 1, 1)
        return spread + pltpu.roll(spread, 32, 1)

    jitter = jitter_ref[...]
    row_at = lax.broadcasted_iota(jnp.int32, (clusters, LANES), 0)
    edge = edge_ref[...]
    edge_at = lax.broadcasted_iota(jnp.int32, edge.shape, 0)
    edge_jitter = jnp.where(edge_at < 3, edge[6:7], edge[7:8]).astype(jnp.int32)
    edge = spread_of(edge, edge_jitter)
    for coord in range(3):
        spread = spread_of(grad_ref[coord], jitter)
        below = spread[:, :LANES]
        above = spread[:, LANES + panels :]
        inner = spread[:, LANES : LANES + panels]
        before = edge[coord : coord + 1, LANES + panels :]
        after = edge[3 + coord : 4 + coord, :LANES]
        first = jnp.where(row_at == 0, before, pltpu.roll(above, 1, 0))
        last = jnp.where(row_at == clusters - 1, after, pltpu.roll(below, clusters - 1, 0))
        inner = jnp.concatenate(
            [
                inner[:, :LANES] + first,
                inner[:, LANES : panels - LANES],
                inner[:, panels - LANES :] + last,
            ],
            axis=1,
        )
        for cluster in range(clusters):
            main_ref[coord : coord + 1, cluster * panels : (cluster + 1) * panels] = inner[
                cluster : cluster + 1
            ]


def sum_kernel(*refs):
    total = refs[0][...]
    for ref in refs[1:-1]:
        total = total + ref[...].astype(jnp.float32)
    refs[-1][...] = total.astype(jnp.bfloat16)


def on_device(positions, areas, density, cotangent, matching, connect):
    clus_count = lax.axis_size("clus")
    sub_count = lax.axis_size("sub")
    rhs_count = lax.axis_size("rhs")
    device = lax.axis_index("clus")
    sub_place = lax.axis_index("sub")
    core = lax.axis_index("rhs")
    clusters, rhs, row_count = density.shape
    panels = row_count * sub_count
    quarter = row_count // rhs_count
    width = rhs * rhs_count
    vmem = pl.BlockSpec(memory_space=pltpu.VMEM)

    nodes_total = clus_count * clusters * panels

    by_coord = jnp.transpose(positions, (1, 0, 2))
    arguments = [
        pltpu.with_memory_space_constraint(array, pltpu.HBM)
        for array in (density, by_coord, areas, connect, cotangent)
    ]
    shapes = [(clusters * (rhs + 5), quarter)] + [(clusters * rhs, quarter)] * (rhs_count - 1)
    shapes.append((clusters * (rhs + 4), row_count))
    *parts, local = pl.pallas_call(
        functools.partial(prepare_kernel, (panels, nodes_total)),
        out_shape=[jax.ShapeDtypeStruct(shape, jnp.bfloat16) for shape in shapes],
        in_specs=[pl.BlockSpec(memory_space=pltpu.HBM)] * len(arguments),
        out_specs=[vmem] * len(shapes),
        scratch_shapes=[pltpu.VMEM(array.shape, array.dtype) for array in arguments]
        + [pltpu.SemaphoreType.DMA((len(arguments),))],
        compiler_params=pltpu.CompilerParams(vmem_limit_bytes=16 * 1024 * 1024),
        name="prepare",
    )(*arguments)
    ring = ring_order(clus_count)
    at_place = [ring.index(index) for index in range(clus_count)]
    ring_place = pick(device, at_place)

    def own_parts(parts, steps):
        arrived = [round_ring(parts[0], steps)]
        for step in range(1, rhs_count):

            def goal(z, c, step=step):
                return (ring[(at_place[z] + steps) % clus_count], c + step)

            arrived.append(moved(parts[step], ("clus", "rhs"), goal))
        return arrived

    arrived = own_parts(parts, 1)

    per_round = 2 * ((clusters // 2 + clus_count - 2) // (clus_count - 1))
    cap = ROUNDS * per_round
    partners = lax.dynamic_slice_in_dim(matching, device * clusters, clusters, 1).reshape(-1)
    here = jnp.tile(jnp.arange(clusters, dtype=jnp.int32), ROUNDS)
    code = here * (2 * clusters) + partners % clusters
    behind = (ring_place - pick(partners // clusters, at_place)) % clus_count
    total_items = ROUNDS * clusters
    order = jnp.arange(total_items, dtype=jnp.int32)
    rank = jnp.sum(
        ((behind[None, :] == behind[:, None]) & (order[None, :] < order[:, None])).astype(jnp.int32),
        axis=1,
    )
    steps = jnp.arange(1, clus_count, dtype=jnp.int32)
    member = behind[None, :] == steps[:, None]
    slots = jnp.arange(cap, dtype=jnp.int32)
    chosen = member[:, None, :] & (rank[None, None, :] == slots[None, :, None])
    listed = jnp.sum(jnp.where(chosen, code[None, None, :] - clusters, 0), axis=2) + clusters
    turns = (jnp.sum(member.astype(jnp.int32), axis=1) + 3) // 2
    length = cap + 6
    items = jnp.pad(listed, ((0, 0), (3, 3)), constant_values=clusters)
    items = jnp.concatenate([turns[:, None], items[:, 1:]], axis=1).reshape(-1)

    locals_ = [local] + [shifted(local, "sub", step) for step in range(1, sub_count)]
    blocks = [
        [block] + [shifted(block, "rhs", step) for step in range(1, rhs_count)] for block in locals_
    ]

    def in_order(blocks):
        return jnp.concatenate(
            [pick((sub_place - place) % sub_count, blocks) for place in range(sub_count)], axis=-1
        )

    jitter_all = in_order([block[clusters * (rhs + 3) :] for block in locals_]).astype(jnp.int32)
    targets = [
        pl.pallas_call(
            target_kernel,
            out_shape=(
                jax.ShapeDtypeStruct((clusters, row_count, LANES), jnp.bfloat16),
                jax.ShapeDtypeStruct((clusters, AUG, row_count), jnp.bfloat16),
            ),
            in_specs=[vmem] * rhs_count,
            out_specs=(vmem, vmem),
            scratch_shapes=[pltpu.VMEM((clusters, AUG, row_count), jnp.float32)],
            compiler_params=pltpu.CompilerParams(vmem_limit_bytes=16 * 1024 * 1024),
            cost_estimate=pl.CostEstimate(flops=2**20, bytes_accessed=2**18, transcendentals=0),
            name=f"targets_{place}",
        )(*blocks[place])
        for place in range(sub_count)
    ]

    arrived, targets = lax.optimization_barrier((arrived, targets))
    source = jnp.concatenate(arrived, axis=0)
    source, parts = lax.optimization_barrier((source, parts))
    from_next = own_parts(parts, -1) if clus_count > 2 else None
    carried = None
    backs, jitter_rows = [], [None]
    for step in range(1, clus_count):
        if 1 < step < clus_count - 1:
            if step > 2:
                source, backs[step - 3] = lax.optimization_barrier((source, backs[step - 3]))
            source = round_ring(source, 1)
        elif step > 1:
            from_next, backs[-1] = lax.optimization_barrier((from_next, backs[-1]))
            source = jnp.concatenate(from_next, axis=0)
        last = step == clus_count - 1
        results = run_step(
            step - 1, length, items, source, targets, locals_, rhs, width, carried, last
        )
        if last:
            pot, pot_out, grad, back = results
        else:
            carried, back = results
        backs.append(back)
        at = clusters * (rhs + 4)
        jitter_rows.append(source[at : at + clusters])

    grad = in_order([grad[..., at * row_count : (at + 1) * row_count] for at in range(sub_count)])
    low_part = (sub_place == 0) & (core == 0)
    high_part = (sub_place == sub_count - 1) & (core == rhs_count - 1)
    uppers = [grad[:, -1, -quarter:]] + [jnp.where(high_part, back[:, -1], 0.0) for back in backs]
    lowers = [grad[:, 0, :quarter]] + [jnp.where(low_part, back[:, 0], 0.0) for back in backs]

    def step_between(index, owner):
        return (at_place[index] - at_place[owner % clus_count]) % clus_count

    def needed(parts, step, offset):
        choices = []
        for index in range(clus_count):
            goal = ring[(at_place[index] - step) % clus_count]
            choices.append(parts[step_between(index, goal + offset)])
        return pick(device, choices)

    nothing = jnp.zeros((2, quarter), jnp.float32)
    returned = jnp.zeros((3, clusters, quarter), jnp.float32)
    upper, lower = needed(uppers, 0, -1), needed(lowers, 0, 1)
    for step in range(1, clus_count):
        rows = [
            backs[step - 1].reshape(3 * clusters, quarter),
            needed(uppers, step, -1),
            needed(lowers, step, 1),
            nothing,
        ]
        home = round_ring(jnp.concatenate(rows, axis=0), -step)
        returned = returned + home[: 3 * clusters].reshape(returned.shape)
        upper = upper + home[3 * clusters : 3 * clusters + 3]
        lower = lower + home[3 * clusters + 3 : 3 * clusters + 6]

    half = pot
    for step in range(1, rhs_count):
        arrived = shifted(pot_out[:, (step - 1) * rhs : step * rhs], "rhs", -step)
        half = half + arrived.astype(jnp.float32)

    half, grad = lax.optimization_barrier((half, grad))
    found = [half[..., :row_count]]
    for step in range(1, sub_count):
        sent = half[..., step * row_count : (step + 1) * row_count].astype(jnp.bfloat16)
        found.append(shifted(sent, "sub", -step))

    quarter_at = sub_place * rhs_count + core
    grad = grad + jnp.concatenate(
        [jnp.where(quarter_at == at, returned, 0.0) for at in range(sub_count * rhs_count)], axis=-1
    )
    share = clusters // sub_count

    blank = jnp.zeros((3, panels - quarter), jnp.float32)
    before = jnp.concatenate([blank, upper], axis=1)
    after = jnp.concatenate([lower, blank], axis=1)
    jitter_float = jitter_all.astype(jnp.float32)
    jitter_before = jnp.concatenate(
        [blank[:1], needed(jitter_rows, 0, -1)[clusters - 1 :].astype(jnp.float32)], axis=1
    )
    jitter_after = jnp.concatenate(
        [needed(jitter_rows, 0, 1)[:1].astype(jnp.float32), blank[:1]], axis=1
    )

    def edge_rows(at):
        first, end = at * share, (at + 1) * share
        inside = at < sub_count - 1
        return jnp.concatenate(
            [
                grad[:, first - 1] if at > 0 else before,
                grad[:, end] if inside else after,
                jnp.where(high_part, jitter_float[first - 1 : first] if at > 0 else jitter_before, 0.0),
                jnp.where(low_part, jitter_float[end : end + 1] if inside else jitter_after, 0.0),
            ],
            axis=0,
        ).reshape(-1, share, panels)

    def packed(place):
        return pick(
            place % sub_count,
            [
                jnp.concatenate([grad[:, at * share : (at + 1) * share], edge_rows(at)], axis=0)
                for at in range(sub_count)
            ],
        )

    summed = packed(sub_place)
    for step in range(1, sub_count):
        summed = summed + shifted(packed(sub_place + step), "sub", step)
    gathered = summed
    for step in range(1, rhs_count):
        gathered = gathered + shifted(summed, "rhs", step)
    own_jitter = pick(
        sub_place, [jitter_all[at * share : (at + 1) * share] for at in range(sub_count)]
    )
    node_grad = pl.pallas_call(
        node_kernel,
        out_shape=jax.ShapeDtypeStruct((3, share * panels), jnp.float32),
        in_specs=[vmem] * 3,
        out_specs=vmem,
        compiler_params=pltpu.CompilerParams(vmem_limit_bytes=16 * 1024 * 1024),
        cost_estimate=pl.CostEstimate(flops=2**20, bytes_accessed=2**18, transcendentals=0),
        name="node_terms",
    )(gathered[:3], own_jitter, gathered[3:].reshape(8, panels))
    potential = pl.pallas_call(
        sum_kernel,
        out_shape=jax.ShapeDtypeStruct((clusters, rhs, row_count), jnp.bfloat16),
        in_specs=[vmem] * sub_count,
        out_specs=vmem,
        compiler_params=pltpu.CompilerParams(vmem_limit_bytes=16 * 1024 * 1024),
        cost_estimate=pl.CostEstimate(flops=2**20, bytes_accessed=2**18, transcendentals=0),
        name="potential_sum",
    )(*found)
    return (potential, node_grad)


def solution(mesh):
    placed = (
        P(("groups", "clus"), None, "sub"),
        P(("groups", "clus"), "sub"),
        P(("groups", "clus"), "rhs", "sub"),
        P(("groups", "clus"), "rhs", "sub"),
        P(None, "groups"),
        P(("groups", "clus"), None, "sub"),
    )
    return jax.shard_map(
        on_device,
        mesh=mesh,
        in_specs=placed,
        out_specs=(P(("groups", "clus"), "rhs", "sub"), P(None, ("groups", "clus", "sub"))),
        check_vma=False,
    )
```

```python
import functools

import jax
import jax.numpy as jnp
from jax import lax
from jax.experimental import pallas as pl
from jax.experimental.pallas import tpu as pltpu
from jax.sharding import PartitionSpec as P

CP = 512
ROUNDS = 5

core_radius = 0.25
jitter_reach = 8
LANES = 128
AUG = 16


def shifted(value, axis, steps):
    count = lax.axis_size(axis)
    pairs = [(source, (source + steps) % count) for source in range(count)]
    return lax.ppermute(value, axis, pairs)


def ring_order(count):
    return [*range(0, count, 2), *reversed(range(1, count, 2))]


def round_ring(value, steps):
    order = ring_order(lax.axis_size("clus"))
    pairs = [(source, order[(at + steps) % len(order)]) for at, source in enumerate(order)]
    return lax.ppermute(value, "clus", pairs)


def moved(value, axes, target):
    counts = [lax.axis_size(axis) for axis in axes]
    pairs = []
    for major in range(counts[0]):
        for minor in range(counts[1]):
            goal = target(major, minor)
            if goal is not None:
                to_major, to_minor = goal[0] % counts[0], goal[1] % counts[1]
                pairs.append((major * counts[1] + minor, to_major * counts[1] + to_minor))
    return lax.ppermute(value, axes, pairs)


def three_parts(value):
    parts = []
    for _ in range(3):
        part = value.astype(jnp.bfloat16).astype(jnp.float32)
        parts.append(part)
        value = value - part
    return parts


def pick(index, choices):
    out = choices[0]
    for place in range(1, len(choices)):
        out = jnp.where(index == place, choices[place], out)
    return out


def fetched(arguments, places, sems):
    copies = []
    for at, (argument, place) in enumerate(zip(arguments, places)):
        copies.append(pltpu.make_async_copy(argument, place, sems.at[at]))
        copies[-1].start()
    for copy in copies:
        copy.wait()


def jitter_of(connect_ref, sizes):
    clusters, _, row_count = connect_ref.shape
    panels, nodes_total = sizes
    first_id = clusters * panels * lax.axis_index("clus") + row_count * lax.axis_index("sub")
    ids = lax.broadcasted_iota(jnp.int32, (clusters, row_count), 0) * panels
    ids = ids + lax.broadcasted_iota(jnp.int32, (clusters, row_count), 1) + first_id
    jitter = connect_ref[:, 0, :] - ids
    jitter = jnp.where(jitter > jitter_reach, jitter - nodes_total, jitter)
    jitter = jnp.where(jitter < -jitter_reach, jitter + nodes_total, jitter)
    return jitter.astype(jnp.float32).astype(jnp.bfloat16)


def prepare_kernel(sizes, *refs):
    arguments, part_refs, local_ref, scratch = refs[:5], refs[5:-7], refs[-7], refs[-6:]
    fetched(arguments, scratch[:5], scratch[5])
    density_ref, by_coord_ref, areas_ref, connect_ref, cot_ref = scratch[:5]
    clusters, rhs, _ = density_ref.shape
    quarter = part_refs[0].shape[1]
    count = len(part_refs)
    core = lax.axis_index("rhs")

    def part_of(array, place):
        return pick(place, [array[:, at * quarter : (at + 1) * quarter] for at in range(count)])

    pos = [by_coord_ref[coord] for coord in range(3)]
    jitter = jitter_of(connect_ref, sizes)
    base = clusters * rhs
    for cluster in range(clusters):
        dens = density_ref[cluster]
        span = slice(cluster * rhs, (cluster + 1) * rhs)
        local_ref[span, :] = cot_ref[cluster]
        for step, part_ref in enumerate(part_refs):
            part_ref[span, :] = part_of(dens, (core + step) % count)
    for at, value in enumerate([*pos, areas_ref[...], jitter]):
        part_refs[0][base + at * clusters : base + (at + 1) * clusters, :] = part_of(value, core)
    for at, value in enumerate([*pos, jitter]):
        local_ref[base + at * clusters : base + (at + 1) * clusters, :] = value


def target_kernel(*refs):
    local_refs, (lhs_ref, aug_ref, aug32) = refs[:-3], refs[-3:]
    clusters, _, row_count = aug_ref.shape
    rhs = local_refs[0].shape[0] // clusters - 4
    base = clusters * rhs
    pos = [
        local_refs[0][base + coord * clusters : base + (coord + 1) * clusters, :].astype(jnp.float32)
        for coord in range(3)
    ]
    square = pos[0] * pos[0] + pos[1] * pos[1] + pos[2] * pos[2] + core_radius * core_radius
    ones = jnp.ones_like(square)
    aug32[...] = jnp.zeros(aug32.shape, jnp.float32)
    for row, value in enumerate([-2.0 * value for value in pos] + three_parts(square) + [ones] * 3):
        aug32[:, row, :] = value
    blank = jnp.zeros((LANES - AUG - rhs * len(local_refs), row_count), jnp.bfloat16)
    for cluster in range(clusters):
        aug = aug32[cluster].astype(jnp.bfloat16)
        aug_ref[cluster] = aug
        rows = [ref[cluster * rhs : (cluster + 1) * rhs, :] for ref in local_refs]
        lhs_ref[cluster] = jnp.concatenate([*rows, aug, blank], axis=0).T


def step_kernel(step, length, rhs, subs, first, last, *refs):
    items, source_ref, refs = refs[0], refs[1], refs[2:]
    lhs_refs, aug_refs, refs = refs[:subs], refs[subs : 2 * subs], refs[2 * subs :]
    if not first:
        acc_in, refs = refs[0], refs[1:]
    if last:
        local_refs, refs = refs[:subs], refs[subs:]
        pot_ref, pot_out_ref, grad_ref, back_ref, acc = refs[:5]
        refs = refs[5:]
    else:
        acc, back_ref = refs[:2]
        refs = refs[2:]
    aug32, left_a, left_b, weight, back, raw_a, raw_b, both = refs
    clusters, rows, panels = acc.shape
    width = rows - AUG
    row_count = panels // subs
    quarter = source_ref.shape[1]
    base = clusters * rhs

    starts = [0] + list(range(base + 5 * clusters, source_ref.shape[0], base))

    there = [
        source_ref[base + coord * clusters : base + (coord + 1) * clusters, :].astype(jnp.float32)
        for coord in range(3)
    ]
    area = source_ref[base + 3 * clusters : base + 4 * clusters, :].astype(jnp.float32)
    square = there[0] * there[0] + there[1] * there[1] + there[2] * there[2]
    ones = jnp.ones_like(square)
    aug32[...] = jnp.zeros(aug32.shape, jnp.float32)
    for row, value in enumerate(there + [ones] * 3 + three_parts(square)):
        aug32[:, row, :] = value
    weight[...] = jnp.zeros(weight.shape, jnp.float32)
    weight[:clusters, :] = CP ** (-0.5) * area
    left_a[...] = jnp.zeros(left_a.shape, left_a.dtype)
    left_b[...] = jnp.zeros(left_b.shape, left_b.dtype)
    for cluster in range(clusters):
        distance_rows = aug32[cluster].astype(jnp.bfloat16)
        left_a[cluster, width:rows, quarter:] = distance_rows
        left_b[cluster, width:rows, :quarter] = distance_rows
        for place, at in enumerate(starts):
            span = slice(place * rhs, (place + 1) * rhs)
            dens = source_ref[at + cluster * rhs : at + (cluster + 1) * rhs, :]
            left_a[cluster, span, :quarter] = dens
            left_b[cluster, span, quarter:] = dens
    back[...] = jnp.zeros(back.shape, jnp.float32)
    if first:
        acc[...] = jnp.zeros(acc.shape, jnp.float32)
    else:
        acc[...] = acc_in[...]
    raw_b[...] = jnp.ones(raw_b.shape, jnp.float32)
    both[:, : 2 * quarter] = jnp.zeros((panels, 2 * quarter), both.dtype)

    halves = [slice(at * quarter, (at + 1) * quarter) for at in range(4)]

    def decoded(place):
        code = items[step * length + place]
        return code // (2 * clusters), code % (2 * clusters)

    part = LANES
    spans = [slice(start, start + part) for start in range(0, panels, part)]

    def products(place, left, raw, span):
        here, mate = decoded(place)
        lhs = jnp.concatenate([ref[here] for ref in lhs_refs], axis=0)[span]
        raw[span, :] = jnp.dot(lhs, left[mate % clusters], preferred_element_type=jnp.float32)

    def pointwise(place, raw, raw_halves, both_halves, span):
        _, mate = decoded(place)
        scale = weight[pl.ds(mate, 1), :]
        for start in range(span.start, span.stop, LANES):
            piece = slice(start, start + LANES)
            inverse = lax.rsqrt(raw[piece, raw_halves[1]])
            kernel = scale * inverse
            both[piece, both_halves[0]] = kernel.astype(jnp.bfloat16)
            weighted = (inverse * inverse) * (kernel * raw[piece, raw_halves[0]])
            both[piece, both_halves[1]] = weighted.astype(jnp.bfloat16)

    def summed(place, left, columns, span):
        here, mate = decoded(place)
        acc[here, :, span] += lax.dot_general(
            left[mate % clusters, :rows, :],
            both[span, columns],
            (((1,), (1,)), ((), ())),
            preferred_element_type=jnp.float32,
        )

    def source_sums(place):
        (here_a, mate_a), (here_b, mate_b) = decoded(place), decoded(place + 1)
        aug = jnp.concatenate(
            [
                jnp.concatenate([ref[here] for ref in aug_refs], axis=1)
                for here in (here_a, here_b)
            ],
            axis=0,
        )
        sums = jnp.dot(aug, both[:, quarter : 3 * quarter], preferred_element_type=jnp.float32)
        back[mate_a % clusters] += sums[:AUG, :quarter]
        back[mate_b % clusters] += sums[AUG:, quarter:]

    forward, backward = (halves[0], halves[1]), (halves[1], halves[0])
    columns_a, columns_b = slice(0, 2 * quarter), slice(2 * quarter, 4 * quarter)

    @pl.loop(0, items[step * length])
    def _(pair):
        turn = 2 * pair + 1
        for span in spans:
            summed(turn, left_a, columns_a, span)
            pointwise(turn + 1, raw_b, backward, (halves[3], halves[2]), span)
            products(turn + 2, left_a, raw_a, span)
        source_sums(turn)
        for span in spans:
            summed(turn + 1, left_b, columns_b, span)
            pointwise(turn + 2, raw_a, forward, (halves[0], halves[1]), span)
            products(turn + 3, left_b, raw_b, span)

    for coord in range(3):
        back_ref[coord] = -0.5 * back[:, coord, :] - there[coord] * back[:, 6, :]
    if last:
        for coord in range(3):
            span = slice(base + coord * clusters, base + (coord + 1) * clusters)
            pos = [ref[span, :] for ref in local_refs]
            pos = jnp.concatenate(pos, axis=1).astype(jnp.float32)
            grad_ref[coord] = acc[:, width + coord, :] - pos * acc[:, width + 3, :]
        pot_ref[...] = acc[:, :rhs, :]
        pot_out_ref[...] = acc[:, rhs:width, :].astype(jnp.bfloat16)


def run_step(step, length, items, source, targets, locals_, rhs, width, carried, last):
    lhss, augs = zip(*targets)
    clusters, _, row_count = augs[0].shape
    subs = len(targets)
    panels = subs * row_count
    quarter = source.shape[1]
    first = carried is None
    vmem = pl.BlockSpec(memory_space=pltpu.VMEM)
    smem = pl.BlockSpec(memory_space=pltpu.SMEM)
    operands = (items, source, *lhss, *augs)
    if not first:
        operands += (carried,)
    acc_shape = (clusters, width + AUG, panels)
    back_shape = jax.ShapeDtypeStruct((3, clusters, quarter), jnp.float32)
    scratch = [
        pltpu.VMEM((clusters, AUG, quarter), jnp.float32),
        pltpu.VMEM((clusters, LANES, 2 * quarter), jnp.bfloat16),
        pltpu.VMEM((clusters, LANES, 2 * quarter), jnp.bfloat16),
        pltpu.VMEM((clusters + 8, quarter), jnp.float32),
        pltpu.VMEM((clusters, AUG, quarter), jnp.float32),
    ]
    scratch += [pltpu.VMEM((panels, 2 * quarter), jnp.float32)] * 2
    scratch += [pltpu.VMEM((panels, 4 * quarter), jnp.bfloat16)]
    if last:
        operands += tuple(locals_)
        out_shape = (
            jax.ShapeDtypeStruct((clusters, rhs, panels), jnp.float32),
            jax.ShapeDtypeStruct((clusters, width - rhs, panels), jnp.bfloat16),
            jax.ShapeDtypeStruct((3, clusters, panels), jnp.float32),
            back_shape,
        )
        scratch = [pltpu.VMEM(acc_shape, jnp.float32)] + scratch
    else:
        out_shape = (jax.ShapeDtypeStruct(acc_shape, jnp.float32), back_shape)
    pairs = (length - 6) * panels * quarter
    return pl.pallas_call(
        functools.partial(step_kernel, step, length, rhs, subs, first, last),
        out_shape=out_shape,
        in_specs=[smem] + [vmem] * (len(operands) - 1),
        out_specs=(vmem,) * len(out_shape),
        scratch_shapes=scratch,
        compiler_params=pltpu.CompilerParams(vmem_limit_bytes=20 * 1024 * 1024),
        cost_estimate=pl.CostEstimate(
            flops=2 * pairs * (2 * width + 3 * AUG), bytes_accessed=6 * 2**20, transcendentals=pairs
        ),
        name=f"near_field_{step}",
    )(*operands)


def node_kernel(grad_ref, jitter_ref, edge_ref, main_ref):
    clusters, panels = jitter_ref.shape
    wide = panels + 2 * LANES

    def spread_of(terms, jitter):
        side = jnp.zeros((terms.shape[0], LANES), jnp.float32)
        terms = 0.25 * terms
        spread = jnp.zeros((terms.shape[0], wide), jnp.float32)
        for offset in range(-jitter_reach, jitter_reach + 1):
            masked = jnp.where(jitter == offset, terms, 0.0)
            masked = jnp.concatenate([side, masked, side], axis=1)
            spread = spread + pltpu.roll(masked, offset % wide, 1)
        spread = spread + pltpu.roll(spread, 1, 1)
        return spread + pltpu.roll(spread, 32, 1)

    jitter = jitter_ref[...]
    row_at = lax.broadcasted_iota(jnp.int32, (clusters, LANES), 0)
    edge = edge_ref[...]
    edge_at = lax.broadcasted_iota(jnp.int32, edge.shape, 0)
    edge_jitter = jnp.where(edge_at < 3, edge[6:7], edge[7:8]).astype(jnp.int32)
    edge = spread_of(edge, edge_jitter)
    for coord in range(3):
        spread = spread_of(grad_ref[coord], jitter)
        below = spread[:, :LANES]
        above = spread[:, LANES + panels :]
        inner = spread[:, LANES : LANES + panels]
        before = edge[coord : coord + 1, LANES + panels :]
        after = edge[3 + coord : 4 + coord, :LANES]
        first = jnp.where(row_at == 0, before, pltpu.roll(above, 1, 0))
        last = jnp.where(row_at == clusters - 1, after, pltpu.roll(below, clusters - 1, 0))
        inner = jnp.concatenate(
            [
                inner[:, :LANES] + first,
                inner[:, LANES : panels - LANES],
                inner[:, panels - LANES :] + last,
            ],
            axis=1,
        )
        for cluster in range(clusters):
            main_ref[coord : coord + 1, cluster * panels : (cluster + 1) * panels] = inner[
                cluster : cluster + 1
            ]


def sum_kernel(*refs):
    total = refs[0][...]
    for ref in refs[1:-1]:
        total = total + ref[...].astype(jnp.float32)
    refs[-1][...] = total.astype(jnp.bfloat16)


def on_device(positions, areas, density, cotangent, matching, connect):
    clus_count = lax.axis_size("clus")
    sub_count = lax.axis_size("sub")
    rhs_count = lax.axis_size("rhs")
    device = lax.axis_index("clus")
    sub_place = lax.axis_index("sub")
    core = lax.axis_index("rhs")
    clusters, rhs, row_count = density.shape
    panels = row_count * sub_count
    quarter = row_count // rhs_count
    width = rhs * rhs_count
    vmem = pl.BlockSpec(memory_space=pltpu.VMEM)

    nodes_total = clus_count * clusters * panels

    by_coord = jnp.transpose(positions, (1, 0, 2))
    arguments = [
        pltpu.with_memory_space_constraint(array, pltpu.HBM)
        for array in (density, by_coord, areas, connect, cotangent)
    ]
    shapes = [(clusters * (rhs + 5), quarter)] + [(clusters * rhs, quarter)] * (rhs_count - 1)
    shapes.append((clusters * (rhs + 4), row_count))
    *parts, local = pl.pallas_call(
        functools.partial(prepare_kernel, (panels, nodes_total)),
        out_shape=[jax.ShapeDtypeStruct(shape, jnp.bfloat16) for shape in shapes],
        in_specs=[pl.BlockSpec(memory_space=pltpu.HBM)] * len(arguments),
        out_specs=[vmem] * len(shapes),
        scratch_shapes=[pltpu.VMEM(array.shape, array.dtype) for array in arguments]
        + [pltpu.SemaphoreType.DMA((len(arguments),))],
        compiler_params=pltpu.CompilerParams(vmem_limit_bytes=16 * 1024 * 1024),
        name="prepare",
    )(*arguments)
    ring = ring_order(clus_count)
    at_place = [ring.index(index) for index in range(clus_count)]
    ring_place = pick(device, at_place)

    def own_parts(parts, steps):
        arrived = [round_ring(parts[0], steps)]
        for step in range(1, rhs_count):

            def goal(z, c, step=step):
                return (ring[(at_place[z] + steps) % clus_count], c + step)

            arrived.append(moved(parts[step], ("clus", "rhs"), goal))
        return arrived

    arrived = own_parts(parts, 1)

    per_round = 2 * ((clusters // 2 + clus_count - 2) // (clus_count - 1))
    cap = ROUNDS * per_round
    partners = lax.dynamic_slice_in_dim(matching, device * clusters, clusters, 1).reshape(-1)
    here = jnp.tile(jnp.arange(clusters, dtype=jnp.int32), ROUNDS)
    code = here * (2 * clusters) + partners % clusters
    behind = (ring_place - pick(partners // clusters, at_place)) % clus_count
    total_items = ROUNDS * clusters
    order = jnp.arange(total_items, dtype=jnp.int32)
    rank = jnp.sum(
        ((behind[None, :] == behind[:, None]) & (order[None, :] < order[:, None])).astype(jnp.int32),
        axis=1,
    )
    steps = jnp.arange(1, clus_count, dtype=jnp.int32)
    member = behind[None, :] == steps[:, None]
    slots = jnp.arange(cap, dtype=jnp.int32)
    chosen = member[:, None, :] & (rank[None, None, :] == slots[None, :, None])
    listed = jnp.sum(jnp.where(chosen, code[None, None, :] - clusters, 0), axis=2) + clusters
    turns = (jnp.sum(member.astype(jnp.int32), axis=1) + 3) // 2
    length = cap + 6
    items = jnp.pad(listed, ((0, 0), (3, 3)), constant_values=clusters)
    items = jnp.concatenate([turns[:, None], items[:, 1:]], axis=1).reshape(-1)

    locals_ = [local] + [shifted(local, "sub", step) for step in range(1, sub_count)]
    blocks = [
        [block] + [shifted(block, "rhs", step) for step in range(1, rhs_count)] for block in locals_
    ]

    def in_order(blocks):
        return jnp.concatenate(
            [pick((sub_place - place) % sub_count, blocks) for place in range(sub_count)], axis=-1
        )

    jitter_all = in_order([block[clusters * (rhs + 3) :] for block in locals_]).astype(jnp.int32)
    targets = [
        pl.pallas_call(
            target_kernel,
            out_shape=(
                jax.ShapeDtypeStruct((clusters, row_count, LANES), jnp.bfloat16),
                jax.ShapeDtypeStruct((clusters, AUG, row_count), jnp.bfloat16),
            ),
            in_specs=[vmem] * rhs_count,
            out_specs=(vmem, vmem),
            scratch_shapes=[pltpu.VMEM((clusters, AUG, row_count), jnp.float32)],
            compiler_params=pltpu.CompilerParams(vmem_limit_bytes=16 * 1024 * 1024),
            cost_estimate=pl.CostEstimate(flops=2**20, bytes_accessed=2**18, transcendentals=0),
            name=f"targets_{place}",
        )(*blocks[place])
        for place in range(sub_count)
    ]

    arrived, targets = lax.optimization_barrier((arrived, targets))
    source = jnp.concatenate(arrived, axis=0)
    source, parts = lax.optimization_barrier((source, parts))
    from_next = own_parts(parts, -1) if clus_count > 2 else None
    carried = None
    backs, jitter_rows = [], [None]
    for step in range(1, clus_count):
        if 1 < step < clus_count - 1:
            if step > 2:
                source, backs[step - 3] = lax.optimization_barrier((source, backs[step - 3]))
            source = round_ring(source, 1)
        elif step > 1:
            from_next, backs[-1] = lax.optimization_barrier((from_next, backs[-1]))
            source = jnp.concatenate(from_next, axis=0)
        last = step == clus_count - 1
        results = run_step(
            step - 1, length, items, source, targets, locals_, rhs, width, carried, last
        )
        if last:
            pot, pot_out, grad, back = results
        else:
            carried, back = results
        backs.append(back)
        at = clusters * (rhs + 4)
        jitter_rows.append(source[at : at + clusters])

    grad = in_order([grad[..., at * row_count : (at + 1) * row_count] for at in range(sub_count)])
    low_part = (sub_place == 0) & (core == 0)
    high_part = (sub_place == sub_count - 1) & (core == rhs_count - 1)
    uppers = [grad[:, -1, -quarter:]] + [jnp.where(high_part, back[:, -1], 0.0) for back in backs]
    lowers = [grad[:, 0, :quarter]] + [jnp.where(low_part, back[:, 0], 0.0) for back in backs]

    def step_between(index, owner):
        return (at_place[index] - at_place[owner % clus_count]) % clus_count

    def needed(parts, step, offset):
        choices = []
        for index in range(clus_count):
            goal = ring[(at_place[index] - step) % clus_count]
            choices.append(parts[step_between(index, goal + offset)])
        return pick(device, choices)

    nothing = jnp.zeros((2, quarter), jnp.float32)
    returned = jnp.zeros((3, clusters, quarter), jnp.float32)
    upper, lower = needed(uppers, 0, -1), needed(lowers, 0, 1)
    for step in range(1, clus_count):
        rows = [
            backs[step - 1].reshape(3 * clusters, quarter),
            needed(uppers, step, -1),
            needed(lowers, step, 1),
            nothing,
        ]
        home = round_ring(jnp.concatenate(rows, axis=0), -step)
        returned = returned + home[: 3 * clusters].reshape(returned.shape)
        upper = upper + home[3 * clusters : 3 * clusters + 3]
        lower = lower + home[3 * clusters + 3 : 3 * clusters + 6]

    half = pot
    for step in range(1, rhs_count):
        arrived = shifted(pot_out[:, (step - 1) * rhs : step * rhs], "rhs", -step)
        half = half + arrived.astype(jnp.float32)

    half, grad = lax.optimization_barrier((half, grad))
    found = [half[..., :row_count]]
    for step in range(1, sub_count):
        sent = half[..., step * row_count : (step + 1) * row_count].astype(jnp.bfloat16)
        found.append(shifted(sent, "sub", -step))

    quarter_at = sub_place * rhs_count + core
    grad = grad + jnp.concatenate(
        [jnp.where(quarter_at == at, returned, 0.0) for at in range(sub_count * rhs_count)], axis=-1
    )
    share = clusters // sub_count

    blank = jnp.zeros((3, panels - quarter), jnp.float32)
    before = jnp.concatenate([blank, upper], axis=1)
    after = jnp.concatenate([lower, blank], axis=1)
    jitter_float = jitter_all.astype(jnp.float32)
    jitter_before = jnp.concatenate(
        [blank[:1], needed(jitter_rows, 0, -1)[clusters - 1 :].astype(jnp.float32)], axis=1
    )
    jitter_after = jnp.concatenate(
        [needed(jitter_rows, 0, 1)[:1].astype(jnp.float32), blank[:1]], axis=1
    )

    def edge_rows(at):
        first, end = at * share, (at + 1) * share
        inside = at < sub_count - 1
        return jnp.concatenate(
            [
                grad[:, first - 1] if at > 0 else before,
                grad[:, end] if inside else after,
                jnp.where(high_part, jitter_float[first - 1 : first] if at > 0 else jitter_before, 0.0),
                jnp.where(low_part, jitter_float[end : end + 1] if inside else jitter_after, 0.0),
            ],
            axis=0,
        ).reshape(-1, share, panels)

    def packed(place):
        return pick(
            place % sub_count,
            [
                jnp.concatenate([grad[:, at * share : (at + 1) * share], edge_rows(at)], axis=0)
                for at in range(sub_count)
            ],
        )

    summed = packed(sub_place)
    for step in range(1, sub_count):
        summed = summed + shifted(packed(sub_place + step), "sub", step)
    gathered = summed
    for step in range(1, rhs_count):
        gathered = gathered + shifted(summed, "rhs", step)
    own_jitter = pick(
        sub_place, [jitter_all[at * share : (at + 1) * share] for at in range(sub_count)]
    )
    node_grad = pl.pallas_call(
        node_kernel,
        out_shape=jax.ShapeDtypeStruct((3, share * panels), jnp.float32),
        in_specs=[vmem] * 3,
        out_specs=vmem,
        compiler_params=pltpu.CompilerParams(vmem_limit_bytes=16 * 1024 * 1024),
        cost_estimate=pl.CostEstimate(flops=2**20, bytes_accessed=2**18, transcendentals=0),
        name="node_terms",
    )(gathered[:3], own_jitter, gathered[3:].reshape(8, panels))
    potential = pl.pallas_call(
        sum_kernel,
        out_shape=jax.ShapeDtypeStruct((clusters, rhs, row_count), jnp.bfloat16),
        in_specs=[vmem] * sub_count,
        out_specs=vmem,
        compiler_params=pltpu.CompilerParams(vmem_limit_bytes=16 * 1024 * 1024),
        cost_estimate=pl.CostEstimate(flops=2**20, bytes_accessed=2**18, transcendentals=0),
        name="potential_sum",
    )(*found)
    return (potential, node_grad)


def solution(mesh):
    placed = (
        P(("groups", "clus"), None, "sub"),
        P(("groups", "clus"), "sub"),
        P(("groups", "clus"), "rhs", "sub"),
        P(("groups", "clus"), "rhs", "sub"),
        P(None, "groups"),
        P(("groups", "clus"), None, "sub"),
    )
    return jax.shard_map(
        on_device,
        mesh=mesh,
        in_specs=placed,
        out_specs=(P(("groups", "clus"), "rhs", "sub"), P(None, ("groups", "clus", "sub"))),
        check_vma=False,
    )
```

```python
import functools

import jax
import jax.numpy as jnp
from jax import lax
from jax.experimental import pallas as pl
from jax.experimental.pallas import tpu as pltpu
from jax.sharding import PartitionSpec as P

CP = 512
ROUNDS = 5

core_radius = 0.25
jitter_reach = 8
LANES = 128
AUG = 16


def shifted(value, axis, steps):
    count = lax.axis_size(axis)
    pairs = [(source, (source + steps) % count) for source in range(count)]
    return lax.ppermute(value, axis, pairs)


def ring_order(count):
    return [*range(0, count, 2), *reversed(range(1, count, 2))]


def round_ring(value, steps):
    order = ring_order(lax.axis_size("clus"))
    pairs = [(source, order[(at + steps) % len(order)]) for at, source in enumerate(order)]
    return lax.ppermute(value, "clus", pairs)


def moved(value, axes, target):
    counts = [lax.axis_size(axis) for axis in axes]
    pairs = []
    for major in range(counts[0]):
        for minor in range(counts[1]):
            goal = target(major, minor)
            if goal is not None:
                to_major, to_minor = goal[0] % counts[0], goal[1] % counts[1]
                pairs.append((major * counts[1] + minor, to_major * counts[1] + to_minor))
    return lax.ppermute(value, axes, pairs)


def three_parts(value):
    parts = []
    for _ in range(3):
        part = value.astype(jnp.bfloat16).astype(jnp.float32)
        parts.append(part)
        value = value - part
    return parts


def pick(index, choices):
    out = choices[0]
    for place in range(1, len(choices)):
        out = jnp.where(index == place, choices[place], out)
    return out


def fetched(arguments, places, sems):
    copies = []
    for at, (argument, place) in enumerate(zip(arguments, places)):
        copies.append(pltpu.make_async_copy(argument, place, sems.at[at]))
        copies[-1].start()
    for copy in copies:
        copy.wait()


def jitter_of(connect_ref, sizes):
    clusters, _, row_count = connect_ref.shape
    panels, nodes_total = sizes
    first_id = clusters * panels * lax.axis_index("clus") + row_count * lax.axis_index("sub")
    ids = lax.broadcasted_iota(jnp.int32, (clusters, row_count), 0) * panels
    ids = ids + lax.broadcasted_iota(jnp.int32, (clusters, row_count), 1) + first_id
    jitter = connect_ref[:, 0, :] - ids
    jitter = jnp.where(jitter > jitter_reach, jitter - nodes_total, jitter)
    jitter = jnp.where(jitter < -jitter_reach, jitter + nodes_total, jitter)
    return jitter.astype(jnp.float32).astype(jnp.bfloat16)


def prepare_kernel(sizes, *refs):
    arguments, part_refs, local_ref, scratch = refs[:5], refs[5:-7], refs[-7], refs[-6:]
    fetched(arguments, scratch[:5], scratch[5])
    density_ref, by_coord_ref, areas_ref, connect_ref, cot_ref = scratch[:5]
    clusters, rhs, _ = density_ref.shape
    quarter = part_refs[0].shape[1]
    count = len(part_refs)
    core = lax.axis_index("rhs")

    def part_of(array, place):
        return pick(place, [array[:, at * quarter : (at + 1) * quarter] for at in range(count)])

    pos = [by_coord_ref[coord] for coord in range(3)]
    jitter = jitter_of(connect_ref, sizes)
    base = clusters * rhs
    for cluster in range(clusters):
        dens = density_ref[cluster]
        span = slice(cluster * rhs, (cluster + 1) * rhs)
        local_ref[span, :] = cot_ref[cluster]
        for step, part_ref in enumerate(part_refs):
            part_ref[span, :] = part_of(dens, (core + step) % count)
    for at, value in enumerate([*pos, areas_ref[...], jitter]):
        part_refs[0][base + at * clusters : base + (at + 1) * clusters, :] = part_of(value, core)
    for at, value in enumerate([*pos, jitter]):
        local_ref[base + at * clusters : base + (at + 1) * clusters, :] = value


def target_kernel(*refs):
    local_refs, (lhs_ref, aug_ref, aug32) = refs[:-3], refs[-3:]
    clusters, _, row_count = aug_ref.shape
    rhs = local_refs[0].shape[0] // clusters - 4
    base = clusters * rhs
    pos = [
        local_refs[0][base + coord * clusters : base + (coord + 1) * clusters, :].astype(jnp.float32)
        for coord in range(3)
    ]
    square = pos[0] * pos[0] + pos[1] * pos[1] + pos[2] * pos[2] + core_radius * core_radius
    ones = jnp.ones_like(square)
    aug32[...] = jnp.zeros(aug32.shape, jnp.float32)
    for row, value in enumerate([-2.0 * value for value in pos] + three_parts(square) + [ones] * 3):
        aug32[:, row, :] = value
    blank = jnp.zeros((LANES - AUG - rhs * len(local_refs), row_count), jnp.bfloat16)
    for cluster in range(clusters):
        aug = aug32[cluster].astype(jnp.bfloat16)
        aug_ref[cluster] = aug
        rows = [ref[cluster * rhs : (cluster + 1) * rhs, :] for ref in local_refs]
        lhs_ref[cluster] = jnp.concatenate([*rows, aug, blank], axis=0).T


def step_kernel(step, length, rhs, subs, first, last, *refs):
    items, source_ref, refs = refs[0], refs[1], refs[2:]
    lhs_refs, aug_refs, refs = refs[:subs], refs[subs : 2 * subs], refs[2 * subs :]
    if not first:
        acc_in, refs = refs[0], refs[1:]
    if last:
        local_refs, refs = refs[:subs], refs[subs:]
        pot_ref, pot_out_ref, grad_ref, back_ref, acc = refs[:5]
        refs = refs[5:]
    else:
        acc, back_ref = refs[:2]
        refs = refs[2:]
    aug32, left_a, left_b, weight, back, raw_a, raw_b, both = refs
    clusters, rows, panels = acc.shape
    width = rows - AUG
    row_count = panels // subs
    quarter = source_ref.shape[1]
    base = clusters * rhs

    starts = [0] + list(range(base + 5 * clusters, source_ref.shape[0], base))

    there = [
        source_ref[base + coord * clusters : base + (coord + 1) * clusters, :].astype(jnp.float32)
        for coord in range(3)
    ]
    area = source_ref[base + 3 * clusters : base + 4 * clusters, :].astype(jnp.float32)
    square = there[0] * there[0] + there[1] * there[1] + there[2] * there[2]
    ones = jnp.ones_like(square)
    aug32[...] = jnp.zeros(aug32.shape, jnp.float32)
    for row, value in enumerate(there + [ones] * 3 + three_parts(square)):
        aug32[:, row, :] = value
    weight[...] = jnp.zeros(weight.shape, jnp.float32)
    weight[:clusters, :] = CP ** (-0.5) * area
    left_a[...] = jnp.zeros(left_a.shape, left_a.dtype)
    left_b[...] = jnp.zeros(left_b.shape, left_b.dtype)
    for cluster in range(clusters):
        distance_rows = aug32[cluster].astype(jnp.bfloat16)
        left_a[cluster, width:rows, quarter:] = distance_rows
        left_b[cluster, width:rows, :quarter] = distance_rows
        for place, at in enumerate(starts):
            span = slice(place * rhs, (place + 1) * rhs)
            dens = source_ref[at + cluster * rhs : at + (cluster + 1) * rhs, :]
            left_a[cluster, span, :quarter] = dens
            left_b[cluster, span, quarter:] = dens
    back[...] = jnp.zeros(back.shape, jnp.float32)
    if first:
        acc[...] = jnp.zeros(acc.shape, jnp.float32)
    else:
        acc[...] = acc_in[...]
    raw_b[...] = jnp.ones(raw_b.shape, jnp.float32)
    both[:, : 2 * quarter] = jnp.zeros((panels, 2 * quarter), both.dtype)

    halves = [slice(at * quarter, (at + 1) * quarter) for at in range(4)]

    def decoded(place):
        code = items[step * length + place]
        return code // (2 * clusters), code % (2 * clusters)

    part = max(2 * LANES, panels // 2)
    spans = [slice(start, start + part) for start in range(0, panels, part)]

    def products(place, left, raw, span):
        here, mate = decoded(place)
        lhs = jnp.concatenate([ref[here] for ref in lhs_refs], axis=0)[span]
        raw[span, :] = jnp.dot(lhs, left[mate % clusters], preferred_element_type=jnp.float32)

    def pointwise(place, raw, raw_halves, both_halves, span):
        _, mate = decoded(place)
        scale = weight[pl.ds(mate, 1), :]
        for start in range(span.start, span.stop, LANES):
            piece = slice(start, start + LANES)
            inverse = lax.rsqrt(raw[piece, raw_halves[1]])
            kernel = scale * inverse
            both[piece, both_halves[0]] = kernel.astype(jnp.bfloat16)
            weighted = (inverse * inverse) * (kernel * raw[piece, raw_halves[0]])
            both[piece, both_halves[1]] = weighted.astype(jnp.bfloat16)

    def summed(place, left, columns, span):
        here, mate = decoded(place)
        acc[here, :, span] += lax.dot_general(
            left[mate % clusters, :rows, :],
            both[span, columns],
            (((1,), (1,)), ((), ())),
            preferred_element_type=jnp.float32,
        )

    def source_sums(place, span):
        aug = [
            jnp.concatenate([ref[decoded(at)[0]] for ref in aug_refs], axis=1)[:, span]
            for at in (place, place + 1)
        ]
        return jnp.dot(
            jnp.concatenate(aug, axis=0),
            both[span, quarter : 3 * quarter],
            preferred_element_type=jnp.float32,
        )

    forward, backward = (halves[0], halves[1]), (halves[1], halves[0])
    columns_a, columns_b = slice(0, 2 * quarter), slice(2 * quarter, 4 * quarter)

    @pl.loop(0, items[step * length])
    def _(pair):
        turn = 2 * pair + 1
        for span in spans:
            summed(turn, left_a, columns_a, span)
            pointwise(turn + 1, raw_b, backward, (halves[3], halves[2]), span)
            products(turn + 2, left_a, raw_a, span)
        sums = jnp.zeros((2 * AUG, 2 * quarter), jnp.float32)
        for span in spans:
            sums = sums + source_sums(turn, span)
            summed(turn + 1, left_b, columns_b, span)
            pointwise(turn + 2, raw_a, forward, (halves[0], halves[1]), span)
            products(turn + 3, left_b, raw_b, span)
        back[decoded(turn)[1] % clusters] += sums[:AUG, :quarter]
        back[decoded(turn + 1)[1] % clusters] += sums[AUG:, quarter:]

    for coord in range(3):
        back_ref[coord] = -0.5 * back[:, coord, :] - there[coord] * back[:, 6, :]
    if last:
        for coord in range(3):
            span = slice(base + coord * clusters, base + (coord + 1) * clusters)
            pos = [ref[span, :] for ref in local_refs]
            pos = jnp.concatenate(pos, axis=1).astype(jnp.float32)
            grad_ref[coord] = acc[:, width + coord, :] - pos * acc[:, width + 3, :]
        pot_ref[...] = acc[:, :rhs, :]
        pot_out_ref[...] = acc[:, rhs:width, :].astype(jnp.bfloat16)


def run_step(step, length, items, source, targets, locals_, rhs, width, carried, last):
    lhss, augs = zip(*targets)
    clusters, _, row_count = augs[0].shape
    subs = len(targets)
    panels = subs * row_count
    quarter = source.shape[1]
    first = carried is None
    vmem = pl.BlockSpec(memory_space=pltpu.VMEM)
    smem = pl.BlockSpec(memory_space=pltpu.SMEM)
    operands = (items, source, *lhss, *augs)
    if not first:
        operands += (carried,)
    acc_shape = (clusters, width + AUG, panels)
    back_shape = jax.ShapeDtypeStruct((3, clusters, quarter), jnp.float32)
    scratch = [
        pltpu.VMEM((clusters, AUG, quarter), jnp.float32),
        pltpu.VMEM((clusters, LANES, 2 * quarter), jnp.bfloat16),
        pltpu.VMEM((clusters, LANES, 2 * quarter), jnp.bfloat16),
        pltpu.VMEM((clusters + 8, quarter), jnp.float32),
        pltpu.VMEM((clusters, AUG, quarter), jnp.float32),
    ]
    scratch += [pltpu.VMEM((panels, 2 * quarter), jnp.float32)] * 2
    scratch += [pltpu.VMEM((panels, 4 * quarter), jnp.bfloat16)]
    if last:
        operands += tuple(locals_)
        out_shape = (
            jax.ShapeDtypeStruct((clusters, rhs, panels), jnp.float32),
            jax.ShapeDtypeStruct((clusters, width - rhs, panels), jnp.bfloat16),
            jax.ShapeDtypeStruct((3, clusters, panels), jnp.float32),
            back_shape,
        )
        scratch = [pltpu.VMEM(acc_shape, jnp.float32)] + scratch
    else:
        out_shape = (jax.ShapeDtypeStruct(acc_shape, jnp.float32), back_shape)
    pairs = (length - 6) * panels * quarter
    return pl.pallas_call(
        functools.partial(step_kernel, step, length, rhs, subs, first, last),
        out_shape=out_shape,
        in_specs=[smem] + [vmem] * (len(operands) - 1),
        out_specs=(vmem,) * len(out_shape),
        scratch_shapes=scratch,
        compiler_params=pltpu.CompilerParams(vmem_limit_bytes=20 * 1024 * 1024),
        cost_estimate=pl.CostEstimate(
            flops=2 * pairs * (2 * width + 3 * AUG), bytes_accessed=6 * 2**20, transcendentals=pairs
        ),
        name=f"near_field_{step}",
    )(*operands)


def node_kernel(grad_ref, jitter_ref, edge_ref, main_ref):
    clusters, panels = jitter_ref.shape
    wide = panels + 2 * LANES

    def spread_of(terms, jitter):
        side = jnp.zeros((terms.shape[0], LANES), jnp.float32)
        terms = 0.25 * terms
        spread = jnp.zeros((terms.shape[0], wide), jnp.float32)
        for offset in range(-jitter_reach, jitter_reach + 1):
            masked = jnp.where(jitter == offset, terms, 0.0)
            masked = jnp.concatenate([side, masked, side], axis=1)
            spread = spread + pltpu.roll(masked, offset % wide, 1)
        spread = spread + pltpu.roll(spread, 1, 1)
        return spread + pltpu.roll(spread, 32, 1)

    jitter = jitter_ref[...]
    row_at = lax.broadcasted_iota(jnp.int32, (clusters, LANES), 0)
    edge = edge_ref[...]
    edge_at = lax.broadcasted_iota(jnp.int32, edge.shape, 0)
    edge_jitter = jnp.where(edge_at < 3, edge[6:7], edge[7:8]).astype(jnp.int32)
    edge = spread_of(edge, edge_jitter)
    for coord in range(3):
        spread = spread_of(grad_ref[coord], jitter)
        below = spread[:, :LANES]
        above = spread[:, LANES + panels :]
        inner = spread[:, LANES : LANES + panels]
        before = edge[coord : coord + 1, LANES + panels :]
        after = edge[3 + coord : 4 + coord, :LANES]
        first = jnp.where(row_at == 0, before, pltpu.roll(above, 1, 0))
        last = jnp.where(row_at == clusters - 1, after, pltpu.roll(below, clusters - 1, 0))
        inner = jnp.concatenate(
            [
                inner[:, :LANES] + first,
                inner[:, LANES : panels - LANES],
                inner[:, panels - LANES :] + last,
            ],
            axis=1,
        )
        for cluster in range(clusters):
            main_ref[coord : coord + 1, cluster * panels : (cluster + 1) * panels] = inner[
                cluster : cluster + 1
            ]


def sum_kernel(*refs):
    total = refs[0][...]
    for ref in refs[1:-1]:
        total = total + ref[...].astype(jnp.float32)
    refs[-1][...] = total.astype(jnp.bfloat16)


def on_device(positions, areas, density, cotangent, matching, connect):
    clus_count = lax.axis_size("clus")
    sub_count = lax.axis_size("sub")
    rhs_count = lax.axis_size("rhs")
    device = lax.axis_index("clus")
    sub_place = lax.axis_index("sub")
    core = lax.axis_index("rhs")
    clusters, rhs, row_count = density.shape
    panels = row_count * sub_count
    quarter = row_count // rhs_count
    width = rhs * rhs_count
    vmem = pl.BlockSpec(memory_space=pltpu.VMEM)

    nodes_total = clus_count * clusters * panels

    by_coord = jnp.transpose(positions, (1, 0, 2))
    arguments = [
        pltpu.with_memory_space_constraint(array, pltpu.HBM)
        for array in (density, by_coord, areas, connect, cotangent)
    ]
    shapes = [(clusters * (rhs + 5), quarter)] + [(clusters * rhs, quarter)] * (rhs_count - 1)
    shapes.append((clusters * (rhs + 4), row_count))
    *parts, local = pl.pallas_call(
        functools.partial(prepare_kernel, (panels, nodes_total)),
        out_shape=[jax.ShapeDtypeStruct(shape, jnp.bfloat16) for shape in shapes],
        in_specs=[pl.BlockSpec(memory_space=pltpu.HBM)] * len(arguments),
        out_specs=[vmem] * len(shapes),
        scratch_shapes=[pltpu.VMEM(array.shape, array.dtype) for array in arguments]
        + [pltpu.SemaphoreType.DMA((len(arguments),))],
        compiler_params=pltpu.CompilerParams(vmem_limit_bytes=16 * 1024 * 1024),
        name="prepare",
    )(*arguments)
    ring = ring_order(clus_count)
    at_place = [ring.index(index) for index in range(clus_count)]
    ring_place = pick(device, at_place)

    def own_parts(parts, steps):
        arrived = [round_ring(parts[0], steps)]
        for step in range(1, rhs_count):

            def goal(z, c, step=step):
                return (ring[(at_place[z] + steps) % clus_count], c + step)

            arrived.append(moved(parts[step], ("clus", "rhs"), goal))
        return arrived

    arrived = own_parts(parts, 1)

    per_round = 2 * ((clusters // 2 + clus_count - 2) // (clus_count - 1))
    cap = ROUNDS * per_round
    partners = lax.dynamic_slice_in_dim(matching, device * clusters, clusters, 1).reshape(-1)
    here = jnp.tile(jnp.arange(clusters, dtype=jnp.int32), ROUNDS)
    code = here * (2 * clusters) + partners % clusters
    behind = (ring_place - pick(partners // clusters, at_place)) % clus_count
    total_items = ROUNDS * clusters
    order = jnp.arange(total_items, dtype=jnp.int32)
    rank = jnp.sum(
        ((behind[None, :] == behind[:, None]) & (order[None, :] < order[:, None])).astype(jnp.int32),
        axis=1,
    )
    steps = jnp.arange(1, clus_count, dtype=jnp.int32)
    member = behind[None, :] == steps[:, None]
    slots = jnp.arange(cap, dtype=jnp.int32)
    chosen = member[:, None, :] & (rank[None, None, :] == slots[None, :, None])
    listed = jnp.sum(jnp.where(chosen, code[None, None, :] - clusters, 0), axis=2) + clusters
    turns = (jnp.sum(member.astype(jnp.int32), axis=1) + 3) // 2
    length = cap + 6
    items = jnp.pad(listed, ((0, 0), (3, 3)), constant_values=clusters)
    items = jnp.concatenate([turns[:, None], items[:, 1:]], axis=1).reshape(-1)

    locals_ = [local] + [shifted(local, "sub", step) for step in range(1, sub_count)]
    blocks = [
        [block] + [shifted(block, "rhs", step) for step in range(1, rhs_count)] for block in locals_
    ]

    def in_order(blocks):
        return jnp.concatenate(
            [pick((sub_place - place) % sub_count, blocks) for place in range(sub_count)], axis=-1
        )

    jitter_all = in_order([block[clusters * (rhs + 3) :] for block in locals_]).astype(jnp.int32)
    targets = [
        pl.pallas_call(
            target_kernel,
            out_shape=(
                jax.ShapeDtypeStruct((clusters, row_count, LANES), jnp.bfloat16),
                jax.ShapeDtypeStruct((clusters, AUG, row_count), jnp.bfloat16),
            ),
            in_specs=[vmem] * rhs_count,
            out_specs=(vmem, vmem),
            scratch_shapes=[pltpu.VMEM((clusters, AUG, row_count), jnp.float32)],
            compiler_params=pltpu.CompilerParams(vmem_limit_bytes=16 * 1024 * 1024),
            cost_estimate=pl.CostEstimate(flops=2**20, bytes_accessed=2**18, transcendentals=0),
            name=f"targets_{place}",
        )(*blocks[place])
        for place in range(sub_count)
    ]

    arrived, targets = lax.optimization_barrier((arrived, targets))
    source = jnp.concatenate(arrived, axis=0)
    source, parts = lax.optimization_barrier((source, parts))
    from_next = own_parts(parts, -1) if clus_count > 2 else None
    carried = None
    backs, jitter_rows = [], [None]
    for step in range(1, clus_count):
        if 1 < step < clus_count - 1:
            if step > 2:
                source, backs[step - 3] = lax.optimization_barrier((source, backs[step - 3]))
            source = round_ring(source, 1)
        elif step > 1:
            from_next, backs[-1] = lax.optimization_barrier((from_next, backs[-1]))
            source = jnp.concatenate(from_next, axis=0)
        last = step == clus_count - 1
        results = run_step(
            step - 1, length, items, source, targets, locals_, rhs, width, carried, last
        )
        if last:
            pot, pot_out, grad, back = results
        else:
            carried, back = results
        backs.append(back)
        at = clusters * (rhs + 4)
        jitter_rows.append(source[at : at + clusters])

    grad = in_order([grad[..., at * row_count : (at + 1) * row_count] for at in range(sub_count)])
    low_part = (sub_place == 0) & (core == 0)
    high_part = (sub_place == sub_count - 1) & (core == rhs_count - 1)
    uppers = [grad[:, -1, -quarter:]] + [jnp.where(high_part, back[:, -1], 0.0) for back in backs]
    lowers = [grad[:, 0, :quarter]] + [jnp.where(low_part, back[:, 0], 0.0) for back in backs]

    def step_between(index, owner):
        return (at_place[index] - at_place[owner % clus_count]) % clus_count

    def needed(parts, step, offset):
        choices = []
        for index in range(clus_count):
            goal = ring[(at_place[index] - step) % clus_count]
            choices.append(parts[step_between(index, goal + offset)])
        return pick(device, choices)

    nothing = jnp.zeros((2, quarter), jnp.float32)
    returned = jnp.zeros((3, clusters, quarter), jnp.float32)
    upper, lower = needed(uppers, 0, -1), needed(lowers, 0, 1)
    for step in range(1, clus_count):
        rows = [
            backs[step - 1].reshape(3 * clusters, quarter),
            needed(uppers, step, -1),
            needed(lowers, step, 1),
            nothing,
        ]
        home = round_ring(jnp.concatenate(rows, axis=0), -step)
        returned = returned + home[: 3 * clusters].reshape(returned.shape)
        upper = upper + home[3 * clusters : 3 * clusters + 3]
        lower = lower + home[3 * clusters + 3 : 3 * clusters + 6]

    half = pot
    for step in range(1, rhs_count):
        arrived = shifted(pot_out[:, (step - 1) * rhs : step * rhs], "rhs", -step)
        half = half + arrived.astype(jnp.float32)

    half, grad = lax.optimization_barrier((half, grad))
    found = [half[..., :row_count]]
    for step in range(1, sub_count):
        sent = half[..., step * row_count : (step + 1) * row_count].astype(jnp.bfloat16)
        found.append(shifted(sent, "sub", -step))

    quarter_at = sub_place * rhs_count + core
    grad = grad + jnp.concatenate(
        [jnp.where(quarter_at == at, returned, 0.0) for at in range(sub_count * rhs_count)], axis=-1
    )
    share = clusters // sub_count

    blank = jnp.zeros((3, panels - quarter), jnp.float32)
    before = jnp.concatenate([blank, upper], axis=1)
    after = jnp.concatenate([lower, blank], axis=1)
    jitter_float = jitter_all.astype(jnp.float32)
    jitter_before = jnp.concatenate(
        [blank[:1], needed(jitter_rows, 0, -1)[clusters - 1 :].astype(jnp.float32)], axis=1
    )
    jitter_after = jnp.concatenate(
        [needed(jitter_rows, 0, 1)[:1].astype(jnp.float32), blank[:1]], axis=1
    )

    def edge_rows(at):
        first, end = at * share, (at + 1) * share
        inside = at < sub_count - 1
        return jnp.concatenate(
            [
                grad[:, first - 1] if at > 0 else before,
                grad[:, end] if inside else after,
                jnp.where(high_part, jitter_float[first - 1 : first] if at > 0 else jitter_before, 0.0),
                jnp.where(low_part, jitter_float[end : end + 1] if inside else jitter_after, 0.0),
            ],
            axis=0,
        ).reshape(-1, share, panels)

    def packed(place):
        return pick(
            place % sub_count,
            [
                jnp.concatenate([grad[:, at * share : (at + 1) * share], edge_rows(at)], axis=0)
                for at in range(sub_count)
            ],
        )

    summed = packed(sub_place)
    for step in range(1, sub_count):
        summed = summed + shifted(packed(sub_place + step), "sub", step)
    gathered = summed
    for step in range(1, rhs_count):
        gathered = gathered + shifted(summed, "rhs", step)
    own_jitter = pick(
        sub_place, [jitter_all[at * share : (at + 1) * share] for at in range(sub_count)]
    )
    node_grad = pl.pallas_call(
        node_kernel,
        out_shape=jax.ShapeDtypeStruct((3, share * panels), jnp.float32),
        in_specs=[vmem] * 3,
        out_specs=vmem,
        compiler_params=pltpu.CompilerParams(vmem_limit_bytes=16 * 1024 * 1024),
        cost_estimate=pl.CostEstimate(flops=2**20, bytes_accessed=2**18, transcendentals=0),
        name="node_terms",
    )(gathered[:3], own_jitter, gathered[3:].reshape(8, panels))
    potential = pl.pallas_call(
        sum_kernel,
        out_shape=jax.ShapeDtypeStruct((clusters, rhs, row_count), jnp.bfloat16),
        in_specs=[vmem] * sub_count,
        out_specs=vmem,
        compiler_params=pltpu.CompilerParams(vmem_limit_bytes=16 * 1024 * 1024),
        cost_estimate=pl.CostEstimate(flops=2**20, bytes_accessed=2**18, transcendentals=0),
        name="potential_sum",
    )(*found)
    return (potential, node_grad)


def solution(mesh):
    placed = (
        P(("groups", "clus"), None, "sub"),
        P(("groups", "clus"), "sub"),
        P(("groups", "clus"), "rhs", "sub"),
        P(("groups", "clus"), "rhs", "sub"),
        P(None, "groups"),
        P(("groups", "clus"), None, "sub"),
    )
    return jax.shard_map(
        on_device,
        mesh=mesh,
        in_specs=placed,
        out_specs=(P(("groups", "clus"), "rhs", "sub"), P(None, ("groups", "clus", "sub"))),
        check_vma=False,
    )
```

```python
import functools

import jax
import jax.numpy as jnp
from jax import lax
from jax.experimental import pallas as pl
from jax.experimental.pallas import tpu as pltpu
from jax.sharding import PartitionSpec as P

CP = 512
ROUNDS = 5

core_radius = 0.25
jitter_reach = 8
LANES = 128
AUG = 16


def shifted(value, axis, steps):
    count = lax.axis_size(axis)
    pairs = [(source, (source + steps) % count) for source in range(count)]
    return lax.ppermute(value, axis, pairs)


def ring_order(count):
    return [*range(0, count, 2), *reversed(range(1, count, 2))]


def round_ring(value, steps):
    order = ring_order(lax.axis_size("clus"))
    pairs = [(source, order[(at + steps) % len(order)]) for at, source in enumerate(order)]
    return lax.ppermute(value, "clus", pairs)


def moved(value, axes, target):
    counts = [lax.axis_size(axis) for axis in axes]
    pairs = []
    for major in range(counts[0]):
        for minor in range(counts[1]):
            goal = target(major, minor)
            if goal is not None:
                to_major, to_minor = goal[0] % counts[0], goal[1] % counts[1]
                pairs.append((major * counts[1] + minor, to_major * counts[1] + to_minor))
    return lax.ppermute(value, axes, pairs)


def three_parts(value):
    parts = []
    for _ in range(3):
        part = value.astype(jnp.bfloat16).astype(jnp.float32)
        parts.append(part)
        value = value - part
    return parts


def pick(index, choices):
    out = choices[0]
    for place in range(1, len(choices)):
        out = jnp.where(index == place, choices[place], out)
    return out


def fetched(arguments, places, sems):
    copies = []
    for at, (argument, place) in enumerate(zip(arguments, places)):
        copies.append(pltpu.make_async_copy(argument, place, sems.at[at]))
        copies[-1].start()
    for copy in copies:
        copy.wait()


def jitter_of(connect_ref, sizes):
    clusters, _, row_count = connect_ref.shape
    panels, nodes_total = sizes
    first_id = clusters * panels * lax.axis_index("clus") + row_count * lax.axis_index("sub")
    ids = lax.broadcasted_iota(jnp.int32, (clusters, row_count), 0) * panels
    ids = ids + lax.broadcasted_iota(jnp.int32, (clusters, row_count), 1) + first_id
    jitter = connect_ref[:, 0, :] - ids
    jitter = jnp.where(jitter > jitter_reach, jitter - nodes_total, jitter)
    jitter = jnp.where(jitter < -jitter_reach, jitter + nodes_total, jitter)
    return jitter.astype(jnp.float32).astype(jnp.bfloat16)


def prepare_kernel(sizes, *refs):
    arguments, part_refs, local_ref, scratch = refs[:5], refs[5:-7], refs[-7], refs[-6:]
    fetched(arguments, scratch[:5], scratch[5])
    density_ref, by_coord_ref, areas_ref, connect_ref, cot_ref = scratch[:5]
    clusters, rhs, _ = density_ref.shape
    quarter = part_refs[0].shape[1]
    count = len(part_refs)
    core = lax.axis_index("rhs")

    def part_of(array, place):
        return pick(place, [array[:, at * quarter : (at + 1) * quarter] for at in range(count)])

    pos = [by_coord_ref[coord] for coord in range(3)]
    jitter = jitter_of(connect_ref, sizes)
    base = clusters * rhs
    for cluster in range(clusters):
        dens = density_ref[cluster]
        span = slice(cluster * rhs, (cluster + 1) * rhs)
        local_ref[span, :] = cot_ref[cluster]
        for step, part_ref in enumerate(part_refs):
            part_ref[span, :] = part_of(dens, (core + step) % count)
    for at, value in enumerate([*pos, areas_ref[...], jitter]):
        part_refs[0][base + at * clusters : base + (at + 1) * clusters, :] = part_of(value, core)
    for at, value in enumerate([*pos, jitter]):
        local_ref[base + at * clusters : base + (at + 1) * clusters, :] = value


def target_kernel(*refs):
    local_refs, (lhs_ref, aug_ref, aug32) = refs[:-3], refs[-3:]
    clusters, _, row_count = aug_ref.shape
    rhs = local_refs[0].shape[0] // clusters - 4
    base = clusters * rhs
    pos = [
        local_refs[0][base + coord * clusters : base + (coord + 1) * clusters, :].astype(jnp.float32)
        for coord in range(3)
    ]
    square = pos[0] * pos[0] + pos[1] * pos[1] + pos[2] * pos[2] + core_radius * core_radius
    ones = jnp.ones_like(square)
    aug32[...] = jnp.zeros(aug32.shape, jnp.float32)
    for row, value in enumerate([-2.0 * value for value in pos] + three_parts(square) + [ones] * 3):
        aug32[:, row, :] = value
    blank = jnp.zeros((LANES - AUG - rhs * len(local_refs), row_count), jnp.bfloat16)
    for cluster in range(clusters):
        aug = aug32[cluster].astype(jnp.bfloat16)
        aug_ref[cluster] = aug
        rows = [ref[cluster * rhs : (cluster + 1) * rhs, :] for ref in local_refs]
        lhs_ref[cluster] = jnp.concatenate([*rows, aug, blank], axis=0).T


def step_kernel(step, length, rhs, subs, first, last, *refs):
    items, source_ref, refs = refs[0], refs[1], refs[2:]
    lhs_refs, aug_refs, refs = refs[:subs], refs[subs : 2 * subs], refs[2 * subs :]
    if not first:
        acc_in, refs = refs[0], refs[1:]
    if last:
        local_refs, refs = refs[:subs], refs[subs:]
        pot_ref, pot_out_ref, grad_ref, back_ref, acc = refs[:5]
        refs = refs[5:]
    else:
        acc, back_ref = refs[:2]
        refs = refs[2:]
    aug32, left_a, left_b, weight, back, raw_a, raw_b, both = refs
    clusters, rows, panels = acc.shape
    width = rows - AUG
    row_count = panels // subs
    quarter = source_ref.shape[1]
    base = clusters * rhs

    starts = [0] + list(range(base + 5 * clusters, source_ref.shape[0], base))

    there = [
        source_ref[base + coord * clusters : base + (coord + 1) * clusters, :].astype(jnp.float32)
        for coord in range(3)
    ]
    area = source_ref[base + 3 * clusters : base + 4 * clusters, :].astype(jnp.float32)
    square = there[0] * there[0] + there[1] * there[1] + there[2] * there[2]
    ones = jnp.ones_like(square)
    aug32[...] = jnp.zeros(aug32.shape, jnp.float32)
    for row, value in enumerate(there + [ones] * 3 + three_parts(square)):
        aug32[:, row, :] = value
    weight[...] = jnp.zeros(weight.shape, jnp.float32)
    weight[:clusters, :] = CP ** (-0.5) * area
    left_a[...] = jnp.zeros(left_a.shape, left_a.dtype)
    left_b[...] = jnp.zeros(left_b.shape, left_b.dtype)
    for cluster in range(clusters):
        distance_rows = aug32[cluster].astype(jnp.bfloat16)
        left_a[cluster, width:rows, quarter:] = distance_rows
        left_b[cluster, width:rows, :quarter] = distance_rows
        for place, at in enumerate(starts):
            span = slice(place * rhs, (place + 1) * rhs)
            dens = source_ref[at + cluster * rhs : at + (cluster + 1) * rhs, :]
            left_a[cluster, span, :quarter] = dens
            left_b[cluster, span, quarter:] = dens
    back[...] = jnp.zeros(back.shape, jnp.float32)
    if first:
        acc[...] = jnp.zeros(acc.shape, jnp.float32)
    else:
        acc[...] = acc_in[...]
    raw_b[...] = jnp.ones(raw_b.shape, jnp.float32)
    both[:, : 2 * quarter] = jnp.zeros((panels, 2 * quarter), both.dtype)

    halves = [slice(at * quarter, (at + 1) * quarter) for at in range(4)]

    def decoded(place):
        code = items[step * length + place]
        return code // (2 * clusters), code % (2 * clusters)

    part = max(2 * LANES, panels // 2)
    spans = [slice(start, start + part) for start in range(0, panels, part)]

    def products(place, left, raw, span):
        here, mate = decoded(place)
        lhs = jnp.concatenate([ref[here] for ref in lhs_refs], axis=0)[span]
        raw[span, :] = jnp.dot(lhs, left[mate % clusters], preferred_element_type=jnp.float32)

    def pointwise(place, raw, raw_halves, both_halves, span):
        _, mate = decoded(place)
        scale = weight[pl.ds(mate, 1), :]
        for start in range(span.start, span.stop, LANES):
            piece = slice(start, start + LANES)
            inverse = lax.rsqrt(raw[piece, raw_halves[1]])
            kernel = scale * inverse
            both[piece, both_halves[0]] = kernel.astype(jnp.bfloat16)
            weighted = (inverse * inverse) * (kernel * raw[piece, raw_halves[0]])
            both[piece, both_halves[1]] = weighted.astype(jnp.bfloat16)

    def summed(place, left, columns, span):
        here, mate = decoded(place)
        acc[here, :, span] += lax.dot_general(
            left[mate % clusters, :rows, :],
            both[span, columns],
            (((1,), (1,)), ((), ())),
            preferred_element_type=jnp.float32,
        )

    def source_sums(place):
        (here_a, mate_a), (here_b, mate_b) = decoded(place), decoded(place + 1)
        aug = jnp.concatenate(
            [
                jnp.concatenate([ref[here] for ref in aug_refs], axis=1)
                for here in (here_a, here_b)
            ],
            axis=0,
        )
        sums = jnp.dot(aug, both[:, quarter : 3 * quarter], preferred_element_type=jnp.float32)
        back[mate_a % clusters] += sums[:AUG, :quarter]
        back[mate_b % clusters] += sums[AUG:, quarter:]

    forward, backward = (halves[0], halves[1]), (halves[1], halves[0])
    columns_a, columns_b = slice(0, 2 * quarter), slice(2 * quarter, 4 * quarter)

    @pl.loop(0, items[step * length])
    def _(pair):
        turn = 2 * pair + 1
        for span in spans:
            early, late = slice(span.start, span.start + LANES), slice(span.start + LANES, span.stop)
            summed(turn, left_a, columns_a, span)
            pointwise(turn + 1, raw_b, backward, (halves[3], halves[2]), early)
            products(turn + 2, left_a, raw_a, span)
            pointwise(turn + 1, raw_b, backward, (halves[3], halves[2]), late)
        source_sums(turn)
        for span in spans:
            early, late = slice(span.start, span.start + LANES), slice(span.start + LANES, span.stop)
            summed(turn + 1, left_b, columns_b, span)
            pointwise(turn + 2, raw_a, forward, (halves[0], halves[1]), early)
            products(turn + 3, left_b, raw_b, span)
            pointwise(turn + 2, raw_a, forward, (halves[0], halves[1]), late)

    for coord in range(3):
        back_ref[coord] = -0.5 * back[:, coord, :] - there[coord] * back[:, 6, :]
    if last:
        for coord in range(3):
            span = slice(base + coord * clusters, base + (coord + 1) * clusters)
            pos = [ref[span, :] for ref in local_refs]
            pos = jnp.concatenate(pos, axis=1).astype(jnp.float32)
            grad_ref[coord] = acc[:, width + coord, :] - pos * acc[:, width + 3, :]
        pot_ref[...] = acc[:, :rhs, :]
        pot_out_ref[...] = acc[:, rhs:width, :].astype(jnp.bfloat16)


def run_step(step, length, items, source, targets, locals_, rhs, width, carried, last):
    lhss, augs = zip(*targets)
    clusters, _, row_count = augs[0].shape
    subs = len(targets)
    panels = subs * row_count
    quarter = source.shape[1]
    first = carried is None
    vmem = pl.BlockSpec(memory_space=pltpu.VMEM)
    smem = pl.BlockSpec(memory_space=pltpu.SMEM)
    operands = (items, source, *lhss, *augs)
    if not first:
        operands += (carried,)
    acc_shape = (clusters, width + AUG, panels)
    back_shape = jax.ShapeDtypeStruct((3, clusters, quarter), jnp.float32)
    scratch = [
        pltpu.VMEM((clusters, AUG, quarter), jnp.float32),
        pltpu.VMEM((clusters, LANES, 2 * quarter), jnp.bfloat16),
        pltpu.VMEM((clusters, LANES, 2 * quarter), jnp.bfloat16),
        pltpu.VMEM((clusters + 8, quarter), jnp.float32),
        pltpu.VMEM((clusters, AUG, quarter), jnp.float32),
    ]
    scratch += [pltpu.VMEM((panels, 2 * quarter), jnp.float32)] * 2
    scratch += [pltpu.VMEM((panels, 4 * quarter), jnp.bfloat16)]
    if last:
        operands += tuple(locals_)
        out_shape = (
            jax.ShapeDtypeStruct((clusters, rhs, panels), jnp.float32),
            jax.ShapeDtypeStruct((clusters, width - rhs, panels), jnp.bfloat16),
            jax.ShapeDtypeStruct((3, clusters, panels), jnp.float32),
            back_shape,
        )
        scratch = [pltpu.VMEM(acc_shape, jnp.float32)] + scratch
    else:
        out_shape = (jax.ShapeDtypeStruct(acc_shape, jnp.float32), back_shape)
    pairs = (length - 6) * panels * quarter
    return pl.pallas_call(
        functools.partial(step_kernel, step, length, rhs, subs, first, last),
        out_shape=out_shape,
        in_specs=[smem] + [vmem] * (len(operands) - 1),
        out_specs=(vmem,) * len(out_shape),
        scratch_shapes=scratch,
        compiler_params=pltpu.CompilerParams(vmem_limit_bytes=20 * 1024 * 1024),
        cost_estimate=pl.CostEstimate(
            flops=2 * pairs * (2 * width + 3 * AUG), bytes_accessed=6 * 2**20, transcendentals=pairs
        ),
        name=f"near_field_{step}",
    )(*operands)


def node_kernel(grad_ref, jitter_ref, edge_ref, main_ref):
    clusters, panels = jitter_ref.shape
    wide = panels + 2 * LANES

    def spread_of(terms, jitter):
        side = jnp.zeros((terms.shape[0], LANES), jnp.float32)
        terms = 0.25 * terms
        spread = jnp.zeros((terms.shape[0], wide), jnp.float32)
        for offset in range(-jitter_reach, jitter_reach + 1):
            masked = jnp.where(jitter == offset, terms, 0.0)
            masked = jnp.concatenate([side, masked, side], axis=1)
            spread = spread + pltpu.roll(masked, offset % wide, 1)
        spread = spread + pltpu.roll(spread, 1, 1)
        return spread + pltpu.roll(spread, 32, 1)

    jitter = jitter_ref[...]
    row_at = lax.broadcasted_iota(jnp.int32, (clusters, LANES), 0)
    edge = edge_ref[...]
    edge_at = lax.broadcasted_iota(jnp.int32, edge.shape, 0)
    edge_jitter = jnp.where(edge_at < 3, edge[6:7], edge[7:8]).astype(jnp.int32)
    edge = spread_of(edge, edge_jitter)
    for coord in range(3):
        spread = spread_of(grad_ref[coord], jitter)
        below = spread[:, :LANES]
        above = spread[:, LANES + panels :]
        inner = spread[:, LANES : LANES + panels]
        before = edge[coord : coord + 1, LANES + panels :]
        after = edge[3 + coord : 4 + coord, :LANES]
        first = jnp.where(row_at == 0, before, pltpu.roll(above, 1, 0))
        last = jnp.where(row_at == clusters - 1, after, pltpu.roll(below, clusters - 1, 0))
        inner = jnp.concatenate(
            [
                inner[:, :LANES] + first,
                inner[:, LANES : panels - LANES],
                inner[:, panels - LANES :] + last,
            ],
            axis=1,
        )
        for cluster in range(clusters):
            main_ref[coord : coord + 1, cluster * panels : (cluster + 1) * panels] = inner[
                cluster : cluster + 1
            ]


def sum_kernel(*refs):
    total = refs[0][...]
    for ref in refs[1:-1]:
        total = total + ref[...].astype(jnp.float32)
    refs[-1][...] = total.astype(jnp.bfloat16)


def on_device(positions, areas, density, cotangent, matching, connect):
    clus_count = lax.axis_size("clus")
    sub_count = lax.axis_size("sub")
    rhs_count = lax.axis_size("rhs")
    device = lax.axis_index("clus")
    sub_place = lax.axis_index("sub")
    core = lax.axis_index("rhs")
    clusters, rhs, row_count = density.shape
    panels = row_count * sub_count
    quarter = row_count // rhs_count
    width = rhs * rhs_count
    vmem = pl.BlockSpec(memory_space=pltpu.VMEM)

    nodes_total = clus_count * clusters * panels

    by_coord = jnp.transpose(positions, (1, 0, 2))
    arguments = [
        pltpu.with_memory_space_constraint(array, pltpu.HBM)
        for array in (density, by_coord, areas, connect, cotangent)
    ]
    shapes = [(clusters * (rhs + 5), quarter)] + [(clusters * rhs, quarter)] * (rhs_count - 1)
    shapes.append((clusters * (rhs + 4), row_count))
    *parts, local = pl.pallas_call(
        functools.partial(prepare_kernel, (panels, nodes_total)),
        out_shape=[jax.ShapeDtypeStruct(shape, jnp.bfloat16) for shape in shapes],
        in_specs=[pl.BlockSpec(memory_space=pltpu.HBM)] * len(arguments),
        out_specs=[vmem] * len(shapes),
        scratch_shapes=[pltpu.VMEM(array.shape, array.dtype) for array in arguments]
        + [pltpu.SemaphoreType.DMA((len(arguments),))],
        compiler_params=pltpu.CompilerParams(vmem_limit_bytes=16 * 1024 * 1024),
        name="prepare",
    )(*arguments)
    ring = ring_order(clus_count)
    at_place = [ring.index(index) for index in range(clus_count)]
    ring_place = pick(device, at_place)

    def own_parts(parts, steps):
        arrived = [round_ring(parts[0], steps)]
        for step in range(1, rhs_count):

            def goal(z, c, step=step):
                return (ring[(at_place[z] + steps) % clus_count], c + step)

            arrived.append(moved(parts[step], ("clus", "rhs"), goal))
        return arrived

    arrived = own_parts(parts, 1)

    per_round = 2 * ((clusters // 2 + clus_count - 2) // (clus_count - 1))
    cap = ROUNDS * per_round
    partners = lax.dynamic_slice_in_dim(matching, device * clusters, clusters, 1).reshape(-1)
    here = jnp.tile(jnp.arange(clusters, dtype=jnp.int32), ROUNDS)
    code = here * (2 * clusters) + partners % clusters
    behind = (ring_place - pick(partners // clusters, at_place)) % clus_count
    total_items = ROUNDS * clusters
    order = jnp.arange(total_items, dtype=jnp.int32)
    rank = jnp.sum(
        ((behind[None, :] == behind[:, None]) & (order[None, :] < order[:, None])).astype(jnp.int32),
        axis=1,
    )
    steps = jnp.arange(1, clus_count, dtype=jnp.int32)
    member = behind[None, :] == steps[:, None]
    slots = jnp.arange(cap, dtype=jnp.int32)
    chosen = member[:, None, :] & (rank[None, None, :] == slots[None, :, None])
    listed = jnp.sum(jnp.where(chosen, code[None, None, :] - clusters, 0), axis=2) + clusters
    turns = (jnp.sum(member.astype(jnp.int32), axis=1) + 3) // 2
    length = cap + 6
    items = jnp.pad(listed, ((0, 0), (3, 3)), constant_values=clusters)
    items = jnp.concatenate([turns[:, None], items[:, 1:]], axis=1).reshape(-1)

    locals_ = [local] + [shifted(local, "sub", step) for step in range(1, sub_count)]
    blocks = [
        [block] + [shifted(block, "rhs", step) for step in range(1, rhs_count)] for block in locals_
    ]

    def in_order(blocks):
        return jnp.concatenate(
            [pick((sub_place - place) % sub_count, blocks) for place in range(sub_count)], axis=-1
        )

    jitter_all = in_order([block[clusters * (rhs + 3) :] for block in locals_]).astype(jnp.int32)
    targets = [
        pl.pallas_call(
            target_kernel,
            out_shape=(
                jax.ShapeDtypeStruct((clusters, row_count, LANES), jnp.bfloat16),
                jax.ShapeDtypeStruct((clusters, AUG, row_count), jnp.bfloat16),
            ),
            in_specs=[vmem] * rhs_count,
            out_specs=(vmem, vmem),
            scratch_shapes=[pltpu.VMEM((clusters, AUG, row_count), jnp.float32)],
            compiler_params=pltpu.CompilerParams(vmem_limit_bytes=16 * 1024 * 1024),
            cost_estimate=pl.CostEstimate(flops=2**20, bytes_accessed=2**18, transcendentals=0),
            name=f"targets_{place}",
        )(*blocks[place])
        for place in range(sub_count)
    ]

    arrived, targets = lax.optimization_barrier((arrived, targets))
    source = jnp.concatenate(arrived, axis=0)
    source, parts = lax.optimization_barrier((source, parts))
    from_next = own_parts(parts, -1) if clus_count > 2 else None
    carried = None
    backs, jitter_rows = [], [None]
    for step in range(1, clus_count):
        if 1 < step < clus_count - 1:
            if step > 2:
                source, backs[step - 3] = lax.optimization_barrier((source, backs[step - 3]))
            source = round_ring(source, 1)
        elif step > 1:
            from_next, backs[-1] = lax.optimization_barrier((from_next, backs[-1]))
            source = jnp.concatenate(from_next, axis=0)
        last = step == clus_count - 1
        results = run_step(
            step - 1, length, items, source, targets, locals_, rhs, width, carried, last
        )
        if last:
            pot, pot_out, grad, back = results
        else:
            carried, back = results
        backs.append(back)
        at = clusters * (rhs + 4)
        jitter_rows.append(source[at : at + clusters])

    grad = in_order([grad[..., at * row_count : (at + 1) * row_count] for at in range(sub_count)])
    low_part = (sub_place == 0) & (core == 0)
    high_part = (sub_place == sub_count - 1) & (core == rhs_count - 1)
    uppers = [grad[:, -1, -quarter:]] + [jnp.where(high_part, back[:, -1], 0.0) for back in backs]
    lowers = [grad[:, 0, :quarter]] + [jnp.where(low_part, back[:, 0], 0.0) for back in backs]

    def step_between(index, owner):
        return (at_place[index] - at_place[owner % clus_count]) % clus_count

    def needed(parts, step, offset):
        choices = []
        for index in range(clus_count):
            goal = ring[(at_place[index] - step) % clus_count]
            choices.append(parts[step_between(index, goal + offset)])
        return pick(device, choices)

    nothing = jnp.zeros((2, quarter), jnp.float32)
    returned = jnp.zeros((3, clusters, quarter), jnp.float32)
    upper, lower = needed(uppers, 0, -1), needed(lowers, 0, 1)
    for step in range(1, clus_count):
        rows = [
            backs[step - 1].reshape(3 * clusters, quarter),
            needed(uppers, step, -1),
            needed(lowers, step, 1),
            nothing,
        ]
        home = round_ring(jnp.concatenate(rows, axis=0), -step)
        returned = returned + home[: 3 * clusters].reshape(returned.shape)
        upper = upper + home[3 * clusters : 3 * clusters + 3]
        lower = lower + home[3 * clusters + 3 : 3 * clusters + 6]

    half = pot
    for step in range(1, rhs_count):
        arrived = shifted(pot_out[:, (step - 1) * rhs : step * rhs], "rhs", -step)
        half = half + arrived.astype(jnp.float32)

    half, grad = lax.optimization_barrier((half, grad))
    found = [half[..., :row_count]]
    for step in range(1, sub_count):
        sent = half[..., step * row_count : (step + 1) * row_count].astype(jnp.bfloat16)
        found.append(shifted(sent, "sub", -step))

    quarter_at = sub_place * rhs_count + core
    grad = grad + jnp.concatenate(
        [jnp.where(quarter_at == at, returned, 0.0) for at in range(sub_count * rhs_count)], axis=-1
    )
    share = clusters // sub_count

    blank = jnp.zeros((3, panels - quarter), jnp.float32)
    before = jnp.concatenate([blank, upper], axis=1)
    after = jnp.concatenate([lower, blank], axis=1)
    jitter_float = jitter_all.astype(jnp.float32)
    jitter_before = jnp.concatenate(
        [blank[:1], needed(jitter_rows, 0, -1)[clusters - 1 :].astype(jnp.float32)], axis=1
    )
    jitter_after = jnp.concatenate(
        [needed(jitter_rows, 0, 1)[:1].astype(jnp.float32), blank[:1]], axis=1
    )

    def edge_rows(at):
        first, end = at * share, (at + 1) * share
        inside = at < sub_count - 1
        return jnp.concatenate(
            [
                grad[:, first - 1] if at > 0 else before,
                grad[:, end] if inside else after,
                jnp.where(high_part, jitter_float[first - 1 : first] if at > 0 else jitter_before, 0.0),
                jnp.where(low_part, jitter_float[end : end + 1] if inside else jitter_after, 0.0),
            ],
            axis=0,
        ).reshape(-1, share, panels)

    def packed(place):
        return pick(
            place % sub_count,
            [
                jnp.concatenate([grad[:, at * share : (at + 1) * share], edge_rows(at)], axis=0)
                for at in range(sub_count)
            ],
        )

    summed = packed(sub_place)
    for step in range(1, sub_count):
        summed = summed + shifted(packed(sub_place + step), "sub", step)
    gathered = summed
    for step in range(1, rhs_count):
        gathered = gathered + shifted(summed, "rhs", step)
    own_jitter = pick(
        sub_place, [jitter_all[at * share : (at + 1) * share] for at in range(sub_count)]
    )
    node_grad = pl.pallas_call(
        node_kernel,
        out_shape=jax.ShapeDtypeStruct((3, share * panels), jnp.float32),
        in_specs=[vmem] * 3,
        out_specs=vmem,
        compiler_params=pltpu.CompilerParams(vmem_limit_bytes=16 * 1024 * 1024),
        cost_estimate=pl.CostEstimate(flops=2**20, bytes_accessed=2**18, transcendentals=0),
        name="node_terms",
    )(gathered[:3], own_jitter, gathered[3:].reshape(8, panels))
    potential = pl.pallas_call(
        sum_kernel,
        out_shape=jax.ShapeDtypeStruct((clusters, rhs, row_count), jnp.bfloat16),
        in_specs=[vmem] * sub_count,
        out_specs=vmem,
        compiler_params=pltpu.CompilerParams(vmem_limit_bytes=16 * 1024 * 1024),
        cost_estimate=pl.CostEstimate(flops=2**20, bytes_accessed=2**18, transcendentals=0),
        name="potential_sum",
    )(*found)
    return (potential, node_grad)


def solution(mesh):
    placed = (
        P(("groups", "clus"), None, "sub"),
        P(("groups", "clus"), "sub"),
        P(("groups", "clus"), "rhs", "sub"),
        P(("groups", "clus"), "rhs", "sub"),
        P(None, "groups"),
        P(("groups", "clus"), None, "sub"),
    )
    return jax.shard_map(
        on_device,
        mesh=mesh,
        in_specs=placed,
        out_specs=(P(("groups", "clus"), "rhs", "sub"), P(None, ("groups", "clus", "sub"))),
        check_vma=False,
    )
```

```python
import functools

import jax
import jax.numpy as jnp
from jax import lax
from jax.experimental import pallas as pl
from jax.experimental.pallas import tpu as pltpu
from jax.sharding import PartitionSpec as P

CP = 512
ROUNDS = 5

core_radius = 0.25
jitter_reach = 8
LANES = 128
AUG = 16


def shifted(value, axis, steps):
    count = lax.axis_size(axis)
    pairs = [(source, (source + steps) % count) for source in range(count)]
    return lax.ppermute(value, axis, pairs)


def ring_order(count):
    return [*range(0, count, 2), *reversed(range(1, count, 2))]


def round_ring(value, steps):
    order = ring_order(lax.axis_size("clus"))
    pairs = [(source, order[(at + steps) % len(order)]) for at, source in enumerate(order)]
    return lax.ppermute(value, "clus", pairs)


def moved(value, axes, target):
    counts = [lax.axis_size(axis) for axis in axes]
    pairs = []
    for major in range(counts[0]):
        for minor in range(counts[1]):
            goal = target(major, minor)
            if goal is not None:
                to_major, to_minor = goal[0] % counts[0], goal[1] % counts[1]
                pairs.append((major * counts[1] + minor, to_major * counts[1] + to_minor))
    return lax.ppermute(value, axes, pairs)


def three_parts(value):
    parts = []
    for _ in range(3):
        part = value.astype(jnp.bfloat16).astype(jnp.float32)
        parts.append(part)
        value = value - part
    return parts


def pick(index, choices):
    out = choices[0]
    for place in range(1, len(choices)):
        out = jnp.where(index == place, choices[place], out)
    return out


def fetched(arguments, places, sems):
    copies = []
    for at, (argument, place) in enumerate(zip(arguments, places)):
        copies.append(pltpu.make_async_copy(argument, place, sems.at[at]))
        copies[-1].start()
    for copy in copies:
        copy.wait()


def jitter_of(connect_ref, sizes):
    clusters, _, row_count = connect_ref.shape
    panels, nodes_total = sizes
    first_id = clusters * panels * lax.axis_index("clus") + row_count * lax.axis_index("sub")
    ids = lax.broadcasted_iota(jnp.int32, (clusters, row_count), 0) * panels
    ids = ids + lax.broadcasted_iota(jnp.int32, (clusters, row_count), 1) + first_id
    jitter = connect_ref[:, 0, :] - ids
    jitter = jnp.where(jitter > jitter_reach, jitter - nodes_total, jitter)
    jitter = jnp.where(jitter < -jitter_reach, jitter + nodes_total, jitter)
    return jitter.astype(jnp.float32).astype(jnp.bfloat16)


def prepare_kernel(sizes, *refs):
    arguments, part_refs, local_ref, scratch = refs[:5], refs[5:-7], refs[-7], refs[-6:]
    fetched(arguments, scratch[:5], scratch[5])
    density_ref, by_coord_ref, areas_ref, connect_ref, cot_ref = scratch[:5]
    clusters, rhs, _ = density_ref.shape
    quarter = part_refs[0].shape[1]
    count = len(part_refs)
    core = lax.axis_index("rhs")

    def part_of(array, place):
        return pick(place, [array[:, at * quarter : (at + 1) * quarter] for at in range(count)])

    pos = [by_coord_ref[coord] for coord in range(3)]
    jitter = jitter_of(connect_ref, sizes)
    base = clusters * rhs
    for cluster in range(clusters):
        dens = density_ref[cluster]
        span = slice(cluster * rhs, (cluster + 1) * rhs)
        local_ref[span, :] = cot_ref[cluster]
        for step, part_ref in enumerate(part_refs):
            part_ref[span, :] = part_of(dens, (core + step) % count)
    for at, value in enumerate([*pos, areas_ref[...], jitter]):
        part_refs[0][base + at * clusters : base + (at + 1) * clusters, :] = part_of(value, core)
    for at, value in enumerate([*pos, jitter]):
        local_ref[base + at * clusters : base + (at + 1) * clusters, :] = value


def target_kernel(*refs):
    local_refs, (lhs_ref, aug_ref, aug32) = refs[:-3], refs[-3:]
    clusters, _, row_count = aug_ref.shape
    rhs = local_refs[0].shape[0] // clusters - 4
    base = clusters * rhs
    pos = [
        local_refs[0][base + coord * clusters : base + (coord + 1) * clusters, :].astype(jnp.float32)
        for coord in range(3)
    ]
    square = pos[0] * pos[0] + pos[1] * pos[1] + pos[2] * pos[2] + core_radius * core_radius
    ones = jnp.ones_like(square)
    aug32[...] = jnp.zeros(aug32.shape, jnp.float32)
    for row, value in enumerate([-2.0 * value for value in pos] + three_parts(square) + [ones] * 3):
        aug32[:, row, :] = value
    blank = jnp.zeros((LANES - AUG - rhs * len(local_refs), row_count), jnp.bfloat16)
    for cluster in range(clusters):
        aug = aug32[cluster].astype(jnp.bfloat16)
        aug_ref[cluster] = aug
        rows = [ref[cluster * rhs : (cluster + 1) * rhs, :] for ref in local_refs]
        lhs_ref[cluster] = jnp.concatenate([*rows, aug, blank], axis=0).T


def step_kernel(step, length, rhs, subs, first, last, *refs):
    items, source_ref, refs = refs[0], refs[1], refs[2:]
    lhs_refs, aug_refs, refs = refs[:subs], refs[subs : 2 * subs], refs[2 * subs :]
    if not first:
        acc_in, refs = refs[0], refs[1:]
    if last:
        local_refs, refs = refs[:subs], refs[subs:]
        pot_ref, pot_out_ref, grad_ref, back_ref, acc = refs[:5]
        refs = refs[5:]
    else:
        acc, back_ref = refs[:2]
        refs = refs[2:]
    aug32, left_a, left_b, weight, back, raw_a, raw_b, both = refs
    clusters, rows, panels = acc.shape
    width = rows - AUG
    row_count = panels // subs
    quarter = source_ref.shape[1]
    base = clusters * rhs

    starts = [0] + list(range(base + 5 * clusters, source_ref.shape[0], base))

    there = [
        source_ref[base + coord * clusters : base + (coord + 1) * clusters, :].astype(jnp.float32)
        for coord in range(3)
    ]
    area = source_ref[base + 3 * clusters : base + 4 * clusters, :].astype(jnp.float32)
    square = there[0] * there[0] + there[1] * there[1] + there[2] * there[2]
    ones = jnp.ones_like(square)
    aug32[...] = jnp.zeros(aug32.shape, jnp.float32)
    for row, value in enumerate(there + [ones] * 3 + three_parts(square)):
        aug32[:, row, :] = value
    weight[...] = jnp.zeros(weight.shape, jnp.float32)
    weight[:clusters, :] = CP ** (-0.5) * area
    left_a[...] = jnp.zeros(left_a.shape, left_a.dtype)
    left_b[...] = jnp.zeros(left_b.shape, left_b.dtype)
    for cluster in range(clusters):
        distance_rows = aug32[cluster].astype(jnp.bfloat16)
        left_a[cluster, width:rows, quarter:] = distance_rows
        left_b[cluster, width:rows, :quarter] = distance_rows
        for place, at in enumerate(starts):
            span = slice(place * rhs, (place + 1) * rhs)
            dens = source_ref[at + cluster * rhs : at + (cluster + 1) * rhs, :]
            left_a[cluster, span, :quarter] = dens
            left_b[cluster, span, quarter:] = dens
    back[...] = jnp.zeros(back.shape, jnp.float32)
    if first:
        acc[...] = jnp.zeros(acc.shape, jnp.float32)
    else:
        acc[...] = acc_in[...]
    raw_b[...] = jnp.ones(raw_b.shape, jnp.float32)
    both[:, : 2 * quarter] = jnp.zeros((panels, 2 * quarter), both.dtype)

    halves = [slice(at * quarter, (at + 1) * quarter) for at in range(4)]

    def decoded(place):
        code = items[step * length + place]
        return code // (2 * clusters), code % (2 * clusters)

    part = max(2 * LANES, panels // 2)
    spans = [slice(start, start + part) for start in range(0, panels, part)]

    def products(place, left, raw, span):
        here, mate = decoded(place)
        lhs = jnp.concatenate([ref[here] for ref in lhs_refs], axis=0)[span]
        raw[span, :] = jnp.dot(lhs, left[mate % clusters], preferred_element_type=jnp.float32)

    def pointwise(place, raw, raw_halves, both_halves, span):
        _, mate = decoded(place)
        scale = weight[pl.ds(mate, 1), :]
        for start in range(span.start, span.stop, LANES):
            piece = slice(start, start + LANES)
            inverse = lax.rsqrt(raw[piece, raw_halves[1]])
            kernel = scale * inverse
            both[piece, both_halves[0]] = kernel.astype(jnp.bfloat16)
            weighted = (inverse * inverse) * (kernel * raw[piece, raw_halves[0]])
            both[piece, both_halves[1]] = weighted.astype(jnp.bfloat16)

    def summed(place, left, columns, span):
        here, mate = decoded(place)
        acc[here, :, span] += lax.dot_general(
            left[mate % clusters, :rows, :],
            both[span, columns],
            (((1,), (1,)), ((), ())),
            preferred_element_type=jnp.float32,
        )

    def source_sums(place):
        (here_a, mate_a), (here_b, mate_b) = decoded(place), decoded(place + 1)
        aug = jnp.concatenate(
            [
                jnp.concatenate([ref[here] for ref in aug_refs], axis=1)
                for here in (here_a, here_b)
            ],
            axis=0,
        )
        sums = jnp.dot(aug, both[:, quarter : 3 * quarter], preferred_element_type=jnp.float32)
        back[mate_a % clusters] += sums[:AUG, :quarter]
        back[mate_b % clusters] += sums[AUG:, quarter:]

    forward, backward = (halves[0], halves[1]), (halves[1], halves[0])
    columns_a, columns_b = slice(0, 2 * quarter), slice(2 * quarter, 4 * quarter)

    @pl.loop(0, items[step * length])
    def _(pair):
        turn = 2 * pair + 1
        for span in spans:
            products(turn + 2, left_a, raw_a, span)
            summed(turn, left_a, columns_a, span)
            pointwise(turn + 1, raw_b, backward, (halves[3], halves[2]), span)
        source_sums(turn)
        for span in spans:
            products(turn + 3, left_b, raw_b, span)
            summed(turn + 1, left_b, columns_b, span)
            pointwise(turn + 2, raw_a, forward, (halves[0], halves[1]), span)

    for coord in range(3):
        back_ref[coord] = -0.5 * back[:, coord, :] - there[coord] * back[:, 6, :]
    if last:
        for coord in range(3):
            span = slice(base + coord * clusters, base + (coord + 1) * clusters)
            pos = [ref[span, :] for ref in local_refs]
            pos = jnp.concatenate(pos, axis=1).astype(jnp.float32)
            grad_ref[coord] = acc[:, width + coord, :] - pos * acc[:, width + 3, :]
        pot_ref[...] = acc[:, :rhs, :]
        pot_out_ref[...] = acc[:, rhs:width, :].astype(jnp.bfloat16)


def run_step(step, length, items, source, targets, locals_, rhs, width, carried, last):
    lhss, augs = zip(*targets)
    clusters, _, row_count = augs[0].shape
    subs = len(targets)
    panels = subs * row_count
    quarter = source.shape[1]
    first = carried is None
    vmem = pl.BlockSpec(memory_space=pltpu.VMEM)
    smem = pl.BlockSpec(memory_space=pltpu.SMEM)
    operands = (items, source, *lhss, *augs)
    if not first:
        operands += (carried,)
    acc_shape = (clusters, width + AUG, panels)
    back_shape = jax.ShapeDtypeStruct((3, clusters, quarter), jnp.float32)
    scratch = [
        pltpu.VMEM((clusters, AUG, quarter), jnp.float32),
        pltpu.VMEM((clusters, LANES, 2 * quarter), jnp.bfloat16),
        pltpu.VMEM((clusters, LANES, 2 * quarter), jnp.bfloat16),
        pltpu.VMEM((clusters + 8, quarter), jnp.float32),
        pltpu.VMEM((clusters, AUG, quarter), jnp.float32),
    ]
    scratch += [pltpu.VMEM((panels, 2 * quarter), jnp.float32)] * 2
    scratch += [pltpu.VMEM((panels, 4 * quarter), jnp.bfloat16)]
    if last:
        operands += tuple(locals_)
        out_shape = (
            jax.ShapeDtypeStruct((clusters, rhs, panels), jnp.float32),
            jax.ShapeDtypeStruct((clusters, width - rhs, panels), jnp.bfloat16),
            jax.ShapeDtypeStruct((3, clusters, panels), jnp.float32),
            back_shape,
        )
        scratch = [pltpu.VMEM(acc_shape, jnp.float32)] + scratch
    else:
        out_shape = (jax.ShapeDtypeStruct(acc_shape, jnp.float32), back_shape)
    pairs = (length - 6) * panels * quarter
    return pl.pallas_call(
        functools.partial(step_kernel, step, length, rhs, subs, first, last),
        out_shape=out_shape,
        in_specs=[smem] + [vmem] * (len(operands) - 1),
        out_specs=(vmem,) * len(out_shape),
        scratch_shapes=scratch,
        compiler_params=pltpu.CompilerParams(vmem_limit_bytes=20 * 1024 * 1024),
        cost_estimate=pl.CostEstimate(
            flops=2 * pairs * (2 * width + 3 * AUG), bytes_accessed=6 * 2**20, transcendentals=pairs
        ),
        name=f"near_field_{step}",
    )(*operands)


def node_kernel(grad_ref, jitter_ref, edge_ref, main_ref):
    clusters, panels = jitter_ref.shape
    wide = panels + 2 * LANES

    def spread_of(terms, jitter):
        side = jnp.zeros((terms.shape[0], LANES), jnp.float32)
        terms = 0.25 * terms
        spread = jnp.zeros((terms.shape[0], wide), jnp.float32)
        for offset in range(-jitter_reach, jitter_reach + 1):
            masked = jnp.where(jitter == offset, terms, 0.0)
            masked = jnp.concatenate([side, masked, side], axis=1)
            spread = spread + pltpu.roll(masked, offset % wide, 1)
        spread = spread + pltpu.roll(spread, 1, 1)
        return spread + pltpu.roll(spread, 32, 1)

    jitter = jitter_ref[...]
    row_at = lax.broadcasted_iota(jnp.int32, (clusters, LANES), 0)
    edge = edge_ref[...]
    edge_at = lax.broadcasted_iota(jnp.int32, edge.shape, 0)
    edge_jitter = jnp.where(edge_at < 3, edge[6:7], edge[7:8]).astype(jnp.int32)
    edge = spread_of(edge, edge_jitter)
    for coord in range(3):
        spread = spread_of(grad_ref[coord], jitter)
        below = spread[:, :LANES]
        above = spread[:, LANES + panels :]
        inner = spread[:, LANES : LANES + panels]
        before = edge[coord : coord + 1, LANES + panels :]
        after = edge[3 + coord : 4 + coord, :LANES]
        first = jnp.where(row_at == 0, before, pltpu.roll(above, 1, 0))
        last = jnp.where(row_at == clusters - 1, after, pltpu.roll(below, clusters - 1, 0))
        inner = jnp.concatenate(
            [
                inner[:, :LANES] + first,
                inner[:, LANES : panels - LANES],
                inner[:, panels - LANES :] + last,
            ],
            axis=1,
        )
        for cluster in range(clusters):
            main_ref[coord : coord + 1, cluster * panels : (cluster + 1) * panels] = inner[
                cluster : cluster + 1
            ]


def sum_kernel(*refs):
    total = refs[0][...]
    for ref in refs[1:-1]:
        total = total + ref[...].astype(jnp.float32)
    refs[-1][...] = total.astype(jnp.bfloat16)


def on_device(positions, areas, density, cotangent, matching, connect):
    clus_count = lax.axis_size("clus")
    sub_count = lax.axis_size("sub")
    rhs_count = lax.axis_size("rhs")
    device = lax.axis_index("clus")
    sub_place = lax.axis_index("sub")
    core = lax.axis_index("rhs")
    clusters, rhs, row_count = density.shape
    panels = row_count * sub_count
    quarter = row_count // rhs_count
    width = rhs * rhs_count
    vmem = pl.BlockSpec(memory_space=pltpu.VMEM)

    nodes_total = clus_count * clusters * panels

    by_coord = jnp.transpose(positions, (1, 0, 2))
    arguments = [
        pltpu.with_memory_space_constraint(array, pltpu.HBM)
        for array in (density, by_coord, areas, connect, cotangent)
    ]
    shapes = [(clusters * (rhs + 5), quarter)] + [(clusters * rhs, quarter)] * (rhs_count - 1)
    shapes.append((clusters * (rhs + 4), row_count))
    *parts, local = pl.pallas_call(
        functools.partial(prepare_kernel, (panels, nodes_total)),
        out_shape=[jax.ShapeDtypeStruct(shape, jnp.bfloat16) for shape in shapes],
        in_specs=[pl.BlockSpec(memory_space=pltpu.HBM)] * len(arguments),
        out_specs=[vmem] * len(shapes),
        scratch_shapes=[pltpu.VMEM(array.shape, array.dtype) for array in arguments]
        + [pltpu.SemaphoreType.DMA((len(arguments),))],
        compiler_params=pltpu.CompilerParams(vmem_limit_bytes=16 * 1024 * 1024),
        name="prepare",
    )(*arguments)
    ring = ring_order(clus_count)
    at_place = [ring.index(index) for index in range(clus_count)]
    ring_place = pick(device, at_place)

    def own_parts(parts, steps):
        arrived = [round_ring(parts[0], steps)]
        for step in range(1, rhs_count):

            def goal(z, c, step=step):
                return (ring[(at_place[z] + steps) % clus_count], c + step)

            arrived.append(moved(parts[step], ("clus", "rhs"), goal))
        return arrived

    arrived = own_parts(parts, 1)

    per_round = 2 * ((clusters // 2 + clus_count - 2) // (clus_count - 1))
    cap = ROUNDS * per_round
    partners = lax.dynamic_slice_in_dim(matching, device * clusters, clusters, 1).reshape(-1)
    here = jnp.tile(jnp.arange(clusters, dtype=jnp.int32), ROUNDS)
    code = here * (2 * clusters) + partners % clusters
    behind = (ring_place - pick(partners // clusters, at_place)) % clus_count
    total_items = ROUNDS * clusters
    order = jnp.arange(total_items, dtype=jnp.int32)
    rank = jnp.sum(
        ((behind[None, :] == behind[:, None]) & (order[None, :] < order[:, None])).astype(jnp.int32),
        axis=1,
    )
    steps = jnp.arange(1, clus_count, dtype=jnp.int32)
    member = behind[None, :] == steps[:, None]
    slots = jnp.arange(cap, dtype=jnp.int32)
    chosen = member[:, None, :] & (rank[None, None, :] == slots[None, :, None])
    listed = jnp.sum(jnp.where(chosen, code[None, None, :] - clusters, 0), axis=2) + clusters
    turns = (jnp.sum(member.astype(jnp.int32), axis=1) + 3) // 2
    length = cap + 6
    items = jnp.pad(listed, ((0, 0), (3, 3)), constant_values=clusters)
    items = jnp.concatenate([turns[:, None], items[:, 1:]], axis=1).reshape(-1)

    locals_ = [local] + [shifted(local, "sub", step) for step in range(1, sub_count)]
    blocks = [
        [block] + [shifted(block, "rhs", step) for step in range(1, rhs_count)] for block in locals_
    ]

    def in_order(blocks):
        return jnp.concatenate(
            [pick((sub_place - place) % sub_count, blocks) for place in range(sub_count)], axis=-1
        )

    jitter_all = in_order([block[clusters * (rhs + 3) :] for block in locals_]).astype(jnp.int32)
    targets = [
        pl.pallas_call(
            target_kernel,
            out_shape=(
                jax.ShapeDtypeStruct((clusters, row_count, LANES), jnp.bfloat16),
                jax.ShapeDtypeStruct((clusters, AUG, row_count), jnp.bfloat16),
            ),
            in_specs=[vmem] * rhs_count,
            out_specs=(vmem, vmem),
            scratch_shapes=[pltpu.VMEM((clusters, AUG, row_count), jnp.float32)],
            compiler_params=pltpu.CompilerParams(vmem_limit_bytes=16 * 1024 * 1024),
            cost_estimate=pl.CostEstimate(flops=2**20, bytes_accessed=2**18, transcendentals=0),
            name=f"targets_{place}",
        )(*blocks[place])
        for place in range(sub_count)
    ]

    arrived, targets = lax.optimization_barrier((arrived, targets))
    source = jnp.concatenate(arrived, axis=0)
    source, parts = lax.optimization_barrier((source, parts))
    from_next = own_parts(parts, -1) if clus_count > 2 else None
    carried = None
    backs, jitter_rows = [], [None]
    for step in range(1, clus_count):
        if 1 < step < clus_count - 1:
            if step > 2:
                source, backs[step - 3] = lax.optimization_barrier((source, backs[step - 3]))
            source = round_ring(source, 1)
        elif step > 1:
            from_next, backs[-1] = lax.optimization_barrier((from_next, backs[-1]))
            source = jnp.concatenate(from_next, axis=0)
        last = step == clus_count - 1
        results = run_step(
            step - 1, length, items, source, targets, locals_, rhs, width, carried, last
        )
        if last:
            pot, pot_out, grad, back = results
        else:
            carried, back = results
        backs.append(back)
        at = clusters * (rhs + 4)
        jitter_rows.append(source[at : at + clusters])

    grad = in_order([grad[..., at * row_count : (at + 1) * row_count] for at in range(sub_count)])
    low_part = (sub_place == 0) & (core == 0)
    high_part = (sub_place == sub_count - 1) & (core == rhs_count - 1)
    uppers = [grad[:, -1, -quarter:]] + [jnp.where(high_part, back[:, -1], 0.0) for back in backs]
    lowers = [grad[:, 0, :quarter]] + [jnp.where(low_part, back[:, 0], 0.0) for back in backs]

    def step_between(index, owner):
        return (at_place[index] - at_place[owner % clus_count]) % clus_count

    def needed(parts, step, offset):
        choices = []
        for index in range(clus_count):
            goal = ring[(at_place[index] - step) % clus_count]
            choices.append(parts[step_between(index, goal + offset)])
        return pick(device, choices)

    nothing = jnp.zeros((2, quarter), jnp.float32)
    returned = jnp.zeros((3, clusters, quarter), jnp.float32)
    upper, lower = needed(uppers, 0, -1), needed(lowers, 0, 1)
    for step in range(1, clus_count):
        rows = [
            backs[step - 1].reshape(3 * clusters, quarter),
            needed(uppers, step, -1),
            needed(lowers, step, 1),
            nothing,
        ]
        home = round_ring(jnp.concatenate(rows, axis=0), -step)
        returned = returned + home[: 3 * clusters].reshape(returned.shape)
        upper = upper + home[3 * clusters : 3 * clusters + 3]
        lower = lower + home[3 * clusters + 3 : 3 * clusters + 6]

    half = pot
    for step in range(1, rhs_count):
        arrived = shifted(pot_out[:, (step - 1) * rhs : step * rhs], "rhs", -step)
        half = half + arrived.astype(jnp.float32)

    half, grad = lax.optimization_barrier((half, grad))
    found = [half[..., :row_count]]
    for step in range(1, sub_count):
        sent = half[..., step * row_count : (step + 1) * row_count].astype(jnp.bfloat16)
        found.append(shifted(sent, "sub", -step))

    quarter_at = sub_place * rhs_count + core
    grad = grad + jnp.concatenate(
        [jnp.where(quarter_at == at, returned, 0.0) for at in range(sub_count * rhs_count)], axis=-1
    )
    share = clusters // sub_count

    blank = jnp.zeros((3, panels - quarter), jnp.float32)
    before = jnp.concatenate([blank, upper], axis=1)
    after = jnp.concatenate([lower, blank], axis=1)
    jitter_float = jitter_all.astype(jnp.float32)
    jitter_before = jnp.concatenate(
        [blank[:1], needed(jitter_rows, 0, -1)[clusters - 1 :].astype(jnp.float32)], axis=1
    )
    jitter_after = jnp.concatenate(
        [needed(jitter_rows, 0, 1)[:1].astype(jnp.float32), blank[:1]], axis=1
    )

    def edge_rows(at):
        first, end = at * share, (at + 1) * share
        inside = at < sub_count - 1
        return jnp.concatenate(
            [
                grad[:, first - 1] if at > 0 else before,
                grad[:, end] if inside else after,
                jnp.where(high_part, jitter_float[first - 1 : first] if at > 0 else jitter_before, 0.0),
                jnp.where(low_part, jitter_float[end : end + 1] if inside else jitter_after, 0.0),
            ],
            axis=0,
        ).reshape(-1, share, panels)

    def packed(place):
        return pick(
            place % sub_count,
            [
                jnp.concatenate([grad[:, at * share : (at + 1) * share], edge_rows(at)], axis=0)
                for at in range(sub_count)
            ],
        )

    summed = packed(sub_place)
    for step in range(1, sub_count):
        summed = summed + shifted(packed(sub_place + step), "sub", step)
    gathered = summed
    for step in range(1, rhs_count):
        gathered = gathered + shifted(summed, "rhs", step)
    own_jitter = pick(
        sub_place, [jitter_all[at * share : (at + 1) * share] for at in range(sub_count)]
    )
    node_grad = pl.pallas_call(
        node_kernel,
        out_shape=jax.ShapeDtypeStruct((3, share * panels), jnp.float32),
        in_specs=[vmem] * 3,
        out_specs=vmem,
        compiler_params=pltpu.CompilerParams(vmem_limit_bytes=16 * 1024 * 1024),
        cost_estimate=pl.CostEstimate(flops=2**20, bytes_accessed=2**18, transcendentals=0),
        name="node_terms",
    )(gathered[:3], own_jitter, gathered[3:].reshape(8, panels))
    potential = pl.pallas_call(
        sum_kernel,
        out_shape=jax.ShapeDtypeStruct((clusters, rhs, row_count), jnp.bfloat16),
        in_specs=[vmem] * sub_count,
        out_specs=vmem,
        compiler_params=pltpu.CompilerParams(vmem_limit_bytes=16 * 1024 * 1024),
        cost_estimate=pl.CostEstimate(flops=2**20, bytes_accessed=2**18, transcendentals=0),
        name="potential_sum",
    )(*found)
    return (potential, node_grad)


def solution(mesh):
    placed = (
        P(("groups", "clus"), None, "sub"),
        P(("groups", "clus"), "sub"),
        P(("groups", "clus"), "rhs", "sub"),
        P(("groups", "clus"), "rhs", "sub"),
        P(None, "groups"),
        P(("groups", "clus"), None, "sub"),
    )
    return jax.shard_map(
        on_device,
        mesh=mesh,
        in_specs=placed,
        out_specs=(P(("groups", "clus"), "rhs", "sub"), P(None, ("groups", "clus", "sub"))),
        check_vma=False,
    )
```

```python
import functools

import jax
import jax.numpy as jnp
from jax import lax
from jax.experimental import pallas as pl
from jax.experimental.pallas import tpu as pltpu
from jax.sharding import PartitionSpec as P

CP = 512
ROUNDS = 5

core_radius = 0.25
jitter_reach = 8
LANES = 128
AUG = 16


def shifted(value, axis, steps):
    count = lax.axis_size(axis)
    pairs = [(source, (source + steps) % count) for source in range(count)]
    return lax.ppermute(value, axis, pairs)


def ring_order(count):
    return [*range(0, count, 2), *reversed(range(1, count, 2))]


def round_ring(value, steps):
    order = ring_order(lax.axis_size("clus"))
    pairs = [(source, order[(at + steps) % len(order)]) for at, source in enumerate(order)]
    return lax.ppermute(value, "clus", pairs)


def moved(value, axes, target):
    counts = [lax.axis_size(axis) for axis in axes]
    pairs = []
    for major in range(counts[0]):
        for minor in range(counts[1]):
            goal = target(major, minor)
            if goal is not None:
                to_major, to_minor = goal[0] % counts[0], goal[1] % counts[1]
                pairs.append((major * counts[1] + minor, to_major * counts[1] + to_minor))
    return lax.ppermute(value, axes, pairs)


def three_parts(value):
    parts = []
    for _ in range(3):
        part = value.astype(jnp.bfloat16).astype(jnp.float32)
        parts.append(part)
        value = value - part
    return parts


def pick(index, choices):
    out = choices[0]
    for place in range(1, len(choices)):
        out = jnp.where(index == place, choices[place], out)
    return out


def fetched(arguments, places, sems):
    copies = []
    for at, (argument, place) in enumerate(zip(arguments, places)):
        copies.append(pltpu.make_async_copy(argument, place, sems.at[at]))
        copies[-1].start()
    for copy in copies:
        copy.wait()


def jitter_of(connect_ref, sizes):
    clusters, _, row_count = connect_ref.shape
    panels, nodes_total = sizes
    first_id = clusters * panels * lax.axis_index("clus") + row_count * lax.axis_index("sub")
    ids = lax.broadcasted_iota(jnp.int32, (clusters, row_count), 0) * panels
    ids = ids + lax.broadcasted_iota(jnp.int32, (clusters, row_count), 1) + first_id
    jitter = connect_ref[:, 0, :] - ids
    jitter = jnp.where(jitter > jitter_reach, jitter - nodes_total, jitter)
    jitter = jnp.where(jitter < -jitter_reach, jitter + nodes_total, jitter)
    return jitter.astype(jnp.float32).astype(jnp.bfloat16)


def prepare_kernel(sizes, *refs):
    arguments, part_refs, local_ref, scratch = refs[:5], refs[5:-7], refs[-7], refs[-6:]
    fetched(arguments, scratch[:5], scratch[5])
    density_ref, by_coord_ref, areas_ref, connect_ref, cot_ref = scratch[:5]
    clusters, rhs, _ = density_ref.shape
    quarter = part_refs[0].shape[1]
    count = len(part_refs)
    core = lax.axis_index("rhs")

    def part_of(array, place):
        return pick(place, [array[:, at * quarter : (at + 1) * quarter] for at in range(count)])

    pos = [by_coord_ref[coord] for coord in range(3)]
    jitter = jitter_of(connect_ref, sizes)
    base = clusters * rhs
    for cluster in range(clusters):
        dens = density_ref[cluster]
        span = slice(cluster * rhs, (cluster + 1) * rhs)
        local_ref[span, :] = cot_ref[cluster]
        for step, part_ref in enumerate(part_refs):
            part_ref[span, :] = part_of(dens, (core + step) % count)
    for at, value in enumerate([*pos, areas_ref[...], jitter]):
        part_refs[0][base + at * clusters : base + (at + 1) * clusters, :] = part_of(value, core)
    for at, value in enumerate([*pos, jitter]):
        local_ref[base + at * clusters : base + (at + 1) * clusters, :] = value


def target_kernel(*refs):
    local_refs, (lhs_ref, aug_ref, aug32) = refs[:-3], refs[-3:]
    clusters, _, row_count = aug_ref.shape
    rhs = local_refs[0].shape[0] // clusters - 4
    base = clusters * rhs
    pos = [
        local_refs[0][base + coord * clusters : base + (coord + 1) * clusters, :].astype(jnp.float32)
        for coord in range(3)
    ]
    square = pos[0] * pos[0] + pos[1] * pos[1] + pos[2] * pos[2] + core_radius * core_radius
    ones = jnp.ones_like(square)
    aug32[...] = jnp.zeros(aug32.shape, jnp.float32)
    for row, value in enumerate([-2.0 * value for value in pos] + three_parts(square) + [ones] * 3):
        aug32[:, row, :] = value
    blank = jnp.zeros((LANES - AUG - rhs * len(local_refs), row_count), jnp.bfloat16)
    for cluster in range(clusters):
        aug = aug32[cluster].astype(jnp.bfloat16)
        aug_ref[cluster] = aug
        rows = [ref[cluster * rhs : (cluster + 1) * rhs, :] for ref in local_refs]
        lhs_ref[cluster] = jnp.concatenate([*rows, aug, blank], axis=0).T


def step_kernel(step, length, rhs, subs, first, last, *refs):
    items, source_ref, refs = refs[0], refs[1], refs[2:]
    lhs_refs, aug_refs, refs = refs[:subs], refs[subs : 2 * subs], refs[2 * subs :]
    if not first:
        acc_in, refs = refs[0], refs[1:]
    if last:
        local_refs, refs = refs[:subs], refs[subs:]
        pot_ref, pot_out_ref, grad_ref, back_ref, acc = refs[:5]
        refs = refs[5:]
    else:
        acc, back_ref = refs[:2]
        refs = refs[2:]
    aug32, left_a, left_b, weight, back, raw_a, raw_b, both = refs
    clusters, rows, panels = acc.shape
    width = rows - AUG
    row_count = panels // subs
    quarter = source_ref.shape[1]
    base = clusters * rhs

    starts = [0] + list(range(base + 5 * clusters, source_ref.shape[0], base))

    there = [
        source_ref[base + coord * clusters : base + (coord + 1) * clusters, :].astype(jnp.float32)
        for coord in range(3)
    ]
    area = source_ref[base + 3 * clusters : base + 4 * clusters, :].astype(jnp.float32)
    square = there[0] * there[0] + there[1] * there[1] + there[2] * there[2]
    ones = jnp.ones_like(square)
    aug32[...] = jnp.zeros(aug32.shape, jnp.float32)
    for row, value in enumerate(there + [ones] * 3 + three_parts(square)):
        aug32[:, row, :] = value
    weight[...] = jnp.zeros(weight.shape, jnp.float32)
    weight[:clusters, :] = CP ** (-0.5) * area
    left_a[...] = jnp.zeros(left_a.shape, left_a.dtype)
    left_b[...] = jnp.zeros(left_b.shape, left_b.dtype)
    for cluster in range(clusters):
        distance_rows = aug32[cluster].astype(jnp.bfloat16)
        left_a[cluster, width:rows, quarter:] = distance_rows
        left_b[cluster, width:rows, :quarter] = distance_rows
        for place, at in enumerate(starts):
            span = slice(place * rhs, (place + 1) * rhs)
            dens = source_ref[at + cluster * rhs : at + (cluster + 1) * rhs, :]
            left_a[cluster, span, :quarter] = dens
            left_b[cluster, span, quarter:] = dens
    back[...] = jnp.zeros(back.shape, jnp.float32)
    if first:
        acc[...] = jnp.zeros(acc.shape, jnp.float32)
    else:
        acc[...] = acc_in[...]
    raw_b[...] = jnp.ones(raw_b.shape, jnp.float32)
    both[:, : 2 * quarter] = jnp.zeros((panels, 2 * quarter), both.dtype)

    halves = [slice(at * quarter, (at + 1) * quarter) for at in range(4)]

    def decoded(place):
        code = items[step * length + place]
        return code // (2 * clusters), code % (2 * clusters)

    part = max(2 * LANES, panels // 2)
    spans = [slice(start, start + part) for start in range(0, panels, part)]

    def products(place, left, raw, span):
        here, mate = decoded(place)
        lhs = jnp.concatenate([ref[here] for ref in lhs_refs], axis=0)[span]
        raw[span, :] = jnp.dot(lhs, left[mate % clusters], preferred_element_type=jnp.float32)

    def pointwise(place, raw, raw_halves, both_halves, span):
        _, mate = decoded(place)
        scale = weight[pl.ds(mate, 1), :]
        for start in range(span.start, span.stop, LANES):
            piece = slice(start, start + LANES)
            inverse = lax.rsqrt(raw[piece, raw_halves[1]])
            kernel = scale * inverse
            both[piece, both_halves[0]] = kernel.astype(jnp.bfloat16)
            weighted = (inverse * inverse) * (kernel * raw[piece, raw_halves[0]])
            both[piece, both_halves[1]] = weighted.astype(jnp.bfloat16)

    def summed(place, left, columns, span):
        here, mate = decoded(place)
        acc[here, :, span] += lax.dot_general(
            left[mate % clusters, :rows, :],
            both[span, columns],
            (((1,), (1,)), ((), ())),
            preferred_element_type=jnp.float32,
        )

    def source_sums(place):
        (here_a, mate_a), (here_b, mate_b) = decoded(place), decoded(place + 1)
        aug = jnp.concatenate(
            [
                jnp.concatenate([ref[here] for ref in aug_refs], axis=1)
                for here in (here_a, here_b)
            ],
            axis=0,
        )
        sums = jnp.dot(aug, both[:, quarter : 3 * quarter], preferred_element_type=jnp.float32)
        back[mate_a % clusters] += sums[:AUG, :quarter]
        back[mate_b % clusters] += sums[AUG:, quarter:]

    forward, backward = (halves[0], halves[1]), (halves[1], halves[0])
    columns_a, columns_b = slice(0, 2 * quarter), slice(2 * quarter, 4 * quarter)

    @pl.loop(0, items[step * length])
    def _(pair):
        turn = 2 * pair + 1
        for span in spans:
            pointwise(turn + 1, raw_b, backward, (halves[3], halves[2]), span)
            summed(turn, left_a, columns_a, span)
            products(turn + 2, left_a, raw_a, span)
        source_sums(turn)
        for span in spans:
            pointwise(turn + 2, raw_a, forward, (halves[0], halves[1]), span)
            summed(turn + 1, left_b, columns_b, span)
            products(turn + 3, left_b, raw_b, span)

    for coord in range(3):
        back_ref[coord] = -0.5 * back[:, coord, :] - there[coord] * back[:, 6, :]
    if last:
        for coord in range(3):
            span = slice(base + coord * clusters, base + (coord + 1) * clusters)
            pos = [ref[span, :] for ref in local_refs]
            pos = jnp.concatenate(pos, axis=1).astype(jnp.float32)
            grad_ref[coord] = acc[:, width + coord, :] - pos * acc[:, width + 3, :]
        pot_ref[...] = acc[:, :rhs, :]
        pot_out_ref[...] = acc[:, rhs:width, :].astype(jnp.bfloat16)


def run_step(step, length, items, source, targets, locals_, rhs, width, carried, last):
    lhss, augs = zip(*targets)
    clusters, _, row_count = augs[0].shape
    subs = len(targets)
    panels = subs * row_count
    quarter = source.shape[1]
    first = carried is None
    vmem = pl.BlockSpec(memory_space=pltpu.VMEM)
    smem = pl.BlockSpec(memory_space=pltpu.SMEM)
    operands = (items, source, *lhss, *augs)
    if not first:
        operands += (carried,)
    acc_shape = (clusters, width + AUG, panels)
    back_shape = jax.ShapeDtypeStruct((3, clusters, quarter), jnp.float32)
    scratch = [
        pltpu.VMEM((clusters, AUG, quarter), jnp.float32),
        pltpu.VMEM((clusters, LANES, 2 * quarter), jnp.bfloat16),
        pltpu.VMEM((clusters, LANES, 2 * quarter), jnp.bfloat16),
        pltpu.VMEM((clusters + 8, quarter), jnp.float32),
        pltpu.VMEM((clusters, AUG, quarter), jnp.float32),
    ]
    scratch += [pltpu.VMEM((panels, 2 * quarter), jnp.float32)] * 2
    scratch += [pltpu.VMEM((panels, 4 * quarter), jnp.bfloat16)]
    if last:
        operands += tuple(locals_)
        out_shape = (
            jax.ShapeDtypeStruct((clusters, rhs, panels), jnp.float32),
            jax.ShapeDtypeStruct((clusters, width - rhs, panels), jnp.bfloat16),
            jax.ShapeDtypeStruct((3, clusters, panels), jnp.float32),
            back_shape,
        )
        scratch = [pltpu.VMEM(acc_shape, jnp.float32)] + scratch
    else:
        out_shape = (jax.ShapeDtypeStruct(acc_shape, jnp.float32), back_shape)
    pairs = (length - 6) * panels * quarter
    return pl.pallas_call(
        functools.partial(step_kernel, step, length, rhs, subs, first, last),
        out_shape=out_shape,
        in_specs=[smem] + [vmem] * (len(operands) - 1),
        out_specs=(vmem,) * len(out_shape),
        scratch_shapes=scratch,
        compiler_params=pltpu.CompilerParams(vmem_limit_bytes=20 * 1024 * 1024),
        cost_estimate=pl.CostEstimate(
            flops=2 * pairs * (2 * width + 3 * AUG), bytes_accessed=6 * 2**20, transcendentals=pairs
        ),
        name=f"near_field_{step}",
    )(*operands)


def node_kernel(grad_ref, jitter_ref, edge_ref, main_ref):
    clusters, panels = jitter_ref.shape
    wide = panels + 2 * LANES

    def spread_of(terms, jitter):
        side = jnp.zeros((terms.shape[0], LANES), jnp.float32)
        terms = 0.25 * terms
        spread = jnp.zeros((terms.shape[0], wide), jnp.float32)
        for offset in range(-jitter_reach, jitter_reach + 1):
            masked = jnp.where(jitter == offset, terms, 0.0)
            masked = jnp.concatenate([side, masked, side], axis=1)
            spread = spread + pltpu.roll(masked, offset % wide, 1)
        spread = spread + pltpu.roll(spread, 1, 1)
        return spread + pltpu.roll(spread, 32, 1)

    jitter = jitter_ref[...]
    row_at = lax.broadcasted_iota(jnp.int32, (clusters, LANES), 0)
    edge = edge_ref[...]
    edge_at = lax.broadcasted_iota(jnp.int32, edge.shape, 0)
    edge_jitter = jnp.where(edge_at < 3, edge[6:7], edge[7:8]).astype(jnp.int32)
    edge = spread_of(edge, edge_jitter)
    for coord in range(3):
        spread = spread_of(grad_ref[coord], jitter)
        below = spread[:, :LANES]
        above = spread[:, LANES + panels :]
        inner = spread[:, LANES : LANES + panels]
        before = edge[coord : coord + 1, LANES + panels :]
        after = edge[3 + coord : 4 + coord, :LANES]
        first = jnp.where(row_at == 0, before, pltpu.roll(above, 1, 0))
        last = jnp.where(row_at == clusters - 1, after, pltpu.roll(below, clusters - 1, 0))
        inner = jnp.concatenate(
            [
                inner[:, :LANES] + first,
                inner[:, LANES : panels - LANES],
                inner[:, panels - LANES :] + last,
            ],
            axis=1,
        )
        for cluster in range(clusters):
            main_ref[coord : coord + 1, cluster * panels : (cluster + 1) * panels] = inner[
                cluster : cluster + 1
            ]


def sum_kernel(*refs):
    total = refs[0][...]
    for ref in refs[1:-1]:
        total = total + ref[...].astype(jnp.float32)
    refs[-1][...] = total.astype(jnp.bfloat16)


def on_device(positions, areas, density, cotangent, matching, connect):
    clus_count = lax.axis_size("clus")
    sub_count = lax.axis_size("sub")
    rhs_count = lax.axis_size("rhs")
    device = lax.axis_index("clus")
    sub_place = lax.axis_index("sub")
    core = lax.axis_index("rhs")
    clusters, rhs, row_count = density.shape
    panels = row_count * sub_count
    quarter = row_count // rhs_count
    width = rhs * rhs_count
    vmem = pl.BlockSpec(memory_space=pltpu.VMEM)

    nodes_total = clus_count * clusters * panels

    by_coord = jnp.transpose(positions, (1, 0, 2))
    arguments = [
        pltpu.with_memory_space_constraint(array, pltpu.HBM)
        for array in (density, by_coord, areas, connect, cotangent)
    ]
    shapes = [(clusters * (rhs + 5), quarter)] + [(clusters * rhs, quarter)] * (rhs_count - 1)
    shapes.append((clusters * (rhs + 4), row_count))
    *parts, local = pl.pallas_call(
        functools.partial(prepare_kernel, (panels, nodes_total)),
        out_shape=[jax.ShapeDtypeStruct(shape, jnp.bfloat16) for shape in shapes],
        in_specs=[pl.BlockSpec(memory_space=pltpu.HBM)] * len(arguments),
        out_specs=[vmem] * len(shapes),
        scratch_shapes=[pltpu.VMEM(array.shape, array.dtype) for array in arguments]
        + [pltpu.SemaphoreType.DMA((len(arguments),))],
        compiler_params=pltpu.CompilerParams(vmem_limit_bytes=16 * 1024 * 1024),
        name="prepare",
    )(*arguments)
    ring = ring_order(clus_count)
    at_place = [ring.index(index) for index in range(clus_count)]
    ring_place = pick(device, at_place)

    def own_parts(parts, steps):
        arrived = [round_ring(parts[0], steps)]
        for step in range(1, rhs_count):

            def goal(z, c, step=step):
                return (ring[(at_place[z] + steps) % clus_count], c + step)

            arrived.append(moved(parts[step], ("clus", "rhs"), goal))
        return arrived

    arrived = own_parts(parts, 1)

    per_round = 2 * ((clusters // 2 + clus_count - 2) // (clus_count - 1))
    cap = ROUNDS * per_round
    partners = lax.dynamic_slice_in_dim(matching, device * clusters, clusters, 1).reshape(-1)
    here = jnp.tile(jnp.arange(clusters, dtype=jnp.int32), ROUNDS)
    code = here * (2 * clusters) + partners % clusters
    behind = (ring_place - pick(partners // clusters, at_place)) % clus_count
    total_items = ROUNDS * clusters
    order = jnp.arange(total_items, dtype=jnp.int32)
    rank = jnp.sum(
        ((behind[None, :] == behind[:, None]) & (order[None, :] < order[:, None])).astype(jnp.int32),
        axis=1,
    )
    steps = jnp.arange(1, clus_count, dtype=jnp.int32)
    member = behind[None, :] == steps[:, None]
    slots = jnp.arange(cap, dtype=jnp.int32)
    chosen = member[:, None, :] & (rank[None, None, :] == slots[None, :, None])
    listed = jnp.sum(jnp.where(chosen, code[None, None, :] - clusters, 0), axis=2) + clusters
    turns = (jnp.sum(member.astype(jnp.int32), axis=1) + 3) // 2
    length = cap + 6
    items = jnp.pad(listed, ((0, 0), (3, 3)), constant_values=clusters)
    items = jnp.concatenate([turns[:, None], items[:, 1:]], axis=1).reshape(-1)

    locals_ = [local] + [shifted(local, "sub", step) for step in range(1, sub_count)]
    blocks = [
        [block] + [shifted(block, "rhs", step) for step in range(1, rhs_count)] for block in locals_
    ]

    def in_order(blocks):
        return jnp.concatenate(
            [pick((sub_place - place) % sub_count, blocks) for place in range(sub_count)], axis=-1
        )

    jitter_all = in_order([block[clusters * (rhs + 3) :] for block in locals_]).astype(jnp.int32)
    targets = [
        pl.pallas_call(
            target_kernel,
            out_shape=(
                jax.ShapeDtypeStruct((clusters, row_count, LANES), jnp.bfloat16),
                jax.ShapeDtypeStruct((clusters, AUG, row_count), jnp.bfloat16),
            ),
            in_specs=[vmem] * rhs_count,
            out_specs=(vmem, vmem),
            scratch_shapes=[pltpu.VMEM((clusters, AUG, row_count), jnp.float32)],
            compiler_params=pltpu.CompilerParams(vmem_limit_bytes=16 * 1024 * 1024),
            cost_estimate=pl.CostEstimate(flops=2**20, bytes_accessed=2**18, transcendentals=0),
            name=f"targets_{place}",
        )(*blocks[place])
        for place in range(sub_count)
    ]

    arrived, targets = lax.optimization_barrier((arrived, targets))
    source = jnp.concatenate(arrived, axis=0)
    source, parts = lax.optimization_barrier((source, parts))
    from_next = own_parts(parts, -1) if clus_count > 2 else None
    carried = None
    backs, jitter_rows = [], [None]
    for step in range(1, clus_count):
        if 1 < step < clus_count - 1:
            if step > 2:
                source, backs[step - 3] = lax.optimization_barrier((source, backs[step - 3]))
            source = round_ring(source, 1)
        elif step > 1:
            from_next, backs[-1] = lax.optimization_barrier((from_next, backs[-1]))
            source = jnp.concatenate(from_next, axis=0)
        last = step == clus_count - 1
        results = run_step(
            step - 1, length, items, source, targets, locals_, rhs, width, carried, last
        )
        if last:
            pot, pot_out, grad, back = results
        else:
            carried, back = results
        backs.append(back)
        at = clusters * (rhs + 4)
        jitter_rows.append(source[at : at + clusters])

    grad = in_order([grad[..., at * row_count : (at + 1) * row_count] for at in range(sub_count)])
    low_part = (sub_place == 0) & (core == 0)
    high_part = (sub_place == sub_count - 1) & (core == rhs_count - 1)
    uppers = [grad[:, -1, -quarter:]] + [jnp.where(high_part, back[:, -1], 0.0) for back in backs]
    lowers = [grad[:, 0, :quarter]] + [jnp.where(low_part, back[:, 0], 0.0) for back in backs]

    def step_between(index, owner):
        return (at_place[index] - at_place[owner % clus_count]) % clus_count

    def needed(parts, step, offset):
        choices = []
        for index in range(clus_count):
            goal = ring[(at_place[index] - step) % clus_count]
            choices.append(parts[step_between(index, goal + offset)])
        return pick(device, choices)

    nothing = jnp.zeros((2, quarter), jnp.float32)
    returned = jnp.zeros((3, clusters, quarter), jnp.float32)
    upper, lower = needed(uppers, 0, -1), needed(lowers, 0, 1)
    for step in range(1, clus_count):
        rows = [
            backs[step - 1].reshape(3 * clusters, quarter),
            needed(uppers, step, -1),
            needed(lowers, step, 1),
            nothing,
        ]
        home = round_ring(jnp.concatenate(rows, axis=0), -step)
        returned = returned + home[: 3 * clusters].reshape(returned.shape)
        upper = upper + home[3 * clusters : 3 * clusters + 3]
        lower = lower + home[3 * clusters + 3 : 3 * clusters + 6]

    half = pot
    for step in range(1, rhs_count):
        arrived = shifted(pot_out[:, (step - 1) * rhs : step * rhs], "rhs", -step)
        half = half + arrived.astype(jnp.float32)

    half, grad = lax.optimization_barrier((half, grad))
    found = [half[..., :row_count]]
    for step in range(1, sub_count):
        sent = half[..., step * row_count : (step + 1) * row_count].astype(jnp.bfloat16)
        found.append(shifted(sent, "sub", -step))

    quarter_at = sub_place * rhs_count + core
    grad = grad + jnp.concatenate(
        [jnp.where(quarter_at == at, returned, 0.0) for at in range(sub_count * rhs_count)], axis=-1
    )
    share = clusters // sub_count

    blank = jnp.zeros((3, panels - quarter), jnp.float32)
    before = jnp.concatenate([blank, upper], axis=1)
    after = jnp.concatenate([lower, blank], axis=1)
    jitter_float = jitter_all.astype(jnp.float32)
    jitter_before = jnp.concatenate(
        [blank[:1], needed(jitter_rows, 0, -1)[clusters - 1 :].astype(jnp.float32)], axis=1
    )
    jitter_after = jnp.concatenate(
        [needed(jitter_rows, 0, 1)[:1].astype(jnp.float32), blank[:1]], axis=1
    )

    def edge_rows(at):
        first, end = at * share, (at + 1) * share
        inside = at < sub_count - 1
        return jnp.concatenate(
            [
                grad[:, first - 1] if at > 0 else before,
                grad[:, end] if inside else after,
                jnp.where(high_part, jitter_float[first - 1 : first] if at > 0 else jitter_before, 0.0),
                jnp.where(low_part, jitter_float[end : end + 1] if inside else jitter_after, 0.0),
            ],
            axis=0,
        ).reshape(-1, share, panels)

    def packed(place):
        return pick(
            place % sub_count,
            [
                jnp.concatenate([grad[:, at * share : (at + 1) * share], edge_rows(at)], axis=0)
                for at in range(sub_count)
            ],
        )

    summed = packed(sub_place)
    for step in range(1, sub_count):
        summed = summed + shifted(packed(sub_place + step), "sub", step)
    gathered = summed
    for step in range(1, rhs_count):
        gathered = gathered + shifted(summed, "rhs", step)
    own_jitter = pick(
        sub_place, [jitter_all[at * share : (at + 1) * share] for at in range(sub_count)]
    )
    node_grad = pl.pallas_call(
        node_kernel,
        out_shape=jax.ShapeDtypeStruct((3, share * panels), jnp.float32),
        in_specs=[vmem] * 3,
        out_specs=vmem,
        compiler_params=pltpu.CompilerParams(vmem_limit_bytes=16 * 1024 * 1024),
        cost_estimate=pl.CostEstimate(flops=2**20, bytes_accessed=2**18, transcendentals=0),
        name="node_terms",
    )(gathered[:3], own_jitter, gathered[3:].reshape(8, panels))
    potential = pl.pallas_call(
        sum_kernel,
        out_shape=jax.ShapeDtypeStruct((clusters, rhs, row_count), jnp.bfloat16),
        in_specs=[vmem] * sub_count,
        out_specs=vmem,
        compiler_params=pltpu.CompilerParams(vmem_limit_bytes=16 * 1024 * 1024),
        cost_estimate=pl.CostEstimate(flops=2**20, bytes_accessed=2**18, transcendentals=0),
        name="potential_sum",
    )(*found)
    return (potential, node_grad)


def solution(mesh):
    placed = (
        P(("groups", "clus"), None, "sub"),
        P(("groups", "clus"), "sub"),
        P(("groups", "clus"), "rhs", "sub"),
        P(("groups", "clus"), "rhs", "sub"),
        P(None, "groups"),
        P(("groups", "clus"), None, "sub"),
    )
    return jax.shard_map(
        on_device,
        mesh=mesh,
        in_specs=placed,
        out_specs=(P(("groups", "clus"), "rhs", "sub"), P(None, ("groups", "clus", "sub"))),
        check_vma=False,
    )
```

```python
import functools

import jax
import jax.numpy as jnp
from jax import lax
from jax.experimental import pallas as pl
from jax.experimental.pallas import tpu as pltpu
from jax.sharding import PartitionSpec as P

CP = 512
ROUNDS = 5

core_radius = 0.25
jitter_reach = 8
LANES = 128
AUG = 16


def shifted(value, axis, steps):
    count = lax.axis_size(axis)
    pairs = [(source, (source + steps) % count) for source in range(count)]
    return lax.ppermute(value, axis, pairs)


def ring_order(count):
    return [*range(0, count, 2), *reversed(range(1, count, 2))]


def round_ring(value, steps):
    order = ring_order(lax.axis_size("clus"))
    pairs = [(source, order[(at + steps) % len(order)]) for at, source in enumerate(order)]
    return lax.ppermute(value, "clus", pairs)


def moved(value, axes, target):
    counts = [lax.axis_size(axis) for axis in axes]
    pairs = []
    for major in range(counts[0]):
        for minor in range(counts[1]):
            goal = target(major, minor)
            if goal is not None:
                to_major, to_minor = goal[0] % counts[0], goal[1] % counts[1]
                pairs.append((major * counts[1] + minor, to_major * counts[1] + to_minor))
    return lax.ppermute(value, axes, pairs)


def three_parts(value):
    parts = []
    for _ in range(3):
        part = value.astype(jnp.bfloat16).astype(jnp.float32)
        parts.append(part)
        value = value - part
    return parts


def pick(index, choices):
    out = choices[0]
    for place in range(1, len(choices)):
        out = jnp.where(index == place, choices[place], out)
    return out


def fetched(arguments, places, sems):
    copies = []
    for at, (argument, place) in enumerate(zip(arguments, places)):
        copies.append(pltpu.make_async_copy(argument, place, sems.at[at]))
        copies[-1].start()
    for copy in copies:
        copy.wait()


def jitter_of(connect_ref, sizes):
    clusters, _, row_count = connect_ref.shape
    panels, nodes_total = sizes
    first_id = clusters * panels * lax.axis_index("clus") + row_count * lax.axis_index("sub")
    ids = lax.broadcasted_iota(jnp.int32, (clusters, row_count), 0) * panels
    ids = ids + lax.broadcasted_iota(jnp.int32, (clusters, row_count), 1) + first_id
    jitter = connect_ref[:, 0, :] - ids
    jitter = jnp.where(jitter > jitter_reach, jitter - nodes_total, jitter)
    jitter = jnp.where(jitter < -jitter_reach, jitter + nodes_total, jitter)
    return jitter.astype(jnp.float32).astype(jnp.bfloat16)


def prepare_kernel(sizes, *refs):
    arguments, part_refs, local_ref, scratch = refs[:5], refs[5:-7], refs[-7], refs[-6:]
    fetched(arguments, scratch[:5], scratch[5])
    density_ref, by_coord_ref, areas_ref, connect_ref, cot_ref = scratch[:5]
    clusters, rhs, _ = density_ref.shape
    quarter = part_refs[0].shape[1]
    count = len(part_refs)
    core = lax.axis_index("rhs")

    def part_of(array, place):
        return pick(place, [array[:, at * quarter : (at + 1) * quarter] for at in range(count)])

    pos = [by_coord_ref[coord] for coord in range(3)]
    jitter = jitter_of(connect_ref, sizes)
    base = clusters * rhs
    for cluster in range(clusters):
        dens = density_ref[cluster]
        span = slice(cluster * rhs, (cluster + 1) * rhs)
        local_ref[span, :] = cot_ref[cluster]
        for step, part_ref in enumerate(part_refs):
            part_ref[span, :] = part_of(dens, (core + step) % count)
    for at, value in enumerate([*pos, areas_ref[...], jitter]):
        part_refs[0][base + at * clusters : base + (at + 1) * clusters, :] = part_of(value, core)
    for at, value in enumerate([*pos, jitter]):
        local_ref[base + at * clusters : base + (at + 1) * clusters, :] = value


def target_kernel(*refs):
    local_refs, (lhs_ref, aug_ref, aug32) = refs[:-3], refs[-3:]
    clusters, _, row_count = aug_ref.shape
    rhs = local_refs[0].shape[0] // clusters - 4
    base = clusters * rhs
    pos = [
        local_refs[0][base + coord * clusters : base + (coord + 1) * clusters, :].astype(jnp.float32)
        for coord in range(3)
    ]
    square = pos[0] * pos[0] + pos[1] * pos[1] + pos[2] * pos[2] + core_radius * core_radius
    ones = jnp.ones_like(square)
    aug32[...] = jnp.zeros(aug32.shape, jnp.float32)
    for row, value in enumerate([-2.0 * value for value in pos] + three_parts(square) + [ones] * 3):
        aug32[:, row, :] = value
    blank = jnp.zeros((LANES - AUG - rhs * len(local_refs), row_count), jnp.bfloat16)
    for cluster in range(clusters):
        aug = aug32[cluster].astype(jnp.bfloat16)
        aug_ref[cluster] = aug
        rows = [ref[cluster * rhs : (cluster + 1) * rhs, :] for ref in local_refs]
        lhs_ref[cluster] = jnp.concatenate([*rows, aug, blank], axis=0).T


def step_kernel(step, length, rhs, subs, first, last, *refs):
    items, source_ref, refs = refs[0], refs[1], refs[2:]
    lhs_refs, aug_refs, refs = refs[:subs], refs[subs : 2 * subs], refs[2 * subs :]
    if not first:
        acc_in, refs = refs[0], refs[1:]
    if last:
        local_refs, refs = refs[:subs], refs[subs:]
        pot_ref, pot_out_ref, grad_ref, back_ref, acc = refs[:5]
        refs = refs[5:]
    else:
        acc, back_ref = refs[:2]
        refs = refs[2:]
    aug32, left_a, left_b, weight, back, raw_a, raw_b, both = refs
    clusters, rows, panels = acc.shape
    width = rows - AUG
    row_count = panels // subs
    quarter = source_ref.shape[1]
    base = clusters * rhs

    starts = [0] + list(range(base + 5 * clusters, source_ref.shape[0], base))

    there = [
        source_ref[base + coord * clusters : base + (coord + 1) * clusters, :].astype(jnp.float32)
        for coord in range(3)
    ]
    area = source_ref[base + 3 * clusters : base + 4 * clusters, :].astype(jnp.float32)
    square = there[0] * there[0] + there[1] * there[1] + there[2] * there[2]
    ones = jnp.ones_like(square)
    aug32[...] = jnp.zeros(aug32.shape, jnp.float32)
    for row, value in enumerate(there + [ones] * 3 + three_parts(square)):
        aug32[:, row, :] = value
    weight[...] = jnp.zeros(weight.shape, jnp.float32)
    weight[:clusters, :] = CP ** (-0.5) * area
    left_a[...] = jnp.zeros(left_a.shape, left_a.dtype)
    left_b[...] = jnp.zeros(left_b.shape, left_b.dtype)
    for cluster in range(clusters):
        distance_rows = aug32[cluster].astype(jnp.bfloat16)
        left_a[cluster, width:rows, quarter:] = distance_rows
        left_b[cluster, width:rows, :quarter] = distance_rows
        for place, at in enumerate(starts):
            span = slice(place * rhs, (place + 1) * rhs)
            dens = source_ref[at + cluster * rhs : at + (cluster + 1) * rhs, :]
            left_a[cluster, span, :quarter] = dens
            left_b[cluster, span, quarter:] = dens
    back[...] = jnp.zeros(back.shape, jnp.float32)
    if first:
        acc[...] = jnp.zeros(acc.shape, jnp.float32)
    else:
        acc[...] = acc_in[...]
    raw_b[...] = jnp.ones(raw_b.shape, jnp.float32)
    both[:, : 2 * quarter] = jnp.zeros((panels, 2 * quarter), both.dtype)

    halves = [slice(at * quarter, (at + 1) * quarter) for at in range(4)]

    def decoded(place):
        code = items[step * length + place]
        return code // (2 * clusters), code % (2 * clusters)

    part = max(2 * LANES, panels // 2)
    spans = [slice(start, start + part) for start in range(0, panels, part)]

    def products(place, left, raw, span):
        here, mate = decoded(place)
        lhs = jnp.concatenate([ref[here] for ref in lhs_refs], axis=0)[span]
        raw[span, :] = jnp.dot(lhs, left[mate % clusters], preferred_element_type=jnp.float32)

    def pointwise(place, raw, raw_halves, both_halves, span):
        _, mate = decoded(place)
        scale = weight[pl.ds(mate, 1), :]
        for start in range(span.start, span.stop, LANES):
            piece = slice(start, start + LANES)
            inverse = lax.rsqrt(raw[piece, raw_halves[1]])
            kernel = scale * inverse
            both[piece, both_halves[0]] = kernel.astype(jnp.bfloat16)
            weighted = (inverse * inverse) * (kernel * raw[piece, raw_halves[0]])
            both[piece, both_halves[1]] = weighted.astype(jnp.bfloat16)

    def summed(place, left, columns, span):
        here, mate = decoded(place)
        acc[here, :, span] += lax.dot_general(
            left[mate % clusters, :rows, :],
            both[span, columns],
            (((1,), (1,)), ((), ())),
            preferred_element_type=jnp.float32,
        )

    def source_sums(place):
        (here_a, mate_a), (here_b, mate_b) = decoded(place), decoded(place + 1)
        aug = jnp.concatenate(
            [
                jnp.concatenate([ref[here] for ref in aug_refs], axis=1)
                for here in (here_a, here_b)
            ],
            axis=0,
        )
        sums = jnp.dot(aug, both[:, quarter : 3 * quarter], preferred_element_type=jnp.float32)
        back[mate_a % clusters] += sums[:AUG, :quarter]
        back[mate_b % clusters] += sums[AUG:, quarter:]

    forward, backward = (halves[0], halves[1]), (halves[1], halves[0])
    columns_a, columns_b = slice(0, 2 * quarter), slice(2 * quarter, 4 * quarter)

    @pl.loop(0, items[step * length])
    def _(pair):
        turn = 2 * pair + 1
        for span in spans:
            pointwise(turn + 1, raw_b, backward, (halves[3], halves[2]), slice(span.start, span.start + LANES))
            summed(turn, left_a, columns_a, span)
            pointwise(turn + 1, raw_b, backward, (halves[3], halves[2]), slice(span.start + LANES, span.stop))
            products(turn + 2, left_a, raw_a, span)
        source_sums(turn)
        for span in spans:
            pointwise(turn + 2, raw_a, forward, (halves[0], halves[1]), slice(span.start, span.start + LANES))
            summed(turn + 1, left_b, columns_b, span)
            pointwise(turn + 2, raw_a, forward, (halves[0], halves[1]), slice(span.start + LANES, span.stop))
            products(turn + 3, left_b, raw_b, span)

    for coord in range(3):
        back_ref[coord] = -0.5 * back[:, coord, :] - there[coord] * back[:, 6, :]
    if last:
        for coord in range(3):
            span = slice(base + coord * clusters, base + (coord + 1) * clusters)
            pos = [ref[span, :] for ref in local_refs]
            pos = jnp.concatenate(pos, axis=1).astype(jnp.float32)
            grad_ref[coord] = acc[:, width + coord, :] - pos * acc[:, width + 3, :]
        pot_ref[...] = acc[:, :rhs, :]
        pot_out_ref[...] = acc[:, rhs:width, :].astype(jnp.bfloat16)


def run_step(step, length, items, source, targets, locals_, rhs, width, carried, last):
    lhss, augs = zip(*targets)
    clusters, _, row_count = augs[0].shape
    subs = len(targets)
    panels = subs * row_count
    quarter = source.shape[1]
    first = carried is None
    vmem = pl.BlockSpec(memory_space=pltpu.VMEM)
    smem = pl.BlockSpec(memory_space=pltpu.SMEM)
    operands = (items, source, *lhss, *augs)
    if not first:
        operands += (carried,)
    acc_shape = (clusters, width + AUG, panels)
    back_shape = jax.ShapeDtypeStruct((3, clusters, quarter), jnp.float32)
    scratch = [
        pltpu.VMEM((clusters, AUG, quarter), jnp.float32),
        pltpu.VMEM((clusters, LANES, 2 * quarter), jnp.bfloat16),
        pltpu.VMEM((clusters, LANES, 2 * quarter), jnp.bfloat16),
        pltpu.VMEM((clusters + 8, quarter), jnp.float32),
        pltpu.VMEM((clusters, AUG, quarter), jnp.float32),
    ]
    scratch += [pltpu.VMEM((panels, 2 * quarter), jnp.float32)] * 2
    scratch += [pltpu.VMEM((panels, 4 * quarter), jnp.bfloat16)]
    if last:
        operands += tuple(locals_)
        out_shape = (
            jax.ShapeDtypeStruct((clusters, rhs, panels), jnp.float32),
            jax.ShapeDtypeStruct((clusters, width - rhs, panels), jnp.bfloat16),
            jax.ShapeDtypeStruct((3, clusters, panels), jnp.float32),
            back_shape,
        )
        scratch = [pltpu.VMEM(acc_shape, jnp.float32)] + scratch
    else:
        out_shape = (jax.ShapeDtypeStruct(acc_shape, jnp.float32), back_shape)
    pairs = (length - 6) * panels * quarter
    return pl.pallas_call(
        functools.partial(step_kernel, step, length, rhs, subs, first, last),
        out_shape=out_shape,
        in_specs=[smem] + [vmem] * (len(operands) - 1),
        out_specs=(vmem,) * len(out_shape),
        scratch_shapes=scratch,
        compiler_params=pltpu.CompilerParams(vmem_limit_bytes=20 * 1024 * 1024),
        cost_estimate=pl.CostEstimate(
            flops=2 * pairs * (2 * width + 3 * AUG), bytes_accessed=6 * 2**20, transcendentals=pairs
        ),
        name=f"near_field_{step}",
    )(*operands)


def node_kernel(grad_ref, jitter_ref, edge_ref, main_ref):
    clusters, panels = jitter_ref.shape
    wide = panels + 2 * LANES

    def spread_of(terms, jitter):
        side = jnp.zeros((terms.shape[0], LANES), jnp.float32)
        terms = 0.25 * terms
        spread = jnp.zeros((terms.shape[0], wide), jnp.float32)
        for offset in range(-jitter_reach, jitter_reach + 1):
            masked = jnp.where(jitter == offset, terms, 0.0)
            masked = jnp.concatenate([side, masked, side], axis=1)
            spread = spread + pltpu.roll(masked, offset % wide, 1)
        spread = spread + pltpu.roll(spread, 1, 1)
        return spread + pltpu.roll(spread, 32, 1)

    jitter = jitter_ref[...]
    row_at = lax.broadcasted_iota(jnp.int32, (clusters, LANES), 0)
    edge = edge_ref[...]
    edge_at = lax.broadcasted_iota(jnp.int32, edge.shape, 0)
    edge_jitter = jnp.where(edge_at < 3, edge[6:7], edge[7:8]).astype(jnp.int32)
    edge = spread_of(edge, edge_jitter)
    for coord in range(3):
        spread = spread_of(grad_ref[coord], jitter)
        below = spread[:, :LANES]
        above = spread[:, LANES + panels :]
        inner = spread[:, LANES : LANES + panels]
        before = edge[coord : coord + 1, LANES + panels :]
        after = edge[3 + coord : 4 + coord, :LANES]
        first = jnp.where(row_at == 0, before, pltpu.roll(above, 1, 0))
        last = jnp.where(row_at == clusters - 1, after, pltpu.roll(below, clusters - 1, 0))
        inner = jnp.concatenate(
            [
                inner[:, :LANES] + first,
                inner[:, LANES : panels - LANES],
                inner[:, panels - LANES :] + last,
            ],
            axis=1,
        )
        for cluster in range(clusters):
            main_ref[coord : coord + 1, cluster * panels : (cluster + 1) * panels] = inner[
                cluster : cluster + 1
            ]


def sum_kernel(*refs):
    total = refs[0][...]
    for ref in refs[1:-1]:
        total = total + ref[...].astype(jnp.float32)
    refs[-1][...] = total.astype(jnp.bfloat16)


def on_device(positions, areas, density, cotangent, matching, connect):
    clus_count = lax.axis_size("clus")
    sub_count = lax.axis_size("sub")
    rhs_count = lax.axis_size("rhs")
    device = lax.axis_index("clus")
    sub_place = lax.axis_index("sub")
    core = lax.axis_index("rhs")
    clusters, rhs, row_count = density.shape
    panels = row_count * sub_count
    quarter = row_count // rhs_count
    width = rhs * rhs_count
    vmem = pl.BlockSpec(memory_space=pltpu.VMEM)

    nodes_total = clus_count * clusters * panels

    by_coord = jnp.transpose(positions, (1, 0, 2))
    arguments = [
        pltpu.with_memory_space_constraint(array, pltpu.HBM)
        for array in (density, by_coord, areas, connect, cotangent)
    ]
    shapes = [(clusters * (rhs + 5), quarter)] + [(clusters * rhs, quarter)] * (rhs_count - 1)
    shapes.append((clusters * (rhs + 4), row_count))
    *parts, local = pl.pallas_call(
        functools.partial(prepare_kernel, (panels, nodes_total)),
        out_shape=[jax.ShapeDtypeStruct(shape, jnp.bfloat16) for shape in shapes],
        in_specs=[pl.BlockSpec(memory_space=pltpu.HBM)] * len(arguments),
        out_specs=[vmem] * len(shapes),
        scratch_shapes=[pltpu.VMEM(array.shape, array.dtype) for array in arguments]
        + [pltpu.SemaphoreType.DMA((len(arguments),))],
        compiler_params=pltpu.CompilerParams(vmem_limit_bytes=16 * 1024 * 1024),
        name="prepare",
    )(*arguments)
    ring = ring_order(clus_count)
    at_place = [ring.index(index) for index in range(clus_count)]
    ring_place = pick(device, at_place)

    def own_parts(parts, steps):
        arrived = [round_ring(parts[0], steps)]
        for step in range(1, rhs_count):

            def goal(z, c, step=step):
                return (ring[(at_place[z] + steps) % clus_count], c + step)

            arrived.append(moved(parts[step], ("clus", "rhs"), goal))
        return arrived

    arrived = own_parts(parts, 1)

    per_round = 2 * ((clusters // 2 + clus_count - 2) // (clus_count - 1))
    cap = ROUNDS * per_round
    partners = lax.dynamic_slice_in_dim(matching, device * clusters, clusters, 1).reshape(-1)
    here = jnp.tile(jnp.arange(clusters, dtype=jnp.int32), ROUNDS)
    code = here * (2 * clusters) + partners % clusters
    behind = (ring_place - pick(partners // clusters, at_place)) % clus_count
    total_items = ROUNDS * clusters
    order = jnp.arange(total_items, dtype=jnp.int32)
    rank = jnp.sum(
        ((behind[None, :] == behind[:, None]) & (order[None, :] < order[:, None])).astype(jnp.int32),
        axis=1,
    )
    steps = jnp.arange(1, clus_count, dtype=jnp.int32)
    member = behind[None, :] == steps[:, None]
    slots = jnp.arange(cap, dtype=jnp.int32)
    chosen = member[:, None, :] & (rank[None, None, :] == slots[None, :, None])
    listed = jnp.sum(jnp.where(chosen, code[None, None, :] - clusters, 0), axis=2) + clusters
    turns = (jnp.sum(member.astype(jnp.int32), axis=1) + 3) // 2
    length = cap + 6
    items = jnp.pad(listed, ((0, 0), (3, 3)), constant_values=clusters)
    items = jnp.concatenate([turns[:, None], items[:, 1:]], axis=1).reshape(-1)

    locals_ = [local] + [shifted(local, "sub", step) for step in range(1, sub_count)]
    blocks = [
        [block] + [shifted(block, "rhs", step) for step in range(1, rhs_count)] for block in locals_
    ]

    def in_order(blocks):
        return jnp.concatenate(
            [pick((sub_place - place) % sub_count, blocks) for place in range(sub_count)], axis=-1
        )

    jitter_all = in_order([block[clusters * (rhs + 3) :] for block in locals_]).astype(jnp.int32)
    targets = [
        pl.pallas_call(
            target_kernel,
            out_shape=(
                jax.ShapeDtypeStruct((clusters, row_count, LANES), jnp.bfloat16),
                jax.ShapeDtypeStruct((clusters, AUG, row_count), jnp.bfloat16),
            ),
            in_specs=[vmem] * rhs_count,
            out_specs=(vmem, vmem),
            scratch_shapes=[pltpu.VMEM((clusters, AUG, row_count), jnp.float32)],
            compiler_params=pltpu.CompilerParams(vmem_limit_bytes=16 * 1024 * 1024),
            cost_estimate=pl.CostEstimate(flops=2**20, bytes_accessed=2**18, transcendentals=0),
            name=f"targets_{place}",
        )(*blocks[place])
        for place in range(sub_count)
    ]

    arrived, targets = lax.optimization_barrier((arrived, targets))
    source = jnp.concatenate(arrived, axis=0)
    source, parts = lax.optimization_barrier((source, parts))
    from_next = own_parts(parts, -1) if clus_count > 2 else None
    carried = None
    backs, jitter_rows = [], [None]
    for step in range(1, clus_count):
        if 1 < step < clus_count - 1:
            if step > 2:
                source, backs[step - 3] = lax.optimization_barrier((source, backs[step - 3]))
            source = round_ring(source, 1)
        elif step > 1:
            from_next, backs[-1] = lax.optimization_barrier((from_next, backs[-1]))
            source = jnp.concatenate(from_next, axis=0)
        last = step == clus_count - 1
        results = run_step(
            step - 1, length, items, source, targets, locals_, rhs, width, carried, last
        )
        if last:
            pot, pot_out, grad, back = results
        else:
            carried, back = results
        backs.append(back)
        at = clusters * (rhs + 4)
        jitter_rows.append(source[at : at + clusters])

    grad = in_order([grad[..., at * row_count : (at + 1) * row_count] for at in range(sub_count)])
    low_part = (sub_place == 0) & (core == 0)
    high_part = (sub_place == sub_count - 1) & (core == rhs_count - 1)
    uppers = [grad[:, -1, -quarter:]] + [jnp.where(high_part, back[:, -1], 0.0) for back in backs]
    lowers = [grad[:, 0, :quarter]] + [jnp.where(low_part, back[:, 0], 0.0) for back in backs]

    def step_between(index, owner):
        return (at_place[index] - at_place[owner % clus_count]) % clus_count

    def needed(parts, step, offset):
        choices = []
        for index in range(clus_count):
            goal = ring[(at_place[index] - step) % clus_count]
            choices.append(parts[step_between(index, goal + offset)])
        return pick(device, choices)

    nothing = jnp.zeros((2, quarter), jnp.float32)
    returned = jnp.zeros((3, clusters, quarter), jnp.float32)
    upper, lower = needed(uppers, 0, -1), needed(lowers, 0, 1)
    for step in range(1, clus_count):
        rows = [
            backs[step - 1].reshape(3 * clusters, quarter),
            needed(uppers, step, -1),
            needed(lowers, step, 1),
            nothing,
        ]
        home = round_ring(jnp.concatenate(rows, axis=0), -step)
        returned = returned + home[: 3 * clusters].reshape(returned.shape)
        upper = upper + home[3 * clusters : 3 * clusters + 3]
        lower = lower + home[3 * clusters + 3 : 3 * clusters + 6]

    half = pot
    for step in range(1, rhs_count):
        arrived = shifted(pot_out[:, (step - 1) * rhs : step * rhs], "rhs", -step)
        half = half + arrived.astype(jnp.float32)

    half, grad = lax.optimization_barrier((half, grad))
    found = [half[..., :row_count]]
    for step in range(1, sub_count):
        sent = half[..., step * row_count : (step + 1) * row_count].astype(jnp.bfloat16)
        found.append(shifted(sent, "sub", -step))

    quarter_at = sub_place * rhs_count + core
    grad = grad + jnp.concatenate(
        [jnp.where(quarter_at == at, returned, 0.0) for at in range(sub_count * rhs_count)], axis=-1
    )
    share = clusters // sub_count

    blank = jnp.zeros((3, panels - quarter), jnp.float32)
    before = jnp.concatenate([blank, upper], axis=1)
    after = jnp.concatenate([lower, blank], axis=1)
    jitter_float = jitter_all.astype(jnp.float32)
    jitter_before = jnp.concatenate(
        [blank[:1], needed(jitter_rows, 0, -1)[clusters - 1 :].astype(jnp.float32)], axis=1
    )
    jitter_after = jnp.concatenate(
        [needed(jitter_rows, 0, 1)[:1].astype(jnp.float32), blank[:1]], axis=1
    )

    def edge_rows(at):
        first, end = at * share, (at + 1) * share
        inside = at < sub_count - 1
        return jnp.concatenate(
            [
                grad[:, first - 1] if at > 0 else before,
                grad[:, end] if inside else after,
                jnp.where(high_part, jitter_float[first - 1 : first] if at > 0 else jitter_before, 0.0),
                jnp.where(low_part, jitter_float[end : end + 1] if inside else jitter_after, 0.0),
            ],
            axis=0,
        ).reshape(-1, share, panels)

    def packed(place):
        return pick(
            place % sub_count,
            [
                jnp.concatenate([grad[:, at * share : (at + 1) * share], edge_rows(at)], axis=0)
                for at in range(sub_count)
            ],
        )

    summed = packed(sub_place)
    for step in range(1, sub_count):
        summed = summed + shifted(packed(sub_place + step), "sub", step)
    gathered = summed
    for step in range(1, rhs_count):
        gathered = gathered + shifted(summed, "rhs", step)
    own_jitter = pick(
        sub_place, [jitter_all[at * share : (at + 1) * share] for at in range(sub_count)]
    )
    node_grad = pl.pallas_call(
        node_kernel,
        out_shape=jax.ShapeDtypeStruct((3, share * panels), jnp.float32),
        in_specs=[vmem] * 3,
        out_specs=vmem,
        compiler_params=pltpu.CompilerParams(vmem_limit_bytes=16 * 1024 * 1024),
        cost_estimate=pl.CostEstimate(flops=2**20, bytes_accessed=2**18, transcendentals=0),
        name="node_terms",
    )(gathered[:3], own_jitter, gathered[3:].reshape(8, panels))
    potential = pl.pallas_call(
        sum_kernel,
        out_shape=jax.ShapeDtypeStruct((clusters, rhs, row_count), jnp.bfloat16),
        in_specs=[vmem] * sub_count,
        out_specs=vmem,
        compiler_params=pltpu.CompilerParams(vmem_limit_bytes=16 * 1024 * 1024),
        cost_estimate=pl.CostEstimate(flops=2**20, bytes_accessed=2**18, transcendentals=0),
        name="potential_sum",
    )(*found)
    return (potential, node_grad)


def solution(mesh):
    placed = (
        P(("groups", "clus"), None, "sub"),
        P(("groups", "clus"), "sub"),
        P(("groups", "clus"), "rhs", "sub"),
        P(("groups", "clus"), "rhs", "sub"),
        P(None, "groups"),
        P(("groups", "clus"), None, "sub"),
    )
    return jax.shard_map(
        on_device,
        mesh=mesh,
        in_specs=placed,
        out_specs=(P(("groups", "clus"), "rhs", "sub"), P(None, ("groups", "clus", "sub"))),
        check_vma=False,
    )
```
